32 devices in a mesh: parts: 2 (over y), sect: 4 (over z), tp: 2 (over x), sub: 2 (over core).
Axes of the slice: x: 2, y: 2, z: 4, core: 2. Of those that a mesh axis runs over, the one named last changes fastest.
Arguments:
- prompt_keys: bfloat16 [8, 8192, 1024], P(('parts', 'sect'), 'sub', 'tp'), parts along dimension 0, may hold values from -6 to 6
- prompt_values: bfloat16 [8, 8192, 1024], P(('parts', 'sect'), 'sub', 'tp'), parts along dimension 0, may hold values from -6 to 6
- lengths: int32 [8], P(('parts', 'sect')), parts along dimension 0, may hold values from 2048 to 8192, as said below
- feature_weight: bfloat16 [8, 128, 128], P('tp'), may hold values from -3 to 3
- queries: bfloat16 [64, 8192], P(('parts', 'sect', 'sub'), 'tp'), parts along dimension 0, may hold values from -6 to 6
- new_keys: bfloat16 [64, 1024], P(('parts', 'sect', 'sub'), 'tp'), parts along dimension 0, may hold values from -6 to 6
- new_values: bfloat16 [64, 1024], P(('parts', 'sect', 'sub'), 'tp'), parts along dimension 0, may hold values from -6 to 6
- row_prompt: int32 [64], P('parts'), parts along dimension 0, may hold values from 0 to 3, as said below
Outputs:
- decoded: bfloat16 [64, 8192], P(('parts', 'sect', 'sub'), 'tp'), parts along dimension 0
The draws below stay inside these ranges and needn't reach their ends.
There are 2 independent parts, one for each index of `parts`. The reference program is written for one: setup_inputs(seed, part) draws one part's arguments, and reference() takes and returns one part's arrays. A program takes and returns all parts, laid end to end along the dimension named above; an argument that names none is the same for every part. Nothing has to cross between parts.
Inputs may be any that keep to these rules, and one draw needn't show every extreme that they name: `lengths`: each prompt holds 2048 to 8192 tokens; some prompt holds exactly 8192. `row_prompt`: every prompt is continued by at least one decode row; the rows are spread unevenly over the prompts.
All inputs are finite; a program needn't handle non-finite values.
Results may differ from the reference program's by a relative error of at most 0.0045.
Values may be sent and summed in bfloat16 or wider, within the bound.
No kernel may reach another device: no remote copies, remote signals or barrier semaphores. Data moves between devices by JAX's collectives and lax.ppermute only.
A program may use at most 64 MiB of HBM per device.

```python
import jax
import jax.numpy as jnp
from jax import lax

HEADS = 64
KVH = 8
DH = 128
FEAT = 128
WINDOW = 64
PMAX = 8192
GROUP = 8
PROMPTS = 4
ROWS = 32


def prompt_base(key):
    drawing, scaling = jax.random.split(key, 2)
    base = jax.random.normal(drawing, (PROMPTS, PMAX, KVH, DH), jnp.float32)
    channel = jnp.exp(jax.random.uniform(scaling, (PROMPTS, 1, KVH, DH), jnp.float32, -0.35, 0.35))
    return jnp.clip(base * channel, -6.0, 6.0)


def draw_prompt_keys(key, part):
    keys = prompt_base(key)
    return keys.reshape(PROMPTS, PMAX, KVH * DH).astype(jnp.bfloat16)


def draw_prompt_values(key, part):
    keys = prompt_base(key)
    key = jax.random.fold_in(key, 37)
    ordering, signing = jax.random.split(key, 2)
    orders = jax.vmap(lambda k: jax.random.permutation(k, DH))(jax.random.split(ordering, KVH)).astype(jnp.int32)
    moved = jnp.stack([jnp.take(keys[:, :, head], orders[head], axis=-1) for head in range(KVH)], axis=2)
    signs = jnp.where(jax.random.bernoulli(signing, 0.5, (PROMPTS, 1, KVH, DH)), 1.0, -1.0).astype(jnp.float32)
    values = jnp.clip(2.0 * signs * moved, -6.0, 6.0)
    return values.reshape(PROMPTS, PMAX, KVH * DH).astype(jnp.bfloat16)


def draw_lengths(key, part):
    key = jax.random.fold_in(key, 11)
    drawing, picking = jax.random.split(key)
    drawn = jax.random.randint(drawing, (PROMPTS,), PMAX // 4, PMAX + 1)
    longest = jax.random.randint(picking, (), 0, PROMPTS)
    return jnp.where(jnp.arange(PROMPTS) == longest, PMAX, drawn).astype(jnp.int32)


def draw_row_prompt(key, part):
    key = jax.random.fold_in(key, 23)
    streams = jax.random.split(key, 5)
    covering = jax.random.permutation(streams[0], PROMPTS).astype(jnp.int32)
    extra_rows = ROWS - PROMPTS
    lower = jax.random.randint(streams[1], (extra_rows,), 0, PROMPTS)
    upper = jax.random.randint(streams[2], (extra_rows,), 0, PROMPTS)
    relabel = jax.random.permutation(streams[3], PROMPTS).astype(jnp.int32)
    skewed = jnp.take(relabel, jnp.minimum(lower, upper))
    joined = jnp.concatenate([covering, skewed.astype(jnp.int32)])
    return jax.random.permutation(streams[4], joined).astype(jnp.int32)


def levels(key, extent, cuts, low, largest):
    level, own = 1.0, jax.random.fold_in(key, 6)
    for position, blocks in cuts:
        draws = jnp.exp(jax.random.uniform(jax.random.fold_in(own, position), (blocks,), jnp.float32, low / len(cuts), largest / len(cuts)))
        level = level * jnp.repeat(draws, extent[position] // blocks).reshape([-1 if axis == position else 1 for axis in range(len(extent))])
    return level


def centred(key, shape, scale, most, cuts=(), kind=jnp.bfloat16):
    values = jax.random.normal(key, shape, jnp.float32) * scale
    if len(cuts) > 0:
        values = levels(key, shape, cuts, -0.22, 0.18) * values
    return jnp.clip(values, min=-most, max=most).astype(kind)


def setup_inputs(seed: int = 0, part: int = 0) -> dict:
    splits = jax.random.split(jax.random.key(seed), 9)
    part_splits = jax.random.split(jax.random.fold_in(splits[8], part), 9)
    prompt_keys = draw_prompt_keys(jax.random.fold_in(jax.random.fold_in(splits[8], part), 71), part)
    prompt_values = draw_prompt_values(jax.random.fold_in(jax.random.fold_in(splits[8], part), 71), part)
    lengths = draw_lengths(jax.random.fold_in(jax.random.fold_in(splits[8], part), 71), part)
    feature_weight = centred(splits[3], (KVH, DH, FEAT), (max(DH // 32, 1)) ** -0.5, 3.0, ((0, 2),))
    queries = centred(part_splits[4], (ROWS, HEADS * DH), 1.0, 6.0, ((0, 8), (1, 2)))
    new_keys = centred(part_splits[5], (ROWS, KVH * DH), 1.0, 6.0, ((0, 8), (1, 2)))
    new_values = centred(part_splits[6], (ROWS, KVH * DH), 1.0, 6.0, ((0, 8), (1, 2)))
    row_prompt = draw_row_prompt(jax.random.fold_in(jax.random.fold_in(splits[8], part), 71), part)
    return dict(prompt_keys=prompt_keys, prompt_values=prompt_values, lengths=lengths, feature_weight=feature_weight, queries=queries, new_keys=new_keys, new_values=new_values, row_prompt=row_prompt)


TAU = 10.0
EPS = 1e-06

def unit_rows(values):
    wide = values.astype(jnp.float32)
    return wide * lax.rsqrt(lax.optimization_barrier(jnp.mean(wide * wide, axis=-1, keepdims=True)) + EPS)

def featurize(values, weight, form):
    proj = jnp.einsum(form, values.astype(jnp.float32), weight.astype(jnp.float32), precision=lax.Precision.HIGHEST)
    return ((jax.nn.elu(proj) + 1.0) / FEAT).astype(jnp.bfloat16)

def reference(prompt_keys, prompt_values, lengths, feature_weight, queries, new_keys, new_values, row_prompt):

    def prefill(inputs):
        keys, values, length = inputs
        keys_heads = keys.reshape(PMAX, KVH, DH)
        values_heads = values.reshape(PMAX, KVH, DH).astype(jnp.float32)
        mapped = featurize(keys_heads, feature_weight, 'tgd,gdf->tgf')
        live = jnp.arange(PMAX, dtype=jnp.int32) < length - WINDOW
        mapped = jnp.where(live[:, None, None], mapped, jnp.zeros_like(mapped))
        mapped = lax.optimization_barrier(mapped).astype(jnp.float32)
        state = jnp.einsum('tgf,tgd->gfd', mapped, values_heads, precision=lax.Precision.HIGHEST)
        norms = lax.optimization_barrier(jnp.sum(mapped, axis=0))
        start = (length - WINDOW).astype(jnp.int32)
        recent_keys = lax.dynamic_slice_in_dim(keys, start, WINDOW, 0)
        recent_values = lax.dynamic_slice_in_dim(values, start, WINDOW, 0)
        return (state, norms, recent_keys, recent_values)
    states, norms, recent_keys, recent_values = lax.map(prefill, (prompt_keys, prompt_values, lengths))
    rows = queries.reshape(ROWS, KVH, GROUP, DH)
    phi = featurize(rows, feature_weight, 'rgqd,gdf->rgqf')
    phi = lax.optimization_barrier(phi).astype(jnp.float32)
    row_states = states[row_prompt]
    row_norms = norms[row_prompt]
    linear_num = jnp.einsum('rgqf,rgfd->rgqd', phi, row_states, precision=lax.Precision.HIGHEST)
    linear_den = jnp.einsum('rgqf,rgf->rgq', phi, row_norms, precision=lax.Precision.HIGHEST)
    window_keys = jnp.concatenate([recent_keys[row_prompt], new_keys[:, None, :]], axis=1).reshape(ROWS, WINDOW + 1, KVH, DH)
    window_values = jnp.concatenate([recent_values[row_prompt], new_values[:, None, :]], axis=1).reshape(ROWS, WINDOW + 1, KVH, DH)
    scores = TAU / DH * jnp.einsum('rgqd,rwgd->rgqw', unit_rows(rows), unit_rows(window_keys), precision=lax.Precision.HIGHEST)
    weights = jnp.exp(scores)
    rounded = lax.optimization_barrier(weights.astype(jnp.bfloat16)).astype(jnp.float32)
    denominator = linear_den + lax.optimization_barrier(jnp.sum(weights, axis=-1))
    numerator = linear_num + jnp.einsum('rgqw,rwgd->rgqd', rounded, window_values.astype(jnp.float32), precision=lax.Precision.HIGHEST)
    return (numerator / denominator[..., None]).astype(jnp.bfloat16).reshape(ROWS, HEADS * DH)
```

```python
import functools

import jax
import jax.numpy as jnp
from jax import lax
from jax.experimental import pallas as pl
from jax.experimental.pallas import tpu as pltpu
from jax.sharding import PartitionSpec as P

WINDOW = 64
TAU = 10.0
EPS = 1e-06
BLOCK = 512
NT = (((1,), (1,)), ((), ()))


def feature(proj):
    return jnp.maximum(proj, 0.0) + jnp.exp(jnp.minimum(proj, 0.0))


def prefill_kernel(limit_ref, keys_ref, values_ref, weight_ref, out_ref, wide_ref, state_ref, norm_ref):
    step = pl.program_id(0)
    heads, head_size, feats = weight_ref.shape
    pairs = heads // 2
    block = keys_ref.shape[1]

    @pl.when(step == 0)
    def _():
        wide_ref[...] = jnp.zeros_like(wide_ref)
        state_ref[...] = jnp.zeros_like(state_ref)
        norm_ref[...] = jnp.zeros_like(norm_ref)
        for g in range(heads):
            half = g % 2
            turned = weight_ref[g].astype(jnp.float32).T.astype(jnp.bfloat16)
            wide_ref[g // 2, half * feats : (half + 1) * feats, half * head_size : (half + 1) * head_size] = turned

    position = step * block + lax.broadcasted_iota(jnp.int32, (1, block), 1)
    live = position < limit_ref[0]
    for j in range(pairs):
        cols = slice(j * 2 * head_size, (j + 1) * 2 * head_size)
        proj = lax.dot_general(wide_ref[j], keys_ref[0, :, cols], NT, preferred_element_type=jnp.float32)
        mapped = jnp.where(live, feature(proj), 0.0)
        total = norm_ref[j]
        for c in range(block // 128):
            total = total + mapped[:, c * 128 : (c + 1) * 128]
        norm_ref[j] = total
        state_ref[j] += jnp.dot(
            mapped.astype(jnp.bfloat16), values_ref[0, :, cols], preferred_element_type=jnp.float32
        )

    @pl.when(step == pl.num_programs(0) - 1)
    def _():
        out_ref[heads * feats :, :] = jnp.zeros((out_ref.shape[0] - heads * feats, head_size), jnp.bfloat16)
        rows = []
        for g in range(heads):
            half = g % 2
            part = state_ref[g // 2, half * feats : (half + 1) * feats, half * head_size : (half + 1) * head_size]
            out_ref[g * feats : (g + 1) * feats, :] = part.astype(jnp.bfloat16)
            sums = norm_ref[g // 2, half * feats : (half + 1) * feats, :]
            rows.append(jnp.sum(sums.T, axis=0, keepdims=True))
        pad = out_ref.shape[0] - heads * feats - heads
        rows.append(jnp.zeros((pad, head_size), jnp.float32))
        out_ref[heads * feats :, :] = jnp.concatenate(rows, axis=0).astype(jnp.bfloat16)


def prefill(keys, values, weight, limit):
    heads, head_size, feats = weight.shape
    span, width = keys.shape[1:]
    spec = pl.BlockSpec((1, BLOCK, width), lambda i: (0, i, 0))
    return pl.pallas_call(
        prefill_kernel,
        grid=(span // BLOCK,),
        in_specs=[
            pl.BlockSpec(memory_space=pltpu.SMEM),
            spec,
            spec,
            pl.BlockSpec(memory_space=pltpu.VMEM),
        ],
        out_specs=pl.BlockSpec(memory_space=pltpu.VMEM),
        out_shape=jax.ShapeDtypeStruct((heads * feats + 16, head_size), jnp.bfloat16),
        scratch_shapes=[
            pltpu.VMEM((heads // 2, 2 * feats, 2 * head_size), jnp.bfloat16),
            pltpu.VMEM((heads // 2, 2 * feats, 2 * head_size), jnp.float32),
            pltpu.VMEM((heads // 2, 2 * feats, 128), jnp.float32),
        ],
        compiler_params=pltpu.CompilerParams(vmem_limit_bytes=32 * 1024 * 1024),
        cost_estimate=pl.CostEstimate(
            flops=4 * span * width * feats, bytes_accessed=4 * span * width, transcendentals=span * width
        ),
        name="prefill",
    )(limit, keys, values, weight)


def decode_kernel(
    info_ref, rows_ref, weight_ref, state_a_ref, state_b_ref, near_a_ref, near_b_ref, *out_refs
):
    heads, head_size, feats = weight_ref.shape
    count = rows_ref.shape[0]
    group = (rows_ref.shape[1] - 2 * heads * head_size) // (heads * head_size)
    keys_at = heads * group * head_size
    values_at = keys_at + heads * head_size
    each = count // len(out_refs)
    window = near_a_ref.shape[1]
    slot = lax.broadcasted_iota(jnp.int32, (1, 2 * window), 1)
    place = jnp.where(slot < window, slot + info_ref[0], slot - window + info_ref[1])
    seen = (place >= info_ref[2] - window) & (place < info_ref[2])
    for g in range(heads):
        cols = slice(g * head_size, (g + 1) * head_size)
        query = jnp.concatenate(
            [
                rows_ref[:, (g * group + h) * head_size : (g * group + h + 1) * head_size]
                for h in range(group)
            ],
            axis=0,
        )
        wide = query.astype(jnp.float32)
        phi = feature(jnp.dot(query, weight_ref[g], preferred_element_type=jnp.float32)).astype(jnp.bfloat16)
        span = slice(g * feats, (g + 1) * feats)
        linear = jnp.dot(phi, state_a_ref[span, :], preferred_element_type=jnp.float32) + jnp.dot(
            phi, state_b_ref[span, :], preferred_element_type=jnp.float32
        )
        at = heads * feats
        norm = (
            state_a_ref[at : at + 16, :].astype(jnp.float32) + state_b_ref[at : at + 16, :].astype(jnp.float32)
        )[g : g + 1]
        den = jnp.sum(phi.astype(jnp.float32) * norm, axis=-1, keepdims=True)
        scale = (TAU / head_size) * lax.rsqrt(jnp.mean(wide * wide, axis=-1, keepdims=True) + EPS)
        keys = jnp.concatenate([near_a_ref[0, :, cols], near_b_ref[0, :, cols]], axis=0)
        values = jnp.concatenate([near_a_ref[1, :, cols], near_b_ref[1, :, cols]], axis=0)
        keys_wide = keys.astype(jnp.float32)
        key_scale = lax.rsqrt(jnp.mean((keys_wide * keys_wide).T, axis=0, keepdims=True) + EPS)
        score = lax.dot_general(query, keys, NT, preferred_element_type=jnp.float32) * scale * key_scale
        weights = jnp.where(seen, jnp.exp(score), 0.0)
        own_key = rows_ref[:, keys_at + g * head_size : keys_at + (g + 1) * head_size].astype(jnp.float32)
        own_value = rows_ref[:, values_at + g * head_size : values_at + (g + 1) * head_size].astype(jnp.float32)
        own_key = own_key * lax.rsqrt(jnp.mean(own_key * own_key, axis=-1, keepdims=True) + EPS)
        own_score = jnp.sum(wide * jnp.concatenate([own_key] * group, axis=0), axis=-1, keepdims=True) * scale
        own_weight = jnp.exp(own_score)
        num = (
            linear * (1.0 / (feats * feats))
            + jnp.dot(weights.astype(jnp.bfloat16), values, preferred_element_type=jnp.float32)
            + own_weight.astype(jnp.bfloat16).astype(jnp.float32) * jnp.concatenate([own_value] * group, axis=0)
        )
        den = den * (1.0 / (feats * feats)) + jnp.sum(weights, axis=-1, keepdims=True) + own_weight
        result = (num / den).astype(jnp.bfloat16)
        for h in range(group):
            at = (g * group + h) * head_size
            for k, out_ref in enumerate(out_refs):
                first = h * count + k * each
                out_ref[:, at : at + head_size] = result[first : first + each]


def decode(info, rows, weight, state_a, state_b, near_a, near_b, parts):
    heads, head_size, feats = weight.shape
    count = rows.shape[0]
    width = rows.shape[1] - 2 * heads * head_size
    vmem = pl.BlockSpec(memory_space=pltpu.VMEM)
    return pl.pallas_call(
        decode_kernel,
        in_specs=[pl.BlockSpec(memory_space=pltpu.SMEM)] + [vmem] * 6,
        out_specs=[vmem] * parts,
        out_shape=[jax.ShapeDtypeStruct((count // parts, width), jnp.bfloat16)] * parts,
        compiler_params=pltpu.CompilerParams(vmem_limit_bytes=32 * 1024 * 1024),
        cost_estimate=pl.CostEstimate(
            flops=10 * count * width * feats, bytes_accessed=4 * count * width, transcendentals=2 * count * width
        ),
        name="decode",
    )(info, rows, weight, state_a, state_b, near_a, near_b)


def body(
    sects, prompt_keys, prompt_values, lengths, feature_weight, queries, new_keys, new_values, row_prompt
):
    span = prompt_keys.shape[1]
    sub = lax.axis_index("sub")
    sect = lax.axis_index("sect")
    length = lengths[0]
    swap = [(0, 1), (1, 0)]

    mine = jnp.concatenate([queries, new_keys, new_values], axis=1)
    blocks = [mine] + [
        lax.ppermute(mine, "sect", [(i, (i + k) % sects) for i in range(sects)]) for k in range(1, sects)
    ]

    def first(half):
        return jnp.clip(length - WINDOW - half * span, 0, span - WINDOW)

    near = jnp.concatenate(
        [
            lax.dynamic_slice_in_dim(prompt_keys, first(sub), WINDOW, 1),
            lax.dynamic_slice_in_dim(prompt_values, first(sub), WINDOW, 1),
        ],
        axis=0,
    )
    far = lax.ppermute(near, "sub", swap)
    info = jnp.stack([sub * span + first(sub), (1 - sub) * span + first(1 - sub), length]).astype(jnp.int32)

    limit = (length - WINDOW - sub * span).reshape(1)
    state = prefill(prompt_keys, prompt_values, feature_weight, limit)
    other = lax.ppermute(state, "sub", swap)
    results = decode(info, jnp.concatenate(blocks, axis=0), feature_weight, state, other, near, far, sects)

    count = queries.shape[0]
    first_row = (sect * lax.axis_size("sub") + sub) * count
    prompts = lax.dynamic_slice_in_dim(row_prompt, first_row, count, 0)
    out = jnp.zeros_like(queries)
    for k, result in enumerate(results):
        if k > 0:
            result = lax.ppermute(result, "sect", [(i, (i - k) % sects) for i in range(sects)])
        out = jnp.where((prompts == (sect + k) % sects)[:, None], result, out)
    return out


def solution(mesh):
    placed = (
        P(("parts", "sect"), "sub", "tp"),
        P(("parts", "sect"), "sub", "tp"),
        P(("parts", "sect")),
        P("tp", None, None),
        P(("parts", "sect", "sub"), "tp"),
        P(("parts", "sect", "sub"), "tp"),
        P(("parts", "sect", "sub"), "tp"),
        P("parts"),
    )
    return jax.shard_map(
        functools.partial(body, mesh.shape["sect"]),
        mesh=mesh,
        in_specs=placed,
        out_specs=P(("parts", "sect", "sub"), "tp"),
        check_vma=False,
    )
```

```python
import functools

import jax
import jax.numpy as jnp
from jax import lax
from jax.experimental import pallas as pl
from jax.experimental.pallas import tpu as pltpu
from jax.sharding import PartitionSpec as P

WINDOW = 64
TAU = 10.0
EPS = 1e-06
BLOCK = 512
NT = (((1,), (1,)), ((), ()))


def feature(proj):
    return jnp.maximum(proj, 0.0) + jnp.exp(jnp.minimum(proj, 0.0))


def pack_kernel(queries_ref, keys_ref, values_ref, out_ref):
    width, each = queries_ref.shape[1], keys_ref.shape[1]
    out_ref[:, :width] = queries_ref[...]
    out_ref[:, width : width + each] = keys_ref[...]
    out_ref[:, width + each :] = values_ref[...]


def pack(queries, new_keys, new_values):
    vmem = pl.BlockSpec(memory_space=pltpu.VMEM)
    width = queries.shape[1] + 2 * new_keys.shape[1]
    return pl.pallas_call(
        pack_kernel,
        in_specs=[vmem] * 3,
        out_specs=vmem,
        out_shape=jax.ShapeDtypeStruct((queries.shape[0], width), jnp.bfloat16),
        name="pack",
    )(queries, new_keys, new_values)


SLAB = WINDOW + 16
MASK_ROW = 8


def prefill_kernel(
    lengths_ref, keys_ref, values_ref, weight_ref, out_ref,
    keys_at, values_at, weight_at, wide_ref, state_ref, norm_ref, weight_sem, load_sem, slab_sem,
):
    heads, head_size, feats = weight_ref.shape
    pairs = heads // 2
    span = keys_ref.shape[1]
    chunks = span // BLOCK
    get_weight = pltpu.make_async_copy(weight_ref, weight_at, weight_sem)
    get_weight.start()
    loads = []
    for c in range(chunks):
        rows = pl.ds(c * BLOCK, BLOCK)
        loads.append(
            [
                pltpu.make_async_copy(keys_ref.at[0, rows, :], keys_at.at[rows, :], load_sem.at[0, c]),
                pltpu.make_async_copy(values_ref.at[0, rows, :], values_at.at[rows, :], load_sem.at[1, c]),
            ]
        )
        for load in loads[-1]:
            load.start()

    state_ref[...] = jnp.zeros_like(state_ref)
    norm_ref[...] = jnp.zeros_like(norm_ref)
    wide_ref[...] = jnp.zeros_like(wide_ref)
    get_weight.wait()
    for g in range(heads):
        half = g % 2
        turned = weight_at[g].astype(jnp.float32).T.astype(jnp.bfloat16)
        wide_ref[g // 2, half * feats : (half + 1) * feats, half * head_size : (half + 1) * head_size] = turned

    begin = lengths_ref[0] - WINDOW - lax.axis_index("sub") * span
    first = jnp.clip(begin, 0, span - SLAB)
    first = pl.multiple_of(first - lax.rem(first, 16), 16)
    slabs = []
    for i, source in enumerate((keys_ref, values_ref)):
        for g in range(heads):
            at = heads * feats + 16 + (i * heads + g) * SLAB
            slabs.append(
                pltpu.make_async_copy(
                    source.at[0, pl.ds(first, SLAB), g * head_size : (g + 1) * head_size],
                    out_ref.at[at : at + SLAB, :],
                    slab_sem.at[i, g],
                )
            )
            slabs[-1].start()

    for c in range(chunks):
        rows = slice(c * BLOCK, (c + 1) * BLOCK)
        for load in loads[c]:
            load.wait()
        position = c * BLOCK + lax.broadcasted_iota(jnp.int32, (1, BLOCK), 1)
        live = position < begin
        for j in range(pairs):
            cols = slice(j * 2 * head_size, (j + 1) * 2 * head_size)
            proj = lax.dot_general(wide_ref[j], keys_at[rows, cols], NT, preferred_element_type=jnp.float32)
            mapped = jnp.where(live, feature(proj), 0.0)
            total = norm_ref[j]
            for k in range(BLOCK // 128):
                total = total + mapped[:, k * 128 : (k + 1) * 128]
            norm_ref[j] = total
            state_ref[j] += jnp.dot(
                mapped.astype(jnp.bfloat16), values_at[rows, cols], preferred_element_type=jnp.float32
            )

    tile = []
    for g in range(heads):
        half = g % 2
        part = state_ref[g // 2, half * feats : (half + 1) * feats, half * head_size : (half + 1) * head_size]
        out_ref[g * feats : (g + 1) * feats, :] = part.astype(jnp.bfloat16)
        sums = norm_ref[g // 2, half * feats : (half + 1) * feats, :]
        tile.append(jnp.sum(sums.T, axis=0, keepdims=True))
    slot = first + lax.broadcasted_iota(jnp.int32, (1, head_size), 1)
    tile.append(jnp.zeros((MASK_ROW - heads, head_size), jnp.float32))
    tile.append(jnp.where((slot >= begin) & (slot < begin + WINDOW), 1.0, 0.0))
    tile.append(jnp.zeros((15 - MASK_ROW, head_size), jnp.float32))
    out_ref[heads * feats : heads * feats + 16, :] = jnp.concatenate(tile, axis=0).astype(jnp.bfloat16)
    for slab in slabs:
        slab.wait()


def prefill(keys, values, weight, lengths):
    heads, head_size, feats = weight.shape
    span, width = keys.shape[1:]
    hbm = pl.BlockSpec(memory_space=pltpu.MemorySpace.HBM)
    vmem = pl.BlockSpec(memory_space=pltpu.VMEM)
    return pl.pallas_call(
        prefill_kernel,
        in_specs=[pl.BlockSpec(memory_space=pltpu.SMEM), hbm, hbm, hbm],
        out_specs=vmem,
        out_shape=jax.ShapeDtypeStruct((heads * feats + 16 + 2 * heads * SLAB, head_size), jnp.bfloat16),
        scratch_shapes=[
            pltpu.VMEM((span, width), jnp.bfloat16),
            pltpu.VMEM((span, width), jnp.bfloat16),
            pltpu.VMEM(weight.shape, jnp.bfloat16),
            pltpu.VMEM((heads // 2, 2 * feats, 2 * head_size), jnp.bfloat16),
            pltpu.VMEM((heads // 2, 2 * feats, 2 * head_size), jnp.float32),
            pltpu.VMEM((heads // 2, 2 * feats, 128), jnp.float32),
            pltpu.SemaphoreType.DMA,
            pltpu.SemaphoreType.DMA((2, span // BLOCK)),
            pltpu.SemaphoreType.DMA((2, heads)),
        ],
        compiler_params=pltpu.CompilerParams(vmem_limit_bytes=52 * 1024 * 1024),
        cost_estimate=pl.CostEstimate(
            flops=4 * span * width * feats, bytes_accessed=4 * span * width, transcendentals=span * width
        ),
        name="prefill",
    )(lengths, keys, values, weight)


def decode_kernel(rows_ref, weight_ref, near_ref, far_ref, *out_refs):
    heads, head_size, feats = weight_ref.shape
    count = rows_ref.shape[0]
    group = (rows_ref.shape[1] - 2 * heads * head_size) // (heads * head_size)
    keys_at = heads * group * head_size
    values_at = keys_at + heads * head_size
    each = count // len(out_refs)
    tile_at = heads * feats
    halves = (near_ref, far_ref)
    tiles = [ref[tile_at : tile_at + 16, :].astype(jnp.float32) for ref in halves]
    for g in range(heads):
        query = jnp.concatenate(
            [
                rows_ref[:, (g * group + h) * head_size : (g * group + h + 1) * head_size]
                for h in range(group)
            ],
            axis=0,
        )
        wide = query.astype(jnp.float32)
        phi = feature(jnp.dot(query, weight_ref[g], preferred_element_type=jnp.float32)).astype(jnp.bfloat16)
        scale = (TAU / head_size) * lax.rsqrt(jnp.mean(wide * wide, axis=-1, keepdims=True) + EPS)
        own_key = rows_ref[:, keys_at + g * head_size : keys_at + (g + 1) * head_size].astype(jnp.float32)
        own_value = rows_ref[:, values_at + g * head_size : values_at + (g + 1) * head_size].astype(jnp.float32)
        own_key = own_key * lax.rsqrt(jnp.mean(own_key * own_key, axis=-1, keepdims=True) + EPS)
        own_score = jnp.sum(wide * jnp.concatenate([own_key] * group, axis=0), axis=-1, keepdims=True) * scale
        own_weight = jnp.exp(own_score)
        num = own_weight.astype(jnp.bfloat16).astype(jnp.float32) * jnp.concatenate([own_value] * group, axis=0)
        den = own_weight
        linear = jnp.zeros_like(num)
        for ref, tile in zip(halves, tiles):
            linear += jnp.dot(phi, ref[g * feats : (g + 1) * feats, :], preferred_element_type=jnp.float32)
            at = tile_at + 16 + g * SLAB
            keys = ref[at : at + SLAB, :]
            at += heads * SLAB
            values = ref[at : at + SLAB, :]
            keys_wide = keys.astype(jnp.float32)
            key_scale = lax.rsqrt(jnp.mean((keys_wide * keys_wide).T, axis=0, keepdims=True) + EPS)
            score = lax.dot_general(query, keys, NT, preferred_element_type=jnp.float32) * scale * key_scale
            weights = jnp.exp(score) * tile[MASK_ROW : MASK_ROW + 1, :SLAB]
            num += jnp.dot(weights.astype(jnp.bfloat16), values, preferred_element_type=jnp.float32)
            den += jnp.sum(weights, axis=-1, keepdims=True)
        norm = (tiles[0] + tiles[1])[g : g + 1]
        back = 1.0 / (feats * feats)
        den += jnp.sum(phi.astype(jnp.float32) * norm, axis=-1, keepdims=True) * back
        result = ((linear * back + num) / den).astype(jnp.bfloat16)
        for h in range(group):
            at = (g * group + h) * head_size
            for k, out_ref in enumerate(out_refs):
                start = h * count + k * each
                out_ref[:, at : at + head_size] = result[start : start + each]


def decode(rows, weight, near, far, parts):
    heads, head_size, feats = weight.shape
    count = rows.shape[0]
    width = rows.shape[1] - 2 * heads * head_size
    vmem = pl.BlockSpec(memory_space=pltpu.VMEM)
    return pl.pallas_call(
        decode_kernel,
        in_specs=[vmem] * 4,
        out_specs=[vmem] * parts,
        out_shape=[jax.ShapeDtypeStruct((count // parts, width), jnp.bfloat16)] * parts,
        compiler_params=pltpu.CompilerParams(vmem_limit_bytes=32 * 1024 * 1024),
        cost_estimate=pl.CostEstimate(
            flops=10 * count * width * feats, bytes_accessed=4 * count * width, transcendentals=2 * count * width
        ),
        name="decode",
    )(rows, weight, near, far)


def body(
    sects, prompt_keys, prompt_values, lengths, feature_weight, queries, new_keys, new_values, row_prompt
):
    sub = lax.axis_index("sub")
    sect = lax.axis_index("sect")
    mine = pack(queries, new_keys, new_values)
    blocks = [mine] + [
        lax.ppermute(mine, "sect", [(i, (i + k) % sects) for i in range(sects)]) for k in range(1, sects)
    ]
    near = prefill(prompt_keys, prompt_values, feature_weight, lengths)
    far = lax.ppermute(near, "sub", [(0, 1), (1, 0)])
    results = decode(jnp.concatenate(blocks, axis=0), feature_weight, near, far, sects)

    count = queries.shape[0]
    first_row = (sect * lax.axis_size("sub") + sub) * count
    prompts = lax.dynamic_slice_in_dim(row_prompt, first_row, count, 0)
    out = jnp.zeros_like(queries)
    for k, result in enumerate(results):
        if k > 0:
            result = lax.ppermute(result, "sect", [(i, (i - k) % sects) for i in range(sects)])
        out = jnp.where((prompts == (sect + k) % sects)[:, None], result, out)
    return out


def solution(mesh):
    placed = (
        P(("parts", "sect"), "sub", "tp"),
        P(("parts", "sect"), "sub", "tp"),
        P(("parts", "sect")),
        P("tp", None, None),
        P(("parts", "sect", "sub"), "tp"),
        P(("parts", "sect", "sub"), "tp"),
        P(("parts", "sect", "sub"), "tp"),
        P("parts"),
    )
    return jax.shard_map(
        functools.partial(body, mesh.shape["sect"]),
        mesh=mesh,
        in_specs=placed,
        out_specs=P(("parts", "sect", "sub"), "tp"),
        check_vma=False,
    )
```

```python
import functools

import jax
import jax.numpy as jnp
from jax import lax
from jax.experimental import pallas as pl
from jax.experimental.pallas import tpu as pltpu
from jax.sharding import PartitionSpec as P

WINDOW = 64
TAU = 10.0
EPS = 1e-06
BLOCK = 512
NT = (((1,), (1,)), ((), ()))


def feature(proj):
    return jnp.maximum(proj, 0.0) + jnp.exp(jnp.minimum(proj, 0.0))


def pack_kernel(queries_ref, keys_ref, values_ref, out_ref):
    width, each = queries_ref.shape[1], keys_ref.shape[1]
    out_ref[:, :width] = queries_ref[...]
    out_ref[:, width : width + each] = keys_ref[...]
    out_ref[:, width + each :] = values_ref[...]


def pack(queries, new_keys, new_values):
    vmem = pl.BlockSpec(memory_space=pltpu.VMEM)
    width = queries.shape[1] + 2 * new_keys.shape[1]
    return pl.pallas_call(
        pack_kernel,
        in_specs=[vmem] * 3,
        out_specs=vmem,
        out_shape=jax.ShapeDtypeStruct((queries.shape[0], width), jnp.bfloat16),
        name="pack",
    )(queries, new_keys, new_values)


SLAB = WINDOW + 16
MASK_ROW = 8


def prefill_kernel(
    lengths_ref, keys_ref, values_ref, weight_ref, out_ref,
    keys_at, values_at, weight_at, wide_ref, state_ref, norm_ref, weight_sem, load_sem, slab_sem,
):
    heads, head_size, feats = weight_ref.shape
    pairs = heads // 2
    span = keys_ref.shape[1]
    chunks = span // BLOCK
    get_weight = pltpu.make_async_copy(weight_ref, weight_at, weight_sem)
    get_weight.start()
    loads = []
    for c in range(chunks):
        rows = pl.ds(c * BLOCK, BLOCK)
        loads.append(
            [
                pltpu.make_async_copy(keys_ref.at[0, rows, :], keys_at.at[rows, :], load_sem.at[0, c]),
                pltpu.make_async_copy(values_ref.at[0, rows, :], values_at.at[rows, :], load_sem.at[1, c]),
            ]
        )
        for load in loads[-1]:
            load.start()

    state_ref[...] = jnp.zeros_like(state_ref)
    norm_ref[...] = jnp.zeros_like(norm_ref)
    wide_ref[...] = jnp.zeros_like(wide_ref)
    get_weight.wait()
    for g in range(heads):
        half = g % 2
        turned = weight_at[g].astype(jnp.float32).T.astype(jnp.bfloat16)
        wide_ref[g // 2, half * feats : (half + 1) * feats, half * head_size : (half + 1) * head_size] = turned

    begin = lengths_ref[0] - WINDOW - lax.axis_index("sub") * span
    first = jnp.clip(begin, 0, span - SLAB)
    first = pl.multiple_of(first - lax.rem(first, 16), 16)
    slabs = []
    for i, source in enumerate((keys_ref, values_ref)):
        for g in range(heads):
            at = heads * feats + 16 + (i * heads + g) * SLAB
            slabs.append(
                pltpu.make_async_copy(
                    source.at[0, pl.ds(first, SLAB), g * head_size : (g + 1) * head_size],
                    out_ref.at[at : at + SLAB, :],
                    slab_sem.at[i, g],
                )
            )
            slabs[-1].start()

    for c in range(chunks):
        rows = slice(c * BLOCK, (c + 1) * BLOCK)
        for load in loads[c]:
            load.wait()
        position = c * BLOCK + lax.broadcasted_iota(jnp.int32, (1, BLOCK), 1)
        live = position < begin
        for j in range(pairs):
            cols = slice(j * 2 * head_size, (j + 1) * 2 * head_size)
            proj = lax.dot_general(wide_ref[j], keys_at[rows, cols], NT, preferred_element_type=jnp.float32)
            mapped = jnp.where(live, feature(proj), 0.0)
            total = norm_ref[j]
            for k in range(BLOCK // 128):
                total = total + mapped[:, k * 128 : (k + 1) * 128]
            norm_ref[j] = total
            state_ref[j] += jnp.dot(
                mapped.astype(jnp.bfloat16), values_at[rows, cols], preferred_element_type=jnp.float32
            )

    tile = []
    for g in range(heads):
        half = g % 2
        part = state_ref[g // 2, half * feats : (half + 1) * feats, half * head_size : (half + 1) * head_size]
        out_ref[g * feats : (g + 1) * feats, :] = part.astype(jnp.bfloat16)
        sums = norm_ref[g // 2, half * feats : (half + 1) * feats, :]
        tile.append(jnp.sum(sums.T, axis=0, keepdims=True))
    slot = first + lax.broadcasted_iota(jnp.int32, (1, head_size), 1)
    tile.append(jnp.zeros((MASK_ROW - heads, head_size), jnp.float32))
    tile.append(jnp.where((slot >= begin) & (slot < begin + WINDOW), 1.0, 0.0))
    tile.append(jnp.zeros((15 - MASK_ROW, head_size), jnp.float32))
    out_ref[heads * feats : heads * feats + 16, :] = jnp.concatenate(tile, axis=0).astype(jnp.bfloat16)
    for slab in slabs:
        slab.wait()


def prefill(keys, values, weight, lengths):
    heads, head_size, feats = weight.shape
    span, width = keys.shape[1:]
    hbm = pl.BlockSpec(memory_space=pltpu.MemorySpace.HBM)
    vmem = pl.BlockSpec(memory_space=pltpu.VMEM)
    return pl.pallas_call(
        prefill_kernel,
        in_specs=[pl.BlockSpec(memory_space=pltpu.SMEM), hbm, hbm, hbm],
        out_specs=vmem,
        out_shape=jax.ShapeDtypeStruct((heads * feats + 16 + 2 * heads * SLAB, head_size), jnp.bfloat16),
        scratch_shapes=[
            pltpu.VMEM((span, width), jnp.bfloat16),
            pltpu.VMEM((span, width), jnp.bfloat16),
            pltpu.VMEM(weight.shape, jnp.bfloat16),
            pltpu.VMEM((heads // 2, 2 * feats, 2 * head_size), jnp.bfloat16),
            pltpu.VMEM((heads // 2, 2 * feats, 2 * head_size), jnp.float32),
            pltpu.VMEM((heads // 2, 2 * feats, 128), jnp.float32),
            pltpu.SemaphoreType.DMA,
            pltpu.SemaphoreType.DMA((2, span // BLOCK)),
            pltpu.SemaphoreType.DMA((2, heads)),
        ],
        compiler_params=pltpu.CompilerParams(vmem_limit_bytes=52 * 1024 * 1024),
        cost_estimate=pl.CostEstimate(
            flops=4 * span * width * feats, bytes_accessed=4 * span * width, transcendentals=span * width
        ),
        name="prefill",
    )(lengths, keys, values, weight)


def decode_kernel(rows_ref, weight_ref, near_ref, far_ref, out_ref):
    heads, head_size, feats = weight_ref.shape
    count = rows_ref.shape[0]
    group = (rows_ref.shape[1] - 2 * heads * head_size) // (heads * head_size)
    keys_at = heads * group * head_size
    values_at = keys_at + heads * head_size
    parts, each = out_ref.shape[:2]
    home = lax.axis_index("sect")
    tile_at = heads * feats
    halves = (near_ref, far_ref)
    tiles = [ref[tile_at : tile_at + 16, :].astype(jnp.float32) for ref in halves]
    for g in range(heads):
        query = jnp.concatenate(
            [
                rows_ref[:, (g * group + h) * head_size : (g * group + h + 1) * head_size]
                for h in range(group)
            ],
            axis=0,
        )
        wide = query.astype(jnp.float32)
        phi = feature(jnp.dot(query, weight_ref[g], preferred_element_type=jnp.float32)).astype(jnp.bfloat16)
        scale = (TAU / head_size) * lax.rsqrt(jnp.mean(wide * wide, axis=-1, keepdims=True) + EPS)
        own_key = rows_ref[:, keys_at + g * head_size : keys_at + (g + 1) * head_size].astype(jnp.float32)
        own_value = rows_ref[:, values_at + g * head_size : values_at + (g + 1) * head_size].astype(jnp.float32)
        own_key = own_key * lax.rsqrt(jnp.mean(own_key * own_key, axis=-1, keepdims=True) + EPS)
        own_score = jnp.sum(wide * jnp.concatenate([own_key] * group, axis=0), axis=-1, keepdims=True) * scale
        own_weight = jnp.exp(own_score)
        num = own_weight.astype(jnp.bfloat16).astype(jnp.float32) * jnp.concatenate([own_value] * group, axis=0)
        den = own_weight
        linear = jnp.zeros_like(num)
        for ref, tile in zip(halves, tiles):
            linear += jnp.dot(phi, ref[g * feats : (g + 1) * feats, :], preferred_element_type=jnp.float32)
            at = tile_at + 16 + g * SLAB
            keys = ref[at : at + SLAB, :]
            at += heads * SLAB
            values = ref[at : at + SLAB, :]
            keys_wide = keys.astype(jnp.float32)
            key_scale = lax.rsqrt(jnp.mean((keys_wide * keys_wide).T, axis=0, keepdims=True) + EPS)
            score = lax.dot_general(query, keys, NT, preferred_element_type=jnp.float32) * scale * key_scale
            weights = jnp.exp(score) * tile[MASK_ROW : MASK_ROW + 1, :SLAB]
            num += jnp.dot(weights.astype(jnp.bfloat16), values, preferred_element_type=jnp.float32)
            den += jnp.sum(weights, axis=-1, keepdims=True)
        norm = (tiles[0] + tiles[1])[g : g + 1]
        back = 1.0 / (feats * feats)
        den += jnp.sum(phi.astype(jnp.float32) * norm, axis=-1, keepdims=True) * back
        result = ((linear * back + num) / den).astype(jnp.bfloat16)
        for h in range(group):
            at = (g * group + h) * head_size
            for k in range(parts):
                start = h * count + k * each
                out_ref[lax.rem(home - k + parts, parts), :, at : at + head_size] = result[start : start + each]


def decode(rows, weight, near, far, parts):
    heads, head_size, feats = weight.shape
    count = rows.shape[0]
    width = rows.shape[1] - 2 * heads * head_size
    vmem = pl.BlockSpec(memory_space=pltpu.VMEM)
    return pl.pallas_call(
        decode_kernel,
        in_specs=[vmem] * 4,
        out_specs=vmem,
        out_shape=jax.ShapeDtypeStruct((parts, count // parts, width), jnp.bfloat16),
        compiler_params=pltpu.CompilerParams(vmem_limit_bytes=32 * 1024 * 1024),
        cost_estimate=pl.CostEstimate(
            flops=10 * count * width * feats, bytes_accessed=4 * count * width, transcendentals=2 * count * width
        ),
        name="decode",
    )(rows, weight, near, far)


def body(
    sects, prompt_keys, prompt_values, lengths, feature_weight, queries, new_keys, new_values, row_prompt
):
    sub = lax.axis_index("sub")
    sect = lax.axis_index("sect")
    mine = pack(queries, new_keys, new_values)
    blocks = [mine] + [
        lax.ppermute(mine, "sect", [(i, (i + k) % sects) for i in range(sects)]) for k in range(1, sects)
    ]
    near = prefill(prompt_keys, prompt_values, feature_weight, lengths)
    far = lax.ppermute(near, "sub", [(0, 1), (1, 0)])
    results = decode(jnp.concatenate(blocks, axis=0), feature_weight, near, far, sects)

    count = queries.shape[0]
    first_row = (sect * lax.axis_size("sub") + sub) * count
    prompts = lax.dynamic_slice_in_dim(row_prompt, first_row, count, 0)
    results = lax.all_to_all(results, "sect", 0, 0, tiled=True)
    out = jnp.zeros_like(queries)
    for k in range(sects):
        out = jnp.where((prompts == k)[:, None], results[k], out)
    return out


def solution(mesh):
    placed = (
        P(("parts", "sect"), "sub", "tp"),
        P(("parts", "sect"), "sub", "tp"),
        P(("parts", "sect")),
        P("tp", None, None),
        P(("parts", "sect", "sub"), "tp"),
        P(("parts", "sect", "sub"), "tp"),
        P(("parts", "sect", "sub"), "tp"),
        P("parts"),
    )
    return jax.shard_map(
        functools.partial(body, mesh.shape["sect"]),
        mesh=mesh,
        in_specs=placed,
        out_specs=P(("parts", "sect", "sub"), "tp"),
        check_vma=False,
    )
```

```python
import functools

import jax
import jax.numpy as jnp
from jax import lax
from jax.experimental import pallas as pl
from jax.experimental.pallas import tpu as pltpu
from jax.sharding import PartitionSpec as P

WINDOW = 64
TAU = 10.0
EPS = 1e-06
BLOCK = 512
NT = (((1,), (1,)), ((), ()))


def feature(proj):
    return jnp.maximum(proj, 0.0) + jnp.exp(jnp.minimum(proj, 0.0))


def pack_kernel(queries_ref, keys_ref, values_ref, out_ref):
    width, each = queries_ref.shape[1], keys_ref.shape[1]
    out_ref[:, :width] = queries_ref[...]
    out_ref[:, width : width + each] = keys_ref[...]
    out_ref[:, width + each :] = values_ref[...]


def pack(queries, new_keys, new_values):
    vmem = pl.BlockSpec(memory_space=pltpu.VMEM)
    width = queries.shape[1] + 2 * new_keys.shape[1]
    return pl.pallas_call(
        pack_kernel,
        in_specs=[vmem] * 3,
        out_specs=vmem,
        out_shape=jax.ShapeDtypeStruct((queries.shape[0], width), jnp.bfloat16),
        name="pack",
    )(queries, new_keys, new_values)


SLAB = WINDOW + 16
MASK_ROW = 8


def prefill_kernel(
    lengths_ref, keys_ref, values_ref, weight_ref, out_ref,
    keys_at, values_at, weight_at, wide_ref, state_ref, norm_ref, weight_sem, load_sem, slab_sem,
):
    heads, head_size, feats = weight_ref.shape
    pairs = heads // 2
    span = keys_ref.shape[1]
    chunks = span // BLOCK
    get_weight = pltpu.make_async_copy(weight_ref, weight_at, weight_sem)
    get_weight.start()
    loads = []
    for c in range(chunks):
        rows = pl.ds(c * BLOCK, BLOCK)
        loads.append(
            [
                pltpu.make_async_copy(keys_ref.at[0, rows, :], keys_at.at[rows, :], load_sem.at[0, c]),
                pltpu.make_async_copy(values_ref.at[0, rows, :], values_at.at[rows, :], load_sem.at[1, c]),
            ]
        )
        for load in loads[-1]:
            load.start()

    state_ref[...] = jnp.zeros_like(state_ref)
    norm_ref[...] = jnp.zeros_like(norm_ref)
    wide_ref[...] = jnp.zeros_like(wide_ref)
    get_weight.wait()
    for g in range(heads):
        half = g % 2
        turned = weight_at[g].astype(jnp.float32).T.astype(jnp.bfloat16)
        wide_ref[g // 2, half * feats : (half + 1) * feats, half * head_size : (half + 1) * head_size] = turned

    begin = lengths_ref[0] - WINDOW - lax.axis_index("sub") * span
    first = jnp.clip(begin, 0, span - SLAB)
    first = pl.multiple_of(first - lax.rem(first, 16), 16)
    slabs = []
    for i, source in enumerate((keys_ref, values_ref)):
        for g in range(heads):
            at = heads * feats + 16 + (i * heads + g) * SLAB
            slabs.append(
                pltpu.make_async_copy(
                    source.at[0, pl.ds(first, SLAB), g * head_size : (g + 1) * head_size],
                    out_ref.at[at : at + SLAB, :],
                    slab_sem.at[i, g],
                )
            )
            slabs[-1].start()

    for c in range(chunks):
        rows = slice(c * BLOCK, (c + 1) * BLOCK)
        for load in loads[c]:
            load.wait()
        position = c * BLOCK + lax.broadcasted_iota(jnp.int32, (1, BLOCK), 1)
        live = position < begin
        for j in range(pairs):
            cols = slice(j * 2 * head_size, (j + 1) * 2 * head_size)
            proj = lax.dot_general(wide_ref[j], keys_at[rows, cols], NT, preferred_element_type=jnp.float32)
            mapped = jnp.where(live, feature(proj), 0.0)
            total = norm_ref[j]
            for k in range(BLOCK // 128):
                total = total + mapped[:, k * 128 : (k + 1) * 128]
            norm_ref[j] = total
            state_ref[j] += jnp.dot(
                mapped.astype(jnp.bfloat16), values_at[rows, cols], preferred_element_type=jnp.float32
            )

    tile = []
    for g in range(heads):
        half = g % 2
        part = state_ref[g // 2, half * feats : (half + 1) * feats, half * head_size : (half + 1) * head_size]
        out_ref[g * feats : (g + 1) * feats, :] = part.astype(jnp.bfloat16)
        sums = norm_ref[g // 2, half * feats : (half + 1) * feats, :]
        tile.append(jnp.sum(sums.T, axis=0, keepdims=True))
    slot = first + lax.broadcasted_iota(jnp.int32, (1, head_size), 1)
    tile.append(jnp.zeros((MASK_ROW - heads, head_size), jnp.float32))
    tile.append(jnp.where((slot >= begin) & (slot < begin + WINDOW), 1.0, 0.0))
    tile.append(jnp.zeros((15 - MASK_ROW, head_size), jnp.float32))
    out_ref[heads * feats : heads * feats + 16, :] = jnp.concatenate(tile, axis=0).astype(jnp.bfloat16)
    for slab in slabs:
        slab.wait()


def prefill(keys, values, weight, lengths):
    heads, head_size, feats = weight.shape
    span, width = keys.shape[1:]
    hbm = pl.BlockSpec(memory_space=pltpu.MemorySpace.HBM)
    vmem = pl.BlockSpec(memory_space=pltpu.VMEM)
    return pl.pallas_call(
        prefill_kernel,
        in_specs=[pl.BlockSpec(memory_space=pltpu.SMEM), hbm, hbm, hbm],
        out_specs=vmem,
        out_shape=jax.ShapeDtypeStruct((heads * feats + 16 + 2 * heads * SLAB, head_size), jnp.bfloat16),
        scratch_shapes=[
            pltpu.VMEM((span, width), jnp.bfloat16),
            pltpu.VMEM((span, width), jnp.bfloat16),
            pltpu.VMEM(weight.shape, jnp.bfloat16),
            pltpu.VMEM((heads // 2, 2 * feats, 2 * head_size), jnp.bfloat16),
            pltpu.VMEM((heads // 2, 2 * feats, 2 * head_size), jnp.float32),
            pltpu.VMEM((heads // 2, 2 * feats, 128), jnp.float32),
            pltpu.SemaphoreType.DMA,
            pltpu.SemaphoreType.DMA((2, span // BLOCK)),
            pltpu.SemaphoreType.DMA((2, heads)),
        ],
        compiler_params=pltpu.CompilerParams(vmem_limit_bytes=52 * 1024 * 1024),
        cost_estimate=pl.CostEstimate(
            flops=4 * span * width * feats, bytes_accessed=4 * span * width, transcendentals=span * width
        ),
        name="prefill",
    )(lengths, keys, values, weight)


def decode_kernel(rows_ref, weight_ref, near_ref, far_ref, *out_refs):
    heads, head_size, feats = weight_ref.shape
    count = rows_ref.shape[0]
    group = (rows_ref.shape[1] - 2 * heads * head_size) // (heads * head_size)
    keys_at = heads * group * head_size
    values_at = keys_at + heads * head_size
    each = count // len(out_refs)
    tile_at = heads * feats
    halves = (near_ref, far_ref)
    tiles = [ref[tile_at : tile_at + 16, :].astype(jnp.float32) for ref in halves]
    for g in range(heads):
        query = jnp.concatenate(
            [
                rows_ref[:, (g * group + h) * head_size : (g * group + h + 1) * head_size]
                for h in range(group)
            ],
            axis=0,
        )
        wide = query.astype(jnp.float32)
        phi = feature(jnp.dot(query, weight_ref[g], preferred_element_type=jnp.float32)).astype(jnp.bfloat16)
        scale = (TAU / head_size) * lax.rsqrt(jnp.mean(wide * wide, axis=-1, keepdims=True) + EPS)
        own_key = rows_ref[:, keys_at + g * head_size : keys_at + (g + 1) * head_size].astype(jnp.float32)
        own_value = rows_ref[:, values_at + g * head_size : values_at + (g + 1) * head_size].astype(jnp.float32)
        own_key = own_key * lax.rsqrt(jnp.mean(own_key * own_key, axis=-1, keepdims=True) + EPS)
        own_score = jnp.sum(wide * jnp.concatenate([own_key] * group, axis=0), axis=-1, keepdims=True) * scale
        own_weight = jnp.exp(own_score)
        num = own_weight.astype(jnp.bfloat16).astype(jnp.float32) * jnp.concatenate([own_value] * group, axis=0)
        den = own_weight
        linear = jnp.zeros_like(num)
        for ref, tile in zip(halves, tiles):
            linear += jnp.dot(phi, ref[g * feats : (g + 1) * feats, :], preferred_element_type=jnp.float32)
            at = tile_at + 16 + g * SLAB
            keys = ref[at : at + SLAB, :]
            at += heads * SLAB
            values = ref[at : at + SLAB, :]
            keys_wide = keys.astype(jnp.float32)
            key_scale = lax.rsqrt(jnp.mean((keys_wide * keys_wide).T, axis=0, keepdims=True) + EPS)
            score = lax.dot_general(query, keys, NT, preferred_element_type=jnp.float32) * scale * key_scale
            weights = jnp.exp(score) * tile[MASK_ROW : MASK_ROW + 1, :SLAB]
            num += jnp.dot(weights.astype(jnp.bfloat16), values, preferred_element_type=jnp.float32)
            den += jnp.sum(weights, axis=-1, keepdims=True)
        norm = (tiles[0] + tiles[1])[g : g + 1]
        back = 1.0 / (feats * feats)
        den += jnp.sum(phi.astype(jnp.float32) * norm, axis=-1, keepdims=True) * back
        result = ((linear * back + num) / den).astype(jnp.bfloat16)
        for h in range(group):
            at = (g * group + h) * head_size
            for k, out_ref in enumerate(out_refs):
                start = h * count + k * each
                out_ref[:, at : at + head_size] = result[start : start + each]


def decode(rows, weight, near, far, parts):
    heads, head_size, feats = weight.shape
    count = rows.shape[0]
    width = rows.shape[1] - 2 * heads * head_size
    vmem = pl.BlockSpec(memory_space=pltpu.VMEM)
    return pl.pallas_call(
        decode_kernel,
        in_specs=[vmem] * 4,
        out_specs=[vmem] * parts,
        out_shape=[jax.ShapeDtypeStruct((count // parts, width), jnp.bfloat16)] * parts,
        compiler_params=pltpu.CompilerParams(vmem_limit_bytes=32 * 1024 * 1024),
        cost_estimate=pl.CostEstimate(
            flops=10 * count * width * feats, bytes_accessed=4 * count * width, transcendentals=2 * count * width
        ),
        name="decode",
    )(rows, weight, near, far)


def body(
    sects, prompt_keys, prompt_values, lengths, feature_weight, queries, new_keys, new_values, row_prompt
):
    sub = lax.axis_index("sub")
    sect = lax.axis_index("sect")
    up = [[(i, i + k) for i in range(sects - k)] for k in range(sects)]
    down = [[(i + k, i) for i in range(sects - k)] for k in range(sects)]
    mine = pack(queries, new_keys, new_values)
    risen = {k: lax.ppermute(mine, "sect", up[k]) for k in range(sects - 1, 0, -1)}
    near = prefill(prompt_keys, prompt_values, feature_weight, lengths)
    far = lax.ppermute(near, "sub", [(0, 1), (1, 0)])
    later, near = lax.optimization_barrier((mine, near))
    sunk = {k: lax.ppermute(later, "sect", down[k]) for k in range(sects - 1, 0, -1)}
    blocks = [mine] + [jnp.where(sect >= k, risen[k], sunk[sects - k]) for k in range(1, sects)]
    results = decode(jnp.concatenate(blocks, axis=0), feature_weight, near, far, sects)

    count = queries.shape[0]
    first_row = (sect * lax.axis_size("sub") + sub) * count
    prompts = lax.dynamic_slice_in_dim(row_prompt, first_row, count, 0)[:, None]
    out = results[0]
    for k in range(sects - 1, 0, -1):
        out = jnp.where(prompts == sect + k, lax.ppermute(results[k], "sect", down[k]), out)
    for k in range(sects - 1, 0, -1):
        out = jnp.where(prompts == sect - k, lax.ppermute(results[sects - k], "sect", up[k]), out)
    return out


def solution(mesh):
    placed = (
        P(("parts", "sect"), "sub", "tp"),
        P(("parts", "sect"), "sub", "tp"),
        P(("parts", "sect")),
        P("tp", None, None),
        P(("parts", "sect", "sub"), "tp"),
        P(("parts", "sect", "sub"), "tp"),
        P(("parts", "sect", "sub"), "tp"),
        P("parts"),
    )
    return jax.shard_map(
        functools.partial(body, mesh.shape["sect"]),
        mesh=mesh,
        in_specs=placed,
        out_specs=P(("parts", "sect", "sub"), "tp"),
        check_vma=False,
    )
```

```python
import functools

import jax
import jax.numpy as jnp
from jax import lax
from jax.experimental import pallas as pl
from jax.experimental.pallas import tpu as pltpu
from jax.sharding import PartitionSpec as P

WINDOW = 64
TAU = 10.0
EPS = 1e-06
BLOCK = 512
NT = (((1,), (1,)), ((), ()))


def feature(proj):
    return jnp.maximum(proj, 0.0) + jnp.exp(jnp.minimum(proj, 0.0))


SLAB = WINDOW + 16
MASK_ROW = 8


def prefill_kernel(
    lengths_ref, keys_ref, values_ref, weight_ref, queries_ref, new_keys_ref, new_values_ref, out_ref, mine_ref,
    keys_at, values_at, weight_at, wide_ref, state_ref, norm_ref,
    weight_sem, load_sem, slab_sem, pack_sem,
):
    heads, head_size, feats = weight_ref.shape
    pairs = heads // 2
    span = keys_ref.shape[1]
    chunks = span // BLOCK
    get_weight = pltpu.make_async_copy(weight_ref, weight_at, weight_sem)
    get_weight.start()
    loads = []
    for c in range(chunks):
        rows = pl.ds(c * BLOCK, BLOCK)
        loads.append(
            [
                pltpu.make_async_copy(keys_ref.at[0, rows, :], keys_at.at[rows, :], load_sem.at[0, c]),
                pltpu.make_async_copy(values_ref.at[0, rows, :], values_at.at[rows, :], load_sem.at[1, c]),
            ]
        )
        for load in loads[-1]:
            load.start()

    packs, at = [], 0
    for i, ref in enumerate((queries_ref, new_keys_ref, new_values_ref)):
        size = ref.shape[1]
        packs.append(pltpu.make_async_copy(ref, mine_ref.at[:, at : at + size], pack_sem.at[i]))
        packs[-1].start()
        at += size

    state_ref[...] = jnp.zeros_like(state_ref)
    norm_ref[...] = jnp.zeros_like(norm_ref)
    wide_ref[...] = jnp.zeros_like(wide_ref)
    get_weight.wait()
    for g in range(heads):
        half = g % 2
        turned = weight_at[g].astype(jnp.float32).T.astype(jnp.bfloat16)
        wide_ref[g // 2, half * feats : (half + 1) * feats, half * head_size : (half + 1) * head_size] = turned

    begin = lengths_ref[0] - WINDOW - lax.axis_index("sub") * span
    first = jnp.clip(begin, 0, span - SLAB)
    first = pl.multiple_of(first - lax.rem(first, 16), 16)
    slabs = []
    for i, source in enumerate((keys_ref, values_ref)):
        for g in range(heads):
            at = heads * feats + 16 + (i * heads + g) * SLAB
            slabs.append(
                pltpu.make_async_copy(
                    source.at[0, pl.ds(first, SLAB), g * head_size : (g + 1) * head_size],
                    out_ref.at[at : at + SLAB, :],
                    slab_sem.at[i, g],
                )
            )
            slabs[-1].start()

    for c in range(chunks):
        rows = slice(c * BLOCK, (c + 1) * BLOCK)
        for load in loads[c]:
            load.wait()
        position = c * BLOCK + lax.broadcasted_iota(jnp.int32, (1, BLOCK), 1)
        live = position < begin
        for j in range(pairs):
            cols = slice(j * 2 * head_size, (j + 1) * 2 * head_size)
            proj = lax.dot_general(wide_ref[j], keys_at[rows, cols], NT, preferred_element_type=jnp.float32)
            mapped = jnp.where(live, feature(proj), 0.0)
            total = norm_ref[j]
            for k in range(BLOCK // 128):
                total = total + mapped[:, k * 128 : (k + 1) * 128]
            norm_ref[j] = total
            state_ref[j] += jnp.dot(
                mapped.astype(jnp.bfloat16), values_at[rows, cols], preferred_element_type=jnp.float32
            )

    tile = []
    for g in range(heads):
        half = g % 2
        part = state_ref[g // 2, half * feats : (half + 1) * feats, half * head_size : (half + 1) * head_size]
        out_ref[g * feats : (g + 1) * feats, :] = part.astype(jnp.bfloat16)
        sums = norm_ref[g // 2, half * feats : (half + 1) * feats, :]
        tile.append(jnp.sum(sums.T, axis=0, keepdims=True))
    slot = first + lax.broadcasted_iota(jnp.int32, (1, head_size), 1)
    tile.append(jnp.zeros((MASK_ROW - heads, head_size), jnp.float32))
    tile.append(jnp.where((slot >= begin) & (slot < begin + WINDOW), 1.0, 0.0))
    tile.append(jnp.zeros((15 - MASK_ROW, head_size), jnp.float32))
    out_ref[heads * feats : heads * feats + 16, :] = jnp.concatenate(tile, axis=0).astype(jnp.bfloat16)
    for copy in slabs + packs:
        copy.wait()


def prefill(keys, values, weight, lengths, queries, new_keys, new_values):
    heads, head_size, feats = weight.shape
    span, width = keys.shape[1:]
    arrays = (keys, values, weight, queries, new_keys, new_values)
    hbm = pl.BlockSpec(memory_space=pltpu.MemorySpace.HBM)
    vmem = pl.BlockSpec(memory_space=pltpu.VMEM)
    return pl.pallas_call(
        prefill_kernel,
        in_specs=[pl.BlockSpec(memory_space=pltpu.SMEM)] + [hbm] * len(arrays),
        out_specs=[vmem, vmem],
        out_shape=[
            jax.ShapeDtypeStruct((heads * feats + 16 + 2 * heads * SLAB, head_size), jnp.bfloat16),
            jax.ShapeDtypeStruct((queries.shape[0], queries.shape[1] + 2 * width), jnp.bfloat16),
        ],
        scratch_shapes=[
            pltpu.VMEM((span, width), jnp.bfloat16),
            pltpu.VMEM((span, width), jnp.bfloat16),
            pltpu.VMEM(weight.shape, jnp.bfloat16),
            pltpu.VMEM((heads // 2, 2 * feats, 2 * head_size), jnp.bfloat16),
            pltpu.VMEM((heads // 2, 2 * feats, 2 * head_size), jnp.float32),
            pltpu.VMEM((heads // 2, 2 * feats, 128), jnp.float32),
            pltpu.SemaphoreType.DMA,
            pltpu.SemaphoreType.DMA((2, span // BLOCK)),
            pltpu.SemaphoreType.DMA((2, heads)),
            pltpu.SemaphoreType.DMA((3,)),
        ],
        compiler_params=pltpu.CompilerParams(vmem_limit_bytes=40 * 1024 * 1024),
        cost_estimate=pl.CostEstimate(
            flops=4 * span * width * feats, bytes_accessed=4 * span * width, transcendentals=span * width
        ),
        name="prefill",
    )(lengths, *[pltpu.with_memory_space_constraint(x, pltpu.MemorySpace.HBM) for x in arrays])


def decode_kernel(rows_ref, weight_ref, near_ref, far_ref, *out_refs):
    heads, head_size, feats = weight_ref.shape
    count = rows_ref.shape[0]
    group = (rows_ref.shape[1] - 2 * heads * head_size) // (heads * head_size)
    keys_at = heads * group * head_size
    values_at = keys_at + heads * head_size
    each = count // len(out_refs)
    tile_at = heads * feats
    halves = (near_ref, far_ref)
    tiles = [ref[tile_at : tile_at + 16, :].astype(jnp.float32) for ref in halves]
    for g in range(heads):
        query = jnp.concatenate(
            [
                rows_ref[:, (g * group + h) * head_size : (g * group + h + 1) * head_size]
                for h in range(group)
            ],
            axis=0,
        )
        wide = query.astype(jnp.float32)
        phi = feature(jnp.dot(query, weight_ref[g], preferred_element_type=jnp.float32)).astype(jnp.bfloat16)
        scale = (TAU / head_size) * lax.rsqrt(jnp.mean(wide * wide, axis=-1, keepdims=True) + EPS)
        own_key = rows_ref[:, keys_at + g * head_size : keys_at + (g + 1) * head_size].astype(jnp.float32)
        own_value = rows_ref[:, values_at + g * head_size : values_at + (g + 1) * head_size].astype(jnp.float32)
        own_key = own_key * lax.rsqrt(jnp.mean(own_key * own_key, axis=-1, keepdims=True) + EPS)
        own_score = jnp.sum(wide * jnp.concatenate([own_key] * group, axis=0), axis=-1, keepdims=True) * scale
        own_weight = jnp.exp(own_score)
        num = own_weight.astype(jnp.bfloat16).astype(jnp.float32) * jnp.concatenate([own_value] * group, axis=0)
        den = own_weight
        linear = jnp.zeros_like(num)
        for ref, tile in zip(halves, tiles):
            linear += jnp.dot(phi, ref[g * feats : (g + 1) * feats, :], preferred_element_type=jnp.float32)
            at = tile_at + 16 + g * SLAB
            keys = ref[at : at + SLAB, :]
            at += heads * SLAB
            values = ref[at : at + SLAB, :]
            keys_wide = keys.astype(jnp.float32)
            key_scale = lax.rsqrt(jnp.mean((keys_wide * keys_wide).T, axis=0, keepdims=True) + EPS)
            score = lax.dot_general(query, keys, NT, preferred_element_type=jnp.float32) * scale * key_scale
            weights = jnp.exp(score) * tile[MASK_ROW : MASK_ROW + 1, :SLAB]
            num += jnp.dot(weights.astype(jnp.bfloat16), values, preferred_element_type=jnp.float32)
            den += jnp.sum(weights, axis=-1, keepdims=True)
        norm = (tiles[0] + tiles[1])[g : g + 1]
        back = 1.0 / (feats * feats)
        den += jnp.sum(phi.astype(jnp.float32) * norm, axis=-1, keepdims=True) * back
        result = ((linear * back + num) / den).astype(jnp.bfloat16)
        for h in range(group):
            at = (g * group + h) * head_size
            for k, out_ref in enumerate(out_refs):
                start = h * count + k * each
                out_ref[:, at : at + head_size] = result[start : start + each]


def decode(rows, weight, near, far, parts):
    heads, head_size, feats = weight.shape
    count = rows.shape[0]
    width = rows.shape[1] - 2 * heads * head_size
    vmem = pl.BlockSpec(memory_space=pltpu.VMEM)
    return pl.pallas_call(
        decode_kernel,
        in_specs=[vmem] * 4,
        out_specs=[vmem] * parts,
        out_shape=[jax.ShapeDtypeStruct((count // parts, width), jnp.bfloat16)] * parts,
        compiler_params=pltpu.CompilerParams(vmem_limit_bytes=32 * 1024 * 1024),
        cost_estimate=pl.CostEstimate(
            flops=10 * count * width * feats, bytes_accessed=4 * count * width, transcendentals=2 * count * width
        ),
        name="decode",
    )(rows, weight, near, far)


def body(
    sects, prompt_keys, prompt_values, lengths, feature_weight, queries, new_keys, new_values, row_prompt
):
    sub = lax.axis_index("sub")
    sect = lax.axis_index("sect")
    near, mine = prefill(prompt_keys, prompt_values, feature_weight, lengths, queries, new_keys, new_values)
    far = lax.ppermute(near, "sub", [(0, 1), (1, 0)])
    blocks = [mine] + [
        lax.ppermute(mine, "sect", [((i + k) % sects, i) for i in range(sects)]) for k in range(1, sects)
    ]
    results = decode(jnp.concatenate(blocks, axis=0), feature_weight, near, far, sects)

    count = queries.shape[0]
    first_row = (sect * lax.axis_size("sub") + sub) * count
    prompts = lax.dynamic_slice_in_dim(row_prompt, first_row, count, 0)
    out = jnp.zeros_like(queries)
    for k, result in enumerate(results):
        if k > 0:
            result = lax.ppermute(result, "sect", [(i, (i + k) % sects) for i in range(sects)])
        out = jnp.where((prompts == (sect - k) % sects)[:, None], result, out)
    return out


def solution(mesh):
    placed = (
        P(("parts", "sect"), "sub", "tp"),
        P(("parts", "sect"), "sub", "tp"),
        P(("parts", "sect")),
        P("tp", None, None),
        P(("parts", "sect", "sub"), "tp"),
        P(("parts", "sect", "sub"), "tp"),
        P(("parts", "sect", "sub"), "tp"),
        P("parts"),
    )
    return jax.shard_map(
        functools.partial(body, mesh.shape["sect"]),
        mesh=mesh,
        in_specs=placed,
        out_specs=P(("parts", "sect", "sub"), "tp"),
        check_vma=False,
    )
```

```python
import functools

import jax
import jax.numpy as jnp
from jax import lax
from jax.experimental import pallas as pl
from jax.experimental.pallas import tpu as pltpu
from jax.sharding import PartitionSpec as P

WINDOW = 64
TAU = 10.0
EPS = 1e-06
BLOCK = 512
NT = (((1,), (1,)), ((), ()))


def feature(proj):
    return jnp.maximum(proj, 0.0) + jnp.exp(jnp.minimum(proj, 0.0))


SLAB = WINDOW + 16
MASK_ROW = 8


def prefill_kernel(
    lengths_ref, keys_ref, values_ref, weight_ref, out_ref,
    keys_at, values_at, weight_at, wide_ref, state_ref, norm_ref,
    weight_sem, load_sem, slab_sem,
):
    heads, head_size, feats = weight_ref.shape
    pairs = heads // 2
    span = keys_ref.shape[1]
    chunks = span // BLOCK
    get_weight = pltpu.make_async_copy(weight_ref, weight_at, weight_sem)
    get_weight.start()
    loads = []
    for c in range(chunks):
        rows = pl.ds(c * BLOCK, BLOCK)
        loads.append(
            [
                pltpu.make_async_copy(keys_ref.at[0, rows, :], keys_at.at[rows, :], load_sem.at[0, c]),
                pltpu.make_async_copy(values_ref.at[0, rows, :], values_at.at[rows, :], load_sem.at[1, c]),
            ]
        )
        for load in loads[-1]:
            load.start()

    state_ref[...] = jnp.zeros_like(state_ref)
    norm_ref[...] = jnp.zeros_like(norm_ref)
    wide_ref[...] = jnp.zeros_like(wide_ref)
    get_weight.wait()
    for g in range(heads):
        half = g % 2
        turned = weight_at[g].astype(jnp.float32).T.astype(jnp.bfloat16)
        wide_ref[g // 2, half * feats : (half + 1) * feats, half * head_size : (half + 1) * head_size] = turned

    begin = lengths_ref[0] - WINDOW - lax.axis_index("sub") * span
    first = jnp.clip(begin, 0, span - SLAB)
    first = pl.multiple_of(first - lax.rem(first, 16), 16)
    slabs = []
    for i, source in enumerate((keys_ref, values_ref)):
        for g in range(heads):
            at = heads * feats + 16 + (i * heads + g) * SLAB
            slabs.append(
                pltpu.make_async_copy(
                    source.at[0, pl.ds(first, SLAB), g * head_size : (g + 1) * head_size],
                    out_ref.at[at : at + SLAB, :],
                    slab_sem.at[i, g],
                )
            )
            slabs[-1].start()

    for c in range(chunks):
        rows = slice(c * BLOCK, (c + 1) * BLOCK)
        for load in loads[c]:
            load.wait()
        position = c * BLOCK + lax.broadcasted_iota(jnp.int32, (1, BLOCK), 1)
        live = position < begin
        for j in range(pairs):
            cols = slice(j * 2 * head_size, (j + 1) * 2 * head_size)
            proj = lax.dot_general(wide_ref[j], keys_at[rows, cols], NT, preferred_element_type=jnp.float32)
            mapped = jnp.where(live, feature(proj), 0.0)
            total = norm_ref[j]
            for k in range(BLOCK // 128):
                total = total + mapped[:, k * 128 : (k + 1) * 128]
            norm_ref[j] = total
            state_ref[j] += jnp.dot(
                mapped.astype(jnp.bfloat16), values_at[rows, cols], preferred_element_type=jnp.float32
            )

    tile = []
    for g in range(heads):
        half = g % 2
        part = state_ref[g // 2, half * feats : (half + 1) * feats, half * head_size : (half + 1) * head_size]
        out_ref[g * feats : (g + 1) * feats, :] = part.astype(jnp.bfloat16)
        sums = norm_ref[g // 2, half * feats : (half + 1) * feats, :]
        tile.append(jnp.sum(sums.T, axis=0, keepdims=True))
    slot = first + lax.broadcasted_iota(jnp.int32, (1, head_size), 1)
    tile.append(jnp.zeros((MASK_ROW - heads, head_size), jnp.float32))
    tile.append(jnp.where((slot >= begin) & (slot < begin + WINDOW), 1.0, 0.0))
    tile.append(jnp.zeros((15 - MASK_ROW, head_size), jnp.float32))
    out_ref[heads * feats : heads * feats + 16, :] = jnp.concatenate(tile, axis=0).astype(jnp.bfloat16)
    for slab in slabs:
        slab.wait()


def prefill(keys, values, weight, lengths):
    heads, head_size, feats = weight.shape
    span, width = keys.shape[1:]
    arrays = (keys, values, weight)
    hbm = pl.BlockSpec(memory_space=pltpu.MemorySpace.HBM)
    vmem = pl.BlockSpec(memory_space=pltpu.VMEM)
    return pl.pallas_call(
        prefill_kernel,
        in_specs=[pl.BlockSpec(memory_space=pltpu.SMEM)] + [hbm] * len(arrays),
        out_specs=vmem,
        out_shape=jax.ShapeDtypeStruct((heads * feats + 16 + 2 * heads * SLAB, head_size), jnp.bfloat16),
        scratch_shapes=[
            pltpu.VMEM((span, width), jnp.bfloat16),
            pltpu.VMEM((span, width), jnp.bfloat16),
            pltpu.VMEM(weight.shape, jnp.bfloat16),
            pltpu.VMEM((heads // 2, 2 * feats, 2 * head_size), jnp.bfloat16),
            pltpu.VMEM((heads // 2, 2 * feats, 2 * head_size), jnp.float32),
            pltpu.VMEM((heads // 2, 2 * feats, 128), jnp.float32),
            pltpu.SemaphoreType.DMA,
            pltpu.SemaphoreType.DMA((2, span // BLOCK)),
            pltpu.SemaphoreType.DMA((2, heads)),
        ],
        compiler_params=pltpu.CompilerParams(vmem_limit_bytes=40 * 1024 * 1024),
        cost_estimate=pl.CostEstimate(
            flops=4 * span * width * feats, bytes_accessed=4 * span * width, transcendentals=span * width
        ),
        name="prefill",
    )(lengths, *[pltpu.with_memory_space_constraint(x, pltpu.MemorySpace.HBM) for x in arrays])


def decode_kernel(rows_ref, weight_ref, near_ref, far_ref, *out_refs):
    heads, head_size, feats = weight_ref.shape
    count, width = rows_ref.shape
    group = width // (heads * head_size)
    each = count // len(out_refs)
    tile_at = heads * feats
    halves = (near_ref, far_ref)
    tiles = [ref[tile_at : tile_at + 16, :].astype(jnp.float32) for ref in halves]
    lane = lax.broadcasted_iota(jnp.int32, (count, head_size), 1)
    dens = jnp.zeros((count, head_size), jnp.float32)
    for g in range(heads):
        query = jnp.concatenate(
            [
                rows_ref[:, (g * group + h) * head_size : (g * group + h + 1) * head_size]
                for h in range(group)
            ],
            axis=0,
        )
        wide = query.astype(jnp.float32)
        phi = feature(jnp.dot(query, weight_ref[g], preferred_element_type=jnp.float32)).astype(jnp.bfloat16)
        scale = (TAU / head_size) * lax.rsqrt(jnp.mean(wide * wide, axis=-1, keepdims=True) + EPS)
        num, den, linear = 0.0, 0.0, 0.0
        for ref, tile in zip(halves, tiles):
            linear += jnp.dot(phi, ref[g * feats : (g + 1) * feats, :], preferred_element_type=jnp.float32)
            at = tile_at + 16 + g * SLAB
            keys = ref[at : at + SLAB, :]
            at += heads * SLAB
            values = ref[at : at + SLAB, :]
            keys_wide = keys.astype(jnp.float32)
            key_scale = lax.rsqrt(jnp.mean((keys_wide * keys_wide).T, axis=0, keepdims=True) + EPS)
            score = lax.dot_general(query, keys, NT, preferred_element_type=jnp.float32) * scale * key_scale
            weights = jnp.exp(score) * tile[MASK_ROW : MASK_ROW + 1, :SLAB]
            num += jnp.dot(weights.astype(jnp.bfloat16), values, preferred_element_type=jnp.float32)
            den += jnp.sum(weights, axis=-1, keepdims=True)
        norm = (tiles[0] + tiles[1])[g : g + 1]
        back = 1.0 / (feats * feats)
        den += jnp.sum(phi.astype(jnp.float32) * norm, axis=-1, keepdims=True) * back
        result = (linear * back + num).astype(jnp.bfloat16)
        for h in range(group):
            head = g * group + h
            dens = jnp.where(lane == head, den[h * count : (h + 1) * count], dens)
            for k, out_ref in enumerate(out_refs):
                start = h * count + k * each
                out_ref[:, head * head_size : (head + 1) * head_size] = result[start : start + each]
    high = dens.astype(jnp.bfloat16)
    low = (dens - high.astype(jnp.float32)).astype(jnp.bfloat16)
    for k, out_ref in enumerate(out_refs):
        out_ref[:, width : width + head_size] = high[k * each : (k + 1) * each]
        out_ref[:, width + head_size :] = low[k * each : (k + 1) * each]


def decode(rows, weight, near, far, parts):
    heads, head_size, feats = weight.shape
    count, width = rows.shape
    vmem = pl.BlockSpec(memory_space=pltpu.VMEM)
    return pl.pallas_call(
        decode_kernel,
        in_specs=[vmem] * 4,
        out_specs=[vmem] * parts,
        out_shape=[jax.ShapeDtypeStruct((count // parts, width + 2 * head_size), jnp.bfloat16)] * parts,
        compiler_params=pltpu.CompilerParams(vmem_limit_bytes=32 * 1024 * 1024),
        cost_estimate=pl.CostEstimate(
            flops=10 * count * width * feats, bytes_accessed=4 * count * width, transcendentals=2 * count * width
        ),
        name="decode",
    )(rows, weight, near, far)


def own_kernel(queries_ref, keys_ref, values_ref, _, num_ref, weight_ref):
    count, width = queries_ref.shape
    head_size = weight_ref.shape[1]
    heads = keys_ref.shape[1] // head_size
    group = width // (heads * head_size)
    lane = lax.broadcasted_iota(jnp.int32, (count, head_size), 1)
    kept = jnp.zeros((count, head_size), jnp.float32)
    for g in range(heads):
        cols = slice(g * head_size, (g + 1) * head_size)
        key = keys_ref[:, cols].astype(jnp.float32)
        value = values_ref[:, cols].astype(jnp.float32)
        key = key * lax.rsqrt(jnp.mean(key * key, axis=-1, keepdims=True) + EPS)
        for h in range(group):
            head = g * group + h
            span = slice(head * head_size, (head + 1) * head_size)
            query = queries_ref[:, span].astype(jnp.float32)
            scale = (TAU / head_size) * lax.rsqrt(jnp.mean(query * query, axis=-1, keepdims=True) + EPS)
            weight = jnp.exp(jnp.sum(query * key, axis=-1, keepdims=True) * scale)
            num_ref[:, span] = weight.astype(jnp.bfloat16).astype(jnp.float32) * value
            kept = jnp.where(lane == head, weight, kept)
    weight_ref[...] = kept


def own(queries, new_keys, new_values, after, head_size):
    vmem = pl.BlockSpec(memory_space=pltpu.VMEM)
    count, width = queries.shape
    return pl.pallas_call(
        own_kernel,
        in_specs=[vmem] * 3 + [pl.BlockSpec(memory_space=pl.ANY)],
        out_specs=[vmem, vmem],
        out_shape=[
            jax.ShapeDtypeStruct((count, width), jnp.float32),
            jax.ShapeDtypeStruct((count, head_size), jnp.float32),
        ],
        cost_estimate=pl.CostEstimate(
            flops=8 * count * width, bytes_accessed=8 * count * width, transcendentals=count * width // head_size
        ),
        name="own",
    )(queries, new_keys, new_values, after)


def finish_kernel(prompts_ref, num_ref, weight_ref, *refs):
    block_refs, out_ref = refs[:-1], refs[-1]
    count, width = out_ref.shape
    head_size = weight_ref.shape[1]
    sects = len(block_refs)
    sect = lax.axis_index("sect")
    first = (sect * lax.axis_size("sub") + lax.axis_index("sub")) * count
    rows = prompts_ref.shape[1]
    row = first + lax.broadcasted_iota(jnp.int32, (count, rows), 0)
    lane = lax.broadcasted_iota(jnp.int32, (count, rows), 1)
    prompt = jnp.sum(jnp.where(lane == row, prompts_ref[...], 0), axis=1, keepdims=True)
    chosen = block_refs[0][...].astype(jnp.float32)
    for k in range(1, sects):
        source = lax.rem(sect - k + sects, sects)
        chosen = jnp.where(prompt == source, block_refs[k][...].astype(jnp.float32), chosen)
    den = chosen[:, width : width + head_size] + chosen[:, width + head_size :] + weight_ref[...]
    scale = 1.0 / den
    for head in range(width // head_size):
        span = slice(head * head_size, (head + 1) * head_size)
        out_ref[:, span] = ((chosen[:, span] + num_ref[:, span]) * scale[:, head : head + 1]).astype(out_ref.dtype)


def finish(row_prompt, num, weight, blocks):
    vmem = pl.BlockSpec(memory_space=pltpu.VMEM)
    return pl.pallas_call(
        finish_kernel,
        in_specs=[vmem] * (3 + len(blocks)),
        out_specs=vmem,
        out_shape=jax.ShapeDtypeStruct(num.shape, jnp.bfloat16),
        name="finish",
    )(row_prompt.reshape(1, -1), num, weight, *blocks)


def body(
    sects, prompt_keys, prompt_values, lengths, feature_weight, queries, new_keys, new_values, row_prompt
):
    blocks = [queries] + [
        lax.ppermute(queries, "sect", [((i + k) % sects, i) for i in range(sects)]) for k in range(1, sects)
    ]
    near = prefill(prompt_keys, prompt_values, feature_weight, lengths)
    far = lax.ppermute(near, "sub", [(0, 1), (1, 0)])
    results = decode(jnp.concatenate(blocks, axis=0), feature_weight, near, far, sects)
    num, weight = own(queries, new_keys, new_values, results[0], feature_weight.shape[1])
    back = [results[0]] + [
        lax.ppermute(results[k], "sect", [(i, (i + k) % sects) for i in range(sects)]) for k in range(1, sects)
    ]
    return finish(row_prompt, num, weight, back)


def solution(mesh):
    placed = (
        P(("parts", "sect"), "sub", "tp"),
        P(("parts", "sect"), "sub", "tp"),
        P(("parts", "sect")),
        P("tp", None, None),
        P(("parts", "sect", "sub"), "tp"),
        P(("parts", "sect", "sub"), "tp"),
        P(("parts", "sect", "sub"), "tp"),
        P("parts"),
    )
    return jax.shard_map(
        functools.partial(body, mesh.shape["sect"]),
        mesh=mesh,
        in_specs=placed,
        out_specs=P(("parts", "sect", "sub"), "tp"),
        check_vma=False,
    )
```

```python
import functools

import jax
import jax.numpy as jnp
from jax import lax
from jax.experimental import pallas as pl
from jax.experimental.pallas import tpu as pltpu
from jax.sharding import PartitionSpec as P

WINDOW = 64
TAU = 10.0
EPS = 1e-06
BLOCK = 512
AHEAD = 3
NT = (((1,), (1,)), ((), ()))


def feature(proj):
    return jnp.maximum(proj, 0.0) + jnp.exp(jnp.minimum(proj, 0.0))


SLAB = WINDOW + 16
MASK_ROW = 8


def prefill_kernel(
    lengths_ref, keys_ref, values_ref, weight_ref, out_ref,
    keys_at, values_at, weight_at, wide_ref, state_ref, norm_ref,
    weight_sem, load_sem, slab_sem,
):
    heads, head_size, feats = weight_ref.shape
    pairs = heads // 2
    span = keys_ref.shape[1]
    chunks = span // BLOCK
    get_weight = pltpu.make_async_copy(weight_ref, weight_at, weight_sem)
    get_weight.start()
    loads = []
    for c in range(chunks):
        rows = pl.ds(c * BLOCK, BLOCK)
        loads.append(
            [
                pltpu.make_async_copy(keys_ref.at[0, rows, :], keys_at.at[rows, :], load_sem.at[0, c]),
                pltpu.make_async_copy(values_ref.at[0, rows, :], values_at.at[rows, :], load_sem.at[1, c]),
            ]
        )

    def fetch(c):
        for priority, load in enumerate(loads[c]):
            load.start(priority=priority)

    for c in range(AHEAD):
        fetch(c)
    state_ref[...] = jnp.zeros_like(state_ref)
    norm_ref[...] = jnp.zeros_like(norm_ref)
    wide_ref[...] = jnp.zeros_like(wide_ref)
    get_weight.wait()
    for g in range(heads):
        half = g % 2
        turned = weight_at[g].astype(jnp.float32).T.astype(jnp.bfloat16)
        wide_ref[g // 2, half * feats : (half + 1) * feats, half * head_size : (half + 1) * head_size] = turned

    begin = lengths_ref[0] - WINDOW - lax.axis_index("sub") * span
    first = jnp.clip(begin, 0, span - SLAB)
    first = pl.multiple_of(first - lax.rem(first, 16), 16)
    slabs = []
    for i, source in enumerate((keys_ref, values_ref)):
        for g in range(heads):
            at = heads * feats + 16 + (i * heads + g) * SLAB
            slabs.append(
                pltpu.make_async_copy(
                    source.at[0, pl.ds(first, SLAB), g * head_size : (g + 1) * head_size],
                    out_ref.at[at : at + SLAB, :],
                    slab_sem.at[i, g],
                )
            )
            slabs[-1].start()

    for c in range(chunks):
        rows = slice(c * BLOCK, (c + 1) * BLOCK)
        for load in loads[c]:
            load.wait()
        if c + AHEAD < chunks:
            fetch(c + AHEAD)
        position = c * BLOCK + lax.broadcasted_iota(jnp.int32, (1, BLOCK), 1)
        live = position < begin
        for j in range(pairs):
            cols = slice(j * 2 * head_size, (j + 1) * 2 * head_size)
            proj = lax.dot_general(wide_ref[j], keys_at[rows, cols], NT, preferred_element_type=jnp.float32)
            mapped = jnp.where(live, feature(proj), 0.0)
            total = norm_ref[j]
            for k in range(BLOCK // 128):
                total = total + mapped[:, k * 128 : (k + 1) * 128]
            norm_ref[j] = total
            state_ref[j] += jnp.dot(
                mapped.astype(jnp.bfloat16), values_at[rows, cols], preferred_element_type=jnp.float32
            )

    tile = []
    for g in range(heads):
        half = g % 2
        part = state_ref[g // 2, half * feats : (half + 1) * feats, half * head_size : (half + 1) * head_size]
        out_ref[g * feats : (g + 1) * feats, :] = part.astype(jnp.bfloat16)
        sums = norm_ref[g // 2, half * feats : (half + 1) * feats, :]
        tile.append(jnp.sum(sums.T, axis=0, keepdims=True))
    slot = first + lax.broadcasted_iota(jnp.int32, (1, head_size), 1)
    tile.append(jnp.zeros((MASK_ROW - heads, head_size), jnp.float32))
    tile.append(jnp.where((slot >= begin) & (slot < begin + WINDOW), 1.0, 0.0))
    tile.append(jnp.zeros((15 - MASK_ROW, head_size), jnp.float32))
    out_ref[heads * feats : heads * feats + 16, :] = jnp.concatenate(tile, axis=0).astype(jnp.bfloat16)
    for slab in slabs:
        slab.wait()


def prefill(keys, values, weight, lengths):
    heads, head_size, feats = weight.shape
    span, width = keys.shape[1:]
    arrays = (keys, values, weight)
    hbm = pl.BlockSpec(memory_space=pltpu.MemorySpace.HBM)
    vmem = pl.BlockSpec(memory_space=pltpu.VMEM)
    return pl.pallas_call(
        prefill_kernel,
        in_specs=[pl.BlockSpec(memory_space=pltpu.SMEM)] + [hbm] * len(arrays),
        out_specs=vmem,
        out_shape=jax.ShapeDtypeStruct((heads * feats + 16 + 2 * heads * SLAB, head_size), jnp.bfloat16),
        scratch_shapes=[
            pltpu.VMEM((span, width), jnp.bfloat16),
            pltpu.VMEM((span, width), jnp.bfloat16),
            pltpu.VMEM(weight.shape, jnp.bfloat16),
            pltpu.VMEM((heads // 2, 2 * feats, 2 * head_size), jnp.bfloat16),
            pltpu.VMEM((heads // 2, 2 * feats, 2 * head_size), jnp.float32),
            pltpu.VMEM((heads // 2, 2 * feats, 128), jnp.float32),
            pltpu.SemaphoreType.DMA,
            pltpu.SemaphoreType.DMA((2, span // BLOCK)),
            pltpu.SemaphoreType.DMA((2, heads)),
        ],
        compiler_params=pltpu.CompilerParams(vmem_limit_bytes=40 * 1024 * 1024),
        cost_estimate=pl.CostEstimate(
            flops=4 * span * width * feats, bytes_accessed=4 * span * width, transcendentals=span * width
        ),
        name="prefill",
    )(lengths, *[pltpu.with_memory_space_constraint(x, pltpu.MemorySpace.HBM) for x in arrays])


def decode_kernel(rows_ref, weight_ref, near_ref, far_ref, *out_refs):
    heads, head_size, feats = weight_ref.shape
    count, width = rows_ref.shape
    group = width // (heads * head_size)
    each = count // len(out_refs)
    tile_at = heads * feats
    halves = (near_ref, far_ref)
    tiles = [ref[tile_at : tile_at + 16, :].astype(jnp.float32) for ref in halves]
    lane = lax.broadcasted_iota(jnp.int32, (count, head_size), 1)
    dens = jnp.zeros((count, head_size), jnp.float32)
    for g in range(heads):
        query = jnp.concatenate(
            [
                rows_ref[:, (g * group + h) * head_size : (g * group + h + 1) * head_size]
                for h in range(group)
            ],
            axis=0,
        )
        wide = query.astype(jnp.float32)
        phi = feature(jnp.dot(query, weight_ref[g], preferred_element_type=jnp.float32)).astype(jnp.bfloat16)
        scale = (TAU / head_size) * lax.rsqrt(jnp.mean(wide * wide, axis=-1, keepdims=True) + EPS)
        num, den, linear = 0.0, 0.0, 0.0
        for ref, tile in zip(halves, tiles):
            linear += jnp.dot(phi, ref[g * feats : (g + 1) * feats, :], preferred_element_type=jnp.float32)
            at = tile_at + 16 + g * SLAB
            keys = ref[at : at + SLAB, :]
            at += heads * SLAB
            values = ref[at : at + SLAB, :]
            keys_wide = keys.astype(jnp.float32)
            key_scale = lax.rsqrt(jnp.mean((keys_wide * keys_wide).T, axis=0, keepdims=True) + EPS)
            score = lax.dot_general(query, keys, NT, preferred_element_type=jnp.float32) * scale * key_scale
            weights = jnp.exp(score) * tile[MASK_ROW : MASK_ROW + 1, :SLAB]
            num += jnp.dot(weights.astype(jnp.bfloat16), values, preferred_element_type=jnp.float32)
            den += jnp.sum(weights, axis=-1, keepdims=True)
        norm = (tiles[0] + tiles[1])[g : g + 1]
        back = 1.0 / (feats * feats)
        den += jnp.sum(phi.astype(jnp.float32) * norm, axis=-1, keepdims=True) * back
        result = (linear * back + num).astype(jnp.bfloat16)
        for h in range(group):
            head = g * group + h
            dens = jnp.where(lane == head, den[h * count : (h + 1) * count], dens)
            for k, out_ref in enumerate(out_refs):
                start = h * count + k * each
                out_ref[:, head * head_size : (head + 1) * head_size] = result[start : start + each]
    high = dens.astype(jnp.bfloat16)
    low = (dens - high.astype(jnp.float32)).astype(jnp.bfloat16)
    for k, out_ref in enumerate(out_refs):
        out_ref[:, width : width + head_size] = high[k * each : (k + 1) * each]
        out_ref[:, width + head_size :] = low[k * each : (k + 1) * each]


def decode(rows, weight, near, far, parts):
    heads, head_size, feats = weight.shape
    count, width = rows.shape
    vmem = pl.BlockSpec(memory_space=pltpu.VMEM)
    return pl.pallas_call(
        decode_kernel,
        in_specs=[vmem] * 4,
        out_specs=[vmem] * parts,
        out_shape=[jax.ShapeDtypeStruct((count // parts, width + 2 * head_size), jnp.bfloat16)] * parts,
        compiler_params=pltpu.CompilerParams(vmem_limit_bytes=32 * 1024 * 1024),
        cost_estimate=pl.CostEstimate(
            flops=10 * count * width * feats, bytes_accessed=4 * count * width, transcendentals=2 * count * width
        ),
        name="decode",
    )(rows, weight, near, far)


def own_kernel(queries_ref, keys_ref, values_ref, _, num_ref, weight_ref):
    count, width = queries_ref.shape
    head_size = weight_ref.shape[1]
    heads = keys_ref.shape[1] // head_size
    group = width // (heads * head_size)
    lane = lax.broadcasted_iota(jnp.int32, (count, head_size), 1)
    kept = jnp.zeros((count, head_size), jnp.float32)
    for g in range(heads):
        cols = slice(g * head_size, (g + 1) * head_size)
        key = keys_ref[:, cols].astype(jnp.float32)
        value = values_ref[:, cols].astype(jnp.float32)
        key = key * lax.rsqrt(jnp.mean(key * key, axis=-1, keepdims=True) + EPS)
        for h in range(group):
            head = g * group + h
            span = slice(head * head_size, (head + 1) * head_size)
            query = queries_ref[:, span].astype(jnp.float32)
            scale = (TAU / head_size) * lax.rsqrt(jnp.mean(query * query, axis=-1, keepdims=True) + EPS)
            weight = jnp.exp(jnp.sum(query * key, axis=-1, keepdims=True) * scale)
            num_ref[:, span] = weight.astype(jnp.bfloat16).astype(jnp.float32) * value
            kept = jnp.where(lane == head, weight, kept)
    weight_ref[...] = kept


def own(queries, new_keys, new_values, after, head_size):
    vmem = pl.BlockSpec(memory_space=pltpu.VMEM)
    count, width = queries.shape
    return pl.pallas_call(
        own_kernel,
        in_specs=[vmem] * 4,
        out_specs=[vmem, vmem],
        out_shape=[
            jax.ShapeDtypeStruct((count, width), jnp.float32),
            jax.ShapeDtypeStruct((count, head_size), jnp.float32),
        ],
        compiler_params=pltpu.CompilerParams(vmem_limit_bytes=8 * 1024 * 1024),
        cost_estimate=pl.CostEstimate(
            flops=8 * count * width, bytes_accessed=8 * count * width, transcendentals=count * width // head_size
        ),
        name="own",
    )(queries, new_keys, new_values, after)


def finish_kernel(prompts_ref, num_ref, weight_ref, *refs):
    block_refs, out_ref = refs[:-1], refs[-1]
    count, width = out_ref.shape
    head_size = weight_ref.shape[1]
    sects = len(block_refs)
    sect = lax.axis_index("sect")
    first = (sect * lax.axis_size("sub") + lax.axis_index("sub")) * count
    rows = prompts_ref.shape[1]
    row = first + lax.broadcasted_iota(jnp.int32, (count, rows), 0)
    lane = lax.broadcasted_iota(jnp.int32, (count, rows), 1)
    prompt = jnp.sum(jnp.where(lane == row, prompts_ref[...], 0), axis=1, keepdims=True)
    chosen = block_refs[0][...].astype(jnp.float32)
    for k in range(1, sects):
        source = lax.rem(sect - k + sects, sects)
        chosen = jnp.where(prompt == source, block_refs[k][...].astype(jnp.float32), chosen)
    den = chosen[:, width : width + head_size] + chosen[:, width + head_size :] + weight_ref[...]
    scale = 1.0 / den
    for head in range(width // head_size):
        span = slice(head * head_size, (head + 1) * head_size)
        out_ref[:, span] = ((chosen[:, span] + num_ref[:, span]) * scale[:, head : head + 1]).astype(out_ref.dtype)


def finish(row_prompt, num, weight, blocks):
    vmem = pl.BlockSpec(memory_space=pltpu.VMEM)
    return pl.pallas_call(
        finish_kernel,
        in_specs=[vmem] * (3 + len(blocks)),
        out_specs=vmem,
        out_shape=jax.ShapeDtypeStruct(num.shape, jnp.bfloat16),
        compiler_params=pltpu.CompilerParams(vmem_limit_bytes=8 * 1024 * 1024),
        name="finish",
    )(row_prompt.reshape(1, -1), num, weight, *blocks)


def body(
    sects, prompt_keys, prompt_values, lengths, feature_weight, queries, new_keys, new_values, row_prompt
):
    blocks = [queries] + [
        lax.ppermute(queries, "sect", [((i + k) % sects, i) for i in range(sects)]) for k in range(1, sects)
    ]
    near = prefill(prompt_keys, prompt_values, feature_weight, lengths)
    far = lax.ppermute(near, "sub", [(0, 1), (1, 0)])
    results = decode(jnp.concatenate(blocks, axis=0), feature_weight, near, far, sects)
    num, weight = own(queries, new_keys, new_values, results[0], feature_weight.shape[1])
    back = [results[0]] + [
        lax.ppermute(results[k], "sect", [(i, (i + k) % sects) for i in range(sects)]) for k in range(1, sects)
    ]
    return finish(row_prompt, num, weight, back)


def solution(mesh):
    placed = (
        P(("parts", "sect"), "sub", "tp"),
        P(("parts", "sect"), "sub", "tp"),
        P(("parts", "sect")),
        P("tp", None, None),
        P(("parts", "sect", "sub"), "tp"),
        P(("parts", "sect", "sub"), "tp"),
        P(("parts", "sect", "sub"), "tp"),
        P("parts"),
    )
    return jax.shard_map(
        functools.partial(body, mesh.shape["sect"]),
        mesh=mesh,
        in_specs=placed,
        out_specs=P(("parts", "sect", "sub"), "tp"),
        check_vma=False,
    )
```

```python
import functools

import jax
import jax.numpy as jnp
from jax import lax
from jax.experimental import pallas as pl
from jax.experimental.pallas import tpu as pltpu
from jax.sharding import PartitionSpec as P

WINDOW = 64
TAU = 10.0
EPS = 1e-06
BLOCK = 512
AHEAD = 3
NT = (((1,), (1,)), ((), ()))
TN = (((0,), (0,)), ((), ()))


def feature(proj):
    return jnp.maximum(proj, 0.0) + jnp.exp(jnp.minimum(proj, 0.0))


SLAB = WINDOW + 16
MASK_ROW = 8


def prefill_kernel(
    lengths_ref, keys_ref, values_ref, weight_ref, out_ref,
    keys_at, values_at, weight_at, wide_ref, state_ref, norm_ref,
    weight_sem, load_sem, slab_sem,
):
    heads, head_size, feats = weight_ref.shape
    pairs = heads // 2
    span = keys_ref.shape[1]
    chunks = span // BLOCK
    get_weight = pltpu.make_async_copy(weight_ref, weight_at, weight_sem)
    get_weight.start()
    loads = []
    for c in range(chunks):
        rows = pl.ds(c * BLOCK, BLOCK)
        loads.append(
            [
                pltpu.make_async_copy(keys_ref.at[0, rows, :], keys_at.at[rows, :], load_sem.at[0, c]),
                pltpu.make_async_copy(values_ref.at[0, rows, :], values_at.at[rows, :], load_sem.at[1, c]),
            ]
        )

    def fetch(c):
        for priority, load in enumerate(loads[c]):
            load.start(priority=priority)

    for c in range(AHEAD):
        fetch(c)
    state_ref[...] = jnp.zeros_like(state_ref)
    norm_ref[...] = jnp.zeros_like(norm_ref)
    wide_ref[...] = jnp.zeros_like(wide_ref)
    get_weight.wait()
    for g in range(heads):
        half = g % 2
        wide_ref[g // 2, half * head_size : (half + 1) * head_size, half * feats : (half + 1) * feats] = weight_at[g]

    begin = lengths_ref[0] - WINDOW - lax.axis_index("sub") * span
    first = jnp.clip(begin, 0, span - SLAB)
    first = pl.multiple_of(first - lax.rem(first, 16), 16)
    slabs = []
    for i, source in enumerate((keys_ref, values_ref)):
        for g in range(heads):
            at = heads * feats + 16 + (i * heads + g) * SLAB
            slabs.append(
                pltpu.make_async_copy(
                    source.at[0, pl.ds(first, SLAB), g * head_size : (g + 1) * head_size],
                    out_ref.at[at : at + SLAB, :],
                    slab_sem.at[i, g],
                )
            )
            slabs[-1].start()

    for c in range(chunks):
        rows = slice(c * BLOCK, (c + 1) * BLOCK)
        for load in loads[c]:
            load.wait()
        if c + AHEAD < chunks:
            fetch(c + AHEAD)
        position = c * BLOCK + lax.broadcasted_iota(jnp.int32, (BLOCK, 1), 0)
        live = position < begin
        for j in range(pairs):
            cols = slice(j * 2 * head_size, (j + 1) * 2 * head_size)
            proj = jnp.dot(keys_at[rows, cols], wide_ref[j], preferred_element_type=jnp.float32)
            mapped = jnp.where(live, feature(proj), 0.0)
            norm_ref[j] += jnp.sum(mapped.reshape(BLOCK // 8, 8, 2 * feats), axis=0)
            state_ref[j] += lax.dot_general(
                values_at[rows, cols], mapped.astype(jnp.bfloat16), TN, preferred_element_type=jnp.float32
            )

    tile = []
    for g in range(heads):
        half = g % 2
        part = state_ref[g // 2, half * head_size : (half + 1) * head_size, half * feats : (half + 1) * feats]
        out_ref[g * head_size : (g + 1) * head_size, :] = part.astype(jnp.bfloat16)
        tile.append(jnp.sum(norm_ref[g // 2, :, half * feats : (half + 1) * feats], axis=0, keepdims=True))
    slot = first + lax.broadcasted_iota(jnp.int32, (1, head_size), 1)
    tile.append(jnp.zeros((MASK_ROW - heads, head_size), jnp.float32))
    tile.append(jnp.where((slot >= begin) & (slot < begin + WINDOW), 1.0, 0.0))
    tile.append(jnp.zeros((15 - MASK_ROW, head_size), jnp.float32))
    out_ref[heads * feats : heads * feats + 16, :] = jnp.concatenate(tile, axis=0).astype(jnp.bfloat16)
    for slab in slabs:
        slab.wait()


def prefill(keys, values, weight, lengths):
    heads, head_size, feats = weight.shape
    span, width = keys.shape[1:]
    arrays = (keys, values, weight)
    hbm = pl.BlockSpec(memory_space=pltpu.MemorySpace.HBM)
    vmem = pl.BlockSpec(memory_space=pltpu.VMEM)
    return pl.pallas_call(
        prefill_kernel,
        in_specs=[pl.BlockSpec(memory_space=pltpu.SMEM)] + [hbm] * len(arrays),
        out_specs=vmem,
        out_shape=jax.ShapeDtypeStruct((heads * feats + 16 + 2 * heads * SLAB, head_size), jnp.bfloat16),
        scratch_shapes=[
            pltpu.VMEM((span, width), jnp.bfloat16),
            pltpu.VMEM((span, width), jnp.bfloat16),
            pltpu.VMEM(weight.shape, jnp.bfloat16),
            pltpu.VMEM((heads // 2, 2 * head_size, 2 * feats), jnp.bfloat16),
            pltpu.VMEM((heads // 2, 2 * head_size, 2 * feats), jnp.float32),
            pltpu.VMEM((heads // 2, 8, 2 * feats), jnp.float32),
            pltpu.SemaphoreType.DMA,
            pltpu.SemaphoreType.DMA((2, span // BLOCK)),
            pltpu.SemaphoreType.DMA((2, heads)),
        ],
        compiler_params=pltpu.CompilerParams(vmem_limit_bytes=40 * 1024 * 1024),
        cost_estimate=pl.CostEstimate(
            flops=4 * span * width * feats, bytes_accessed=4 * span * width, transcendentals=span * width
        ),
        name="prefill",
    )(lengths, *[pltpu.with_memory_space_constraint(x, pltpu.MemorySpace.HBM) for x in arrays])


def decode_kernel(rows_ref, weight_ref, near_ref, far_ref, *out_refs):
    heads, head_size, feats = weight_ref.shape
    count, width = rows_ref.shape
    group = width // (heads * head_size)
    each = count // len(out_refs)
    tile_at = heads * feats
    halves = (near_ref, far_ref)
    tiles = [ref[tile_at : tile_at + 16, :].astype(jnp.float32) for ref in halves]
    lane = lax.broadcasted_iota(jnp.int32, (count, head_size), 1)
    dens = jnp.zeros((count, head_size), jnp.float32)
    for g in range(heads):
        query = jnp.concatenate(
            [
                rows_ref[:, (g * group + h) * head_size : (g * group + h + 1) * head_size]
                for h in range(group)
            ],
            axis=0,
        )
        wide = query.astype(jnp.float32)
        phi = feature(jnp.dot(query, weight_ref[g], preferred_element_type=jnp.float32)).astype(jnp.bfloat16)
        scale = (TAU / head_size) * lax.rsqrt(jnp.mean(wide * wide, axis=-1, keepdims=True) + EPS)
        num, den, linear = 0.0, 0.0, 0.0
        for ref, tile in zip(halves, tiles):
            linear += lax.dot_general(
                phi, ref[g * head_size : (g + 1) * head_size, :], NT, preferred_element_type=jnp.float32
            )
            at = tile_at + 16 + g * SLAB
            keys = ref[at : at + SLAB, :]
            at += heads * SLAB
            values = ref[at : at + SLAB, :]
            keys_wide = keys.astype(jnp.float32)
            key_scale = lax.rsqrt(jnp.mean((keys_wide * keys_wide).T, axis=0, keepdims=True) + EPS)
            score = lax.dot_general(query, keys, NT, preferred_element_type=jnp.float32) * scale * key_scale
            weights = jnp.exp(score) * tile[MASK_ROW : MASK_ROW + 1, :SLAB]
            num += jnp.dot(weights.astype(jnp.bfloat16), values, preferred_element_type=jnp.float32)
            den += jnp.sum(weights, axis=-1, keepdims=True)
        norm = (tiles[0] + tiles[1])[g : g + 1]
        back = 1.0 / (feats * feats)
        den += jnp.sum(phi.astype(jnp.float32) * norm, axis=-1, keepdims=True) * back
        result = (linear * back + num).astype(jnp.bfloat16)
        for h in range(group):
            head = g * group + h
            dens = jnp.where(lane == head, den[h * count : (h + 1) * count], dens)
            for k, out_ref in enumerate(out_refs):
                start = h * count + k * each
                out_ref[:, head * head_size : (head + 1) * head_size] = result[start : start + each]
    high = dens.astype(jnp.bfloat16)
    low = (dens - high.astype(jnp.float32)).astype(jnp.bfloat16)
    for k, out_ref in enumerate(out_refs):
        out_ref[:, width : width + head_size] = high[k * each : (k + 1) * each]
        out_ref[:, width + head_size :] = low[k * each : (k + 1) * each]


def decode(rows, weight, near, far, parts):
    heads, head_size, feats = weight.shape
    count, width = rows.shape
    vmem = pl.BlockSpec(memory_space=pltpu.VMEM)
    return pl.pallas_call(
        decode_kernel,
        in_specs=[vmem] * 4,
        out_specs=[vmem] * parts,
        out_shape=[jax.ShapeDtypeStruct((count // parts, width + 2 * head_size), jnp.bfloat16)] * parts,
        compiler_params=pltpu.CompilerParams(vmem_limit_bytes=32 * 1024 * 1024),
        cost_estimate=pl.CostEstimate(
            flops=10 * count * width * feats, bytes_accessed=4 * count * width, transcendentals=2 * count * width
        ),
        name="decode",
    )(rows, weight, near, far)


def own_kernel(queries_ref, keys_ref, values_ref, _, num_ref, weight_ref):
    count, width = queries_ref.shape
    head_size = weight_ref.shape[1]
    heads = keys_ref.shape[1] // head_size
    group = width // (heads * head_size)
    lane = lax.broadcasted_iota(jnp.int32, (count, head_size), 1)
    kept = jnp.zeros((count, head_size), jnp.float32)
    for g in range(heads):
        cols = slice(g * head_size, (g + 1) * head_size)
        key = keys_ref[:, cols].astype(jnp.float32)
        value = values_ref[:, cols].astype(jnp.float32)
        key = key * lax.rsqrt(jnp.mean(key * key, axis=-1, keepdims=True) + EPS)
        for h in range(group):
            head = g * group + h
            span = slice(head * head_size, (head + 1) * head_size)
            query = queries_ref[:, span].astype(jnp.float32)
            scale = (TAU / head_size) * lax.rsqrt(jnp.mean(query * query, axis=-1, keepdims=True) + EPS)
            weight = jnp.exp(jnp.sum(query * key, axis=-1, keepdims=True) * scale)
            num_ref[:, span] = weight.astype(jnp.bfloat16).astype(jnp.float32) * value
            kept = jnp.where(lane == head, weight, kept)
    weight_ref[...] = kept


def own(queries, new_keys, new_values, after, head_size):
    vmem = pl.BlockSpec(memory_space=pltpu.VMEM)
    count, width = queries.shape
    return pl.pallas_call(
        own_kernel,
        in_specs=[vmem] * 4,
        out_specs=[vmem, vmem],
        out_shape=[
            jax.ShapeDtypeStruct((count, width), jnp.float32),
            jax.ShapeDtypeStruct((count, head_size), jnp.float32),
        ],
        compiler_params=pltpu.CompilerParams(vmem_limit_bytes=8 * 1024 * 1024),
        cost_estimate=pl.CostEstimate(
            flops=8 * count * width, bytes_accessed=8 * count * width, transcendentals=count * width // head_size
        ),
        name="own",
    )(queries, new_keys, new_values, after)


def finish_kernel(prompts_ref, num_ref, weight_ref, *refs):
    block_refs, out_ref = refs[:-1], refs[-1]
    count, width = out_ref.shape
    head_size = weight_ref.shape[1]
    sects = len(block_refs)
    sect = lax.axis_index("sect")
    first = (sect * lax.axis_size("sub") + lax.axis_index("sub")) * count
    rows = prompts_ref.shape[1]
    row = first + lax.broadcasted_iota(jnp.int32, (count, rows), 0)
    lane = lax.broadcasted_iota(jnp.int32, (count, rows), 1)
    prompt = jnp.sum(jnp.where(lane == row, prompts_ref[...], 0), axis=1, keepdims=True)
    chosen = block_refs[0][...].astype(jnp.float32)
    for k in range(1, sects):
        source = lax.rem(sect - k + sects, sects)
        chosen = jnp.where(prompt == source, block_refs[k][...].astype(jnp.float32), chosen)
    den = chosen[:, width : width + head_size] + chosen[:, width + head_size :] + weight_ref[...]
    scale = 1.0 / den
    for head in range(width // head_size):
        span = slice(head * head_size, (head + 1) * head_size)
        out_ref[:, span] = ((chosen[:, span] + num_ref[:, span]) * scale[:, head : head + 1]).astype(out_ref.dtype)


def finish(row_prompt, num, weight, blocks):
    vmem = pl.BlockSpec(memory_space=pltpu.VMEM)
    return pl.pallas_call(
        finish_kernel,
        in_specs=[vmem] * (3 + len(blocks)),
        out_specs=vmem,
        out_shape=jax.ShapeDtypeStruct(num.shape, jnp.bfloat16),
        compiler_params=pltpu.CompilerParams(vmem_limit_bytes=8 * 1024 * 1024),
        name="finish",
    )(row_prompt.reshape(1, -1), num, weight, *blocks)


def body(
    sects, prompt_keys, prompt_values, lengths, feature_weight, queries, new_keys, new_values, row_prompt
):
    blocks = [queries] + [
        lax.ppermute(queries, "sect", [((i + k) % sects, i) for i in range(sects)]) for k in range(1, sects)
    ]
    near = prefill(prompt_keys, prompt_values, feature_weight, lengths)
    far = lax.ppermute(near, "sub", [(0, 1), (1, 0)])
    results = decode(jnp.concatenate(blocks, axis=0), feature_weight, near, far, sects)
    num, weight = own(queries, new_keys, new_values, results[0], feature_weight.shape[1])
    back = [results[0]] + [
        lax.ppermute(results[k], "sect", [(i, (i + k) % sects) for i in range(sects)]) for k in range(1, sects)
    ]
    return finish(row_prompt, num, weight, back)


def solution(mesh):
    placed = (
        P(("parts", "sect"), "sub", "tp"),
        P(("parts", "sect"), "sub", "tp"),
        P(("parts", "sect")),
        P("tp", None, None),
        P(("parts", "sect", "sub"), "tp"),
        P(("parts", "sect", "sub"), "tp"),
        P(("parts", "sect", "sub"), "tp"),
        P("parts"),
    )
    return jax.shard_map(
        functools.partial(body, mesh.shape["sect"]),
        mesh=mesh,
        in_specs=placed,
        out_specs=P(("parts", "sect", "sub"), "tp"),
        check_vma=False,
    )
```

```python
import functools

import jax
import jax.numpy as jnp
from jax import lax
from jax.experimental import pallas as pl
from jax.experimental.pallas import tpu as pltpu
from jax.sharding import PartitionSpec as P

WINDOW = 64
TAU = 10.0
EPS = 1e-06
BLOCK = 512
AHEAD = 3
NT = (((1,), (1,)), ((), ()))


def feature(proj):
    return jnp.maximum(proj, 0.0) + jnp.exp(jnp.minimum(proj, 0.0))


SLAB = WINDOW + 16
MASK_ROW = 8


def prefill_kernel(
    lengths_ref, keys_ref, values_ref, weight_ref, out_ref,
    keys_at, values_at, weight_at, wide_ref, proj_ref, state_ref, norm_ref,
    weight_sem, load_sem, slab_sem,
):
    heads, head_size, feats = weight_ref.shape
    pairs = heads // 2
    span = keys_ref.shape[1]
    chunks = span // BLOCK
    get_weight = pltpu.make_async_copy(weight_ref, weight_at, weight_sem)
    get_weight.start()
    loads = []
    for c in range(chunks):
        rows = pl.ds(c * BLOCK, BLOCK)
        loads.append(
            [
                pltpu.make_async_copy(keys_ref.at[0, rows, :], keys_at.at[rows, :], load_sem.at[0, c]),
                pltpu.make_async_copy(values_ref.at[0, rows, :], values_at.at[rows, :], load_sem.at[1, c]),
            ]
        )

    def fetch(c):
        for priority, load in enumerate(loads[c]):
            load.start(priority=priority)

    for c in range(AHEAD):
        fetch(c)
    state_ref[...] = jnp.zeros_like(state_ref)
    norm_ref[...] = jnp.zeros_like(norm_ref)
    wide_ref[...] = jnp.zeros_like(wide_ref)
    get_weight.wait()
    for g in range(heads):
        half = g % 2
        turned = weight_at[g].astype(jnp.float32).T.astype(jnp.bfloat16)
        wide_ref[g // 2, half * feats : (half + 1) * feats, half * head_size : (half + 1) * head_size] = turned

    begin = lengths_ref[0] - WINDOW - lax.axis_index("sub") * span
    first = jnp.clip(begin, 0, span - SLAB)
    first = pl.multiple_of(first - lax.rem(first, 16), 16)
    slabs = []
    for i, source in enumerate((keys_ref, values_ref)):
        for g in range(heads):
            at = heads * feats + 16 + (i * heads + g) * SLAB
            slabs.append(
                pltpu.make_async_copy(
                    source.at[0, pl.ds(first, SLAB), g * head_size : (g + 1) * head_size],
                    out_ref.at[at : at + SLAB, :],
                    slab_sem.at[i, g],
                )
            )
            slabs[-1].start()

    def project(c):
        for load in loads[c]:
            load.wait()
        if c + AHEAD < chunks:
            fetch(c + AHEAD)
        for j in range(pairs):
            proj = lax.dot_general(
                wide_ref[j],
                keys_at[c * BLOCK : (c + 1) * BLOCK, j * 2 * head_size : (j + 1) * 2 * head_size],
                NT,
                preferred_element_type=jnp.float32,
            )
            proj_ref[c % 2, j] = proj.astype(jnp.bfloat16)

    def collect(c):
        position = c * BLOCK + lax.broadcasted_iota(jnp.int32, (1, BLOCK), 1)
        live = jnp.where(position < begin, 1.0, 0.0).astype(jnp.bfloat16)
        for j in range(pairs):
            mapped = feature(proj_ref[c % 2, j]) * live
            some = [mapped[:, k * 128 : (k + 1) * 128] for k in range(BLOCK // 128)]
            while len(some) > 1:
                some = [x + y for x, y in zip(some[::2], some[1::2])]
            norm_ref[j] += some[0].astype(jnp.float32)
            state_ref[j] += jnp.dot(
                mapped,
                values_at[c * BLOCK : (c + 1) * BLOCK, j * 2 * head_size : (j + 1) * 2 * head_size],
                preferred_element_type=jnp.float32,
            )

    project(0)
    for c in range(chunks):
        if c + 1 < chunks:
            project(c + 1)
        collect(c)

    tile = []
    for g in range(heads):
        half = g % 2
        part = state_ref[g // 2, half * feats : (half + 1) * feats, half * head_size : (half + 1) * head_size]
        out_ref[g * feats : (g + 1) * feats, :] = part.astype(jnp.bfloat16)
        sums = norm_ref[g // 2, half * feats : (half + 1) * feats, :]
        tile.append(jnp.sum(sums.T, axis=0, keepdims=True))
    slot = first + lax.broadcasted_iota(jnp.int32, (1, head_size), 1)
    tile.append(jnp.zeros((MASK_ROW - heads, head_size), jnp.float32))
    tile.append(jnp.where((slot >= begin) & (slot < begin + WINDOW), 1.0, 0.0))
    tile.append(jnp.zeros((15 - MASK_ROW, head_size), jnp.float32))
    out_ref[heads * feats : heads * feats + 16, :] = jnp.concatenate(tile, axis=0).astype(jnp.bfloat16)
    for slab in slabs:
        slab.wait()


def prefill(keys, values, weight, lengths):
    heads, head_size, feats = weight.shape
    span, width = keys.shape[1:]
    arrays = (keys, values, weight)
    hbm = pl.BlockSpec(memory_space=pltpu.MemorySpace.HBM)
    vmem = pl.BlockSpec(memory_space=pltpu.VMEM)
    return pl.pallas_call(
        prefill_kernel,
        in_specs=[pl.BlockSpec(memory_space=pltpu.SMEM)] + [hbm] * len(arrays),
        out_specs=vmem,
        out_shape=jax.ShapeDtypeStruct((heads * feats + 16 + 2 * heads * SLAB, head_size), jnp.bfloat16),
        scratch_shapes=[
            pltpu.VMEM((span, width), jnp.bfloat16),
            pltpu.VMEM((span, width), jnp.bfloat16),
            pltpu.VMEM(weight.shape, jnp.bfloat16),
            pltpu.VMEM((heads // 2, 2 * feats, 2 * head_size), jnp.bfloat16),
            pltpu.VMEM((2, heads // 2, 2 * feats, BLOCK), jnp.bfloat16),
            pltpu.VMEM((heads // 2, 2 * feats, 2 * head_size), jnp.float32),
            pltpu.VMEM((heads // 2, 2 * feats, 128), jnp.float32),
            pltpu.SemaphoreType.DMA,
            pltpu.SemaphoreType.DMA((2, span // BLOCK)),
            pltpu.SemaphoreType.DMA((2, heads)),
        ],
        compiler_params=pltpu.CompilerParams(vmem_limit_bytes=40 * 1024 * 1024),
        cost_estimate=pl.CostEstimate(
            flops=4 * span * width * feats, bytes_accessed=4 * span * width, transcendentals=span * width
        ),
        name="prefill",
    )(lengths, *[pltpu.with_memory_space_constraint(x, pltpu.MemorySpace.HBM) for x in arrays])


def decode_kernel(rows_ref, weight_ref, near_ref, far_ref, *out_refs):
    heads, head_size, feats = weight_ref.shape
    count, width = rows_ref.shape
    group = width // (heads * head_size)
    each = count // len(out_refs)
    tile_at = heads * feats
    halves = (near_ref, far_ref)
    tiles = [ref[tile_at : tile_at + 16, :].astype(jnp.float32) for ref in halves]
    lane = lax.broadcasted_iota(jnp.int32, (count, head_size), 1)
    dens = jnp.zeros((count, head_size), jnp.float32)
    for g in range(heads):
        query = jnp.concatenate(
            [
                rows_ref[:, (g * group + h) * head_size : (g * group + h + 1) * head_size]
                for h in range(group)
            ],
            axis=0,
        )
        wide = query.astype(jnp.float32)
        phi = feature(jnp.dot(query, weight_ref[g], preferred_element_type=jnp.float32)).astype(jnp.bfloat16)
        scale = (TAU / head_size) * lax.rsqrt(jnp.mean(wide * wide, axis=-1, keepdims=True) + EPS)
        num, den, linear = 0.0, 0.0, 0.0
        for ref, tile in zip(halves, tiles):
            linear += jnp.dot(phi, ref[g * feats : (g + 1) * feats, :], preferred_element_type=jnp.float32)
            at = tile_at + 16 + g * SLAB
            keys = ref[at : at + SLAB, :]
            at += heads * SLAB
            values = ref[at : at + SLAB, :]
            keys_wide = keys.astype(jnp.float32)
            key_scale = lax.rsqrt(jnp.mean((keys_wide * keys_wide).T, axis=0, keepdims=True) + EPS)
            score = lax.dot_general(query, keys, NT, preferred_element_type=jnp.float32) * scale * key_scale
            weights = jnp.exp(score) * tile[MASK_ROW : MASK_ROW + 1, :SLAB]
            num += jnp.dot(weights.astype(jnp.bfloat16), values, preferred_element_type=jnp.float32)
            den += jnp.sum(weights, axis=-1, keepdims=True)
        norm = (tiles[0] + tiles[1])[g : g + 1]
        back = 1.0 / (feats * feats)
        den += jnp.sum(phi.astype(jnp.float32) * norm, axis=-1, keepdims=True) * back
        result = (linear * back + num).astype(jnp.bfloat16)
        for h in range(group):
            head = g * group + h
            dens = jnp.where(lane == head, den[h * count : (h + 1) * count], dens)
            for k, out_ref in enumerate(out_refs):
                start = h * count + k * each
                out_ref[:, head * head_size : (head + 1) * head_size] = result[start : start + each]
    high = dens.astype(jnp.bfloat16)
    low = (dens - high.astype(jnp.float32)).astype(jnp.bfloat16)
    for k, out_ref in enumerate(out_refs):
        out_ref[:, width : width + head_size] = high[k * each : (k + 1) * each]
        out_ref[:, width + head_size :] = low[k * each : (k + 1) * each]


def decode(rows, weight, near, far, parts):
    heads, head_size, feats = weight.shape
    count, width = rows.shape
    vmem = pl.BlockSpec(memory_space=pltpu.VMEM)
    return pl.pallas_call(
        decode_kernel,
        in_specs=[vmem] * 4,
        out_specs=[vmem] * parts,
        out_shape=[jax.ShapeDtypeStruct((count // parts, width + 2 * head_size), jnp.bfloat16)] * parts,
        compiler_params=pltpu.CompilerParams(vmem_limit_bytes=32 * 1024 * 1024),
        cost_estimate=pl.CostEstimate(
            flops=10 * count * width * feats, bytes_accessed=4 * count * width, transcendentals=2 * count * width
        ),
        name="decode",
    )(rows, weight, near, far)


def own_kernel(queries_ref, keys_ref, values_ref, _, num_ref, weight_ref):
    count, width = queries_ref.shape
    head_size = weight_ref.shape[1]
    heads = keys_ref.shape[1] // head_size
    group = width // (heads * head_size)
    lane = lax.broadcasted_iota(jnp.int32, (count, head_size), 1)
    kept = jnp.zeros((count, head_size), jnp.float32)
    for g in range(heads):
        cols = slice(g * head_size, (g + 1) * head_size)
        key = keys_ref[:, cols].astype(jnp.float32)
        value = values_ref[:, cols].astype(jnp.float32)
        key = key * lax.rsqrt(jnp.mean(key * key, axis=-1, keepdims=True) + EPS)
        for h in range(group):
            head = g * group + h
            span = slice(head * head_size, (head + 1) * head_size)
            query = queries_ref[:, span].astype(jnp.float32)
            scale = (TAU / head_size) * lax.rsqrt(jnp.mean(query * query, axis=-1, keepdims=True) + EPS)
            weight = jnp.exp(jnp.sum(query * key, axis=-1, keepdims=True) * scale)
            num_ref[:, span] = weight.astype(jnp.bfloat16).astype(jnp.float32) * value
            kept = jnp.where(lane == head, weight, kept)
    weight_ref[...] = kept


def own(queries, new_keys, new_values, after, head_size):
    vmem = pl.BlockSpec(memory_space=pltpu.VMEM)
    count, width = queries.shape
    return pl.pallas_call(
        own_kernel,
        in_specs=[vmem] * 4,
        out_specs=[vmem, vmem],
        out_shape=[
            jax.ShapeDtypeStruct((count, width), jnp.float32),
            jax.ShapeDtypeStruct((count, head_size), jnp.float32),
        ],
        compiler_params=pltpu.CompilerParams(vmem_limit_bytes=8 * 1024 * 1024),
        cost_estimate=pl.CostEstimate(
            flops=8 * count * width, bytes_accessed=8 * count * width, transcendentals=count * width // head_size
        ),
        name="own",
    )(queries, new_keys, new_values, after)


def finish_kernel(prompts_ref, num_ref, weight_ref, *refs):
    block_refs, out_ref = refs[:-1], refs[-1]
    count, width = out_ref.shape
    head_size = weight_ref.shape[1]
    sects = len(block_refs)
    sect = lax.axis_index("sect")
    first = (sect * lax.axis_size("sub") + lax.axis_index("sub")) * count
    rows = prompts_ref.shape[1]
    row = first + lax.broadcasted_iota(jnp.int32, (count, rows), 0)
    lane = lax.broadcasted_iota(jnp.int32, (count, rows), 1)
    prompt = jnp.sum(jnp.where(lane == row, prompts_ref[...], 0), axis=1, keepdims=True)
    chosen = block_refs[0][...].astype(jnp.float32)
    for k in range(1, sects):
        source = lax.rem(sect - k + sects, sects)
        chosen = jnp.where(prompt == source, block_refs[k][...].astype(jnp.float32), chosen)
    den = chosen[:, width : width + head_size] + chosen[:, width + head_size :] + weight_ref[...]
    scale = 1.0 / den
    for head in range(width // head_size):
        span = slice(head * head_size, (head + 1) * head_size)
        out_ref[:, span] = ((chosen[:, span] + num_ref[:, span]) * scale[:, head : head + 1]).astype(out_ref.dtype)


def finish(row_prompt, num, weight, blocks):
    vmem = pl.BlockSpec(memory_space=pltpu.VMEM)
    return pl.pallas_call(
        finish_kernel,
        in_specs=[vmem] * (3 + len(blocks)),
        out_specs=vmem,
        out_shape=jax.ShapeDtypeStruct(num.shape, jnp.bfloat16),
        compiler_params=pltpu.CompilerParams(vmem_limit_bytes=8 * 1024 * 1024),
        name="finish",
    )(row_prompt.reshape(1, -1), num, weight, *blocks)


def body(
    sects, prompt_keys, prompt_values, lengths, feature_weight, queries, new_keys, new_values, row_prompt
):
    blocks = [queries] + [
        lax.ppermute(queries, "sect", [((i + k) % sects, i) for i in range(sects)]) for k in range(1, sects)
    ]
    near = prefill(prompt_keys, prompt_values, feature_weight, lengths)
    far = lax.ppermute(near, "sub", [(0, 1), (1, 0)])
    results = decode(jnp.concatenate(blocks, axis=0), feature_weight, near, far, sects)
    num, weight = own(queries, new_keys, new_values, results[0], feature_weight.shape[1])
    back = [results[0]] + [
        lax.ppermute(results[k], "sect", [(i, (i + k) % sects) for i in range(sects)]) for k in range(1, sects)
    ]
    return finish(row_prompt, num, weight, back)


def solution(mesh):
    placed = (
        P(("parts", "sect"), "sub", "tp"),
        P(("parts", "sect"), "sub", "tp"),
        P(("parts", "sect")),
        P("tp", None, None),
        P(("parts", "sect", "sub"), "tp"),
        P(("parts", "sect", "sub"), "tp"),
        P(("parts", "sect", "sub"), "tp"),
        P("parts"),
    )
    return jax.shard_map(
        functools.partial(body, mesh.shape["sect"]),
        mesh=mesh,
        in_specs=placed,
        out_specs=P(("parts", "sect", "sub"), "tp"),
        check_vma=False,
    )
```

```python
import functools

import jax
import jax.numpy as jnp
from jax import lax
from jax.experimental import pallas as pl
from jax.experimental.pallas import tpu as pltpu
from jax.sharding import PartitionSpec as P

WINDOW = 64
TAU = 10.0
EPS = 1e-06
BLOCK = 1024
AHEAD = 2
NT = (((1,), (1,)), ((), ()))


def feature(proj):
    return jnp.maximum(proj, 0.0) + jnp.exp(jnp.minimum(proj, 0.0))


SLAB = WINDOW + 16
MASK_ROW = 8


def prefill_kernel(
    lengths_ref, keys_ref, values_ref, weight_ref, out_ref,
    keys_at, values_at, weight_at, wide_ref, proj_ref, state_ref, norm_ref,
    weight_sem, load_sem, slab_sem,
):
    heads, head_size, feats = weight_ref.shape
    pairs = heads // 2
    span = keys_ref.shape[1]
    cuts = [0, BLOCK // 4] + list(range(BLOCK, span + 1, BLOCK))
    chunks = len(cuts) - 1
    get_weight = pltpu.make_async_copy(weight_ref, weight_at, weight_sem)
    get_weight.start()
    loads = []
    for c in range(chunks):
        rows = pl.ds(cuts[c], cuts[c + 1] - cuts[c])
        loads.append(
            [
                pltpu.make_async_copy(keys_ref.at[0, rows, :], keys_at.at[rows, :], load_sem.at[0, c]),
                pltpu.make_async_copy(values_ref.at[0, rows, :], values_at.at[rows, :], load_sem.at[1, c]),
            ]
        )

    def fetch(c):
        for priority, load in enumerate(loads[c]):
            load.start(priority=priority)

    for c in range(AHEAD):
        fetch(c)
    wide_ref[...] = jnp.zeros_like(wide_ref)
    get_weight.wait()
    for g in range(heads):
        half = g % 2
        turned = weight_at[g].astype(jnp.float32).T.astype(jnp.bfloat16)
        wide_ref[g // 2, half * feats : (half + 1) * feats, half * head_size : (half + 1) * head_size] = turned

    begin = lengths_ref[0] - WINDOW - lax.axis_index("sub") * span
    first = jnp.clip(begin, 0, span - SLAB)
    first = pl.multiple_of(first - lax.rem(first, 16), 16)
    slabs = []
    for i, source in enumerate((keys_ref, values_ref)):
        for g in range(heads):
            at = heads * feats + 16 + (i * heads + g) * SLAB
            slabs.append(
                pltpu.make_async_copy(
                    source.at[0, pl.ds(first, SLAB), g * head_size : (g + 1) * head_size],
                    out_ref.at[at : at + SLAB, :],
                    slab_sem.at[i, g],
                )
            )
            slabs[-1].start()

    def project(c):
        for load in loads[c]:
            load.wait()
        if c + AHEAD < chunks:
            fetch(c + AHEAD)
        for j in range(pairs):
            proj = lax.dot_general(
                wide_ref[j],
                keys_at[cuts[c] : cuts[c + 1], j * 2 * head_size : (j + 1) * 2 * head_size],
                NT,
                preferred_element_type=jnp.float32,
            )
            proj_ref[c % 2, j, :, : cuts[c + 1] - cuts[c]] = proj.astype(jnp.bfloat16)

    def collect(c):
        size = cuts[c + 1] - cuts[c]
        position = cuts[c] + lax.broadcasted_iota(jnp.int32, (1, size), 1)
        live = jnp.where(position < begin, 1.0, 0.0).astype(jnp.bfloat16)
        for j in range(pairs):
            mapped = feature(proj_ref[c % 2, j, :, :size]) * live
            some = [mapped[:, k * 128 : (k + 1) * 128] for k in range(size // 128)]
            while len(some) > 1:
                some = [x + y for x, y in zip(some[::2], some[1::2])] + some[len(some) // 2 * 2 :]
            total = some[0].astype(jnp.float32)
            part = jnp.dot(
                mapped,
                values_at[cuts[c] : cuts[c + 1], j * 2 * head_size : (j + 1) * 2 * head_size],
                preferred_element_type=jnp.float32,
            )
            norm_ref[j] = total if c == 0 else norm_ref[j] + total
            state_ref[j] = part if c == 0 else state_ref[j] + part

    project(0)
    for c in range(chunks):
        if c + 1 < chunks:
            project(c + 1)
        collect(c)

    tile = []
    for g in range(heads):
        half = g % 2
        part = state_ref[g // 2, half * feats : (half + 1) * feats, half * head_size : (half + 1) * head_size]
        out_ref[g * feats : (g + 1) * feats, :] = part.astype(jnp.bfloat16)
        sums = norm_ref[g // 2, half * feats : (half + 1) * feats, :]
        tile.append(jnp.sum(sums.T, axis=0, keepdims=True))
    slot = first + lax.broadcasted_iota(jnp.int32, (1, head_size), 1)
    tile.append(jnp.zeros((MASK_ROW - heads, head_size), jnp.float32))
    tile.append(jnp.where((slot >= begin) & (slot < begin + WINDOW), 1.0, 0.0))
    tile.append(jnp.zeros((15 - MASK_ROW, head_size), jnp.float32))
    out_ref[heads * feats : heads * feats + 16, :] = jnp.concatenate(tile, axis=0).astype(jnp.bfloat16)
    for slab in slabs:
        slab.wait()


def prefill(keys, values, weight, lengths):
    heads, head_size, feats = weight.shape
    span, width = keys.shape[1:]
    arrays = (keys, values, weight)
    hbm = pl.BlockSpec(memory_space=pltpu.MemorySpace.HBM)
    vmem = pl.BlockSpec(memory_space=pltpu.VMEM)
    return pl.pallas_call(
        prefill_kernel,
        in_specs=[pl.BlockSpec(memory_space=pltpu.SMEM)] + [hbm] * len(arrays),
        out_specs=vmem,
        out_shape=jax.ShapeDtypeStruct((heads * feats + 16 + 2 * heads * SLAB, head_size), jnp.bfloat16),
        scratch_shapes=[
            pltpu.VMEM((span, width), jnp.bfloat16),
            pltpu.VMEM((span, width), jnp.bfloat16),
            pltpu.VMEM(weight.shape, jnp.bfloat16),
            pltpu.VMEM((heads // 2, 2 * feats, 2 * head_size), jnp.bfloat16),
            pltpu.VMEM((2, heads // 2, 2 * feats, BLOCK), jnp.bfloat16),
            pltpu.VMEM((heads // 2, 2 * feats, 2 * head_size), jnp.float32),
            pltpu.VMEM((heads // 2, 2 * feats, 128), jnp.float32),
            pltpu.SemaphoreType.DMA,
            pltpu.SemaphoreType.DMA((2, span // BLOCK + 1)),
            pltpu.SemaphoreType.DMA((2, heads)),
        ],
        compiler_params=pltpu.CompilerParams(vmem_limit_bytes=40 * 1024 * 1024),
        cost_estimate=pl.CostEstimate(
            flops=4 * span * width * feats, bytes_accessed=4 * span * width, transcendentals=span * width
        ),
        name="prefill",
    )(lengths, *[pltpu.with_memory_space_constraint(x, pltpu.MemorySpace.HBM) for x in arrays])


def decode_kernel(rows_ref, weight_ref, near_ref, far_ref, *out_refs):
    heads, head_size, feats = weight_ref.shape
    count, width = rows_ref.shape
    group = width // (heads * head_size)
    each = count // len(out_refs)
    tile_at = heads * feats
    halves = (near_ref, far_ref)
    tiles = [ref[tile_at : tile_at + 16, :].astype(jnp.float32) for ref in halves]
    lane = lax.broadcasted_iota(jnp.int32, (count, head_size), 1)
    dens = jnp.zeros((count, head_size), jnp.float32)
    for g in range(heads):
        query = jnp.concatenate(
            [
                rows_ref[:, (g * group + h) * head_size : (g * group + h + 1) * head_size]
                for h in range(group)
            ],
            axis=0,
        )
        wide = query.astype(jnp.float32)
        phi = feature(jnp.dot(query, weight_ref[g], preferred_element_type=jnp.float32)).astype(jnp.bfloat16)
        scale = (TAU / head_size) * lax.rsqrt(jnp.mean(wide * wide, axis=-1, keepdims=True) + EPS)
        num, den, linear = 0.0, 0.0, 0.0
        for ref, tile in zip(halves, tiles):
            linear += jnp.dot(phi, ref[g * feats : (g + 1) * feats, :], preferred_element_type=jnp.float32)
            at = tile_at + 16 + g * SLAB
            keys = ref[at : at + SLAB, :]
            at += heads * SLAB
            values = ref[at : at + SLAB, :]
            keys_wide = keys.astype(jnp.float32)
            key_scale = lax.rsqrt(jnp.mean((keys_wide * keys_wide).T, axis=0, keepdims=True) + EPS)
            score = lax.dot_general(query, keys, NT, preferred_element_type=jnp.float32) * scale * key_scale
            weights = jnp.exp(score) * tile[MASK_ROW : MASK_ROW + 1, :SLAB]
            num += jnp.dot(weights.astype(jnp.bfloat16), values, preferred_element_type=jnp.float32)
            den += jnp.sum(weights, axis=-1, keepdims=True)
        norm = (tiles[0] + tiles[1])[g : g + 1]
        back = 1.0 / (feats * feats)
        den += jnp.sum(phi.astype(jnp.float32) * norm, axis=-1, keepdims=True) * back
        result = (linear * back + num).astype(jnp.bfloat16)
        for h in range(group):
            head = g * group + h
            dens = jnp.where(lane == head, den[h * count : (h + 1) * count], dens)
            for k, out_ref in enumerate(out_refs):
                start = h * count + k * each
                out_ref[:, head * head_size : (head + 1) * head_size] = result[start : start + each]
    high = dens.astype(jnp.bfloat16)
    low = (dens - high.astype(jnp.float32)).astype(jnp.bfloat16)
    for k, out_ref in enumerate(out_refs):
        out_ref[:, width : width + head_size] = high[k * each : (k + 1) * each]
        out_ref[:, width + head_size :] = low[k * each : (k + 1) * each]


def decode(rows, weight, near, far, parts):
    heads, head_size, feats = weight.shape
    count, width = rows.shape
    vmem = pl.BlockSpec(memory_space=pltpu.VMEM)
    return pl.pallas_call(
        decode_kernel,
        in_specs=[vmem] * 4,
        out_specs=[vmem] * parts,
        out_shape=[jax.ShapeDtypeStruct((count // parts, width + 2 * head_size), jnp.bfloat16)] * parts,
        compiler_params=pltpu.CompilerParams(vmem_limit_bytes=32 * 1024 * 1024),
        cost_estimate=pl.CostEstimate(
            flops=10 * count * width * feats, bytes_accessed=4 * count * width, transcendentals=2 * count * width
        ),
        name="decode",
    )(rows, weight, near, far)


def own_kernel(queries_ref, keys_ref, values_ref, _, num_ref, weight_ref):
    count, width = queries_ref.shape
    head_size = weight_ref.shape[1]
    heads = keys_ref.shape[1] // head_size
    group = width // (heads * head_size)
    lane = lax.broadcasted_iota(jnp.int32, (count, head_size), 1)
    kept = jnp.zeros((count, head_size), jnp.float32)
    for g in range(heads):
        cols = slice(g * head_size, (g + 1) * head_size)
        key = keys_ref[:, cols].astype(jnp.float32)
        value = values_ref[:, cols].astype(jnp.float32)
        key = key * lax.rsqrt(jnp.mean(key * key, axis=-1, keepdims=True) + EPS)
        for h in range(group):
            head = g * group + h
            span = slice(head * head_size, (head + 1) * head_size)
            query = queries_ref[:, span].astype(jnp.float32)
            scale = (TAU / head_size) * lax.rsqrt(jnp.mean(query * query, axis=-1, keepdims=True) + EPS)
            weight = jnp.exp(jnp.sum(query * key, axis=-1, keepdims=True) * scale)
            num_ref[:, span] = weight.astype(jnp.bfloat16).astype(jnp.float32) * value
            kept = jnp.where(lane == head, weight, kept)
    weight_ref[...] = kept


def own(queries, new_keys, new_values, after, head_size):
    vmem = pl.BlockSpec(memory_space=pltpu.VMEM)
    count, width = queries.shape
    return pl.pallas_call(
        own_kernel,
        in_specs=[vmem] * 4,
        out_specs=[vmem, vmem],
        out_shape=[
            jax.ShapeDtypeStruct((count, width), jnp.float32),
            jax.ShapeDtypeStruct((count, head_size), jnp.float32),
        ],
        compiler_params=pltpu.CompilerParams(vmem_limit_bytes=8 * 1024 * 1024),
        cost_estimate=pl.CostEstimate(
            flops=8 * count * width, bytes_accessed=8 * count * width, transcendentals=count * width // head_size
        ),
        name="own",
    )(queries, new_keys, new_values, after)


def finish_kernel(prompts_ref, num_ref, weight_ref, *refs):
    block_refs, out_ref = refs[:-1], refs[-1]
    count, width = out_ref.shape
    head_size = weight_ref.shape[1]
    sects = len(block_refs)
    sect = lax.axis_index("sect")
    first = (sect * lax.axis_size("sub") + lax.axis_index("sub")) * count
    rows = prompts_ref.shape[1]
    row = first + lax.broadcasted_iota(jnp.int32, (count, rows), 0)
    lane = lax.broadcasted_iota(jnp.int32, (count, rows), 1)
    prompt = jnp.sum(jnp.where(lane == row, prompts_ref[...], 0), axis=1, keepdims=True)
    chosen = block_refs[0][...].astype(jnp.float32)
    for k in range(1, sects):
        source = lax.rem(sect - k + sects, sects)
        chosen = jnp.where(prompt == source, block_refs[k][...].astype(jnp.float32), chosen)
    den = chosen[:, width : width + head_size] + chosen[:, width + head_size :] + weight_ref[...]
    scale = 1.0 / den
    for head in range(width // head_size):
        span = slice(head * head_size, (head + 1) * head_size)
        out_ref[:, span] = ((chosen[:, span] + num_ref[:, span]) * scale[:, head : head + 1]).astype(out_ref.dtype)


def finish(row_prompt, num, weight, blocks):
    vmem = pl.BlockSpec(memory_space=pltpu.VMEM)
    return pl.pallas_call(
        finish_kernel,
        in_specs=[vmem] * (3 + len(blocks)),
        out_specs=vmem,
        out_shape=jax.ShapeDtypeStruct(num.shape, jnp.bfloat16),
        compiler_params=pltpu.CompilerParams(vmem_limit_bytes=8 * 1024 * 1024),
        name="finish",
    )(row_prompt.reshape(1, -1), num, weight, *blocks)


def body(
    sects, prompt_keys, prompt_values, lengths, feature_weight, queries, new_keys, new_values, row_prompt
):
    blocks = [queries] + [
        lax.ppermute(queries, "sect", [((i + k) % sects, i) for i in range(sects)]) for k in range(1, sects)
    ]
    near = prefill(prompt_keys, prompt_values, feature_weight, lengths)
    far = lax.ppermute(near, "sub", [(0, 1), (1, 0)])
    results = decode(jnp.concatenate(blocks, axis=0), feature_weight, near, far, sects)
    num, weight = own(queries, new_keys, new_values, results[0], feature_weight.shape[1])
    back = [results[0]] + [
        lax.ppermute(results[k], "sect", [(i, (i + k) % sects) for i in range(sects)]) for k in range(1, sects)
    ]
    return finish(row_prompt, num, weight, back)


def solution(mesh):
    placed = (
        P(("parts", "sect"), "sub", "tp"),
        P(("parts", "sect"), "sub", "tp"),
        P(("parts", "sect")),
        P("tp", None, None),
        P(("parts", "sect", "sub"), "tp"),
        P(("parts", "sect", "sub"), "tp"),
        P(("parts", "sect", "sub"), "tp"),
        P("parts"),
    )
    return jax.shard_map(
        functools.partial(body, mesh.shape["sect"]),
        mesh=mesh,
        in_specs=placed,
        out_specs=P(("parts", "sect", "sub"), "tp"),
        check_vma=False,
    )
```

```python
import functools

import jax
import jax.numpy as jnp
from jax import lax
from jax.experimental import pallas as pl
from jax.experimental.pallas import tpu as pltpu
from jax.sharding import PartitionSpec as P

WINDOW = 64
TAU = 10.0
EPS = 1e-06
BLOCK = 256
AHEAD = 8
NT = (((1,), (1,)), ((), ()))


def feature(proj):
    return jnp.maximum(proj, 0.0) + jnp.exp(jnp.minimum(proj, 0.0))


SLAB = WINDOW + 16
MASK_ROW = 8


def prefill_kernel(
    lengths_ref, keys_ref, values_ref, weight_ref, out_ref,
    keys_at, values_at, weight_at, wide_ref, proj_ref, state_ref, norm_ref,
    weight_sem, load_sem, slab_sem,
):
    heads, head_size, feats = weight_ref.shape
    pairs = heads // 2
    span = keys_ref.shape[1]
    cuts = list(range(0, span + 1, BLOCK))
    chunks = len(cuts) - 1
    get_weight = pltpu.make_async_copy(weight_ref, weight_at, weight_sem)
    get_weight.start()
    loads = []
    for c in range(chunks):
        rows = pl.ds(cuts[c], cuts[c + 1] - cuts[c])
        loads.append(
            [
                pltpu.make_async_copy(keys_ref.at[0, rows, :], keys_at.at[rows, :], load_sem.at[0, c]),
                pltpu.make_async_copy(values_ref.at[0, rows, :], values_at.at[rows, :], load_sem.at[1, c]),
            ]
        )

    def fetch(c):
        for priority, load in enumerate(loads[c]):
            load.start(priority=priority)

    for c in range(AHEAD):
        fetch(c)
    wide_ref[...] = jnp.zeros_like(wide_ref)
    get_weight.wait()
    for g in range(heads):
        half = g % 2
        turned = weight_at[g].astype(jnp.float32).T.astype(jnp.bfloat16)
        wide_ref[g // 2, half * feats : (half + 1) * feats, half * head_size : (half + 1) * head_size] = turned

    begin = lengths_ref[0] - WINDOW - lax.axis_index("sub") * span
    first = jnp.clip(begin, 0, span - SLAB)
    first = pl.multiple_of(first - lax.rem(first, 16), 16)
    slabs = []
    for i, source in enumerate((keys_ref, values_ref)):
        for g in range(heads):
            at = heads * feats + 16 + (i * heads + g) * SLAB
            slabs.append(
                pltpu.make_async_copy(
                    source.at[0, pl.ds(first, SLAB), g * head_size : (g + 1) * head_size],
                    out_ref.at[at : at + SLAB, :],
                    slab_sem.at[i, g],
                )
            )
            slabs[-1].start()

    def project(c):
        for load in loads[c]:
            load.wait()
        if c + AHEAD < chunks:
            fetch(c + AHEAD)
        for j in range(pairs):
            proj = lax.dot_general(
                wide_ref[j],
                keys_at[cuts[c] : cuts[c + 1], j * 2 * head_size : (j + 1) * 2 * head_size],
                NT,
                preferred_element_type=jnp.float32,
            )
            proj_ref[c % 2, j, :, : cuts[c + 1] - cuts[c]] = proj.astype(jnp.bfloat16)

    def collect(c):
        size = cuts[c + 1] - cuts[c]
        position = cuts[c] + lax.broadcasted_iota(jnp.int32, (1, size), 1)
        live = jnp.where(position < begin, 1.0, 0.0).astype(jnp.bfloat16)
        for j in range(pairs):
            mapped = feature(proj_ref[c % 2, j, :, :size]) * live
            some = [mapped[:, k * 128 : (k + 1) * 128] for k in range(size // 128)]
            while len(some) > 1:
                some = [x + y for x, y in zip(some[::2], some[1::2])] + some[len(some) // 2 * 2 :]
            total = some[0].astype(jnp.float32)
            part = jnp.dot(
                mapped,
                values_at[cuts[c] : cuts[c + 1], j * 2 * head_size : (j + 1) * 2 * head_size],
                preferred_element_type=jnp.float32,
            )
            norm_ref[j] = total if c == 0 else norm_ref[j] + total
            state_ref[j] = part if c == 0 else state_ref[j] + part

    project(0)
    for c in range(chunks):
        if c + 1 < chunks:
            project(c + 1)
        collect(c)

    tile = []
    for g in range(heads):
        half = g % 2
        part = state_ref[g // 2, half * feats : (half + 1) * feats, half * head_size : (half + 1) * head_size]
        out_ref[g * feats : (g + 1) * feats, :] = part.astype(jnp.bfloat16)
        sums = norm_ref[g // 2, half * feats : (half + 1) * feats, :]
        tile.append(jnp.sum(sums.T, axis=0, keepdims=True))
    slot = first + lax.broadcasted_iota(jnp.int32, (1, head_size), 1)
    tile.append(jnp.zeros((MASK_ROW - heads, head_size), jnp.float32))
    tile.append(jnp.where((slot >= begin) & (slot < begin + WINDOW), 1.0, 0.0))
    tile.append(jnp.zeros((15 - MASK_ROW, head_size), jnp.float32))
    out_ref[heads * feats : heads * feats + 16, :] = jnp.concatenate(tile, axis=0).astype(jnp.bfloat16)
    for slab in slabs:
        slab.wait()


def prefill(keys, values, weight, lengths):
    heads, head_size, feats = weight.shape
    span, width = keys.shape[1:]
    arrays = (keys, values, weight)
    hbm = pl.BlockSpec(memory_space=pltpu.MemorySpace.HBM)
    vmem = pl.BlockSpec(memory_space=pltpu.VMEM)
    return pl.pallas_call(
        prefill_kernel,
        in_specs=[pl.BlockSpec(memory_space=pltpu.SMEM)] + [hbm] * len(arrays),
        out_specs=vmem,
        out_shape=jax.ShapeDtypeStruct((heads * feats + 16 + 2 * heads * SLAB, head_size), jnp.bfloat16),
        scratch_shapes=[
            pltpu.VMEM((span, width), jnp.bfloat16),
            pltpu.VMEM((span, width), jnp.bfloat16),
            pltpu.VMEM(weight.shape, jnp.bfloat16),
            pltpu.VMEM((heads // 2, 2 * feats, 2 * head_size), jnp.bfloat16),
            pltpu.VMEM((2, heads // 2, 2 * feats, BLOCK), jnp.bfloat16),
            pltpu.VMEM((heads // 2, 2 * feats, 2 * head_size), jnp.float32),
            pltpu.VMEM((heads // 2, 2 * feats, 128), jnp.float32),
            pltpu.SemaphoreType.DMA,
            pltpu.SemaphoreType.DMA((2, span // BLOCK + 1)),
            pltpu.SemaphoreType.DMA((2, heads)),
        ],
        compiler_params=pltpu.CompilerParams(vmem_limit_bytes=40 * 1024 * 1024),
        cost_estimate=pl.CostEstimate(
            flops=4 * span * width * feats, bytes_accessed=4 * span * width, transcendentals=span * width
        ),
        name="prefill",
    )(lengths, *[pltpu.with_memory_space_constraint(x, pltpu.MemorySpace.HBM) for x in arrays])


def decode_kernel(rows_ref, weight_ref, near_ref, far_ref, *out_refs):
    heads, head_size, feats = weight_ref.shape
    count, width = rows_ref.shape
    group = width // (heads * head_size)
    each = count // len(out_refs)
    tile_at = heads * feats
    halves = (near_ref, far_ref)
    tiles = [ref[tile_at : tile_at + 16, :].astype(jnp.float32) for ref in halves]
    lane = lax.broadcasted_iota(jnp.int32, (count, head_size), 1)
    dens = jnp.zeros((count, head_size), jnp.float32)
    for g in range(heads):
        query = jnp.concatenate(
            [
                rows_ref[:, (g * group + h) * head_size : (g * group + h + 1) * head_size]
                for h in range(group)
            ],
            axis=0,
        )
        wide = query.astype(jnp.float32)
        phi = feature(jnp.dot(query, weight_ref[g], preferred_element_type=jnp.float32)).astype(jnp.bfloat16)
        scale = (TAU / head_size) * lax.rsqrt(jnp.mean(wide * wide, axis=-1, keepdims=True) + EPS)
        num, den, linear = 0.0, 0.0, 0.0
        for ref, tile in zip(halves, tiles):
            linear += jnp.dot(phi, ref[g * feats : (g + 1) * feats, :], preferred_element_type=jnp.float32)
            at = tile_at + 16 + g * SLAB
            keys = ref[at : at + SLAB, :]
            at += heads * SLAB
            values = ref[at : at + SLAB, :]
            keys_wide = keys.astype(jnp.float32)
            key_scale = lax.rsqrt(jnp.mean((keys_wide * keys_wide).T, axis=0, keepdims=True) + EPS)
            score = lax.dot_general(query, keys, NT, preferred_element_type=jnp.float32) * scale * key_scale
            weights = jnp.exp(score) * tile[MASK_ROW : MASK_ROW + 1, :SLAB]
            num += jnp.dot(weights.astype(jnp.bfloat16), values, preferred_element_type=jnp.float32)
            den += jnp.sum(weights, axis=-1, keepdims=True)
        norm = (tiles[0] + tiles[1])[g : g + 1]
        back = 1.0 / (feats * feats)
        den += jnp.sum(phi.astype(jnp.float32) * norm, axis=-1, keepdims=True) * back
        result = (linear * back + num).astype(jnp.bfloat16)
        for h in range(group):
            head = g * group + h
            dens = jnp.where(lane == head, den[h * count : (h + 1) * count], dens)
            for k, out_ref in enumerate(out_refs):
                start = h * count + k * each
                out_ref[:, head * head_size : (head + 1) * head_size] = result[start : start + each]
    high = dens.astype(jnp.bfloat16)
    low = (dens - high.astype(jnp.float32)).astype(jnp.bfloat16)
    for k, out_ref in enumerate(out_refs):
        out_ref[:, width : width + head_size] = high[k * each : (k + 1) * each]
        out_ref[:, width + head_size :] = low[k * each : (k + 1) * each]


def decode(rows, weight, near, far, parts):
    heads, head_size, feats = weight.shape
    count, width = rows.shape
    vmem = pl.BlockSpec(memory_space=pltpu.VMEM)
    return pl.pallas_call(
        decode_kernel,
        in_specs=[vmem] * 4,
        out_specs=[vmem] * parts,
        out_shape=[jax.ShapeDtypeStruct((count // parts, width + 2 * head_size), jnp.bfloat16)] * parts,
        compiler_params=pltpu.CompilerParams(vmem_limit_bytes=32 * 1024 * 1024),
        cost_estimate=pl.CostEstimate(
            flops=10 * count * width * feats, bytes_accessed=4 * count * width, transcendentals=2 * count * width
        ),
        name="decode",
    )(rows, weight, near, far)


def own_kernel(queries_ref, keys_ref, values_ref, _, num_ref, weight_ref):
    count, width = queries_ref.shape
    head_size = weight_ref.shape[1]
    heads = keys_ref.shape[1] // head_size
    group = width // (heads * head_size)
    lane = lax.broadcasted_iota(jnp.int32, (count, head_size), 1)
    kept = jnp.zeros((count, head_size), jnp.float32)
    for g in range(heads):
        cols = slice(g * head_size, (g + 1) * head_size)
        key = keys_ref[:, cols].astype(jnp.float32)
        value = values_ref[:, cols].astype(jnp.float32)
        key = key * lax.rsqrt(jnp.mean(key * key, axis=-1, keepdims=True) + EPS)
        for h in range(group):
            head = g * group + h
            span = slice(head * head_size, (head + 1) * head_size)
            query = queries_ref[:, span].astype(jnp.float32)
            scale = (TAU / head_size) * lax.rsqrt(jnp.mean(query * query, axis=-1, keepdims=True) + EPS)
            weight = jnp.exp(jnp.sum(query * key, axis=-1, keepdims=True) * scale)
            num_ref[:, span] = weight.astype(jnp.bfloat16).astype(jnp.float32) * value
            kept = jnp.where(lane == head, weight, kept)
    weight_ref[...] = kept


def own(queries, new_keys, new_values, after, head_size):
    vmem = pl.BlockSpec(memory_space=pltpu.VMEM)
    count, width = queries.shape
    return pl.pallas_call(
        own_kernel,
        in_specs=[vmem] * 4,
        out_specs=[vmem, vmem],
        out_shape=[
            jax.ShapeDtypeStruct((count, width), jnp.float32),
            jax.ShapeDtypeStruct((count, head_size), jnp.float32),
        ],
        compiler_params=pltpu.CompilerParams(vmem_limit_bytes=8 * 1024 * 1024),
        cost_estimate=pl.CostEstimate(
            flops=8 * count * width, bytes_accessed=8 * count * width, transcendentals=count * width // head_size
        ),
        name="own",
    )(queries, new_keys, new_values, after)


def finish_kernel(prompts_ref, num_ref, weight_ref, *refs):
    block_refs, out_ref = refs[:-1], refs[-1]
    count, width = out_ref.shape
    head_size = weight_ref.shape[1]
    sects = len(block_refs)
    sect = lax.axis_index("sect")
    first = (sect * lax.axis_size("sub") + lax.axis_index("sub")) * count
    rows = prompts_ref.shape[1]
    row = first + lax.broadcasted_iota(jnp.int32, (count, rows), 0)
    lane = lax.broadcasted_iota(jnp.int32, (count, rows), 1)
    prompt = jnp.sum(jnp.where(lane == row, prompts_ref[...], 0), axis=1, keepdims=True)
    chosen = block_refs[0][...].astype(jnp.float32)
    for k in range(1, sects):
        source = lax.rem(sect - k + sects, sects)
        chosen = jnp.where(prompt == source, block_refs[k][...].astype(jnp.float32), chosen)
    den = chosen[:, width : width + head_size] + chosen[:, width + head_size :] + weight_ref[...]
    scale = 1.0 / den
    for head in range(width // head_size):
        span = slice(head * head_size, (head + 1) * head_size)
        out_ref[:, span] = ((chosen[:, span] + num_ref[:, span]) * scale[:, head : head + 1]).astype(out_ref.dtype)


def finish(row_prompt, num, weight, blocks):
    vmem = pl.BlockSpec(memory_space=pltpu.VMEM)
    return pl.pallas_call(
        finish_kernel,
        in_specs=[vmem] * (3 + len(blocks)),
        out_specs=vmem,
        out_shape=jax.ShapeDtypeStruct(num.shape, jnp.bfloat16),
        compiler_params=pltpu.CompilerParams(vmem_limit_bytes=8 * 1024 * 1024),
        name="finish",
    )(row_prompt.reshape(1, -1), num, weight, *blocks)


def body(
    sects, prompt_keys, prompt_values, lengths, feature_weight, queries, new_keys, new_values, row_prompt
):
    blocks = [queries] + [
        lax.ppermute(queries, "sect", [((i + k) % sects, i) for i in range(sects)]) for k in range(1, sects)
    ]
    near = prefill(prompt_keys, prompt_values, feature_weight, lengths)
    far = lax.ppermute(near, "sub", [(0, 1), (1, 0)])
    results = decode(jnp.concatenate(blocks, axis=0), feature_weight, near, far, sects)
    num, weight = own(queries, new_keys, new_values, results[0], feature_weight.shape[1])
    back = [results[0]] + [
        lax.ppermute(results[k], "sect", [(i, (i + k) % sects) for i in range(sects)]) for k in range(1, sects)
    ]
    return finish(row_prompt, num, weight, back)


def solution(mesh):
    placed = (
        P(("parts", "sect"), "sub", "tp"),
        P(("parts", "sect"), "sub", "tp"),
        P(("parts", "sect")),
        P("tp", None, None),
        P(("parts", "sect", "sub"), "tp"),
        P(("parts", "sect", "sub"), "tp"),
        P(("parts", "sect", "sub"), "tp"),
        P("parts"),
    )
    return jax.shard_map(
        functools.partial(body, mesh.shape["sect"]),
        mesh=mesh,
        in_specs=placed,
        out_specs=P(("parts", "sect", "sub"), "tp"),
        check_vma=False,
    )
```

```python
import functools

import jax
import jax.numpy as jnp
from jax import lax
from jax.experimental import pallas as pl
from jax.experimental.pallas import tpu as pltpu
from jax.sharding import PartitionSpec as P

WINDOW = 64
TAU = 10.0
EPS = 1e-06
BLOCK = 512
AHEAD = 2
NT = (((1,), (1,)), ((), ()))


def feature(proj):
    return jnp.maximum(proj, 0.0) + jnp.exp(jnp.minimum(proj, 0.0))


SLAB = WINDOW + 16
MASK_ROW = 8


def paired(sects):
    return sects & (sects - 1) == 0


def partner(sect, k, sects):
    return sect ^ k if paired(sects) else (sect + k) % sects


def home_order(sects):
    return list(range(2, sects)) + [1]


def prefill_kernel(
    lengths_ref, keys_ref, values_ref, weight_ref, out_ref,
    keys_at, values_at, weight_at, wide_ref, proj_ref, state_ref, norm_ref,
    weight_sem, load_sem, slab_sem,
):
    heads, head_size, feats = weight_ref.shape
    pairs = heads // 2
    span = keys_ref.shape[1]
    chunks = span // BLOCK
    get_weight = pltpu.make_async_copy(weight_ref, weight_at, weight_sem)
    get_weight.start()
    loads = [
        [
            pltpu.make_async_copy(
                source.at[0, pl.ds(c * BLOCK, BLOCK), :], place.at[pl.ds(c * BLOCK, BLOCK), :], load_sem.at[i, c]
            )
            for c in range(chunks)
        ]
        for i, (source, place) in enumerate(((keys_ref, keys_at), (values_ref, values_at)))
    ]
    for c in range(AHEAD):
        for load in loads:
            load[c].start()

    state_ref[...] = jnp.zeros_like(state_ref)
    norm_ref[...] = jnp.zeros_like(norm_ref)
    wide_ref[...] = jnp.zeros_like(wide_ref)
    get_weight.wait()
    for g in range(heads):
        half = g % 2
        turned = weight_at[g].astype(jnp.float32).T.astype(jnp.bfloat16)
        wide_ref[g // 2, half * feats : (half + 1) * feats, half * head_size : (half + 1) * head_size] = turned

    begin = lengths_ref[0] - WINDOW - lax.axis_index("sub") * span
    first = jnp.clip(begin, 0, span - SLAB)
    first = pl.multiple_of(first - lax.rem(first, 16), 16)
    slabs = []
    for i, source in enumerate((keys_ref, values_ref)):
        for g in range(heads):
            at = heads * feats + 16 + (i * heads + g) * SLAB
            slabs.append(
                pltpu.make_async_copy(
                    source.at[0, pl.ds(first, SLAB), g * head_size : (g + 1) * head_size],
                    out_ref.at[at : at + SLAB, :],
                    slab_sem.at[i, g],
                )
            )
            slabs[-1].start()

    def arrive(i, c):
        loads[i][c].wait()
        if c + AHEAD < chunks:
            loads[i][c + AHEAD].start()

    def project(c):
        arrive(0, c)
        for j in range(pairs):
            proj = lax.dot_general(
                wide_ref[j],
                keys_at[c * BLOCK : (c + 1) * BLOCK, j * 2 * head_size : (j + 1) * 2 * head_size],
                NT,
                preferred_element_type=jnp.float32,
            )
            proj_ref[c % 2, j] = proj.astype(jnp.bfloat16)

    def collect(c):
        arrive(1, c)
        position = c * BLOCK + lax.broadcasted_iota(jnp.int32, (1, BLOCK), 1)
        live = jnp.where(position < begin, 1.0, 0.0).astype(jnp.bfloat16)
        for j in range(pairs):
            mapped = feature(proj_ref[c % 2, j]) * live
            some = [mapped[:, k * 128 : (k + 1) * 128] for k in range(BLOCK // 128)]
            while len(some) > 1:
                some = [x + y for x, y in zip(some[::2], some[1::2])]
            norm_ref[j] += some[0].astype(jnp.float32)
            state_ref[j] += jnp.dot(
                mapped,
                values_at[c * BLOCK : (c + 1) * BLOCK, j * 2 * head_size : (j + 1) * 2 * head_size],
                preferred_element_type=jnp.float32,
            )

    project(0)
    for c in range(chunks):
        if c + 1 < chunks:
            project(c + 1)
        collect(c)

    tile = []
    for g in range(heads):
        half = g % 2
        part = state_ref[g // 2, half * feats : (half + 1) * feats, half * head_size : (half + 1) * head_size]
        out_ref[g * feats : (g + 1) * feats, :] = part.astype(jnp.bfloat16)
        sums = norm_ref[g // 2, half * feats : (half + 1) * feats, :]
        tile.append(jnp.sum(sums.T, axis=0, keepdims=True))
    slot = first + lax.broadcasted_iota(jnp.int32, (1, head_size), 1)
    tile.append(jnp.zeros((MASK_ROW - heads, head_size), jnp.float32))
    tile.append(jnp.where((slot >= begin) & (slot < begin + WINDOW), 1.0, 0.0))
    tile.append(jnp.zeros((15 - MASK_ROW, head_size), jnp.float32))
    out_ref[heads * feats : heads * feats + 16, :] = jnp.concatenate(tile, axis=0).astype(jnp.bfloat16)
    for slab in slabs:
        slab.wait()


def prefill(keys, values, weight, lengths):
    heads, head_size, feats = weight.shape
    span, width = keys.shape[1:]
    arrays = (keys, values, weight)
    hbm = pl.BlockSpec(memory_space=pltpu.MemorySpace.HBM)
    vmem = pl.BlockSpec(memory_space=pltpu.VMEM)
    return pl.pallas_call(
        prefill_kernel,
        in_specs=[pl.BlockSpec(memory_space=pltpu.SMEM)] + [hbm] * len(arrays),
        out_specs=vmem,
        out_shape=jax.ShapeDtypeStruct((heads * feats + 16 + 2 * heads * SLAB, head_size), jnp.bfloat16),
        scratch_shapes=[
            pltpu.VMEM((span, width), jnp.bfloat16),
            pltpu.VMEM((span, width), jnp.bfloat16),
            pltpu.VMEM(weight.shape, jnp.bfloat16),
            pltpu.VMEM((heads // 2, 2 * feats, 2 * head_size), jnp.bfloat16),
            pltpu.VMEM((2, heads // 2, 2 * feats, BLOCK), jnp.bfloat16),
            pltpu.VMEM((heads // 2, 2 * feats, 2 * head_size), jnp.float32),
            pltpu.VMEM((heads // 2, 2 * feats, 128), jnp.float32),
            pltpu.SemaphoreType.DMA,
            pltpu.SemaphoreType.DMA((2, span // BLOCK)),
            pltpu.SemaphoreType.DMA((2, heads)),
        ],
        compiler_params=pltpu.CompilerParams(vmem_limit_bytes=40 * 1024 * 1024),
        cost_estimate=pl.CostEstimate(
            flops=4 * span * width * feats, bytes_accessed=4 * span * width, transcendentals=span * width
        ),
        name="prefill",
    )(lengths, *[pltpu.with_memory_space_constraint(x, pltpu.MemorySpace.HBM) for x in arrays])


def decode_kernel(rows_ref, weight_ref, near_ref, far_ref, *out_refs):
    heads, head_size, feats = weight_ref.shape
    count, width = rows_ref.shape
    group = width // (heads * head_size)
    each = count // len(out_refs)
    tile_at = heads * feats
    halves = (near_ref, far_ref)
    tiles = [ref[tile_at : tile_at + 16, :].astype(jnp.float32) for ref in halves]
    lane = lax.broadcasted_iota(jnp.int32, (count, head_size), 1)
    dens = jnp.zeros((count, head_size), jnp.float32)
    for g in range(heads):
        query = jnp.concatenate(
            [
                rows_ref[:, (g * group + h) * head_size : (g * group + h + 1) * head_size]
                for h in range(group)
            ],
            axis=0,
        )
        wide = query.astype(jnp.float32)
        phi = feature(jnp.dot(query, weight_ref[g], preferred_element_type=jnp.float32)).astype(jnp.bfloat16)
        scale = (TAU / head_size) * lax.rsqrt(jnp.mean(wide * wide, axis=-1, keepdims=True) + EPS)
        num, den, linear = 0.0, 0.0, 0.0
        for ref, tile in zip(halves, tiles):
            linear += jnp.dot(phi, ref[g * feats : (g + 1) * feats, :], preferred_element_type=jnp.float32)
            at = tile_at + 16 + g * SLAB
            keys = ref[at : at + SLAB, :]
            at += heads * SLAB
            values = ref[at : at + SLAB, :]
            keys_wide = keys.astype(jnp.float32)
            key_scale = lax.rsqrt(jnp.mean((keys_wide * keys_wide).T, axis=0, keepdims=True) + EPS)
            score = lax.dot_general(query, keys, NT, preferred_element_type=jnp.float32) * scale * key_scale
            weights = jnp.exp(score) * tile[MASK_ROW : MASK_ROW + 1, :SLAB]
            num += jnp.dot(weights.astype(jnp.bfloat16), values, preferred_element_type=jnp.float32)
            den += jnp.sum(weights, axis=-1, keepdims=True)
        norm = (tiles[0] + tiles[1])[g : g + 1]
        back = 1.0 / (feats * feats)
        den += jnp.sum(phi.astype(jnp.float32) * norm, axis=-1, keepdims=True) * back
        result = (linear * back + num).astype(jnp.bfloat16)
        for h in range(group):
            head = g * group + h
            dens = jnp.where(lane == head, den[h * count : (h + 1) * count], dens)
            for k, out_ref in enumerate(out_refs):
                start = h * count + k * each
                out_ref[:, head * head_size : (head + 1) * head_size] = result[start : start + each]
    high = dens.astype(jnp.bfloat16)
    low = (dens - high.astype(jnp.float32)).astype(jnp.bfloat16)
    for k, out_ref in enumerate(out_refs):
        out_ref[:, width : width + head_size] = high[k * each : (k + 1) * each]
        out_ref[:, width + head_size :] = low[k * each : (k + 1) * each]


def decode(rows, weight, near, far, parts):
    heads, head_size, feats = weight.shape
    count, width = rows.shape
    vmem = pl.BlockSpec(memory_space=pltpu.VMEM)
    return pl.pallas_call(
        decode_kernel,
        in_specs=[vmem] * 4,
        out_specs=[vmem] * parts,
        out_shape=[jax.ShapeDtypeStruct((count // parts, width + 2 * head_size), jnp.bfloat16)] * parts,
        compiler_params=pltpu.CompilerParams(vmem_limit_bytes=32 * 1024 * 1024),
        cost_estimate=pl.CostEstimate(
            flops=10 * count * width * feats, bytes_accessed=4 * count * width, transcendentals=2 * count * width
        ),
        name="decode",
    )(rows, weight, near, far)


def own_kernel(queries_ref, keys_ref, values_ref, _, num_ref, weight_ref):
    count, width = queries_ref.shape
    head_size = weight_ref.shape[1]
    heads = keys_ref.shape[1] // head_size
    group = width // (heads * head_size)
    lane = lax.broadcasted_iota(jnp.int32, (count, head_size), 1)
    kept = jnp.zeros((count, head_size), jnp.float32)
    for g in range(heads):
        cols = slice(g * head_size, (g + 1) * head_size)
        key = keys_ref[:, cols].astype(jnp.float32)
        value = values_ref[:, cols].astype(jnp.float32)
        key = key * lax.rsqrt(jnp.mean(key * key, axis=-1, keepdims=True) + EPS)
        for h in range(group):
            head = g * group + h
            span = slice(head * head_size, (head + 1) * head_size)
            query = queries_ref[:, span].astype(jnp.float32)
            scale = (TAU / head_size) * lax.rsqrt(jnp.mean(query * query, axis=-1, keepdims=True) + EPS)
            weight = jnp.exp(jnp.sum(query * key, axis=-1, keepdims=True) * scale)
            num_ref[:, span] = weight.astype(jnp.bfloat16).astype(jnp.float32) * value
            kept = jnp.where(lane == head, weight, kept)
    weight_ref[...] = kept


def own(queries, new_keys, new_values, after, head_size):
    vmem = pl.BlockSpec(memory_space=pltpu.VMEM)
    count, width = queries.shape
    return pl.pallas_call(
        own_kernel,
        in_specs=[vmem] * 4,
        out_specs=[vmem, vmem],
        out_shape=[
            jax.ShapeDtypeStruct((count, width), jnp.float32),
            jax.ShapeDtypeStruct((count, head_size), jnp.float32),
        ],
        compiler_params=pltpu.CompilerParams(vmem_limit_bytes=8 * 1024 * 1024),
        cost_estimate=pl.CostEstimate(
            flops=8 * count * width, bytes_accessed=8 * count * width, transcendentals=count * width // head_size
        ),
        name="own",
    )(queries, new_keys, new_values, after)


def finish_kernel(prompts_ref, num_ref, weight_ref, *refs):
    block_refs, out_ref = refs[:-1], refs[-1]
    count, width = out_ref.shape
    head_size = weight_ref.shape[1]
    sects = len(block_refs)
    sect = lax.axis_index("sect")
    first = (sect * lax.axis_size("sub") + lax.axis_index("sub")) * count
    rows = prompts_ref.shape[1]
    row = first + lax.broadcasted_iota(jnp.int32, (count, rows), 0)
    lane = lax.broadcasted_iota(jnp.int32, (count, rows), 1)
    prompt = jnp.sum(jnp.where(lane == row, prompts_ref[...], 0), axis=1, keepdims=True)
    chosen = block_refs[0][...].astype(jnp.float32)
    for k, ref in zip(home_order(sects), block_refs[1:]):
        source = partner(sect, k if paired(sects) else sects - k, sects)
        chosen = jnp.where(prompt == source, ref[...].astype(jnp.float32), chosen)
    den = chosen[:, width : width + head_size] + chosen[:, width + head_size :] + weight_ref[...]
    scale = 1.0 / den
    for head in range(width // head_size):
        span = slice(head * head_size, (head + 1) * head_size)
        out_ref[:, span] = ((chosen[:, span] + num_ref[:, span]) * scale[:, head : head + 1]).astype(out_ref.dtype)


def finish(row_prompt, num, weight, blocks):
    vmem = pl.BlockSpec(memory_space=pltpu.VMEM)
    return pl.pallas_call(
        finish_kernel,
        in_specs=[vmem] * (3 + len(blocks)),
        out_specs=vmem,
        out_shape=jax.ShapeDtypeStruct(num.shape, jnp.bfloat16),
        compiler_params=pltpu.CompilerParams(vmem_limit_bytes=8 * 1024 * 1024),
        name="finish",
    )(row_prompt.reshape(1, -1), num, weight, *blocks)


def body(
    sects, prompt_keys, prompt_values, lengths, feature_weight, queries, new_keys, new_values, row_prompt
):
    asked = {k: lax.ppermute(queries, "sect", [(partner(i, k, sects), i) for i in range(sects)]) for k in range(1, sects)}
    near = prefill(prompt_keys, prompt_values, feature_weight, lengths)
    far = lax.ppermute(near, "sub", [(0, 1), (1, 0)])
    blocks = [asked[k] for k in range(sects - 1, 0, -1)] + [queries]
    results = decode(jnp.concatenate(blocks, axis=0), feature_weight, near, far, sects)[::-1]
    num, weight = own(queries, new_keys, new_values, results[0], feature_weight.shape[1])
    back = [
        lax.ppermute(results[k], "sect", [(i, partner(i, k, sects)) for i in range(sects)])
        for k in home_order(sects)
    ]
    return finish(row_prompt, num, weight, [results[0]] + back)


def solution(mesh):
    placed = (
        P(("parts", "sect"), "sub", "tp"),
        P(("parts", "sect"), "sub", "tp"),
        P(("parts", "sect")),
        P("tp", None, None),
        P(("parts", "sect", "sub"), "tp"),
        P(("parts", "sect", "sub"), "tp"),
        P(("parts", "sect", "sub"), "tp"),
        P("parts"),
    )
    return jax.shard_map(
        functools.partial(body, mesh.shape["sect"]),
        mesh=mesh,
        in_specs=placed,
        out_specs=P(("parts", "sect", "sub"), "tp"),
        check_vma=False,
    )
```

```python
import functools

import jax
import jax.numpy as jnp
from jax import lax
from jax.experimental import pallas as pl
from jax.experimental.pallas import tpu as pltpu
from jax.sharding import PartitionSpec as P

WINDOW = 64
TAU = 10.0
EPS = 1e-06
BLOCK = 512
AHEAD = 3
NT = (((1,), (1,)), ((), ()))


def feature(proj):
    return jnp.maximum(proj, 0.0) + jnp.exp(jnp.minimum(proj, 0.0))


SLAB = WINDOW + 16
MASK_ROW = 8


def prefill_kernel(
    lengths_ref, keys_ref, values_ref, weight_ref, out_ref,
    keys_at, values_at, weight_at, wide_ref, proj_ref, mapped_ref, state_ref, norm_ref,
    weight_sem, load_sem, slab_sem,
):
    heads, head_size, feats = weight_ref.shape
    pairs = heads // 2
    span = keys_ref.shape[1]
    chunks = span // BLOCK
    get_weight = pltpu.make_async_copy(weight_ref, weight_at, weight_sem)
    get_weight.start()
    loads = []
    for c in range(chunks):
        rows = pl.ds(c * BLOCK, BLOCK)
        loads.append(
            [
                pltpu.make_async_copy(keys_ref.at[0, rows, :], keys_at.at[rows, :], load_sem.at[0, c]),
                pltpu.make_async_copy(values_ref.at[0, rows, :], values_at.at[rows, :], load_sem.at[1, c]),
            ]
        )

    def fetch(c):
        for priority, load in enumerate(loads[c]):
            load.start(priority=priority)

    for c in range(AHEAD):
        fetch(c)
    state_ref[...] = jnp.zeros_like(state_ref)
    norm_ref[...] = jnp.zeros_like(norm_ref)
    wide_ref[...] = jnp.zeros_like(wide_ref)
    get_weight.wait()
    for g in range(heads):
        half = g % 2
        turned = weight_at[g].astype(jnp.float32).T.astype(jnp.bfloat16)
        wide_ref[g // 2, half * feats : (half + 1) * feats, half * head_size : (half + 1) * head_size] = turned

    begin = lengths_ref[0] - WINDOW - lax.axis_index("sub") * span
    first = jnp.clip(begin, 0, span - SLAB)
    first = pl.multiple_of(first - lax.rem(first, 16), 16)
    slabs = []
    for i, source in enumerate((keys_ref, values_ref)):
        for g in range(heads):
            at = heads * feats + 16 + (i * heads + g) * SLAB
            slabs.append(
                pltpu.make_async_copy(
                    source.at[0, pl.ds(first, SLAB), g * head_size : (g + 1) * head_size],
                    out_ref.at[at : at + SLAB, :],
                    slab_sem.at[i, g],
                )
            )
            slabs[-1].start()

    def project(c):
        for load in loads[c]:
            load.wait()
        if c + AHEAD < chunks:
            fetch(c + AHEAD)
        for j in range(pairs):
            proj = lax.dot_general(
                wide_ref[j],
                keys_at[c * BLOCK : (c + 1) * BLOCK, j * 2 * head_size : (j + 1) * 2 * head_size],
                NT,
                preferred_element_type=jnp.float32,
            )
            proj_ref[c % 2, j] = proj.astype(jnp.bfloat16)

    def featurize(c):
        position = c * BLOCK + lax.broadcasted_iota(jnp.int32, (1, BLOCK), 1)
        live = jnp.where(position < begin, 1.0, 0.0).astype(jnp.bfloat16)
        for j in range(pairs):
            mapped = feature(proj_ref[c % 2, j]) * live
            some = [mapped[:, k * 128 : (k + 1) * 128] for k in range(BLOCK // 128)]
            while len(some) > 1:
                some = [x + y for x, y in zip(some[::2], some[1::2])]
            norm_ref[j] += some[0].astype(jnp.float32)
            mapped_ref[c % 2, j] = mapped

    def collect(c):
        for j in range(pairs):
            state_ref[j] += jnp.dot(
                mapped_ref[c % 2, j],
                values_at[c * BLOCK : (c + 1) * BLOCK, j * 2 * head_size : (j + 1) * 2 * head_size],
                preferred_element_type=jnp.float32,
            )

    for step in range(chunks + 2):
        if step < chunks:
            project(step)
        if 0 <= step - 1 < chunks:
            featurize(step - 1)
        if step >= 2:
            collect(step - 2)

    tile = []
    for g in range(heads):
        half = g % 2
        part = state_ref[g // 2, half * feats : (half + 1) * feats, half * head_size : (half + 1) * head_size]
        out_ref[g * feats : (g + 1) * feats, :] = part.astype(jnp.bfloat16)
        sums = norm_ref[g // 2, half * feats : (half + 1) * feats, :]
        tile.append(jnp.sum(sums.T, axis=0, keepdims=True))
    slot = first + lax.broadcasted_iota(jnp.int32, (1, head_size), 1)
    tile.append(jnp.zeros((MASK_ROW - heads, head_size), jnp.float32))
    tile.append(jnp.where((slot >= begin) & (slot < begin + WINDOW), 1.0, 0.0))
    tile.append(jnp.zeros((15 - MASK_ROW, head_size), jnp.float32))
    out_ref[heads * feats : heads * feats + 16, :] = jnp.concatenate(tile, axis=0).astype(jnp.bfloat16)
    for slab in slabs:
        slab.wait()


def prefill(keys, values, weight, lengths):
    heads, head_size, feats = weight.shape
    span, width = keys.shape[1:]
    arrays = (keys, values, weight)
    hbm = pl.BlockSpec(memory_space=pltpu.MemorySpace.HBM)
    vmem = pl.BlockSpec(memory_space=pltpu.VMEM)
    return pl.pallas_call(
        prefill_kernel,
        in_specs=[pl.BlockSpec(memory_space=pltpu.SMEM)] + [hbm] * len(arrays),
        out_specs=vmem,
        out_shape=jax.ShapeDtypeStruct((heads * feats + 16 + 2 * heads * SLAB, head_size), jnp.bfloat16),
        scratch_shapes=[
            pltpu.VMEM((span, width), jnp.bfloat16),
            pltpu.VMEM((span, width), jnp.bfloat16),
            pltpu.VMEM(weight.shape, jnp.bfloat16),
            pltpu.VMEM((heads // 2, 2 * feats, 2 * head_size), jnp.bfloat16),
            pltpu.VMEM((2, heads // 2, 2 * feats, BLOCK), jnp.bfloat16),
            pltpu.VMEM((2, heads // 2, 2 * feats, BLOCK), jnp.bfloat16),
            pltpu.VMEM((heads // 2, 2 * feats, 2 * head_size), jnp.float32),
            pltpu.VMEM((heads // 2, 2 * feats, 128), jnp.float32),
            pltpu.SemaphoreType.DMA,
            pltpu.SemaphoreType.DMA((2, span // BLOCK)),
            pltpu.SemaphoreType.DMA((2, heads)),
        ],
        compiler_params=pltpu.CompilerParams(vmem_limit_bytes=40 * 1024 * 1024),
        cost_estimate=pl.CostEstimate(
            flops=4 * span * width * feats, bytes_accessed=4 * span * width, transcendentals=span * width
        ),
        name="prefill",
    )(lengths, *[pltpu.with_memory_space_constraint(x, pltpu.MemorySpace.HBM) for x in arrays])


def decode_kernel(rows_ref, weight_ref, near_ref, far_ref, *out_refs):
    heads, head_size, feats = weight_ref.shape
    count, width = rows_ref.shape
    group = width // (heads * head_size)
    each = count // len(out_refs)
    tile_at = heads * feats
    halves = (near_ref, far_ref)
    tiles = [ref[tile_at : tile_at + 16, :].astype(jnp.float32) for ref in halves]
    lane = lax.broadcasted_iota(jnp.int32, (count, head_size), 1)
    dens = jnp.zeros((count, head_size), jnp.float32)
    for g in range(heads):
        query = jnp.concatenate(
            [
                rows_ref[:, (g * group + h) * head_size : (g * group + h + 1) * head_size]
                for h in range(group)
            ],
            axis=0,
        )
        wide = query.astype(jnp.float32)
        phi = feature(jnp.dot(query, weight_ref[g], preferred_element_type=jnp.float32)).astype(jnp.bfloat16)
        scale = (TAU / head_size) * lax.rsqrt(jnp.mean(wide * wide, axis=-1, keepdims=True) + EPS)
        num, den, linear = 0.0, 0.0, 0.0
        for ref, tile in zip(halves, tiles):
            linear += jnp.dot(phi, ref[g * feats : (g + 1) * feats, :], preferred_element_type=jnp.float32)
            at = tile_at + 16 + g * SLAB
            keys = ref[at : at + SLAB, :]
            at += heads * SLAB
            values = ref[at : at + SLAB, :]
            keys_wide = keys.astype(jnp.float32)
            key_scale = lax.rsqrt(jnp.mean((keys_wide * keys_wide).T, axis=0, keepdims=True) + EPS)
            score = lax.dot_general(query, keys, NT, preferred_element_type=jnp.float32) * scale * key_scale
            weights = jnp.exp(score) * tile[MASK_ROW : MASK_ROW + 1, :SLAB]
            num += jnp.dot(weights.astype(jnp.bfloat16), values, preferred_element_type=jnp.float32)
            den += jnp.sum(weights, axis=-1, keepdims=True)
        norm = (tiles[0] + tiles[1])[g : g + 1]
        back = 1.0 / (feats * feats)
        den += jnp.sum(phi.astype(jnp.float32) * norm, axis=-1, keepdims=True) * back
        result = (linear * back + num).astype(jnp.bfloat16)
        for h in range(group):
            head = g * group + h
            dens = jnp.where(lane == head, den[h * count : (h + 1) * count], dens)
            for k, out_ref in enumerate(out_refs):
                start = h * count + k * each
                out_ref[:, head * head_size : (head + 1) * head_size] = result[start : start + each]
    high = dens.astype(jnp.bfloat16)
    low = (dens - high.astype(jnp.float32)).astype(jnp.bfloat16)
    for k, out_ref in enumerate(out_refs):
        out_ref[:, width : width + head_size] = high[k * each : (k + 1) * each]
        out_ref[:, width + head_size :] = low[k * each : (k + 1) * each]


def decode(rows, weight, near, far, parts):
    heads, head_size, feats = weight.shape
    count, width = rows.shape
    vmem = pl.BlockSpec(memory_space=pltpu.VMEM)
    return pl.pallas_call(
        decode_kernel,
        in_specs=[vmem] * 4,
        out_specs=[vmem] * parts,
        out_shape=[jax.ShapeDtypeStruct((count // parts, width + 2 * head_size), jnp.bfloat16)] * parts,
        compiler_params=pltpu.CompilerParams(vmem_limit_bytes=32 * 1024 * 1024),
        cost_estimate=pl.CostEstimate(
            flops=10 * count * width * feats, bytes_accessed=4 * count * width, transcendentals=2 * count * width
        ),
        name="decode",
    )(rows, weight, near, far)


def own_kernel(queries_ref, keys_ref, values_ref, _, num_ref, weight_ref):
    count, width = queries_ref.shape
    head_size = weight_ref.shape[1]
    heads = keys_ref.shape[1] // head_size
    group = width // (heads * head_size)
    lane = lax.broadcasted_iota(jnp.int32, (count, head_size), 1)
    kept = jnp.zeros((count, head_size), jnp.float32)
    for g in range(heads):
        cols = slice(g * head_size, (g + 1) * head_size)
        key = keys_ref[:, cols].astype(jnp.float32)
        value = values_ref[:, cols].astype(jnp.float32)
        key = key * lax.rsqrt(jnp.mean(key * key, axis=-1, keepdims=True) + EPS)
        for h in range(group):
            head = g * group + h
            span = slice(head * head_size, (head + 1) * head_size)
            query = queries_ref[:, span].astype(jnp.float32)
            scale = (TAU / head_size) * lax.rsqrt(jnp.mean(query * query, axis=-1, keepdims=True) + EPS)
            weight = jnp.exp(jnp.sum(query * key, axis=-1, keepdims=True) * scale)
            num_ref[:, span] = weight.astype(jnp.bfloat16).astype(jnp.float32) * value
            kept = jnp.where(lane == head, weight, kept)
    weight_ref[...] = kept


def own(queries, new_keys, new_values, after, head_size):
    vmem = pl.BlockSpec(memory_space=pltpu.VMEM)
    count, width = queries.shape
    return pl.pallas_call(
        own_kernel,
        in_specs=[vmem] * 4,
        out_specs=[vmem, vmem],
        out_shape=[
            jax.ShapeDtypeStruct((count, width), jnp.float32),
            jax.ShapeDtypeStruct((count, head_size), jnp.float32),
        ],
        compiler_params=pltpu.CompilerParams(vmem_limit_bytes=8 * 1024 * 1024),
        cost_estimate=pl.CostEstimate(
            flops=8 * count * width, bytes_accessed=8 * count * width, transcendentals=count * width // head_size
        ),
        name="own",
    )(queries, new_keys, new_values, after)


def finish_kernel(prompts_ref, num_ref, weight_ref, *refs):
    block_refs, out_ref = refs[:-1], refs[-1]
    count, width = out_ref.shape
    head_size = weight_ref.shape[1]
    sects = len(block_refs)
    sect = lax.axis_index("sect")
    first = (sect * lax.axis_size("sub") + lax.axis_index("sub")) * count
    rows = prompts_ref.shape[1]
    row = first + lax.broadcasted_iota(jnp.int32, (count, rows), 0)
    lane = lax.broadcasted_iota(jnp.int32, (count, rows), 1)
    prompt = jnp.sum(jnp.where(lane == row, prompts_ref[...], 0), axis=1, keepdims=True)
    chosen = block_refs[0][...].astype(jnp.float32)
    for k in range(1, sects):
        source = lax.rem(sect - k + sects, sects)
        chosen = jnp.where(prompt == source, block_refs[k][...].astype(jnp.float32), chosen)
    den = chosen[:, width : width + head_size] + chosen[:, width + head_size :] + weight_ref[...]
    scale = 1.0 / den
    for head in range(width // head_size):
        span = slice(head * head_size, (head + 1) * head_size)
        out_ref[:, span] = ((chosen[:, span] + num_ref[:, span]) * scale[:, head : head + 1]).astype(out_ref.dtype)


def finish(row_prompt, num, weight, blocks):
    vmem = pl.BlockSpec(memory_space=pltpu.VMEM)
    return pl.pallas_call(
        finish_kernel,
        in_specs=[vmem] * (3 + len(blocks)),
        out_specs=vmem,
        out_shape=jax.ShapeDtypeStruct(num.shape, jnp.bfloat16),
        compiler_params=pltpu.CompilerParams(vmem_limit_bytes=8 * 1024 * 1024),
        name="finish",
    )(row_prompt.reshape(1, -1), num, weight, *blocks)


def body(
    sects, prompt_keys, prompt_values, lengths, feature_weight, queries, new_keys, new_values, row_prompt
):
    blocks = [queries] + [
        lax.ppermute(queries, "sect", [((i + k) % sects, i) for i in range(sects)]) for k in range(1, sects)
    ]
    near = prefill(prompt_keys, prompt_values, feature_weight, lengths)
    far = lax.ppermute(near, "sub", [(0, 1), (1, 0)])
    results = decode(jnp.concatenate(blocks, axis=0), feature_weight, near, far, sects)
    num, weight = own(queries, new_keys, new_values, results[0], feature_weight.shape[1])
    back = [results[0]] + [
        lax.ppermute(results[k], "sect", [(i, (i + k) % sects) for i in range(sects)]) for k in range(1, sects)
    ]
    return finish(row_prompt, num, weight, back)


def solution(mesh):
    placed = (
        P(("parts", "sect"), "sub", "tp"),
        P(("parts", "sect"), "sub", "tp"),
        P(("parts", "sect")),
        P("tp", None, None),
        P(("parts", "sect", "sub"), "tp"),
        P(("parts", "sect", "sub"), "tp"),
        P(("parts", "sect", "sub"), "tp"),
        P("parts"),
    )
    return jax.shard_map(
        functools.partial(body, mesh.shape["sect"]),
        mesh=mesh,
        in_specs=placed,
        out_specs=P(("parts", "sect", "sub"), "tp"),
        check_vma=False,
    )
```

```python
import functools

import jax
import jax.numpy as jnp
from jax import lax
from jax.experimental import pallas as pl
from jax.experimental.pallas import tpu as pltpu
from jax.sharding import PartitionSpec as P

WINDOW = 64
TAU = 10.0
EPS = 1e-06
BLOCK = 512
AHEAD = 3
NT = (((1,), (1,)), ((), ()))


def feature(proj):
    return jnp.maximum(proj, 0.0) + jnp.exp(jnp.minimum(proj, 0.0))


SLAB = WINDOW + 16
MASK_ROW = 8


def prefill_kernel(
    lengths_ref, keys_ref, values_ref, weight_ref, out_ref,
    weight_at, wide_ref, proj_ref, state_ref, norm_ref,
    weight_sem, slab_sem,
):
    heads, head_size, feats = weight_ref.shape
    pairs = heads // 2
    span = keys_ref.shape[1]
    keys_at, values_at = keys_ref.at[0], values_ref.at[0]
    chunks = span // BLOCK
    get_weight = pltpu.make_async_copy(weight_ref, weight_at, weight_sem)
    get_weight.start()
    state_ref[...] = jnp.zeros_like(state_ref)
    norm_ref[...] = jnp.zeros_like(norm_ref)
    wide_ref[...] = jnp.zeros_like(wide_ref)
    get_weight.wait()
    for g in range(heads):
        half = g % 2
        turned = weight_at[g].astype(jnp.float32).T.astype(jnp.bfloat16)
        wide_ref[g // 2, half * feats : (half + 1) * feats, half * head_size : (half + 1) * head_size] = turned

    begin = lengths_ref[0] - WINDOW - lax.axis_index("sub") * span
    first = jnp.clip(begin, 0, span - SLAB)
    first = pl.multiple_of(first - lax.rem(first, 16), 16)
    slabs = []
    for i, source in enumerate((keys_ref, values_ref)):
        for g in range(heads):
            at = heads * feats + 16 + (i * heads + g) * SLAB
            slabs.append(
                pltpu.make_async_copy(
                    source.at[0, pl.ds(first, SLAB), g * head_size : (g + 1) * head_size],
                    out_ref.at[at : at + SLAB, :],
                    slab_sem.at[i, g],
                )
            )
            slabs[-1].start()

    def project(c):
        for j in range(pairs):
            proj = lax.dot_general(
                wide_ref[j],
                keys_at[c * BLOCK : (c + 1) * BLOCK, j * 2 * head_size : (j + 1) * 2 * head_size],
                NT,
                preferred_element_type=jnp.float32,
            )
            proj_ref[c % 2, j] = proj.astype(jnp.bfloat16)

    def collect(c):
        position = c * BLOCK + lax.broadcasted_iota(jnp.int32, (1, BLOCK), 1)
        live = jnp.where(position < begin, 1.0, 0.0).astype(jnp.bfloat16)
        for j in range(pairs):
            mapped = feature(proj_ref[c % 2, j]) * live
            some = [mapped[:, k * 128 : (k + 1) * 128] for k in range(BLOCK // 128)]
            while len(some) > 1:
                some = [x + y for x, y in zip(some[::2], some[1::2])]
            norm_ref[j] += some[0].astype(jnp.float32)
            state_ref[j] += jnp.dot(
                mapped,
                values_at[c * BLOCK : (c + 1) * BLOCK, j * 2 * head_size : (j + 1) * 2 * head_size],
                preferred_element_type=jnp.float32,
            )

    project(0)
    for c in range(chunks):
        if c + 1 < chunks:
            project(c + 1)
        collect(c)

    tile = []
    for g in range(heads):
        half = g % 2
        part = state_ref[g // 2, half * feats : (half + 1) * feats, half * head_size : (half + 1) * head_size]
        out_ref[g * feats : (g + 1) * feats, :] = part.astype(jnp.bfloat16)
        sums = norm_ref[g // 2, half * feats : (half + 1) * feats, :]
        tile.append(jnp.sum(sums.T, axis=0, keepdims=True))
    slot = first + lax.broadcasted_iota(jnp.int32, (1, head_size), 1)
    tile.append(jnp.zeros((MASK_ROW - heads, head_size), jnp.float32))
    tile.append(jnp.where((slot >= begin) & (slot < begin + WINDOW), 1.0, 0.0))
    tile.append(jnp.zeros((15 - MASK_ROW, head_size), jnp.float32))
    out_ref[heads * feats : heads * feats + 16, :] = jnp.concatenate(tile, axis=0).astype(jnp.bfloat16)
    for slab in slabs:
        slab.wait()


def prefill(keys, values, weight, lengths):
    heads, head_size, feats = weight.shape
    span, width = keys.shape[1:]
    hbm = pl.BlockSpec(memory_space=pltpu.MemorySpace.HBM)
    vmem = pl.BlockSpec(memory_space=pltpu.VMEM)
    return pl.pallas_call(
        prefill_kernel,
        in_specs=[pl.BlockSpec(memory_space=pltpu.SMEM), vmem, vmem, hbm],
        out_specs=vmem,
        out_shape=jax.ShapeDtypeStruct((heads * feats + 16 + 2 * heads * SLAB, head_size), jnp.bfloat16),
        scratch_shapes=[
            pltpu.VMEM(weight.shape, jnp.bfloat16),
            pltpu.VMEM((heads // 2, 2 * feats, 2 * head_size), jnp.bfloat16),
            pltpu.VMEM((2, heads // 2, 2 * feats, BLOCK), jnp.bfloat16),
            pltpu.VMEM((heads // 2, 2 * feats, 2 * head_size), jnp.float32),
            pltpu.VMEM((heads // 2, 2 * feats, 128), jnp.float32),
            pltpu.SemaphoreType.DMA,
            pltpu.SemaphoreType.DMA((2, heads)),
        ],
        compiler_params=pltpu.CompilerParams(vmem_limit_bytes=16 * 1024 * 1024),
        cost_estimate=pl.CostEstimate(
            flops=4 * span * width * feats, bytes_accessed=4 * span * width, transcendentals=span * width
        ),
        name="prefill",
    )(
        lengths,
        pltpu.with_memory_space_constraint(keys, pltpu.MemorySpace.VMEM),
        pltpu.with_memory_space_constraint(values, pltpu.MemorySpace.VMEM),
        pltpu.with_memory_space_constraint(weight, pltpu.MemorySpace.HBM),
    )


def decode_kernel(rows_ref, weight_ref, near_ref, far_ref, *out_refs):
    heads, head_size, feats = weight_ref.shape
    count, width = rows_ref.shape
    group = width // (heads * head_size)
    each = count // len(out_refs)
    tile_at = heads * feats
    halves = (near_ref, far_ref)
    tiles = [ref[tile_at : tile_at + 16, :].astype(jnp.float32) for ref in halves]
    lane = lax.broadcasted_iota(jnp.int32, (count, head_size), 1)
    dens = jnp.zeros((count, head_size), jnp.float32)
    for g in range(heads):
        query = jnp.concatenate(
            [
                rows_ref[:, (g * group + h) * head_size : (g * group + h + 1) * head_size]
                for h in range(group)
            ],
            axis=0,
        )
        wide = query.astype(jnp.float32)
        phi = feature(jnp.dot(query, weight_ref[g], preferred_element_type=jnp.float32)).astype(jnp.bfloat16)
        scale = (TAU / head_size) * lax.rsqrt(jnp.mean(wide * wide, axis=-1, keepdims=True) + EPS)
        num, den, linear = 0.0, 0.0, 0.0
        for ref, tile in zip(halves, tiles):
            linear += jnp.dot(phi, ref[g * feats : (g + 1) * feats, :], preferred_element_type=jnp.float32)
            at = tile_at + 16 + g * SLAB
            keys = ref[at : at + SLAB, :]
            at += heads * SLAB
            values = ref[at : at + SLAB, :]
            keys_wide = keys.astype(jnp.float32)
            key_scale = lax.rsqrt(jnp.mean((keys_wide * keys_wide).T, axis=0, keepdims=True) + EPS)
            score = lax.dot_general(query, keys, NT, preferred_element_type=jnp.float32) * scale * key_scale
            weights = jnp.exp(score) * tile[MASK_ROW : MASK_ROW + 1, :SLAB]
            num += jnp.dot(weights.astype(jnp.bfloat16), values, preferred_element_type=jnp.float32)
            den += jnp.sum(weights, axis=-1, keepdims=True)
        norm = (tiles[0] + tiles[1])[g : g + 1]
        back = 1.0 / (feats * feats)
        den += jnp.sum(phi.astype(jnp.float32) * norm, axis=-1, keepdims=True) * back
        result = (linear * back + num).astype(jnp.bfloat16)
        for h in range(group):
            head = g * group + h
            dens = jnp.where(lane == head, den[h * count : (h + 1) * count], dens)
            for k, out_ref in enumerate(out_refs):
                start = h * count + k * each
                out_ref[:, head * head_size : (head + 1) * head_size] = result[start : start + each]
    high = dens.astype(jnp.bfloat16)
    low = (dens - high.astype(jnp.float32)).astype(jnp.bfloat16)
    for k, out_ref in enumerate(out_refs):
        out_ref[:, width : width + head_size] = high[k * each : (k + 1) * each]
        out_ref[:, width + head_size :] = low[k * each : (k + 1) * each]


def decode(rows, weight, near, far, parts):
    heads, head_size, feats = weight.shape
    count, width = rows.shape
    vmem = pl.BlockSpec(memory_space=pltpu.VMEM)
    return pl.pallas_call(
        decode_kernel,
        in_specs=[vmem] * 4,
        out_specs=[vmem] * parts,
        out_shape=[jax.ShapeDtypeStruct((count // parts, width + 2 * head_size), jnp.bfloat16)] * parts,
        compiler_params=pltpu.CompilerParams(vmem_limit_bytes=32 * 1024 * 1024),
        cost_estimate=pl.CostEstimate(
            flops=10 * count * width * feats, bytes_accessed=4 * count * width, transcendentals=2 * count * width
        ),
        name="decode",
    )(rows, weight, near, far)


def own_kernel(queries_ref, keys_ref, values_ref, _, num_ref, weight_ref):
    count, width = queries_ref.shape
    head_size = weight_ref.shape[1]
    heads = keys_ref.shape[1] // head_size
    group = width // (heads * head_size)
    lane = lax.broadcasted_iota(jnp.int32, (count, head_size), 1)
    kept = jnp.zeros((count, head_size), jnp.float32)
    for g in range(heads):
        cols = slice(g * head_size, (g + 1) * head_size)
        key = keys_ref[:, cols].astype(jnp.float32)
        value = values_ref[:, cols].astype(jnp.float32)
        key = key * lax.rsqrt(jnp.mean(key * key, axis=-1, keepdims=True) + EPS)
        for h in range(group):
            head = g * group + h
            span = slice(head * head_size, (head + 1) * head_size)
            query = queries_ref[:, span].astype(jnp.float32)
            scale = (TAU / head_size) * lax.rsqrt(jnp.mean(query * query, axis=-1, keepdims=True) + EPS)
            weight = jnp.exp(jnp.sum(query * key, axis=-1, keepdims=True) * scale)
            num_ref[:, span] = weight.astype(jnp.bfloat16).astype(jnp.float32) * value
            kept = jnp.where(lane == head, weight, kept)
    weight_ref[...] = kept


def own(queries, new_keys, new_values, after, head_size):
    vmem = pl.BlockSpec(memory_space=pltpu.VMEM)
    count, width = queries.shape
    return pl.pallas_call(
        own_kernel,
        in_specs=[vmem] * 4,
        out_specs=[vmem, vmem],
        out_shape=[
            jax.ShapeDtypeStruct((count, width), jnp.float32),
            jax.ShapeDtypeStruct((count, head_size), jnp.float32),
        ],
        compiler_params=pltpu.CompilerParams(vmem_limit_bytes=8 * 1024 * 1024),
        cost_estimate=pl.CostEstimate(
            flops=8 * count * width, bytes_accessed=8 * count * width, transcendentals=count * width // head_size
        ),
        name="own",
    )(queries, new_keys, new_values, after)


def finish_kernel(prompts_ref, num_ref, weight_ref, *refs):
    block_refs, out_ref = refs[:-1], refs[-1]
    count, width = out_ref.shape
    head_size = weight_ref.shape[1]
    sects = len(block_refs)
    sect = lax.axis_index("sect")
    first = (sect * lax.axis_size("sub") + lax.axis_index("sub")) * count
    rows = prompts_ref.shape[1]
    row = first + lax.broadcasted_iota(jnp.int32, (count, rows), 0)
    lane = lax.broadcasted_iota(jnp.int32, (count, rows), 1)
    prompt = jnp.sum(jnp.where(lane == row, prompts_ref[...], 0), axis=1, keepdims=True)
    chosen = block_refs[0][...].astype(jnp.float32)
    for k in range(1, sects):
        source = lax.rem(sect - k + sects, sects)
        chosen = jnp.where(prompt == source, block_refs[k][...].astype(jnp.float32), chosen)
    den = chosen[:, width : width + head_size] + chosen[:, width + head_size :] + weight_ref[...]
    scale = 1.0 / den
    for head in range(width // head_size):
        span = slice(head * head_size, (head + 1) * head_size)
        out_ref[:, span] = ((chosen[:, span] + num_ref[:, span]) * scale[:, head : head + 1]).astype(out_ref.dtype)


def finish(row_prompt, num, weight, blocks):
    vmem = pl.BlockSpec(memory_space=pltpu.VMEM)
    return pl.pallas_call(
        finish_kernel,
        in_specs=[vmem] * (3 + len(blocks)),
        out_specs=vmem,
        out_shape=jax.ShapeDtypeStruct(num.shape, jnp.bfloat16),
        compiler_params=pltpu.CompilerParams(vmem_limit_bytes=8 * 1024 * 1024),
        name="finish",
    )(row_prompt.reshape(1, -1), num, weight, *blocks)


def body(
    sects, prompt_keys, prompt_values, lengths, feature_weight, queries, new_keys, new_values, row_prompt
):
    asked = [
        lax.ppermute(queries, "sect", [((i + k) % sects, i) for i in range(sects)]) for k in range(sects - 1, 0, -1)
    ]
    blocks = [queries] + asked[::-1]
    stay = [(0, 0), (1, 1)]
    prompt_keys = lax.ppermute(prompt_keys, "sub", stay)
    prompt_values = lax.ppermute(prompt_values, "sub", stay)
    near = prefill(prompt_keys, prompt_values, feature_weight, lengths)
    far = lax.ppermute(near, "sub", [(0, 1), (1, 0)])
    results = decode(jnp.concatenate(blocks, axis=0), feature_weight, near, far, sects)
    num, weight = own(queries, new_keys, new_values, results[0], feature_weight.shape[1])
    back = [results[0]] + [
        lax.ppermute(results[k], "sect", [(i, (i + k) % sects) for i in range(sects)]) for k in range(1, sects)
    ]
    return finish(row_prompt, num, weight, back)


def solution(mesh):
    placed = (
        P(("parts", "sect"), "sub", "tp"),
        P(("parts", "sect"), "sub", "tp"),
        P(("parts", "sect")),
        P("tp", None, None),
        P(("parts", "sect", "sub"), "tp"),
        P(("parts", "sect", "sub"), "tp"),
        P(("parts", "sect", "sub"), "tp"),
        P("parts"),
    )
    return jax.shard_map(
        functools.partial(body, mesh.shape["sect"]),
        mesh=mesh,
        in_specs=placed,
        out_specs=P(("parts", "sect", "sub"), "tp"),
        check_vma=False,
    )
```

```python
import functools

import jax
import jax.numpy as jnp
from jax import lax
from jax.experimental import pallas as pl
from jax.experimental.pallas import tpu as pltpu
from jax.sharding import PartitionSpec as P

WINDOW = 64
TAU = 10.0
EPS = 1e-06
BLOCK = 512
NT = (((1,), (1,)), ((), ()))


def feature(proj):
    return jnp.maximum(proj, 0.0) + jnp.exp(jnp.minimum(proj, 0.0))


def pack_kernel(queries_ref, keys_ref, values_ref, out_ref, sems):
    copies, at = [], 0
    for i, ref in enumerate((queries_ref, keys_ref, values_ref)):
        size = ref.shape[1]
        copies.append(pltpu.make_async_copy(ref, out_ref.at[:, at : at + size], sems.at[i]))
        copies[-1].start()
        at += size
    for copy in copies:
        copy.wait()


def pack(queries, new_keys, new_values):
    width = queries.shape[1] + 2 * new_keys.shape[1]
    arrays = [pltpu.with_memory_space_constraint(x, pltpu.MemorySpace.HBM) for x in (queries, new_keys, new_values)]
    return pl.pallas_call(
        pack_kernel,
        in_specs=[pl.BlockSpec(memory_space=pltpu.MemorySpace.HBM)] * 3,
        out_specs=pl.BlockSpec(memory_space=pltpu.VMEM),
        out_shape=jax.ShapeDtypeStruct((queries.shape[0], width), jnp.bfloat16),
        scratch_shapes=[pltpu.SemaphoreType.DMA((3,))],
        compiler_params=pltpu.CompilerParams(vmem_limit_bytes=8 * 1024 * 1024),
        cost_estimate=pl.CostEstimate(flops=10**10, bytes_accessed=2**25, transcendentals=0),
        name="pack",
    )(*arrays)


SLAB = WINDOW + 16
MASK_ROW = 8


def prefill_kernel(
    lengths_ref, keys_ref, values_ref, weight_ref, out_ref,
    wide_ref, proj_ref, state_ref, norm_ref,
    slab_sem,
):
    heads, head_size, feats = weight_ref.shape
    pairs = heads // 2
    span = keys_ref.shape[1]
    keys_at, values_at = keys_ref.at[0], values_ref.at[0]
    chunks = span // BLOCK
    state_ref[...] = jnp.zeros_like(state_ref)
    norm_ref[...] = jnp.zeros_like(norm_ref)
    wide_ref[...] = jnp.zeros_like(wide_ref)
    for g in range(heads):
        half = g % 2
        turned = weight_ref[g].astype(jnp.float32).T.astype(jnp.bfloat16)
        wide_ref[g // 2, half * feats : (half + 1) * feats, half * head_size : (half + 1) * head_size] = turned

    begin = lengths_ref[0] - WINDOW - lax.axis_index("sub") * span
    first = jnp.clip(begin, 0, span - SLAB)
    first = pl.multiple_of(first - lax.rem(first, 16), 16)
    slabs = []
    for i, source in enumerate((keys_ref, values_ref)):
        for g in range(heads):
            at = heads * feats + 16 + (i * heads + g) * SLAB
            slabs.append(
                pltpu.make_async_copy(
                    source.at[0, pl.ds(first, SLAB), g * head_size : (g + 1) * head_size],
                    out_ref.at[at : at + SLAB, :],
                    slab_sem.at[i, g],
                )
            )
            slabs[-1].start()

    def project(c):
        for j in range(pairs):
            proj = lax.dot_general(
                wide_ref[j],
                keys_at[c * BLOCK : (c + 1) * BLOCK, j * 2 * head_size : (j + 1) * 2 * head_size],
                NT,
                preferred_element_type=jnp.float32,
            )
            proj_ref[c % 2, j] = proj.astype(jnp.bfloat16)

    def collect(c):
        position = c * BLOCK + lax.broadcasted_iota(jnp.int32, (1, BLOCK), 1)
        live = jnp.where(position < begin, 1.0, 0.0).astype(jnp.bfloat16)
        for j in range(pairs):
            mapped = feature(proj_ref[c % 2, j]) * live
            some = [mapped[:, k * 128 : (k + 1) * 128] for k in range(BLOCK // 128)]
            while len(some) > 1:
                some = [x + y for x, y in zip(some[::2], some[1::2])]
            norm_ref[j] += some[0].astype(jnp.float32)
            state_ref[j] += jnp.dot(
                mapped,
                values_at[c * BLOCK : (c + 1) * BLOCK, j * 2 * head_size : (j + 1) * 2 * head_size],
                preferred_element_type=jnp.float32,
            )

    project(0)
    for c in range(chunks):
        if c + 1 < chunks:
            project(c + 1)
        collect(c)

    tile = []
    for g in range(heads):
        half = g % 2
        part = state_ref[g // 2, half * feats : (half + 1) * feats, half * head_size : (half + 1) * head_size]
        out_ref[g * feats : (g + 1) * feats, :] = part.astype(jnp.bfloat16)
        sums = norm_ref[g // 2, half * feats : (half + 1) * feats, :]
        tile.append(jnp.sum(sums.T, axis=0, keepdims=True))
    slot = first + lax.broadcasted_iota(jnp.int32, (1, head_size), 1)
    tile.append(jnp.zeros((MASK_ROW - heads, head_size), jnp.float32))
    tile.append(jnp.where((slot >= begin) & (slot < begin + WINDOW), 1.0, 0.0))
    tile.append(jnp.zeros((15 - MASK_ROW, head_size), jnp.float32))
    out_ref[heads * feats : heads * feats + 16, :] = jnp.concatenate(tile, axis=0).astype(jnp.bfloat16)
    for slab in slabs:
        slab.wait()


def prefill(keys, values, weight, lengths):
    heads, head_size, feats = weight.shape
    span, width = keys.shape[1:]
    vmem = pl.BlockSpec(memory_space=pltpu.VMEM)
    return pl.pallas_call(
        prefill_kernel,
        in_specs=[pl.BlockSpec(memory_space=pltpu.SMEM), vmem, vmem, vmem],
        out_specs=vmem,
        out_shape=jax.ShapeDtypeStruct((heads * feats + 16 + 2 * heads * SLAB, head_size), jnp.bfloat16),
        scratch_shapes=[
            pltpu.VMEM((heads // 2, 2 * feats, 2 * head_size), jnp.bfloat16),
            pltpu.VMEM((2, heads // 2, 2 * feats, BLOCK), jnp.bfloat16),
            pltpu.VMEM((heads // 2, 2 * feats, 2 * head_size), jnp.float32),
            pltpu.VMEM((heads // 2, 2 * feats, 128), jnp.float32),
            pltpu.SemaphoreType.DMA((2, heads)),
        ],
        compiler_params=pltpu.CompilerParams(vmem_limit_bytes=16 * 1024 * 1024),
        cost_estimate=pl.CostEstimate(
            flops=4 * span * width * feats, bytes_accessed=4 * span * width, transcendentals=span * width
        ),
        name="prefill",
    )(
        lengths,
        pltpu.with_memory_space_constraint(keys, pltpu.MemorySpace.VMEM),
        pltpu.with_memory_space_constraint(values, pltpu.MemorySpace.VMEM),
        pltpu.with_memory_space_constraint(weight, pltpu.MemorySpace.VMEM),
    )


def decode_kernel(rows_ref, weight_ref, near_ref, far_ref, *out_refs):
    heads, head_size, feats = weight_ref.shape
    count = rows_ref.shape[0]
    group = (rows_ref.shape[1] - 2 * heads * head_size) // (heads * head_size)
    keys_at = heads * group * head_size
    values_at = keys_at + heads * head_size
    each = count // len(out_refs)
    tile_at = heads * feats
    halves = (near_ref, far_ref)
    tiles = [ref[tile_at : tile_at + 16, :].astype(jnp.float32) for ref in halves]
    for g in range(heads):
        query = jnp.concatenate(
            [
                rows_ref[:, (g * group + h) * head_size : (g * group + h + 1) * head_size]
                for h in range(group)
            ],
            axis=0,
        )
        wide = query.astype(jnp.float32)
        phi = feature(jnp.dot(query, weight_ref[g], preferred_element_type=jnp.float32)).astype(jnp.bfloat16)
        scale = (TAU / head_size) * lax.rsqrt(jnp.mean(wide * wide, axis=-1, keepdims=True) + EPS)
        own_key = rows_ref[:, keys_at + g * head_size : keys_at + (g + 1) * head_size].astype(jnp.float32)
        own_value = rows_ref[:, values_at + g * head_size : values_at + (g + 1) * head_size].astype(jnp.float32)
        own_key = own_key * lax.rsqrt(jnp.mean(own_key * own_key, axis=-1, keepdims=True) + EPS)
        own_score = jnp.sum(wide * jnp.concatenate([own_key] * group, axis=0), axis=-1, keepdims=True) * scale
        own_weight = jnp.exp(own_score)
        num = own_weight.astype(jnp.bfloat16).astype(jnp.float32) * jnp.concatenate([own_value] * group, axis=0)
        den = own_weight
        linear = jnp.zeros_like(num)
        for ref, tile in zip(halves, tiles):
            linear += jnp.dot(phi, ref[g * feats : (g + 1) * feats, :], preferred_element_type=jnp.float32)
            at = tile_at + 16 + g * SLAB
            keys = ref[at : at + SLAB, :]
            at += heads * SLAB
            values = ref[at : at + SLAB, :]
            keys_wide = keys.astype(jnp.float32)
            key_scale = lax.rsqrt(jnp.mean((keys_wide * keys_wide).T, axis=0, keepdims=True) + EPS)
            score = lax.dot_general(query, keys, NT, preferred_element_type=jnp.float32) * scale * key_scale
            weights = jnp.exp(score) * tile[MASK_ROW : MASK_ROW + 1, :SLAB]
            num += jnp.dot(weights.astype(jnp.bfloat16), values, preferred_element_type=jnp.float32)
            den += jnp.sum(weights, axis=-1, keepdims=True)
        norm = (tiles[0] + tiles[1])[g : g + 1]
        back = 1.0 / (feats * feats)
        den += jnp.sum(phi.astype(jnp.float32) * norm, axis=-1, keepdims=True) * back
        result = ((linear * back + num) / den).astype(jnp.bfloat16)
        for h in range(group):
            at = (g * group + h) * head_size
            for k, out_ref in enumerate(out_refs):
                start = h * count + k * each
                out_ref[:, at : at + head_size] = result[start : start + each]


def decode(rows, weight, near, far, parts):
    heads, head_size, feats = weight.shape
    count = rows.shape[0]
    width = rows.shape[1] - 2 * heads * head_size
    vmem = pl.BlockSpec(memory_space=pltpu.VMEM)
    return pl.pallas_call(
        decode_kernel,
        in_specs=[vmem] * 4,
        out_specs=[vmem] * parts,
        out_shape=[jax.ShapeDtypeStruct((count // parts, width), jnp.bfloat16)] * parts,
        compiler_params=pltpu.CompilerParams(vmem_limit_bytes=32 * 1024 * 1024),
        cost_estimate=pl.CostEstimate(
            flops=10 * count * width * feats, bytes_accessed=4 * count * width, transcendentals=2 * count * width
        ),
        name="decode",
    )(rows, weight, near, far)


def body(
    sects, prompt_keys, prompt_values, lengths, feature_weight, queries, new_keys, new_values, row_prompt
):
    sub = lax.axis_index("sub")
    sect = lax.axis_index("sect")
    mine = pack(queries, new_keys, new_values)
    blocks = [mine] + [
        lax.ppermute(mine, "sect", [((i + k) % sects, i) for i in range(sects)]) for k in range(1, sects)
    ]
    near = prefill(prompt_keys, prompt_values, feature_weight, lengths)
    far = lax.ppermute(near, "sub", [(0, 1), (1, 0)])
    results = decode(jnp.concatenate(blocks, axis=0), feature_weight, near, far, sects)

    count = queries.shape[0]
    first_row = (sect * lax.axis_size("sub") + sub) * count
    prompts = lax.dynamic_slice_in_dim(row_prompt, first_row, count, 0)
    out = results[0]
    for k in range(1, sects):
        result = lax.ppermute(results[k], "sect", [(i, (i + k) % sects) for i in range(sects)])
        out = jnp.where((prompts == (sect - k) % sects)[:, None], result, out)
    return out


def solution(mesh):
    placed = (
        P(("parts", "sect"), "sub", "tp"),
        P(("parts", "sect"), "sub", "tp"),
        P(("parts", "sect")),
        P("tp", None, None),
        P(("parts", "sect", "sub"), "tp"),
        P(("parts", "sect", "sub"), "tp"),
        P(("parts", "sect", "sub"), "tp"),
        P("parts"),
    )
    return jax.shard_map(
        functools.partial(body, mesh.shape["sect"]),
        mesh=mesh,
        in_specs=placed,
        out_specs=P(("parts", "sect", "sub"), "tp"),
        check_vma=False,
    )
```

```python
import functools

import jax
import jax.numpy as jnp
from jax import lax
from jax.experimental import pallas as pl
from jax.experimental.pallas import tpu as pltpu
from jax.sharding import PartitionSpec as P

WINDOW = 64
TAU = 10.0
EPS = 1e-06
BLOCK = 512
NT = (((1,), (1,)), ((), ()))


def feature(proj):
    return jnp.maximum(proj, 0.0) + jnp.exp(jnp.minimum(proj, 0.0))


def pack_kernel(queries_ref, keys_ref, values_ref, out_ref, sems):
    copies, at = [], 0
    for i, ref in enumerate((queries_ref, keys_ref, values_ref)):
        size = ref.shape[1]
        copies.append(pltpu.make_async_copy(ref, out_ref.at[:, at : at + size], sems.at[i]))
        copies[-1].start()
        at += size
    for copy in copies:
        copy.wait()


def pack(queries, new_keys, new_values):
    width = queries.shape[1] + 2 * new_keys.shape[1]
    arrays = [pltpu.with_memory_space_constraint(x, pltpu.MemorySpace.HBM) for x in (queries, new_keys, new_values)]
    return pl.pallas_call(
        pack_kernel,
        in_specs=[pl.BlockSpec(memory_space=pltpu.MemorySpace.HBM)] * 3,
        out_specs=pl.BlockSpec(memory_space=pltpu.VMEM),
        out_shape=jax.ShapeDtypeStruct((queries.shape[0], width), jnp.bfloat16),
        scratch_shapes=[pltpu.SemaphoreType.DMA((3,))],
        compiler_params=pltpu.CompilerParams(vmem_limit_bytes=8 * 1024 * 1024),
        cost_estimate=pl.CostEstimate(flops=10**10, bytes_accessed=2**25, transcendentals=0),
        name="pack",
    )(*arrays)


SLAB = WINDOW + 16
MASK_ROW = 8


def prefill_kernel(
    lengths_ref, keys_ref, values_ref, weight_ref, out_ref,
    wide_ref, proj_ref, state_ref, norm_ref,
    slab_sem,
):
    heads, head_size, feats = weight_ref.shape
    pairs = heads // 2
    span = keys_ref.shape[1]
    keys_at, values_at = keys_ref.at[0], values_ref.at[0]
    chunks = span // BLOCK
    state_ref[...] = jnp.zeros_like(state_ref)
    norm_ref[...] = jnp.zeros_like(norm_ref)
    wide_ref[...] = jnp.zeros_like(wide_ref)
    for g in range(heads):
        half = g % 2
        turned = weight_ref[g].astype(jnp.float32).T.astype(jnp.bfloat16)
        wide_ref[g // 2, half * feats : (half + 1) * feats, half * head_size : (half + 1) * head_size] = turned

    begin = lengths_ref[0] - WINDOW - lax.axis_index("sub") * span
    first = jnp.clip(begin, 0, span - SLAB)
    first = pl.multiple_of(first - lax.rem(first, 16), 16)
    slabs = []
    for i, source in enumerate((keys_ref, values_ref)):
        for g in range(heads):
            at = heads * feats + 16 + (i * heads + g) * SLAB
            slabs.append(
                pltpu.make_async_copy(
                    source.at[0, pl.ds(first, SLAB), g * head_size : (g + 1) * head_size],
                    out_ref.at[at : at + SLAB, :],
                    slab_sem.at[i, g],
                )
            )
            slabs[-1].start()

    def project(c):
        for j in range(pairs):
            proj = lax.dot_general(
                wide_ref[j],
                keys_at[c * BLOCK : (c + 1) * BLOCK, j * 2 * head_size : (j + 1) * 2 * head_size],
                NT,
                preferred_element_type=jnp.float32,
            )
            proj_ref[c % 2, j] = proj.astype(jnp.bfloat16)

    def collect(c):
        position = c * BLOCK + lax.broadcasted_iota(jnp.int32, (1, BLOCK), 1)
        live = jnp.where(position < begin, 1.0, 0.0).astype(jnp.bfloat16)
        for j in range(pairs):
            mapped = feature(proj_ref[c % 2, j]) * live
            some = [mapped[:, k * 128 : (k + 1) * 128] for k in range(BLOCK // 128)]
            while len(some) > 1:
                some = [x + y for x, y in zip(some[::2], some[1::2])]
            norm_ref[j] += some[0].astype(jnp.float32)
            state_ref[j] += jnp.dot(
                mapped,
                values_at[c * BLOCK : (c + 1) * BLOCK, j * 2 * head_size : (j + 1) * 2 * head_size],
                preferred_element_type=jnp.float32,
            )

    project(0)
    for c in range(chunks):
        if c + 1 < chunks:
            project(c + 1)
        collect(c)

    tile = []
    for g in range(heads):
        half = g % 2
        part = state_ref[g // 2, half * feats : (half + 1) * feats, half * head_size : (half + 1) * head_size]
        out_ref[g * feats : (g + 1) * feats, :] = part.astype(jnp.bfloat16)
        sums = norm_ref[g // 2, half * feats : (half + 1) * feats, :]
        tile.append(jnp.sum(sums.T, axis=0, keepdims=True))
    slot = first + lax.broadcasted_iota(jnp.int32, (1, head_size), 1)
    tile.append(jnp.zeros((MASK_ROW - heads, head_size), jnp.float32))
    tile.append(jnp.where((slot >= begin) & (slot < begin + WINDOW), 1.0, 0.0))
    tile.append(jnp.zeros((15 - MASK_ROW, head_size), jnp.float32))
    out_ref[heads * feats : heads * feats + 16, :] = jnp.concatenate(tile, axis=0).astype(jnp.bfloat16)
    for slab in slabs:
        slab.wait()


def prefill(keys, values, weight, lengths):
    heads, head_size, feats = weight.shape
    span, width = keys.shape[1:]
    vmem = pl.BlockSpec(memory_space=pltpu.VMEM)
    return pl.pallas_call(
        prefill_kernel,
        in_specs=[pl.BlockSpec(memory_space=pltpu.SMEM), vmem, vmem, vmem],
        out_specs=vmem,
        out_shape=jax.ShapeDtypeStruct((heads * feats + 16 + 2 * heads * SLAB, head_size), jnp.bfloat16),
        scratch_shapes=[
            pltpu.VMEM((heads // 2, 2 * feats, 2 * head_size), jnp.bfloat16),
            pltpu.VMEM((2, heads // 2, 2 * feats, BLOCK), jnp.bfloat16),
            pltpu.VMEM((heads // 2, 2 * feats, 2 * head_size), jnp.float32),
            pltpu.VMEM((heads // 2, 2 * feats, 128), jnp.float32),
            pltpu.SemaphoreType.DMA((2, heads)),
        ],
        compiler_params=pltpu.CompilerParams(vmem_limit_bytes=16 * 1024 * 1024),
        cost_estimate=pl.CostEstimate(
            flops=4 * span * width * feats, bytes_accessed=4 * span * width, transcendentals=span * width
        ),
        name="prefill",
    )(
        lengths,
        pltpu.with_memory_space_constraint(keys, pltpu.MemorySpace.VMEM),
        pltpu.with_memory_space_constraint(values, pltpu.MemorySpace.VMEM),
        pltpu.with_memory_space_constraint(weight, pltpu.MemorySpace.VMEM),
    )


def decode_kernel(rows_ref, weight_ref, near_ref, far_ref, *out_refs):
    heads, head_size, feats = weight_ref.shape
    count = rows_ref.shape[0]
    group = (rows_ref.shape[1] - 2 * heads * head_size) // (heads * head_size)
    keys_at = heads * group * head_size
    values_at = keys_at + heads * head_size
    each = count // len(out_refs)
    tile_at = heads * feats
    halves = (near_ref, far_ref)
    tiles = [ref[tile_at : tile_at + 16, :].astype(jnp.float32) for ref in halves]
    for g in range(heads):
        query = jnp.concatenate(
            [
                rows_ref[:, (g * group + h) * head_size : (g * group + h + 1) * head_size]
                for h in range(group)
            ],
            axis=0,
        )
        wide = query.astype(jnp.float32)
        phi = feature(jnp.dot(query, weight_ref[g], preferred_element_type=jnp.float32)).astype(jnp.bfloat16)
        scale = (TAU / head_size) * lax.rsqrt(jnp.mean(wide * wide, axis=-1, keepdims=True) + EPS)
        own_key = rows_ref[:, keys_at + g * head_size : keys_at + (g + 1) * head_size].astype(jnp.float32)
        own_value = rows_ref[:, values_at + g * head_size : values_at + (g + 1) * head_size].astype(jnp.float32)
        own_key = own_key * lax.rsqrt(jnp.mean(own_key * own_key, axis=-1, keepdims=True) + EPS)
        own_score = jnp.sum(wide * jnp.concatenate([own_key] * group, axis=0), axis=-1, keepdims=True) * scale
        own_weight = jnp.exp(own_score)
        num = own_weight.astype(jnp.bfloat16).astype(jnp.float32) * jnp.concatenate([own_value] * group, axis=0)
        den = own_weight
        linear = jnp.zeros_like(num)
        for ref, tile in zip(halves, tiles):
            linear += jnp.dot(phi, ref[g * feats : (g + 1) * feats, :], preferred_element_type=jnp.float32)
            at = tile_at + 16 + g * SLAB
            keys = ref[at : at + SLAB, :]
            at += heads * SLAB
            values = ref[at : at + SLAB, :]
            keys_wide = keys.astype(jnp.float32)
            key_scale = lax.rsqrt(jnp.mean((keys_wide * keys_wide).T, axis=0, keepdims=True) + EPS)
            score = lax.dot_general(query, keys, NT, preferred_element_type=jnp.float32) * scale * key_scale
            weights = jnp.exp(score) * tile[MASK_ROW : MASK_ROW + 1, :SLAB]
            num += jnp.dot(weights.astype(jnp.bfloat16), values, preferred_element_type=jnp.float32)
            den += jnp.sum(weights, axis=-1, keepdims=True)
        norm = (tiles[0] + tiles[1])[g : g + 1]
        back = 1.0 / (feats * feats)
        den += jnp.sum(phi.astype(jnp.float32) * norm, axis=-1, keepdims=True) * back
        result = ((linear * back + num) / den).astype(jnp.bfloat16)
        for h in range(group):
            at = (g * group + h) * head_size
            for k, out_ref in enumerate(out_refs):
                start = h * count + k * each
                out_ref[:, at : at + head_size] = result[start : start + each]


def decode(rows, weight, near, far, parts):
    heads, head_size, feats = weight.shape
    count = rows.shape[0]
    width = rows.shape[1] - 2 * heads * head_size
    vmem = pl.BlockSpec(memory_space=pltpu.VMEM)
    return pl.pallas_call(
        decode_kernel,
        in_specs=[vmem] * 4,
        out_specs=[vmem] * parts,
        out_shape=[jax.ShapeDtypeStruct((count // parts, width), jnp.bfloat16)] * parts,
        compiler_params=pltpu.CompilerParams(vmem_limit_bytes=32 * 1024 * 1024),
        cost_estimate=pl.CostEstimate(
            flops=10 * count * width * feats, bytes_accessed=4 * count * width, transcendentals=2 * count * width
        ),
        name="decode",
    )(rows, weight, near, far)


def body(
    sects, prompt_keys, prompt_values, lengths, feature_weight, queries, new_keys, new_values, row_prompt
):
    sub = lax.axis_index("sub")
    sect = lax.axis_index("sect")
    mine = pack(queries, new_keys, new_values)
    blocks = [mine] + [
        lax.ppermute(mine, "sect", [((i + k) % sects, i) for i in range(sects)]) for k in range(1, sects)
    ]
    near = prefill(prompt_keys, prompt_values, feature_weight, lengths)
    far = lax.ppermute(near, "sub", [(0, 1), (1, 0)])
    results = decode(jnp.concatenate(blocks, axis=0), feature_weight, near, far, sects)

    count = queries.shape[0]
    first_row = (sect * lax.axis_size("sub") + sub) * count
    prompts = lax.dynamic_slice_in_dim(row_prompt, first_row, count, 0)
    out = results[0]
    for k in range(sects - 1, 0, -1):
        result = lax.ppermute(results[k], "sect", [(i, (i + k) % sects) for i in range(sects)])
        out = jnp.where((prompts == (sect - k) % sects)[:, None], result, out)
    return out


def solution(mesh):
    placed = (
        P(("parts", "sect"), "sub", "tp"),
        P(("parts", "sect"), "sub", "tp"),
        P(("parts", "sect")),
        P("tp", None, None),
        P(("parts", "sect", "sub"), "tp"),
        P(("parts", "sect", "sub"), "tp"),
        P(("parts", "sect", "sub"), "tp"),
        P("parts"),
    )
    return jax.shard_map(
        functools.partial(body, mesh.shape["sect"]),
        mesh=mesh,
        in_specs=placed,
        out_specs=P(("parts", "sect", "sub"), "tp"),
        check_vma=False,
    )
```

```python
import functools

import jax
import jax.numpy as jnp
from jax import lax
from jax.experimental import pallas as pl
from jax.experimental.pallas import tpu as pltpu
from jax.sharding import PartitionSpec as P

WINDOW = 64
TAU = 10.0
EPS = 1e-06
BLOCK = 512
NT = (((1,), (1,)), ((), ()))


def feature(proj):
    return jnp.maximum(proj, 0.0) + jnp.exp(jnp.minimum(proj, 0.0))


def pack_kernel(queries_ref, keys_ref, values_ref, out_ref, sems):
    copies, at = [], 0
    for i, ref in enumerate((queries_ref, keys_ref, values_ref)):
        size = ref.shape[1]
        copies.append(pltpu.make_async_copy(ref, out_ref.at[:, at : at + size], sems.at[i]))
        copies[-1].start()
        at += size
    for copy in copies:
        copy.wait()


def pack(queries, new_keys, new_values):
    width = queries.shape[1] + 2 * new_keys.shape[1]
    arrays = [pltpu.with_memory_space_constraint(x, pltpu.MemorySpace.HBM) for x in (queries, new_keys, new_values)]
    return pl.pallas_call(
        pack_kernel,
        in_specs=[pl.BlockSpec(memory_space=pltpu.MemorySpace.HBM)] * 3,
        out_specs=pl.BlockSpec(memory_space=pltpu.VMEM),
        out_shape=jax.ShapeDtypeStruct((queries.shape[0], width), jnp.bfloat16),
        scratch_shapes=[pltpu.SemaphoreType.DMA((3,))],
        compiler_params=pltpu.CompilerParams(vmem_limit_bytes=8 * 1024 * 1024),
        cost_estimate=pl.CostEstimate(flops=10**10, bytes_accessed=2**25, transcendentals=0),
        name="pack",
    )(*arrays)


SLAB = WINDOW + 16
MASK_ROW = 8


def prefill_kernel(
    lengths_ref, keys_ref, values_ref, weight_ref, out_ref,
    wide_ref, proj_ref, state_ref, norm_ref,
    slab_sem,
):
    heads, head_size, feats = weight_ref.shape
    pairs = heads // 2
    span = keys_ref.shape[1]
    keys_at, values_at = keys_ref.at[0], values_ref.at[0]
    chunks = span // BLOCK
    state_ref[...] = jnp.zeros_like(state_ref)
    norm_ref[...] = jnp.zeros_like(norm_ref)
    wide_ref[...] = jnp.zeros_like(wide_ref)
    for g in range(heads):
        half = g % 2
        turned = weight_ref[g].astype(jnp.float32).T.astype(jnp.bfloat16)
        wide_ref[g // 2, half * feats : (half + 1) * feats, half * head_size : (half + 1) * head_size] = turned

    begin = lengths_ref[0] - WINDOW - lax.axis_index("sub") * span
    first = jnp.clip(begin, 0, span - SLAB)
    first = pl.multiple_of(first - lax.rem(first, 16), 16)
    slabs = []
    for i, source in enumerate((keys_ref, values_ref)):
        for g in range(heads):
            at = heads * feats + 16 + (i * heads + g) * SLAB
            slabs.append(
                pltpu.make_async_copy(
                    source.at[0, pl.ds(first, SLAB), g * head_size : (g + 1) * head_size],
                    out_ref.at[at : at + SLAB, :],
                    slab_sem.at[i, g],
                )
            )
            slabs[-1].start()

    def project(c):
        for j in range(pairs):
            proj = lax.dot_general(
                wide_ref[j],
                keys_at[c * BLOCK : (c + 1) * BLOCK, j * 2 * head_size : (j + 1) * 2 * head_size],
                NT,
                preferred_element_type=jnp.float32,
            )
            proj_ref[c % 2, j] = proj.astype(jnp.bfloat16)

    def collect(c):
        position = c * BLOCK + lax.broadcasted_iota(jnp.int32, (1, BLOCK), 1)
        live = jnp.where(position < begin, 1.0, 0.0).astype(jnp.bfloat16)
        for j in range(pairs):
            mapped = feature(proj_ref[c % 2, j]) * live
            some = [mapped[:, k * 128 : (k + 1) * 128] for k in range(BLOCK // 128)]
            while len(some) > 1:
                some = [x + y for x, y in zip(some[::2], some[1::2])]
            norm_ref[j] += some[0].astype(jnp.float32)
            state_ref[j] += jnp.dot(
                mapped,
                values_at[c * BLOCK : (c + 1) * BLOCK, j * 2 * head_size : (j + 1) * 2 * head_size],
                preferred_element_type=jnp.float32,
            )

    project(0)
    for c in range(chunks):
        if c + 1 < chunks:
            project(c + 1)
        collect(c)

    tile = []
    for g in range(heads):
        half = g % 2
        part = state_ref[g // 2, half * feats : (half + 1) * feats, half * head_size : (half + 1) * head_size]
        out_ref[g * feats : (g + 1) * feats, :] = part.astype(jnp.bfloat16)
        sums = norm_ref[g // 2, half * feats : (half + 1) * feats, :]
        tile.append(jnp.sum(sums.T, axis=0, keepdims=True))
    slot = first + lax.broadcasted_iota(jnp.int32, (1, head_size), 1)
    tile.append(jnp.zeros((MASK_ROW - heads, head_size), jnp.float32))
    tile.append(jnp.where((slot >= begin) & (slot < begin + WINDOW), 1.0, 0.0))
    tile.append(jnp.zeros((15 - MASK_ROW, head_size), jnp.float32))
    out_ref[heads * feats : heads * feats + 16, :] = jnp.concatenate(tile, axis=0).astype(jnp.bfloat16)
    for slab in slabs:
        slab.wait()


def prefill(keys, values, weight, lengths):
    heads, head_size, feats = weight.shape
    span, width = keys.shape[1:]
    vmem = pl.BlockSpec(memory_space=pltpu.VMEM)
    return pl.pallas_call(
        prefill_kernel,
        in_specs=[pl.BlockSpec(memory_space=pltpu.SMEM), vmem, vmem, vmem],
        out_specs=vmem,
        out_shape=jax.ShapeDtypeStruct((heads * feats + 16 + 2 * heads * SLAB, head_size), jnp.bfloat16),
        scratch_shapes=[
            pltpu.VMEM((heads // 2, 2 * feats, 2 * head_size), jnp.bfloat16),
            pltpu.VMEM((2, heads // 2, 2 * feats, BLOCK), jnp.bfloat16),
            pltpu.VMEM((heads // 2, 2 * feats, 2 * head_size), jnp.float32),
            pltpu.VMEM((heads // 2, 2 * feats, 128), jnp.float32),
            pltpu.SemaphoreType.DMA((2, heads)),
        ],
        compiler_params=pltpu.CompilerParams(vmem_limit_bytes=16 * 1024 * 1024),
        cost_estimate=pl.CostEstimate(
            flops=4 * span * width * feats, bytes_accessed=4 * span * width, transcendentals=span * width
        ),
        name="prefill",
    )(
        lengths,
        pltpu.with_memory_space_constraint(keys, pltpu.MemorySpace.VMEM),
        pltpu.with_memory_space_constraint(values, pltpu.MemorySpace.VMEM),
        pltpu.with_memory_space_constraint(weight, pltpu.MemorySpace.VMEM),
    )


def share(query, phi, scale, ref, g, heads):
    head_size = query.shape[1]
    feats = phi.shape[1]
    tile_at = heads * feats
    tile = ref[tile_at : tile_at + 16, :].astype(jnp.float32)
    linear = jnp.dot(phi, ref[g * feats : (g + 1) * feats, :], preferred_element_type=jnp.float32)
    at = tile_at + 16 + g * SLAB
    keys = ref[at : at + SLAB, :]
    at += heads * SLAB
    values = ref[at : at + SLAB, :]
    keys_wide = keys.astype(jnp.float32)
    key_scale = lax.rsqrt(jnp.mean((keys_wide * keys_wide).T, axis=0, keepdims=True) + EPS)
    score = lax.dot_general(query, keys, NT, preferred_element_type=jnp.float32) * scale * key_scale
    weights = jnp.exp(score) * tile[MASK_ROW : MASK_ROW + 1, :SLAB]
    back = 1.0 / (feats * feats)
    num = linear * back + jnp.dot(weights.astype(jnp.bfloat16), values, preferred_element_type=jnp.float32)
    den = jnp.sum(weights, axis=-1, keepdims=True)
    return num, den + jnp.sum(phi.astype(jnp.float32) * tile[g : g + 1], axis=-1, keepdims=True) * back


def begin_kernel(rows_ref, weight_ref, near_ref, query_ref, phi_ref, num_ref, den_ref, scale_ref):
    heads, head_size, feats = weight_ref.shape
    group = (rows_ref.shape[1] - 2 * heads * head_size) // (heads * head_size)
    keys_at = heads * group * head_size
    values_at = keys_at + heads * head_size
    for g in range(heads):
        query = jnp.concatenate(
            [
                rows_ref[:, (g * group + h) * head_size : (g * group + h + 1) * head_size]
                for h in range(group)
            ],
            axis=0,
        )
        wide = query.astype(jnp.float32)
        phi = feature(jnp.dot(query, weight_ref[g], preferred_element_type=jnp.float32)).astype(jnp.bfloat16)
        scale = (TAU / head_size) * lax.rsqrt(jnp.mean(wide * wide, axis=-1, keepdims=True) + EPS)
        own_key = rows_ref[:, keys_at + g * head_size : keys_at + (g + 1) * head_size].astype(jnp.float32)
        own_value = rows_ref[:, values_at + g * head_size : values_at + (g + 1) * head_size].astype(jnp.float32)
        own_key = own_key * lax.rsqrt(jnp.mean(own_key * own_key, axis=-1, keepdims=True) + EPS)
        own_score = jnp.sum(wide * jnp.concatenate([own_key] * group, axis=0), axis=-1, keepdims=True) * scale
        own_weight = jnp.exp(own_score)
        num, den = share(query, phi, scale, near_ref, g, heads)
        num += own_weight.astype(jnp.bfloat16).astype(jnp.float32) * jnp.concatenate([own_value] * group, axis=0)
        query_ref[g] = query
        phi_ref[g] = phi
        num_ref[g] = num
        den_ref[g] = jnp.broadcast_to(den + own_weight, num.shape)
        scale_ref[g] = jnp.broadcast_to(scale, num.shape)


def end_kernel(query_ref, phi_ref, num_ref, den_ref, scale_ref, far_ref, *out_refs):
    heads, asked, head_size = query_ref.shape
    each, width = out_refs[0].shape
    group = width // (heads * head_size)
    count = asked // group
    for g in range(heads):
        num, den = share(query_ref[g], phi_ref[g], scale_ref[g][:, :1], far_ref, g, heads)
        result = ((num_ref[g] + num) / (den_ref[g] + den)).astype(jnp.bfloat16)
        for h in range(group):
            at = (g * group + h) * head_size
            for k, out_ref in enumerate(out_refs):
                start = h * count + k * each
                out_ref[:, at : at + head_size] = result[start : start + each]


def begin(rows, weight, near):
    heads, head_size, feats = weight.shape
    count = rows.shape[0]
    group = (rows.shape[1] - 2 * heads * head_size) // (heads * head_size)
    shape = (heads, group * count, head_size)
    vmem = pl.BlockSpec(memory_space=pltpu.VMEM)
    return pl.pallas_call(
        begin_kernel,
        in_specs=[vmem] * 3,
        out_specs=[vmem] * 5,
        out_shape=[jax.ShapeDtypeStruct(shape, jnp.bfloat16)] * 2 + [jax.ShapeDtypeStruct(shape, jnp.float32)] * 3,
        compiler_params=pltpu.CompilerParams(vmem_limit_bytes=32 * 1024 * 1024),
        cost_estimate=pl.CostEstimate(
            flops=6 * count * rows.shape[1] * feats, bytes_accessed=4 * rows.size, transcendentals=2 * rows.size
        ),
        name="begin",
    )(rows, weight, near)


def end(started, far, count, width, parts):
    vmem = pl.BlockSpec(memory_space=pltpu.VMEM)
    return pl.pallas_call(
        end_kernel,
        in_specs=[vmem] * 6,
        out_specs=[vmem] * parts,
        out_shape=[jax.ShapeDtypeStruct((count, width), jnp.bfloat16)] * parts,
        compiler_params=pltpu.CompilerParams(vmem_limit_bytes=32 * 1024 * 1024),
        cost_estimate=pl.CostEstimate(
            flops=4 * started[0].size * 128, bytes_accessed=4 * started[0].size, transcendentals=started[0].size
        ),
        name="end",
    )(*started, far)


def body(
    sects, prompt_keys, prompt_values, lengths, feature_weight, queries, new_keys, new_values, row_prompt
):
    sub = lax.axis_index("sub")
    sect = lax.axis_index("sect")
    mine = pack(queries, new_keys, new_values)
    blocks = [mine] + [
        lax.ppermute(mine, "sect", [((i + k) % sects, i) for i in range(sects)]) for k in range(1, sects)
    ]
    near = prefill(prompt_keys, prompt_values, feature_weight, lengths)
    far = lax.ppermute(near, "sub", [(0, 1), (1, 0)])
    started = begin(jnp.concatenate(blocks, axis=0), feature_weight, near)
    results = end(started, far, *queries.shape, sects)

    count = queries.shape[0]
    first_row = (sect * lax.axis_size("sub") + sub) * count
    prompts = lax.dynamic_slice_in_dim(row_prompt, first_row, count, 0)
    out = results[0]
    for k in range(sects - 1, 0, -1):
        result = lax.ppermute(results[k], "sect", [(i, (i + k) % sects) for i in range(sects)])
        out = jnp.where((prompts == (sect - k) % sects)[:, None], result, out)
    return out


def solution(mesh):
    placed = (
        P(("parts", "sect"), "sub", "tp"),
        P(("parts", "sect"), "sub", "tp"),
        P(("parts", "sect")),
        P("tp", None, None),
        P(("parts", "sect", "sub"), "tp"),
        P(("parts", "sect", "sub"), "tp"),
        P(("parts", "sect", "sub"), "tp"),
        P("parts"),
    )
    return jax.shard_map(
        functools.partial(body, mesh.shape["sect"]),
        mesh=mesh,
        in_specs=placed,
        out_specs=P(("parts", "sect", "sub"), "tp"),
        check_vma=False,
    )
```

```python
import functools

import jax
import jax.numpy as jnp
from jax import lax
from jax.experimental import pallas as pl
from jax.experimental.pallas import tpu as pltpu
from jax.sharding import PartitionSpec as P

WINDOW = 64
TAU = 10.0
EPS = 1e-06
BLOCK = 512
NT = (((1,), (1,)), ((), ()))


def feature(proj):
    return jnp.maximum(proj, 0.0) + jnp.exp(jnp.minimum(proj, 0.0))


def pack_kernel(queries_ref, keys_ref, values_ref, out_ref, sems):
    copies, at = [], 0
    for i, ref in enumerate((queries_ref, keys_ref, values_ref)):
        size = ref.shape[1]
        copies.append(pltpu.make_async_copy(ref, out_ref.at[:, at : at + size], sems.at[i]))
        copies[-1].start()
        at += size
    for copy in copies:
        copy.wait()


def pack(queries, new_keys, new_values):
    width = queries.shape[1] + 2 * new_keys.shape[1]
    arrays = [pltpu.with_memory_space_constraint(x, pltpu.MemorySpace.HBM) for x in (queries, new_keys, new_values)]
    return pl.pallas_call(
        pack_kernel,
        in_specs=[pl.BlockSpec(memory_space=pltpu.MemorySpace.HBM)] * 3,
        out_specs=pl.BlockSpec(memory_space=pltpu.VMEM),
        out_shape=jax.ShapeDtypeStruct((queries.shape[0], width), jnp.bfloat16),
        scratch_shapes=[pltpu.SemaphoreType.DMA((3,))],
        compiler_params=pltpu.CompilerParams(vmem_limit_bytes=8 * 1024 * 1024),
        cost_estimate=pl.CostEstimate(flops=10**10, bytes_accessed=2**25, transcendentals=0),
        name="pack",
    )(*arrays)


SLAB = WINDOW + 16
MASK_ROW = 8


def prefill_kernel(
    lengths_ref, keys_ref, values_ref, weight_ref, out_ref,
    wide_ref, proj_ref, state_ref, norm_ref,
    slab_sem,
):
    heads, head_size, feats = weight_ref.shape
    pairs = heads // 2
    span = keys_ref.shape[1]
    keys_at, values_at = keys_ref.at[0], values_ref.at[0]
    chunks = span // BLOCK
    state_ref[...] = jnp.zeros_like(state_ref)
    norm_ref[...] = jnp.zeros_like(norm_ref)
    wide_ref[...] = jnp.zeros_like(wide_ref)
    for g in range(heads):
        half = g % 2
        turned = weight_ref[g].astype(jnp.float32).T.astype(jnp.bfloat16)
        wide_ref[g // 2, half * feats : (half + 1) * feats, half * head_size : (half + 1) * head_size] = turned

    begin = lengths_ref[0] - WINDOW - lax.axis_index("sub") * span
    first = jnp.clip(begin, 0, span - SLAB)
    first = pl.multiple_of(first - lax.rem(first, 16), 16)
    slabs = []
    for i, source in enumerate((keys_ref, values_ref)):
        for g in range(heads):
            at = heads * feats + 16 + (i * heads + g) * SLAB
            slabs.append(
                pltpu.make_async_copy(
                    source.at[0, pl.ds(first, SLAB), g * head_size : (g + 1) * head_size],
                    out_ref.at[at : at + SLAB, :],
                    slab_sem.at[i, g],
                )
            )
            slabs[-1].start()

    def project(c):
        for j in range(pairs):
            proj = lax.dot_general(
                wide_ref[j],
                keys_at[c * BLOCK : (c + 1) * BLOCK, j * 2 * head_size : (j + 1) * 2 * head_size],
                NT,
                preferred_element_type=jnp.float32,
            )
            proj_ref[c % 2, j] = proj.astype(jnp.bfloat16)

    def collect(c):
        position = c * BLOCK + lax.broadcasted_iota(jnp.int32, (1, BLOCK), 1)
        live = jnp.where(position < begin, 1.0, 0.0).astype(jnp.bfloat16)
        for j in range(pairs):
            mapped = feature(proj_ref[c % 2, j]) * live
            some = [mapped[:, k * 128 : (k + 1) * 128] for k in range(BLOCK // 128)]
            while len(some) > 1:
                some = [x + y for x, y in zip(some[::2], some[1::2])]
            norm_ref[j] += some[0].astype(jnp.float32)
            state_ref[j] += jnp.dot(
                mapped,
                values_at[c * BLOCK : (c + 1) * BLOCK, j * 2 * head_size : (j + 1) * 2 * head_size],
                preferred_element_type=jnp.float32,
            )

    project(0)
    for c in range(chunks):
        if c + 1 < chunks:
            project(c + 1)
        collect(c)

    tile = []
    for g in range(heads):
        half = g % 2
        part = state_ref[g // 2, half * feats : (half + 1) * feats, half * head_size : (half + 1) * head_size]
        out_ref[g * feats : (g + 1) * feats, :] = part.astype(jnp.bfloat16)
        sums = norm_ref[g // 2, half * feats : (half + 1) * feats, :]
        tile.append(jnp.sum(sums.T, axis=0, keepdims=True))
    slot = first + lax.broadcasted_iota(jnp.int32, (1, head_size), 1)
    tile.append(jnp.zeros((MASK_ROW - heads, head_size), jnp.float32))
    tile.append(jnp.where((slot >= begin) & (slot < begin + WINDOW), 1.0, 0.0))
    tile.append(jnp.zeros((15 - MASK_ROW, head_size), jnp.float32))
    out_ref[heads * feats : heads * feats + 16, :] = jnp.concatenate(tile, axis=0).astype(jnp.bfloat16)
    for slab in slabs:
        slab.wait()


def prefill(keys, values, weight, lengths):
    heads, head_size, feats = weight.shape
    span, width = keys.shape[1:]
    vmem = pl.BlockSpec(memory_space=pltpu.VMEM)
    return pl.pallas_call(
        prefill_kernel,
        in_specs=[pl.BlockSpec(memory_space=pltpu.SMEM), vmem, vmem, vmem],
        out_specs=vmem,
        out_shape=jax.ShapeDtypeStruct((heads * feats + 16 + 2 * heads * SLAB, head_size), jnp.bfloat16),
        scratch_shapes=[
            pltpu.VMEM((heads // 2, 2 * feats, 2 * head_size), jnp.bfloat16),
            pltpu.VMEM((2, heads // 2, 2 * feats, BLOCK), jnp.bfloat16),
            pltpu.VMEM((heads // 2, 2 * feats, 2 * head_size), jnp.float32),
            pltpu.VMEM((heads // 2, 2 * feats, 128), jnp.float32),
            pltpu.SemaphoreType.DMA((2, heads)),
        ],
        compiler_params=pltpu.CompilerParams(vmem_limit_bytes=16 * 1024 * 1024),
        cost_estimate=pl.CostEstimate(
            flops=4 * span * width * feats, bytes_accessed=4 * span * width, transcendentals=span * width
        ),
        name="prefill",
    )(
        lengths,
        pltpu.with_memory_space_constraint(keys, pltpu.MemorySpace.VMEM),
        pltpu.with_memory_space_constraint(values, pltpu.MemorySpace.VMEM),
        pltpu.with_memory_space_constraint(weight, pltpu.MemorySpace.VMEM),
    )


def share(query, phi, scale, ref, g, heads):
    head_size = query.shape[1]
    feats = phi.shape[1]
    tile_at = heads * feats
    tile = ref[tile_at : tile_at + 16, :].astype(jnp.float32)
    linear = jnp.dot(phi, ref[g * feats : (g + 1) * feats, :], preferred_element_type=jnp.float32)
    at = tile_at + 16 + g * SLAB
    keys = ref[at : at + SLAB, :]
    at += heads * SLAB
    values = ref[at : at + SLAB, :]
    keys_wide = keys.astype(jnp.float32)
    key_scale = lax.rsqrt(jnp.mean((keys_wide * keys_wide).T, axis=0, keepdims=True) + EPS)
    score = lax.dot_general(query, keys, NT, preferred_element_type=jnp.float32) * scale * key_scale
    weights = jnp.exp(score) * tile[MASK_ROW : MASK_ROW + 1, :SLAB]
    back = 1.0 / (feats * feats)
    num = linear * back + jnp.dot(weights.astype(jnp.bfloat16), values, preferred_element_type=jnp.float32)
    den = jnp.sum(weights, axis=-1, keepdims=True)
    return num, den + jnp.sum(phi.astype(jnp.float32) * tile[g : g + 1], axis=-1, keepdims=True) * back


def begin_kernel(rows_ref, weight_ref, near_ref, query_ref, phi_ref, num_ref, den_ref, scale_ref):
    heads, head_size, feats = weight_ref.shape
    group = (rows_ref.shape[1] - 2 * heads * head_size) // (heads * head_size)
    keys_at = heads * group * head_size
    values_at = keys_at + heads * head_size
    for g in range(heads):
        query = jnp.concatenate(
            [
                rows_ref[:, (g * group + h) * head_size : (g * group + h + 1) * head_size]
                for h in range(group)
            ],
            axis=0,
        )
        wide = query.astype(jnp.float32)
        phi = feature(jnp.dot(query, weight_ref[g], preferred_element_type=jnp.float32)).astype(jnp.bfloat16)
        scale = (TAU / head_size) * lax.rsqrt(jnp.mean(wide * wide, axis=-1, keepdims=True) + EPS)
        own_key = rows_ref[:, keys_at + g * head_size : keys_at + (g + 1) * head_size].astype(jnp.float32)
        own_value = rows_ref[:, values_at + g * head_size : values_at + (g + 1) * head_size].astype(jnp.float32)
        own_key = own_key * lax.rsqrt(jnp.mean(own_key * own_key, axis=-1, keepdims=True) + EPS)
        own_score = jnp.sum(wide * jnp.concatenate([own_key] * group, axis=0), axis=-1, keepdims=True) * scale
        own_weight = jnp.exp(own_score)
        num, den = share(query, phi, scale, near_ref, g, heads)
        num += own_weight.astype(jnp.bfloat16).astype(jnp.float32) * jnp.concatenate([own_value] * group, axis=0)
        query_ref[g] = query
        phi_ref[g] = phi
        num_ref[g] = num
        den_ref[g] = jnp.broadcast_to(den + own_weight, num.shape)
        scale_ref[g] = jnp.broadcast_to(scale, num.shape)


def end_kernel(query_ref, phi_ref, num_ref, den_ref, scale_ref, far_ref, *out_refs):
    heads, asked, head_size = query_ref.shape
    each, width = out_refs[0].shape
    group = width // (heads * head_size)
    count = asked // group
    for g in range(heads):
        num, den = share(query_ref[g], phi_ref[g], scale_ref[g][:, :1], far_ref, g, heads)
        result = ((num_ref[g] + num) / (den_ref[g] + den)).astype(jnp.bfloat16)
        for h in range(group):
            at = (g * group + h) * head_size
            for k, out_ref in enumerate(out_refs):
                start = h * count + k * each
                out_ref[:, at : at + head_size] = result[start : start + each]


def begin(rows, weight, near):
    heads, head_size, feats = weight.shape
    count = rows.shape[0]
    group = (rows.shape[1] - 2 * heads * head_size) // (heads * head_size)
    shape = (heads, group * count, head_size)
    vmem = pl.BlockSpec(memory_space=pltpu.VMEM)
    return pl.pallas_call(
        begin_kernel,
        in_specs=[vmem] * 3,
        out_specs=[vmem] * 5,
        out_shape=[jax.ShapeDtypeStruct(shape, jnp.bfloat16)] * 2 + [jax.ShapeDtypeStruct(shape, jnp.float32)] * 3,
        compiler_params=pltpu.CompilerParams(vmem_limit_bytes=32 * 1024 * 1024),
        cost_estimate=pl.CostEstimate(
            flops=6 * count * rows.shape[1] * feats, bytes_accessed=4 * rows.size, transcendentals=2 * rows.size
        ),
        name="begin",
    )(rows, weight, near)


def end(started, far, count, width, parts):
    vmem = pl.BlockSpec(memory_space=pltpu.VMEM)
    return pl.pallas_call(
        end_kernel,
        in_specs=[vmem] * 6,
        out_specs=[vmem] * parts,
        out_shape=[jax.ShapeDtypeStruct((count, width), jnp.bfloat16)] * parts,
        compiler_params=pltpu.CompilerParams(vmem_limit_bytes=32 * 1024 * 1024),
        cost_estimate=pl.CostEstimate(
            flops=4 * started[0].size * 128, bytes_accessed=4 * started[0].size, transcendentals=started[0].size
        ),
        name="end",
    )(*started, far)


def body(
    sects, prompt_keys, prompt_values, lengths, feature_weight, queries, new_keys, new_values, row_prompt
):
    sub = lax.axis_index("sub")
    sect = lax.axis_index("sect")
    shifts = list(range(1, sects))
    shifts[:2] = shifts[:2][::-1]
    mine = pack(queries, new_keys, new_values)
    blocks = [mine] + [lax.ppermute(mine, "sect", [((i + k) % sects, i) for i in range(sects)]) for k in shifts]
    near = prefill(prompt_keys, prompt_values, feature_weight, lengths)
    far = lax.ppermute(near, "sub", [(0, 1), (1, 0)])
    started = begin(jnp.concatenate(blocks, axis=0), feature_weight, near)
    results = end(started, far, *queries.shape, sects)
    results = dict(zip([0] + shifts, results))

    count = queries.shape[0]
    first_row = (sect * lax.axis_size("sub") + sub) * count
    prompts = lax.dynamic_slice_in_dim(row_prompt, first_row, count, 0)
    out = results[0]
    for k in range(sects - 1, 0, -1):
        result = lax.ppermute(results[k], "sect", [(i, (i + k) % sects) for i in range(sects)])
        out = jnp.where((prompts == (sect - k) % sects)[:, None], result, out)
    return out


def solution(mesh):
    placed = (
        P(("parts", "sect"), "sub", "tp"),
        P(("parts", "sect"), "sub", "tp"),
        P(("parts", "sect")),
        P("tp", None, None),
        P(("parts", "sect", "sub"), "tp"),
        P(("parts", "sect", "sub"), "tp"),
        P(("parts", "sect", "sub"), "tp"),
        P("parts"),
    )
    return jax.shard_map(
        functools.partial(body, mesh.shape["sect"]),
        mesh=mesh,
        in_specs=placed,
        out_specs=P(("parts", "sect", "sub"), "tp"),
        check_vma=False,
    )
```

```python
import functools

import jax
import jax.numpy as jnp
from jax import lax
from jax.experimental import pallas as pl
from jax.experimental.pallas import tpu as pltpu
from jax.sharding import PartitionSpec as P

WINDOW = 64
TAU = 10.0
EPS = 1e-06
BLOCK = 1024
NT = (((1,), (1,)), ((), ()))


def feature(proj):
    return jnp.maximum(proj, 0.0) + jnp.exp(jnp.minimum(proj, 0.0))


def pack_kernel(queries_ref, keys_ref, values_ref, out_ref, sems):
    copies, at = [], 0
    for i, ref in enumerate((queries_ref, keys_ref, values_ref)):
        size = ref.shape[1]
        copies.append(pltpu.make_async_copy(ref, out_ref.at[:, at : at + size], sems.at[i]))
        copies[-1].start()
        at += size
    for copy in copies:
        copy.wait()


def pack(queries, new_keys, new_values):
    width = queries.shape[1] + 2 * new_keys.shape[1]
    arrays = [pltpu.with_memory_space_constraint(x, pltpu.MemorySpace.HBM) for x in (queries, new_keys, new_values)]
    return pl.pallas_call(
        pack_kernel,
        in_specs=[pl.BlockSpec(memory_space=pltpu.MemorySpace.HBM)] * 3,
        out_specs=pl.BlockSpec(memory_space=pltpu.VMEM),
        out_shape=jax.ShapeDtypeStruct((queries.shape[0], width), jnp.bfloat16),
        scratch_shapes=[pltpu.SemaphoreType.DMA((3,))],
        compiler_params=pltpu.CompilerParams(vmem_limit_bytes=8 * 1024 * 1024),
        cost_estimate=pl.CostEstimate(flops=10**10, bytes_accessed=2**25, transcendentals=0),
        name="pack",
    )(*arrays)


SLAB = WINDOW + 16
MASK_ROW = 8


def prefill_kernel(
    lengths_ref, keys_ref, values_ref, weight_ref, out_ref,
    wide_ref, proj_ref, state_ref, norm_ref,
    slab_sem,
):
    heads, head_size, feats = weight_ref.shape
    pairs = heads // 2
    span = keys_ref.shape[1]
    keys_at, values_at = keys_ref.at[0], values_ref.at[0]
    chunks = span // BLOCK
    state_ref[...] = jnp.zeros_like(state_ref)
    norm_ref[...] = jnp.zeros_like(norm_ref)
    wide_ref[...] = jnp.zeros_like(wide_ref)
    for g in range(heads):
        half = g % 2
        turned = weight_ref[g].astype(jnp.float32).T.astype(jnp.bfloat16)
        wide_ref[g // 2, half * feats : (half + 1) * feats, half * head_size : (half + 1) * head_size] = turned

    begin = lengths_ref[0] - WINDOW - lax.axis_index("sub") * span
    first = jnp.clip(begin, 0, span - SLAB)
    first = pl.multiple_of(first - lax.rem(first, 16), 16)
    slabs = []
    for i, source in enumerate((keys_ref, values_ref)):
        for g in range(heads):
            at = heads * feats + 16 + (i * heads + g) * SLAB
            slabs.append(
                pltpu.make_async_copy(
                    source.at[0, pl.ds(first, SLAB), g * head_size : (g + 1) * head_size],
                    out_ref.at[at : at + SLAB, :],
                    slab_sem.at[i, g],
                )
            )
            slabs[-1].start()

    def project(c):
        for j in range(pairs):
            proj = lax.dot_general(
                wide_ref[j],
                keys_at[c * BLOCK : (c + 1) * BLOCK, j * 2 * head_size : (j + 1) * 2 * head_size],
                NT,
                preferred_element_type=jnp.float32,
            )
            proj_ref[c % 2, j] = proj.astype(jnp.bfloat16)

    def collect(c):
        position = c * BLOCK + lax.broadcasted_iota(jnp.int32, (1, BLOCK), 1)
        live = jnp.where(position < begin, 1.0, 0.0).astype(jnp.bfloat16)
        for j in range(pairs):
            mapped = feature(proj_ref[c % 2, j]) * live
            some = [mapped[:, k * 128 : (k + 1) * 128] for k in range(BLOCK // 128)]
            while len(some) > 1:
                some = [x + y for x, y in zip(some[::2], some[1::2])]
            norm_ref[j] += some[0].astype(jnp.float32)
            state_ref[j] += jnp.dot(
                mapped,
                values_at[c * BLOCK : (c + 1) * BLOCK, j * 2 * head_size : (j + 1) * 2 * head_size],
                preferred_element_type=jnp.float32,
            )

    project(0)
    for c in range(chunks):
        if c + 1 < chunks:
            project(c + 1)
        collect(c)

    tile = []
    for g in range(heads):
        half = g % 2
        part = state_ref[g // 2, half * feats : (half + 1) * feats, half * head_size : (half + 1) * head_size]
        out_ref[g * feats : (g + 1) * feats, :] = part.astype(jnp.bfloat16)
        sums = norm_ref[g // 2, half * feats : (half + 1) * feats, :]
        tile.append(jnp.sum(sums.T, axis=0, keepdims=True))
    slot = first + lax.broadcasted_iota(jnp.int32, (1, head_size), 1)
    tile.append(jnp.zeros((MASK_ROW - heads, head_size), jnp.float32))
    tile.append(jnp.where((slot >= begin) & (slot < begin + WINDOW), 1.0, 0.0))
    tile.append(jnp.zeros((15 - MASK_ROW, head_size), jnp.float32))
    out_ref[heads * feats : heads * feats + 16, :] = jnp.concatenate(tile, axis=0).astype(jnp.bfloat16)
    for slab in slabs:
        slab.wait()


def prefill(keys, values, weight, lengths):
    heads, head_size, feats = weight.shape
    span, width = keys.shape[1:]
    vmem = pl.BlockSpec(memory_space=pltpu.VMEM)
    return pl.pallas_call(
        prefill_kernel,
        in_specs=[pl.BlockSpec(memory_space=pltpu.SMEM), vmem, vmem, vmem],
        out_specs=vmem,
        out_shape=jax.ShapeDtypeStruct((heads * feats + 16 + 2 * heads * SLAB, head_size), jnp.bfloat16),
        scratch_shapes=[
            pltpu.VMEM((heads // 2, 2 * feats, 2 * head_size), jnp.bfloat16),
            pltpu.VMEM((2, heads // 2, 2 * feats, BLOCK), jnp.bfloat16),
            pltpu.VMEM((heads // 2, 2 * feats, 2 * head_size), jnp.float32),
            pltpu.VMEM((heads // 2, 2 * feats, 128), jnp.float32),
            pltpu.SemaphoreType.DMA((2, heads)),
        ],
        compiler_params=pltpu.CompilerParams(vmem_limit_bytes=16 * 1024 * 1024),
        cost_estimate=pl.CostEstimate(
            flops=4 * span * width * feats, bytes_accessed=4 * span * width, transcendentals=span * width
        ),
        name="prefill",
    )(
        lengths,
        pltpu.with_memory_space_constraint(keys, pltpu.MemorySpace.VMEM),
        pltpu.with_memory_space_constraint(values, pltpu.MemorySpace.VMEM),
        pltpu.with_memory_space_constraint(weight, pltpu.MemorySpace.VMEM),
    )


def share(query, phi, scale, ref, g, heads):
    head_size = query.shape[1]
    feats = phi.shape[1]
    tile_at = heads * feats
    tile = ref[tile_at : tile_at + 16, :].astype(jnp.float32)
    linear = jnp.dot(phi, ref[g * feats : (g + 1) * feats, :], preferred_element_type=jnp.float32)
    at = tile_at + 16 + g * SLAB
    keys = ref[at : at + SLAB, :]
    at += heads * SLAB
    values = ref[at : at + SLAB, :]
    keys_wide = keys.astype(jnp.float32)
    key_scale = lax.rsqrt(jnp.mean((keys_wide * keys_wide).T, axis=0, keepdims=True) + EPS)
    score = lax.dot_general(query, keys, NT, preferred_element_type=jnp.float32) * scale * key_scale
    weights = jnp.exp(score) * tile[MASK_ROW : MASK_ROW + 1, :SLAB]
    back = 1.0 / (feats * feats)
    num = linear * back + jnp.dot(weights.astype(jnp.bfloat16), values, preferred_element_type=jnp.float32)
    den = jnp.sum(weights, axis=-1, keepdims=True)
    return num, den + jnp.sum(phi.astype(jnp.float32) * tile[g : g + 1], axis=-1, keepdims=True) * back


def begin_kernel(rows_ref, weight_ref, near_ref, query_ref, phi_ref, num_ref, den_ref, scale_ref):
    heads, head_size, feats = weight_ref.shape
    group = (rows_ref.shape[1] - 2 * heads * head_size) // (heads * head_size)
    keys_at = heads * group * head_size
    values_at = keys_at + heads * head_size
    for g in range(heads):
        query = jnp.concatenate(
            [
                rows_ref[:, (g * group + h) * head_size : (g * group + h + 1) * head_size]
                for h in range(group)
            ],
            axis=0,
        )
        wide = query.astype(jnp.float32)
        phi = feature(jnp.dot(query, weight_ref[g], preferred_element_type=jnp.float32)).astype(jnp.bfloat16)
        scale = (TAU / head_size) * lax.rsqrt(jnp.mean(wide * wide, axis=-1, keepdims=True) + EPS)
        own_key = rows_ref[:, keys_at + g * head_size : keys_at + (g + 1) * head_size].astype(jnp.float32)
        own_value = rows_ref[:, values_at + g * head_size : values_at + (g + 1) * head_size].astype(jnp.float32)
        own_key = own_key * lax.rsqrt(jnp.mean(own_key * own_key, axis=-1, keepdims=True) + EPS)
        own_score = jnp.sum(wide * jnp.concatenate([own_key] * group, axis=0), axis=-1, keepdims=True) * scale
        own_weight = jnp.exp(own_score)
        num, den = share(query, phi, scale, near_ref, g, heads)
        num += own_weight.astype(jnp.bfloat16).astype(jnp.float32) * jnp.concatenate([own_value] * group, axis=0)
        query_ref[g] = query
        phi_ref[g] = phi
        num_ref[g] = num
        den_ref[g] = jnp.broadcast_to(den + own_weight, num.shape)
        scale_ref[g] = jnp.broadcast_to(scale, num.shape)


def end_kernel(query_ref, phi_ref, num_ref, den_ref, scale_ref, far_ref, *out_refs):
    heads, asked, head_size = query_ref.shape
    each, width = out_refs[0].shape
    group = width // (heads * head_size)
    count = asked // group
    for g in range(heads):
        num, den = share(query_ref[g], phi_ref[g], scale_ref[g][:, :1], far_ref, g, heads)
        result = ((num_ref[g] + num) / (den_ref[g] + den)).astype(jnp.bfloat16)
        for h in range(group):
            at = (g * group + h) * head_size
            for k, out_ref in enumerate(out_refs):
                start = h * count + k * each
                out_ref[:, at : at + head_size] = result[start : start + each]


def begin(rows, weight, near):
    heads, head_size, feats = weight.shape
    count = rows.shape[0]
    group = (rows.shape[1] - 2 * heads * head_size) // (heads * head_size)
    shape = (heads, group * count, head_size)
    vmem = pl.BlockSpec(memory_space=pltpu.VMEM)
    return pl.pallas_call(
        begin_kernel,
        in_specs=[vmem] * 3,
        out_specs=[vmem] * 5,
        out_shape=[jax.ShapeDtypeStruct(shape, jnp.bfloat16)] * 2 + [jax.ShapeDtypeStruct(shape, jnp.float32)] * 3,
        compiler_params=pltpu.CompilerParams(vmem_limit_bytes=32 * 1024 * 1024),
        cost_estimate=pl.CostEstimate(
            flops=6 * count * rows.shape[1] * feats, bytes_accessed=4 * rows.size, transcendentals=2 * rows.size
        ),
        name="begin",
    )(rows, weight, near)


def end(started, far, count, width, parts):
    vmem = pl.BlockSpec(memory_space=pltpu.VMEM)
    return pl.pallas_call(
        end_kernel,
        in_specs=[vmem] * 6,
        out_specs=[vmem] * parts,
        out_shape=[jax.ShapeDtypeStruct((count, width), jnp.bfloat16)] * parts,
        compiler_params=pltpu.CompilerParams(vmem_limit_bytes=32 * 1024 * 1024),
        cost_estimate=pl.CostEstimate(
            flops=4 * started[0].size * 128, bytes_accessed=4 * started[0].size, transcendentals=started[0].size
        ),
        name="end",
    )(*started, far)


def body(
    sects, prompt_keys, prompt_values, lengths, feature_weight, queries, new_keys, new_values, row_prompt
):
    sub = lax.axis_index("sub")
    sect = lax.axis_index("sect")
    shifts = list(range(1, sects))
    shifts[:2] = shifts[:2][::-1]
    mine = pack(queries, new_keys, new_values)
    blocks = [mine] + [lax.ppermute(mine, "sect", [((i + k) % sects, i) for i in range(sects)]) for k in shifts]
    near = prefill(prompt_keys, prompt_values, feature_weight, lengths)
    far = lax.ppermute(near, "sub", [(0, 1), (1, 0)])
    started = begin(jnp.concatenate(blocks, axis=0), feature_weight, near)
    results = end(started, far, *queries.shape, sects)
    results = dict(zip([0] + shifts, results))

    count = queries.shape[0]
    first_row = (sect * lax.axis_size("sub") + sub) * count
    prompts = lax.dynamic_slice_in_dim(row_prompt, first_row, count, 0)
    out = results[0]
    for k in range(sects - 1, 0, -1):
        result = lax.ppermute(results[k], "sect", [(i, (i + k) % sects) for i in range(sects)])
        out = jnp.where((prompts == (sect - k) % sects)[:, None], result, out)
    return out


def solution(mesh):
    placed = (
        P(("parts", "sect"), "sub", "tp"),
        P(("parts", "sect"), "sub", "tp"),
        P(("parts", "sect")),
        P("tp", None, None),
        P(("parts", "sect", "sub"), "tp"),
        P(("parts", "sect", "sub"), "tp"),
        P(("parts", "sect", "sub"), "tp"),
        P("parts"),
    )
    return jax.shard_map(
        functools.partial(body, mesh.shape["sect"]),
        mesh=mesh,
        in_specs=placed,
        out_specs=P(("parts", "sect", "sub"), "tp"),
        check_vma=False,
    )
```

```python
import functools

import jax
import jax.numpy as jnp
from jax import lax
from jax.experimental import pallas as pl
from jax.experimental.pallas import tpu as pltpu
from jax.sharding import PartitionSpec as P

WINDOW = 64
TAU = 10.0
EPS = 1e-06
BLOCK = 256
NT = (((1,), (1,)), ((), ()))


def feature(proj):
    return jnp.maximum(proj, 0.0) + jnp.exp(jnp.minimum(proj, 0.0))


def pack_kernel(queries_ref, keys_ref, values_ref, out_ref, sems):
    copies, at = [], 0
    for i, ref in enumerate((queries_ref, keys_ref, values_ref)):
        size = ref.shape[1]
        copies.append(pltpu.make_async_copy(ref, out_ref.at[:, at : at + size], sems.at[i]))
        copies[-1].start()
        at += size
    for copy in copies:
        copy.wait()


def pack(queries, new_keys, new_values):
    width = queries.shape[1] + 2 * new_keys.shape[1]
    arrays = [pltpu.with_memory_space_constraint(x, pltpu.MemorySpace.HBM) for x in (queries, new_keys, new_values)]
    return pl.pallas_call(
        pack_kernel,
        in_specs=[pl.BlockSpec(memory_space=pltpu.MemorySpace.HBM)] * 3,
        out_specs=pl.BlockSpec(memory_space=pltpu.VMEM),
        out_shape=jax.ShapeDtypeStruct((queries.shape[0], width), jnp.bfloat16),
        scratch_shapes=[pltpu.SemaphoreType.DMA((3,))],
        compiler_params=pltpu.CompilerParams(vmem_limit_bytes=8 * 1024 * 1024),
        cost_estimate=pl.CostEstimate(flops=10**10, bytes_accessed=2**25, transcendentals=0),
        name="pack",
    )(*arrays)


SLAB = WINDOW + 16
MASK_ROW = 8


def prefill_kernel(
    lengths_ref, keys_ref, values_ref, weight_ref, out_ref,
    wide_ref, proj_ref, state_ref, norm_ref,
    slab_sem,
):
    heads, head_size, feats = weight_ref.shape
    pairs = heads // 2
    span = keys_ref.shape[1]
    keys_at, values_at = keys_ref.at[0], values_ref.at[0]
    chunks = span // BLOCK
    state_ref[...] = jnp.zeros_like(state_ref)
    norm_ref[...] = jnp.zeros_like(norm_ref)
    wide_ref[...] = jnp.zeros_like(wide_ref)
    for g in range(heads):
        half = g % 2
        turned = weight_ref[g].astype(jnp.float32).T.astype(jnp.bfloat16)
        wide_ref[g // 2, half * feats : (half + 1) * feats, half * head_size : (half + 1) * head_size] = turned

    begin = lengths_ref[0] - WINDOW - lax.axis_index("sub") * span
    first = jnp.clip(begin, 0, span - SLAB)
    first = pl.multiple_of(first - lax.rem(first, 16), 16)
    slabs = []
    for i, source in enumerate((keys_ref, values_ref)):
        for g in range(heads):
            at = heads * feats + 16 + (i * heads + g) * SLAB
            slabs.append(
                pltpu.make_async_copy(
                    source.at[0, pl.ds(first, SLAB), g * head_size : (g + 1) * head_size],
                    out_ref.at[at : at + SLAB, :],
                    slab_sem.at[i, g],
                )
            )
            slabs[-1].start()

    def project(c):
        for j in range(pairs):
            proj = lax.dot_general(
                wide_ref[j],
                keys_at[c * BLOCK : (c + 1) * BLOCK, j * 2 * head_size : (j + 1) * 2 * head_size],
                NT,
                preferred_element_type=jnp.float32,
            )
            proj_ref[c % 2, j] = proj.astype(jnp.bfloat16)

    def collect(c):
        position = c * BLOCK + lax.broadcasted_iota(jnp.int32, (1, BLOCK), 1)
        live = jnp.where(position < begin, 1.0, 0.0).astype(jnp.bfloat16)
        for j in range(pairs):
            mapped = feature(proj_ref[c % 2, j]) * live
            some = [mapped[:, k * 128 : (k + 1) * 128] for k in range(BLOCK // 128)]
            while len(some) > 1:
                some = [x + y for x, y in zip(some[::2], some[1::2])]
            norm_ref[j] += some[0].astype(jnp.float32)
            state_ref[j] += jnp.dot(
                mapped,
                values_at[c * BLOCK : (c + 1) * BLOCK, j * 2 * head_size : (j + 1) * 2 * head_size],
                preferred_element_type=jnp.float32,
            )

    project(0)
    for c in range(chunks):
        if c + 1 < chunks:
            project(c + 1)
        collect(c)

    tile = []
    for g in range(heads):
        half = g % 2
        part = state_ref[g // 2, half * feats : (half + 1) * feats, half * head_size : (half + 1) * head_size]
        out_ref[g * feats : (g + 1) * feats, :] = part.astype(jnp.bfloat16)
        sums = norm_ref[g // 2, half * feats : (half + 1) * feats, :]
        tile.append(jnp.sum(sums.T, axis=0, keepdims=True))
    slot = first + lax.broadcasted_iota(jnp.int32, (1, head_size), 1)
    tile.append(jnp.zeros((MASK_ROW - heads, head_size), jnp.float32))
    tile.append(jnp.where((slot >= begin) & (slot < begin + WINDOW), 1.0, 0.0))
    tile.append(jnp.zeros((15 - MASK_ROW, head_size), jnp.float32))
    out_ref[heads * feats : heads * feats + 16, :] = jnp.concatenate(tile, axis=0).astype(jnp.bfloat16)
    for slab in slabs:
        slab.wait()


def prefill(keys, values, weight, lengths):
    heads, head_size, feats = weight.shape
    span, width = keys.shape[1:]
    vmem = pl.BlockSpec(memory_space=pltpu.VMEM)
    return pl.pallas_call(
        prefill_kernel,
        in_specs=[pl.BlockSpec(memory_space=pltpu.SMEM), vmem, vmem, vmem],
        out_specs=vmem,
        out_shape=jax.ShapeDtypeStruct((heads * feats + 16 + 2 * heads * SLAB, head_size), jnp.bfloat16),
        scratch_shapes=[
            pltpu.VMEM((heads // 2, 2 * feats, 2 * head_size), jnp.bfloat16),
            pltpu.VMEM((2, heads // 2, 2 * feats, BLOCK), jnp.bfloat16),
            pltpu.VMEM((heads // 2, 2 * feats, 2 * head_size), jnp.float32),
            pltpu.VMEM((heads // 2, 2 * feats, 128), jnp.float32),
            pltpu.SemaphoreType.DMA((2, heads)),
        ],
        compiler_params=pltpu.CompilerParams(vmem_limit_bytes=16 * 1024 * 1024),
        cost_estimate=pl.CostEstimate(
            flops=4 * span * width * feats, bytes_accessed=4 * span * width, transcendentals=span * width
        ),
        name="prefill",
    )(
        lengths,
        pltpu.with_memory_space_constraint(keys, pltpu.MemorySpace.VMEM),
        pltpu.with_memory_space_constraint(values, pltpu.MemorySpace.VMEM),
        pltpu.with_memory_space_constraint(weight, pltpu.MemorySpace.VMEM),
    )


def share(query, phi, scale, ref, g, heads):
    head_size = query.shape[1]
    feats = phi.shape[1]
    tile_at = heads * feats
    tile = ref[tile_at : tile_at + 16, :].astype(jnp.float32)
    linear = jnp.dot(phi, ref[g * feats : (g + 1) * feats, :], preferred_element_type=jnp.float32)
    at = tile_at + 16 + g * SLAB
    keys = ref[at : at + SLAB, :]
    at += heads * SLAB
    values = ref[at : at + SLAB, :]
    keys_wide = keys.astype(jnp.float32)
    key_scale = lax.rsqrt(jnp.mean((keys_wide * keys_wide).T, axis=0, keepdims=True) + EPS)
    score = lax.dot_general(query, keys, NT, preferred_element_type=jnp.float32) * scale * key_scale
    weights = jnp.exp(score) * tile[MASK_ROW : MASK_ROW + 1, :SLAB]
    back = 1.0 / (feats * feats)
    num = linear * back + jnp.dot(weights.astype(jnp.bfloat16), values, preferred_element_type=jnp.float32)
    den = jnp.sum(weights, axis=-1, keepdims=True)
    return num, den + jnp.sum(phi.astype(jnp.float32) * tile[g : g + 1], axis=-1, keepdims=True) * back


def begin_kernel(rows_ref, weight_ref, near_ref, query_ref, phi_ref, num_ref, den_ref, scale_ref):
    heads, head_size, feats = weight_ref.shape
    group = (rows_ref.shape[1] - 2 * heads * head_size) // (heads * head_size)
    keys_at = heads * group * head_size
    values_at = keys_at + heads * head_size
    for g in range(heads):
        query = jnp.concatenate(
            [
                rows_ref[:, (g * group + h) * head_size : (g * group + h + 1) * head_size]
                for h in range(group)
            ],
            axis=0,
        )
        wide = query.astype(jnp.float32)
        phi = feature(jnp.dot(query, weight_ref[g], preferred_element_type=jnp.float32)).astype(jnp.bfloat16)
        scale = (TAU / head_size) * lax.rsqrt(jnp.mean(wide * wide, axis=-1, keepdims=True) + EPS)
        own_key = rows_ref[:, keys_at + g * head_size : keys_at + (g + 1) * head_size].astype(jnp.float32)
        own_value = rows_ref[:, values_at + g * head_size : values_at + (g + 1) * head_size].astype(jnp.float32)
        own_key = own_key * lax.rsqrt(jnp.mean(own_key * own_key, axis=-1, keepdims=True) + EPS)
        own_score = jnp.sum(wide * jnp.concatenate([own_key] * group, axis=0), axis=-1, keepdims=True) * scale
        own_weight = jnp.exp(own_score)
        num, den = share(query, phi, scale, near_ref, g, heads)
        num += own_weight.astype(jnp.bfloat16).astype(jnp.float32) * jnp.concatenate([own_value] * group, axis=0)
        query_ref[g] = query
        phi_ref[g] = phi
        num_ref[g] = num
        den_ref[g] = jnp.broadcast_to(den + own_weight, num.shape)
        scale_ref[g] = jnp.broadcast_to(scale, num.shape)


def end_kernel(query_ref, phi_ref, num_ref, den_ref, scale_ref, far_ref, *out_refs):
    heads, asked, head_size = query_ref.shape
    each, width = out_refs[0].shape
    group = width // (heads * head_size)
    count = asked // group
    for g in range(heads):
        num, den = share(query_ref[g], phi_ref[g], scale_ref[g][:, :1], far_ref, g, heads)
        result = ((num_ref[g] + num) / (den_ref[g] + den)).astype(jnp.bfloat16)
        for h in range(group):
            at = (g * group + h) * head_size
            for k, out_ref in enumerate(out_refs):
                start = h * count + k * each
                out_ref[:, at : at + head_size] = result[start : start + each]


def begin(rows, weight, near):
    heads, head_size, feats = weight.shape
    count = rows.shape[0]
    group = (rows.shape[1] - 2 * heads * head_size) // (heads * head_size)
    shape = (heads, group * count, head_size)
    vmem = pl.BlockSpec(memory_space=pltpu.VMEM)
    return pl.pallas_call(
        begin_kernel,
        in_specs=[vmem] * 3,
        out_specs=[vmem] * 5,
        out_shape=[jax.ShapeDtypeStruct(shape, jnp.bfloat16)] * 2 + [jax.ShapeDtypeStruct(shape, jnp.float32)] * 3,
        compiler_params=pltpu.CompilerParams(vmem_limit_bytes=32 * 1024 * 1024),
        cost_estimate=pl.CostEstimate(
            flops=6 * count * rows.shape[1] * feats, bytes_accessed=4 * rows.size, transcendentals=2 * rows.size
        ),
        name="begin",
    )(rows, weight, near)


def end(started, far, count, width, parts):
    vmem = pl.BlockSpec(memory_space=pltpu.VMEM)
    return pl.pallas_call(
        end_kernel,
        in_specs=[vmem] * 6,
        out_specs=[vmem] * parts,
        out_shape=[jax.ShapeDtypeStruct((count, width), jnp.bfloat16)] * parts,
        compiler_params=pltpu.CompilerParams(vmem_limit_bytes=32 * 1024 * 1024),
        cost_estimate=pl.CostEstimate(
            flops=4 * started[0].size * 128, bytes_accessed=4 * started[0].size, transcendentals=started[0].size
        ),
        name="end",
    )(*started, far)


def body(
    sects, prompt_keys, prompt_values, lengths, feature_weight, queries, new_keys, new_values, row_prompt
):
    sub = lax.axis_index("sub")
    sect = lax.axis_index("sect")
    shifts = list(range(1, sects))
    shifts[:2] = shifts[:2][::-1]
    mine = pack(queries, new_keys, new_values)
    blocks = [mine] + [lax.ppermute(mine, "sect", [((i + k) % sects, i) for i in range(sects)]) for k in shifts]
    near = prefill(prompt_keys, prompt_values, feature_weight, lengths)
    far = lax.ppermute(near, "sub", [(0, 1), (1, 0)])
    started = begin(jnp.concatenate(blocks, axis=0), feature_weight, near)
    results = end(started, far, *queries.shape, sects)
    results = dict(zip([0] + shifts, results))

    count = queries.shape[0]
    first_row = (sect * lax.axis_size("sub") + sub) * count
    prompts = lax.dynamic_slice_in_dim(row_prompt, first_row, count, 0)
    out = results[0]
    for k in range(sects - 1, 0, -1):
        result = lax.ppermute(results[k], "sect", [(i, (i + k) % sects) for i in range(sects)])
        out = jnp.where((prompts == (sect - k) % sects)[:, None], result, out)
    return out


def solution(mesh):
    placed = (
        P(("parts", "sect"), "sub", "tp"),
        P(("parts", "sect"), "sub", "tp"),
        P(("parts", "sect")),
        P("tp", None, None),
        P(("parts", "sect", "sub"), "tp"),
        P(("parts", "sect", "sub"), "tp"),
        P(("parts", "sect", "sub"), "tp"),
        P("parts"),
    )
    return jax.shard_map(
        functools.partial(body, mesh.shape["sect"]),
        mesh=mesh,
        in_specs=placed,
        out_specs=P(("parts", "sect", "sub"), "tp"),
        check_vma=False,
    )
```

```python
import functools

import jax
import jax.numpy as jnp
from jax import lax
from jax.experimental import pallas as pl
from jax.experimental.pallas import tpu as pltpu
from jax.sharding import PartitionSpec as P

WINDOW = 64
TAU = 10.0
EPS = 1e-06
BLOCK = 256
NT = (((1,), (1,)), ((), ()))


def paired(sects):
    return sects & (sects - 1) == 0


def shifted(sect, k, sects):
    return (sect + k) % sects


def partner(sect, k, sects):
    return sect ^ k if paired(sects) else shifted(sect, k, sects)


def feature(proj):
    return jnp.maximum(proj, 0.0) + jnp.exp(jnp.minimum(proj, 0.0))


def pack_kernel(queries_ref, keys_ref, values_ref, out_ref, sems):
    copies, at = [], 0
    for i, ref in enumerate((queries_ref, keys_ref, values_ref)):
        size = ref.shape[1]
        copies.append(pltpu.make_async_copy(ref, out_ref.at[:, at : at + size], sems.at[i]))
        copies[-1].start()
        at += size
    for copy in copies:
        copy.wait()


def pack(queries, new_keys, new_values):
    width = queries.shape[1] + 2 * new_keys.shape[1]
    arrays = [pltpu.with_memory_space_constraint(x, pltpu.MemorySpace.HBM) for x in (queries, new_keys, new_values)]
    return pl.pallas_call(
        pack_kernel,
        in_specs=[pl.BlockSpec(memory_space=pltpu.MemorySpace.HBM)] * 3,
        out_specs=pl.BlockSpec(memory_space=pltpu.VMEM),
        out_shape=jax.ShapeDtypeStruct((queries.shape[0], width), jnp.bfloat16),
        scratch_shapes=[pltpu.SemaphoreType.DMA((3,))],
        compiler_params=pltpu.CompilerParams(vmem_limit_bytes=8 * 1024 * 1024),
        cost_estimate=pl.CostEstimate(flops=10**10, bytes_accessed=2**25, transcendentals=0),
        name="pack",
    )(*arrays)


SLAB = WINDOW + 16
MASK_ROW = 8


def prefill_kernel(
    lengths_ref, keys_ref, values_ref, weight_ref, out_ref,
    wide_ref, proj_ref, state_ref, norm_ref,
    slab_sem,
):
    heads, head_size, feats = weight_ref.shape
    pairs = heads // 2
    span = keys_ref.shape[1]
    keys_at, values_at = keys_ref.at[0], values_ref.at[0]
    chunks = span // BLOCK
    state_ref[...] = jnp.zeros_like(state_ref)
    norm_ref[...] = jnp.zeros_like(norm_ref)
    wide_ref[...] = jnp.zeros_like(wide_ref)
    for g in range(heads):
        half = g % 2
        turned = weight_ref[g].astype(jnp.float32).T.astype(jnp.bfloat16)
        wide_ref[g // 2, half * feats : (half + 1) * feats, half * head_size : (half + 1) * head_size] = turned

    begin = lengths_ref[0] - WINDOW - lax.axis_index("sub") * span
    first = jnp.clip(begin, 0, span - SLAB)
    first = pl.multiple_of(first - lax.rem(first, 16), 16)
    slabs = []
    for i, source in enumerate((keys_ref, values_ref)):
        for g in range(heads):
            at = heads * feats + 16 + (i * heads + g) * SLAB
            slabs.append(
                pltpu.make_async_copy(
                    source.at[0, pl.ds(first, SLAB), g * head_size : (g + 1) * head_size],
                    out_ref.at[at : at + SLAB, :],
                    slab_sem.at[i, g],
                )
            )
            slabs[-1].start()

    def project(c):
        for j in range(pairs):
            proj = lax.dot_general(
                wide_ref[j],
                keys_at[c * BLOCK : (c + 1) * BLOCK, j * 2 * head_size : (j + 1) * 2 * head_size],
                NT,
                preferred_element_type=jnp.float32,
            )
            proj_ref[c % 2, j] = proj.astype(jnp.bfloat16)

    def collect(c):
        position = c * BLOCK + lax.broadcasted_iota(jnp.int32, (1, BLOCK), 1)
        live = jnp.where(position < begin, 1.0, 0.0).astype(jnp.bfloat16)
        for j in range(pairs):
            mapped = feature(proj_ref[c % 2, j]) * live
            some = [mapped[:, k * 128 : (k + 1) * 128] for k in range(BLOCK // 128)]
            while len(some) > 1:
                some = [x + y for x, y in zip(some[::2], some[1::2])]
            norm_ref[j] += some[0].astype(jnp.float32)
            state_ref[j] += jnp.dot(
                mapped,
                values_at[c * BLOCK : (c + 1) * BLOCK, j * 2 * head_size : (j + 1) * 2 * head_size],
                preferred_element_type=jnp.float32,
            )

    project(0)
    for c in range(chunks):
        if c + 1 < chunks:
            project(c + 1)
        collect(c)

    tile = []
    for g in range(heads):
        half = g % 2
        part = state_ref[g // 2, half * feats : (half + 1) * feats, half * head_size : (half + 1) * head_size]
        out_ref[g * feats : (g + 1) * feats, :] = part.astype(jnp.bfloat16)
        sums = norm_ref[g // 2, half * feats : (half + 1) * feats, :]
        tile.append(jnp.sum(sums.T, axis=0, keepdims=True))
    slot = first + lax.broadcasted_iota(jnp.int32, (1, head_size), 1)
    tile.append(jnp.zeros((MASK_ROW - heads, head_size), jnp.float32))
    tile.append(jnp.where((slot >= begin) & (slot < begin + WINDOW), 1.0, 0.0))
    tile.append(jnp.zeros((15 - MASK_ROW, head_size), jnp.float32))
    out_ref[heads * feats : heads * feats + 16, :] = jnp.concatenate(tile, axis=0).astype(jnp.bfloat16)
    for slab in slabs:
        slab.wait()


def prefill(keys, values, weight, lengths):
    heads, head_size, feats = weight.shape
    span, width = keys.shape[1:]
    vmem = pl.BlockSpec(memory_space=pltpu.VMEM)
    return pl.pallas_call(
        prefill_kernel,
        in_specs=[pl.BlockSpec(memory_space=pltpu.SMEM), vmem, vmem, vmem],
        out_specs=vmem,
        out_shape=jax.ShapeDtypeStruct((heads * feats + 16 + 2 * heads * SLAB, head_size), jnp.bfloat16),
        scratch_shapes=[
            pltpu.VMEM((heads // 2, 2 * feats, 2 * head_size), jnp.bfloat16),
            pltpu.VMEM((2, heads // 2, 2 * feats, BLOCK), jnp.bfloat16),
            pltpu.VMEM((heads // 2, 2 * feats, 2 * head_size), jnp.float32),
            pltpu.VMEM((heads // 2, 2 * feats, 128), jnp.float32),
            pltpu.SemaphoreType.DMA((2, heads)),
        ],
        compiler_params=pltpu.CompilerParams(vmem_limit_bytes=16 * 1024 * 1024),
        cost_estimate=pl.CostEstimate(
            flops=4 * span * width * feats, bytes_accessed=4 * span * width, transcendentals=span * width
        ),
        name="prefill",
    )(
        lengths,
        pltpu.with_memory_space_constraint(keys, pltpu.MemorySpace.VMEM),
        pltpu.with_memory_space_constraint(values, pltpu.MemorySpace.VMEM),
        pltpu.with_memory_space_constraint(weight, pltpu.MemorySpace.VMEM),
    )


def share(query, phi, scale, ref, g, heads):
    head_size = query.shape[1]
    feats = phi.shape[1]
    tile_at = heads * feats
    tile = ref[tile_at : tile_at + 16, :].astype(jnp.float32)
    linear = jnp.dot(phi, ref[g * feats : (g + 1) * feats, :], preferred_element_type=jnp.float32)
    at = tile_at + 16 + g * SLAB
    keys = ref[at : at + SLAB, :]
    at += heads * SLAB
    values = ref[at : at + SLAB, :]
    keys_wide = keys.astype(jnp.float32)
    key_scale = lax.rsqrt(jnp.mean((keys_wide * keys_wide).T, axis=0, keepdims=True) + EPS)
    score = lax.dot_general(query, keys, NT, preferred_element_type=jnp.float32) * scale * key_scale
    weights = jnp.exp(score) * tile[MASK_ROW : MASK_ROW + 1, :SLAB]
    back = 1.0 / (feats * feats)
    num = linear * back + jnp.dot(weights.astype(jnp.bfloat16), values, preferred_element_type=jnp.float32)
    den = jnp.sum(weights, axis=-1, keepdims=True)
    return num, den + jnp.sum(phi.astype(jnp.float32) * tile[g : g + 1], axis=-1, keepdims=True) * back


def begin_kernel(rows_ref, weight_ref, near_ref, query_ref, phi_ref, num_ref, den_ref, scale_ref):
    heads, head_size, feats = weight_ref.shape
    group = (rows_ref.shape[1] - 2 * heads * head_size) // (heads * head_size)
    keys_at = heads * group * head_size
    values_at = keys_at + heads * head_size
    for g in range(heads):
        query = jnp.concatenate(
            [
                rows_ref[:, (g * group + h) * head_size : (g * group + h + 1) * head_size]
                for h in range(group)
            ],
            axis=0,
        )
        wide = query.astype(jnp.float32)
        phi = feature(jnp.dot(query, weight_ref[g], preferred_element_type=jnp.float32)).astype(jnp.bfloat16)
        scale = (TAU / head_size) * lax.rsqrt(jnp.mean(wide * wide, axis=-1, keepdims=True) + EPS)
        own_key = rows_ref[:, keys_at + g * head_size : keys_at + (g + 1) * head_size].astype(jnp.float32)
        own_value = rows_ref[:, values_at + g * head_size : values_at + (g + 1) * head_size].astype(jnp.float32)
        own_key = own_key * lax.rsqrt(jnp.mean(own_key * own_key, axis=-1, keepdims=True) + EPS)
        own_score = jnp.sum(wide * jnp.concatenate([own_key] * group, axis=0), axis=-1, keepdims=True) * scale
        own_weight = jnp.exp(own_score)
        num, den = share(query, phi, scale, near_ref, g, heads)
        num += own_weight.astype(jnp.bfloat16).astype(jnp.float32) * jnp.concatenate([own_value] * group, axis=0)
        query_ref[g] = query
        phi_ref[g] = phi
        num_ref[g] = num
        den_ref[g] = jnp.broadcast_to(den + own_weight, num.shape)
        scale_ref[g] = jnp.broadcast_to(scale, num.shape)


def end_kernel(query_ref, phi_ref, num_ref, den_ref, scale_ref, far_ref, *out_refs):
    heads, asked, head_size = query_ref.shape
    each, width = out_refs[0].shape
    group = width // (heads * head_size)
    count = asked // group
    for g in range(heads):
        num, den = share(query_ref[g], phi_ref[g], scale_ref[g][:, :1], far_ref, g, heads)
        result = ((num_ref[g] + num) / (den_ref[g] + den)).astype(jnp.bfloat16)
        for h in range(group):
            at = (g * group + h) * head_size
            for k, out_ref in enumerate(out_refs):
                start = h * count + k * each
                out_ref[:, at : at + head_size] = result[start : start + each]


def begin(rows, weight, near):
    heads, head_size, feats = weight.shape
    count = rows.shape[0]
    group = (rows.shape[1] - 2 * heads * head_size) // (heads * head_size)
    shape = (heads, group * count, head_size)
    vmem = pl.BlockSpec(memory_space=pltpu.VMEM)
    return pl.pallas_call(
        begin_kernel,
        in_specs=[vmem] * 3,
        out_specs=[vmem] * 5,
        out_shape=[jax.ShapeDtypeStruct(shape, jnp.bfloat16)] * 2 + [jax.ShapeDtypeStruct(shape, jnp.float32)] * 3,
        compiler_params=pltpu.CompilerParams(vmem_limit_bytes=32 * 1024 * 1024),
        cost_estimate=pl.CostEstimate(
            flops=6 * count * rows.shape[1] * feats, bytes_accessed=4 * rows.size, transcendentals=2 * rows.size
        ),
        name="begin",
    )(rows, weight, near)


def end(started, far, count, width, parts):
    vmem = pl.BlockSpec(memory_space=pltpu.VMEM)
    return pl.pallas_call(
        end_kernel,
        in_specs=[vmem] * 6,
        out_specs=[vmem] * parts,
        out_shape=[jax.ShapeDtypeStruct((count, width), jnp.bfloat16)] * parts,
        compiler_params=pltpu.CompilerParams(vmem_limit_bytes=32 * 1024 * 1024),
        cost_estimate=pl.CostEstimate(
            flops=4 * started[0].size * 128, bytes_accessed=4 * started[0].size, transcendentals=started[0].size
        ),
        name="end",
    )(*started, far)


def body(
    sects, prompt_keys, prompt_values, lengths, feature_weight, queries, new_keys, new_values, row_prompt
):
    sub = lax.axis_index("sub")
    sect = lax.axis_index("sect")
    steps = list(range(1, sects))
    steps[:2] = steps[:2][::-1]
    mine = pack(queries, new_keys, new_values)
    ask = shifted if sects == 4 else partner
    asked = {k: lax.ppermute(mine, "sect", [(ask(i, k, sects), i) for i in range(sects)]) for k in steps}
    if sects == 4:
        odd = (sect & 1) == 1
        asked[1], asked[3] = jnp.where(odd, asked[3], asked[1]), jnp.where(odd, asked[1], asked[3])
    blocks = [mine] + [asked[k] for k in steps]
    near = prefill(prompt_keys, prompt_values, feature_weight, lengths)
    far = lax.ppermute(near, "sub", [(0, 1), (1, 0)])
    started = begin(jnp.concatenate(blocks, axis=0), feature_weight, near)
    results = end(started, far, *queries.shape, sects)
    results = dict(zip([0] + steps, results))

    count = queries.shape[0]
    first_row = (sect * lax.axis_size("sub") + sub) * count
    prompts = lax.dynamic_slice_in_dim(row_prompt, first_row, count, 0)
    out = results[0]
    for k in range(1, sects):
        result = lax.ppermute(results[k], "sect", [(i, partner(i, k, sects)) for i in range(sects)])
        source = partner(sect, k if paired(sects) else sects - k, sects)
        out = jnp.where((prompts == source)[:, None], result, out)
    return out


def solution(mesh):
    placed = (
        P(("parts", "sect"), "sub", "tp"),
        P(("parts", "sect"), "sub", "tp"),
        P(("parts", "sect")),
        P("tp", None, None),
        P(("parts", "sect", "sub"), "tp"),
        P(("parts", "sect", "sub"), "tp"),
        P(("parts", "sect", "sub"), "tp"),
        P("parts"),
    )
    return jax.shard_map(
        functools.partial(body, mesh.shape["sect"]),
        mesh=mesh,
        in_specs=placed,
        out_specs=P(("parts", "sect", "sub"), "tp"),
        check_vma=False,
    )
```

```python
import functools

import jax
import jax.numpy as jnp
from jax import lax
from jax.experimental import pallas as pl
from jax.experimental.pallas import tpu as pltpu
from jax.sharding import PartitionSpec as P

WINDOW = 64
TAU = 10.0
EPS = 1e-06
BLOCK = 256
NT = (((1,), (1,)), ((), ()))


def paired(sects):
    return sects & (sects - 1) == 0


def shifted(sect, k, sects):
    return (sect + k) % sects


def partner(sect, k, sects):
    return sect ^ k if paired(sects) else shifted(sect, k, sects)


def feature(proj):
    return jnp.maximum(proj, 0.0) + jnp.exp(jnp.minimum(proj, 0.0))


def pack_kernel(queries_ref, keys_ref, values_ref, out_ref, sems):
    copies, at = [], 0
    for i, ref in enumerate((queries_ref, keys_ref, values_ref)):
        size = ref.shape[1]
        copies.append(pltpu.make_async_copy(ref, out_ref.at[:, at : at + size], sems.at[i]))
        copies[-1].start()
        at += size
    for copy in copies:
        copy.wait()


def pack(queries, new_keys, new_values):
    width = queries.shape[1] + 2 * new_keys.shape[1]
    arrays = [pltpu.with_memory_space_constraint(x, pltpu.MemorySpace.HBM) for x in (queries, new_keys, new_values)]
    return pl.pallas_call(
        pack_kernel,
        in_specs=[pl.BlockSpec(memory_space=pltpu.MemorySpace.HBM)] * 3,
        out_specs=pl.BlockSpec(memory_space=pltpu.VMEM),
        out_shape=jax.ShapeDtypeStruct((queries.shape[0], width), jnp.bfloat16),
        scratch_shapes=[pltpu.SemaphoreType.DMA((3,))],
        compiler_params=pltpu.CompilerParams(vmem_limit_bytes=8 * 1024 * 1024),
        cost_estimate=pl.CostEstimate(flops=10**10, bytes_accessed=2**25, transcendentals=0),
        name="pack",
    )(*arrays)


SLAB = WINDOW + 16
MASK_ROW = 8


def prefill_kernel(
    lengths_ref, keys_ref, values_ref, weight_ref, out_ref,
    wide_ref, proj_ref, state_ref, norm_ref,
    slab_sem,
):
    heads, head_size, feats = weight_ref.shape
    pairs = heads // 2
    span = keys_ref.shape[1]
    keys_at, values_at = keys_ref.at[0], values_ref.at[0]
    chunks = span // BLOCK
    state_ref[...] = jnp.zeros_like(state_ref)
    norm_ref[...] = jnp.zeros_like(norm_ref)
    wide_ref[...] = jnp.zeros_like(wide_ref)
    for g in range(heads):
        half = g % 2
        turned = weight_ref[g].astype(jnp.float32).T.astype(jnp.bfloat16)
        wide_ref[g // 2, half * feats : (half + 1) * feats, half * head_size : (half + 1) * head_size] = turned

    begin = lengths_ref[0] - WINDOW - lax.axis_index("sub") * span
    first = jnp.clip(begin, 0, span - SLAB)
    first = pl.multiple_of(first - lax.rem(first, 16), 16)
    slabs = []
    for i, source in enumerate((keys_ref, values_ref)):
        for g in range(heads):
            at = heads * feats + 16 + (i * heads + g) * SLAB
            slabs.append(
                pltpu.make_async_copy(
                    source.at[0, pl.ds(first, SLAB), g * head_size : (g + 1) * head_size],
                    out_ref.at[at : at + SLAB, :],
                    slab_sem.at[i, g],
                )
            )
            slabs[-1].start()

    def project(c):
        for j in range(pairs):
            proj = lax.dot_general(
                wide_ref[j],
                keys_at[c * BLOCK : (c + 1) * BLOCK, j * 2 * head_size : (j + 1) * 2 * head_size],
                NT,
                preferred_element_type=jnp.float32,
            )
            proj_ref[c % 2, j] = proj.astype(jnp.bfloat16)

    def collect(c):
        position = c * BLOCK + lax.broadcasted_iota(jnp.int32, (1, BLOCK), 1)
        live = jnp.where(position < begin, 1.0, 0.0).astype(jnp.bfloat16)
        for j in range(pairs):
            mapped = feature(proj_ref[c % 2, j]) * live
            some = [mapped[:, k * 128 : (k + 1) * 128] for k in range(BLOCK // 128)]
            while len(some) > 1:
                some = [x + y for x, y in zip(some[::2], some[1::2])]
            norm_ref[j] += some[0].astype(jnp.float32)
            state_ref[j] += jnp.dot(
                mapped,
                values_at[c * BLOCK : (c + 1) * BLOCK, j * 2 * head_size : (j + 1) * 2 * head_size],
                preferred_element_type=jnp.float32,
            )

    project(0)
    for c in range(chunks):
        if c + 1 < chunks:
            project(c + 1)
        collect(c)

    tile = []
    for g in range(heads):
        half = g % 2
        part = state_ref[g // 2, half * feats : (half + 1) * feats, half * head_size : (half + 1) * head_size]
        out_ref[g * feats : (g + 1) * feats, :] = part.astype(jnp.bfloat16)
        sums = norm_ref[g // 2, half * feats : (half + 1) * feats, :]
        tile.append(jnp.sum(sums.T, axis=0, keepdims=True))
    slot = first + lax.broadcasted_iota(jnp.int32, (1, head_size), 1)
    tile.append(jnp.zeros((MASK_ROW - heads, head_size), jnp.float32))
    tile.append(jnp.where((slot >= begin) & (slot < begin + WINDOW), 1.0, 0.0))
    tile.append(jnp.zeros((15 - MASK_ROW, head_size), jnp.float32))
    out_ref[heads * feats : heads * feats + 16, :] = jnp.concatenate(tile, axis=0).astype(jnp.bfloat16)
    for slab in slabs:
        slab.wait()


def prefill(keys, values, weight, lengths):
    heads, head_size, feats = weight.shape
    span, width = keys.shape[1:]
    vmem = pl.BlockSpec(memory_space=pltpu.VMEM)
    return pl.pallas_call(
        prefill_kernel,
        in_specs=[pl.BlockSpec(memory_space=pltpu.SMEM), vmem, vmem, vmem],
        out_specs=vmem,
        out_shape=jax.ShapeDtypeStruct((heads * feats + 16 + 2 * heads * SLAB, head_size), jnp.bfloat16),
        scratch_shapes=[
            pltpu.VMEM((heads // 2, 2 * feats, 2 * head_size), jnp.bfloat16),
            pltpu.VMEM((2, heads // 2, 2 * feats, BLOCK), jnp.bfloat16),
            pltpu.VMEM((heads // 2, 2 * feats, 2 * head_size), jnp.float32),
            pltpu.VMEM((heads // 2, 2 * feats, 128), jnp.float32),
            pltpu.SemaphoreType.DMA((2, heads)),
        ],
        compiler_params=pltpu.CompilerParams(vmem_limit_bytes=16 * 1024 * 1024),
        cost_estimate=pl.CostEstimate(
            flops=4 * span * width * feats, bytes_accessed=4 * span * width, transcendentals=span * width
        ),
        name="prefill",
    )(
        lengths,
        pltpu.with_memory_space_constraint(keys, pltpu.MemorySpace.VMEM),
        pltpu.with_memory_space_constraint(values, pltpu.MemorySpace.VMEM),
        pltpu.with_memory_space_constraint(weight, pltpu.MemorySpace.VMEM),
    )


def share(query, phi, scale, ref, g, heads):
    head_size = query.shape[1]
    feats = phi.shape[1]
    tile_at = heads * feats
    tile = ref[tile_at : tile_at + 16, :].astype(jnp.float32)
    linear = jnp.dot(phi, ref[g * feats : (g + 1) * feats, :], preferred_element_type=jnp.float32)
    at = tile_at + 16 + g * SLAB
    keys = ref[at : at + SLAB, :]
    at += heads * SLAB
    values = ref[at : at + SLAB, :]
    keys_wide = keys.astype(jnp.float32)
    key_scale = lax.rsqrt(jnp.mean((keys_wide * keys_wide).T, axis=0, keepdims=True) + EPS)
    score = lax.dot_general(query, keys, NT, preferred_element_type=jnp.float32) * scale * key_scale
    weights = jnp.exp(score) * tile[MASK_ROW : MASK_ROW + 1, :SLAB]
    back = 1.0 / (feats * feats)
    num = linear * back + jnp.dot(weights.astype(jnp.bfloat16), values, preferred_element_type=jnp.float32)
    den = jnp.sum(weights, axis=-1, keepdims=True)
    return num, den + jnp.sum(phi.astype(jnp.float32) * tile[g : g + 1], axis=-1, keepdims=True) * back


def begin_kernel(rows_ref, weight_ref, near_ref, query_ref, phi_ref, num_ref, den_ref, scale_ref):
    heads, head_size, feats = weight_ref.shape
    group = (rows_ref.shape[1] - 2 * heads * head_size) // (heads * head_size)
    keys_at = heads * group * head_size
    values_at = keys_at + heads * head_size
    for g in range(heads):
        query = jnp.concatenate(
            [
                rows_ref[:, (g * group + h) * head_size : (g * group + h + 1) * head_size]
                for h in range(group)
            ],
            axis=0,
        )
        wide = query.astype(jnp.float32)
        phi = feature(jnp.dot(query, weight_ref[g], preferred_element_type=jnp.float32)).astype(jnp.bfloat16)
        scale = (TAU / head_size) * lax.rsqrt(jnp.mean(wide * wide, axis=-1, keepdims=True) + EPS)
        own_key = rows_ref[:, keys_at + g * head_size : keys_at + (g + 1) * head_size].astype(jnp.float32)
        own_value = rows_ref[:, values_at + g * head_size : values_at + (g + 1) * head_size].astype(jnp.float32)
        own_key = own_key * lax.rsqrt(jnp.mean(own_key * own_key, axis=-1, keepdims=True) + EPS)
        own_score = jnp.sum(wide * jnp.concatenate([own_key] * group, axis=0), axis=-1, keepdims=True) * scale
        own_weight = jnp.exp(own_score)
        num, den = share(query, phi, scale, near_ref, g, heads)
        num += own_weight.astype(jnp.bfloat16).astype(jnp.float32) * jnp.concatenate([own_value] * group, axis=0)
        query_ref[g] = query
        phi_ref[g] = phi
        num_ref[g] = num
        den_ref[g] = jnp.broadcast_to(den + own_weight, num.shape)
        scale_ref[g] = jnp.broadcast_to(scale, num.shape)


def end_kernel(each, query_ref, phi_ref, num_ref, den_ref, scale_ref, far_ref, *out_refs):
    heads, asked, _ = query_ref.shape
    block = out_refs[0].shape[0] // heads
    count = each * len(out_refs)
    for g in range(heads):
        num, den = share(query_ref[g], phi_ref[g], scale_ref[g][:, :1], far_ref, g, heads)
        result = (num_ref[g] + num) / (den_ref[g] + den)
        for k, out_ref in enumerate(out_refs):
            rows = [result[h * count + k * each : h * count + (k + 1) * each] for h in range(asked // count)]
            out_ref[g * block : (g + 1) * block, :] = jnp.concatenate(rows, axis=0).astype(jnp.bfloat16)


def begin(rows, weight, near):
    heads, head_size, feats = weight.shape
    count = rows.shape[0]
    group = (rows.shape[1] - 2 * heads * head_size) // (heads * head_size)
    shape = (heads, group * count, head_size)
    vmem = pl.BlockSpec(memory_space=pltpu.VMEM)
    return pl.pallas_call(
        begin_kernel,
        in_specs=[vmem] * 3,
        out_specs=[vmem] * 5,
        out_shape=[jax.ShapeDtypeStruct(shape, jnp.bfloat16)] * 2 + [jax.ShapeDtypeStruct(shape, jnp.float32)] * 3,
        compiler_params=pltpu.CompilerParams(vmem_limit_bytes=32 * 1024 * 1024),
        cost_estimate=pl.CostEstimate(
            flops=6 * count * rows.shape[1] * feats, bytes_accessed=4 * rows.size, transcendentals=2 * rows.size
        ),
        name="begin",
    )(rows, weight, near)


def end(started, far, count, width, parts):
    head_size = started[0].shape[2]
    vmem = pl.BlockSpec(memory_space=pltpu.VMEM)
    return pl.pallas_call(
        functools.partial(end_kernel, count),
        in_specs=[vmem] * 6,
        out_specs=[vmem] * parts,
        out_shape=[jax.ShapeDtypeStruct((count * width // head_size, head_size), jnp.bfloat16)] * parts,
        compiler_params=pltpu.CompilerParams(vmem_limit_bytes=32 * 1024 * 1024),
        cost_estimate=pl.CostEstimate(
            flops=4 * started[0].size * 128, bytes_accessed=4 * started[0].size, transcendentals=started[0].size
        ),
        name="end",
    )(*started, far)


def finish_kernel(prompts_ref, *refs):
    block_refs, out_ref = refs[:-1], refs[-1]
    each, width = out_ref.shape
    rows, head_size = block_refs[0].shape
    sects = len(block_refs)
    sect = lax.axis_index("sect")
    first = (sect * lax.axis_size("sub") + lax.axis_index("sub")) * each
    shape = (rows, prompts_ref.shape[1])
    row = first + lax.rem(lax.broadcasted_iota(jnp.int32, shape, 0), each)
    lane = lax.broadcasted_iota(jnp.int32, shape, 1)
    prompt = jnp.sum(jnp.where(lane == row, prompts_ref[...], 0), axis=1, keepdims=True)
    chosen = block_refs[0][...].astype(jnp.float32)
    for k, ref in zip(range(sects - 1, 0, -1), block_refs[1:]):
        source = partner(sect, k if paired(sects) else sects - k, sects)
        chosen = jnp.where(prompt == source, ref[...].astype(jnp.float32), chosen)
    for head in range(width // head_size):
        part = chosen[head * each : (head + 1) * each].astype(jnp.bfloat16)
        out_ref[:, head * head_size : (head + 1) * head_size] = part


def finish(row_prompt, blocks, shape):
    vmem = pl.BlockSpec(memory_space=pltpu.VMEM)
    return pl.pallas_call(
        finish_kernel,
        in_specs=[vmem] * (1 + len(blocks)),
        out_specs=vmem,
        out_shape=jax.ShapeDtypeStruct(shape, jnp.bfloat16),
        compiler_params=pltpu.CompilerParams(vmem_limit_bytes=8 * 1024 * 1024),
        name="finish",
    )(row_prompt.reshape(1, -1), *blocks)


def body(
    sects, prompt_keys, prompt_values, lengths, feature_weight, queries, new_keys, new_values, row_prompt
):
    sect = lax.axis_index("sect")
    steps = list(range(1, sects))
    steps[:2] = steps[:2][::-1]
    mine = pack(queries, new_keys, new_values)
    ask = shifted if sects == 4 else partner
    asked = {k: lax.ppermute(mine, "sect", [(ask(i, k, sects), i) for i in range(sects)]) for k in steps}
    if sects == 4:
        odd = (sect & 1) == 1
        asked[1], asked[3] = jnp.where(odd, asked[3], asked[1]), jnp.where(odd, asked[1], asked[3])
    blocks = [mine] + [asked[k] for k in steps]
    near = prefill(prompt_keys, prompt_values, feature_weight, lengths)
    far = lax.ppermute(near, "sub", [(0, 1), (1, 0)])
    started = begin(jnp.concatenate(blocks, axis=0), feature_weight, near)
    results = end(started, far, *queries.shape, sects)
    results = dict(zip([0] + steps, results))

    back = [
        lax.ppermute(results[k], "sect", [(i, partner(i, k, sects)) for i in range(sects)])
        for k in range(sects - 1, 0, -1)
    ]
    return finish(row_prompt, [results[0]] + back, queries.shape)


def solution(mesh):
    placed = (
        P(("parts", "sect"), "sub", "tp"),
        P(("parts", "sect"), "sub", "tp"),
        P(("parts", "sect")),
        P("tp", None, None),
        P(("parts", "sect", "sub"), "tp"),
        P(("parts", "sect", "sub"), "tp"),
        P(("parts", "sect", "sub"), "tp"),
        P("parts"),
    )
    return jax.shard_map(
        functools.partial(body, mesh.shape["sect"]),
        mesh=mesh,
        in_specs=placed,
        out_specs=P(("parts", "sect", "sub"), "tp"),
        check_vma=False,
    )
```

```python
import functools

import jax
import jax.numpy as jnp
from jax import lax
from jax.experimental import pallas as pl
from jax.experimental.pallas import tpu as pltpu
from jax.sharding import PartitionSpec as P

WINDOW = 64
TAU = 10.0
EPS = 1e-06
BLOCK = 256
NT = (((1,), (1,)), ((), ()))


def paired(sects):
    return sects & (sects - 1) == 0


def shifted(sect, k, sects):
    return (sect + k) % sects


def partner(sect, k, sects):
    return sect ^ k if paired(sects) else shifted(sect, k, sects)


def feature(proj):
    return jnp.maximum(proj, 0.0) + jnp.exp(jnp.minimum(proj, 0.0))


def pack_kernel(queries_ref, keys_ref, values_ref, out_ref, sems):
    copies, at = [], 0
    for i, ref in enumerate((queries_ref, keys_ref, values_ref)):
        size = ref.shape[1]
        copies.append(pltpu.make_async_copy(ref, out_ref.at[:, at : at + size], sems.at[i]))
        copies[-1].start()
        at += size
    for copy in copies:
        copy.wait()


def pack(queries, new_keys, new_values):
    width = queries.shape[1] + 2 * new_keys.shape[1]
    arrays = [pltpu.with_memory_space_constraint(x, pltpu.MemorySpace.HBM) for x in (queries, new_keys, new_values)]
    return pl.pallas_call(
        pack_kernel,
        in_specs=[pl.BlockSpec(memory_space=pltpu.MemorySpace.HBM)] * 3,
        out_specs=pl.BlockSpec(memory_space=pltpu.VMEM),
        out_shape=jax.ShapeDtypeStruct((queries.shape[0], width), jnp.bfloat16),
        scratch_shapes=[pltpu.SemaphoreType.DMA((3,))],
        compiler_params=pltpu.CompilerParams(vmem_limit_bytes=8 * 1024 * 1024),
        cost_estimate=pl.CostEstimate(flops=10**10, bytes_accessed=2**25, transcendentals=0),
        name="pack",
    )(*arrays)


SLAB = WINDOW + 16
MASK_ROW = 8


def prefill_kernel(
    lengths_ref, keys_ref, values_ref, weight_ref, out_ref,
    wide_ref, proj_ref, state_ref, norm_ref,
    slab_sem,
):
    heads, head_size, feats = weight_ref.shape
    pairs = heads // 2
    span = keys_ref.shape[1]
    keys_at, values_at = keys_ref.at[0], values_ref.at[0]
    chunks = span // BLOCK
    state_ref[...] = jnp.zeros_like(state_ref)
    norm_ref[...] = jnp.zeros_like(norm_ref)
    wide_ref[...] = jnp.zeros_like(wide_ref)
    for g in range(heads):
        half = g % 2
        turned = weight_ref[g].astype(jnp.float32).T.astype(jnp.bfloat16)
        wide_ref[g // 2, half * feats : (half + 1) * feats, half * head_size : (half + 1) * head_size] = turned

    begin = lengths_ref[0] - WINDOW - lax.axis_index("sub") * span
    first = jnp.clip(begin, 0, span - SLAB)
    first = pl.multiple_of(first - lax.rem(first, 16), 16)
    slabs = []
    for i, source in enumerate((keys_ref, values_ref)):
        for g in range(heads):
            at = heads * feats + 16 + (i * heads + g) * SLAB
            slabs.append(
                pltpu.make_async_copy(
                    source.at[0, pl.ds(first, SLAB), g * head_size : (g + 1) * head_size],
                    out_ref.at[at : at + SLAB, :],
                    slab_sem.at[i, g],
                )
            )
            slabs[-1].start()

    def project(c):
        for j in range(pairs):
            proj = lax.dot_general(
                wide_ref[j],
                keys_at[c * BLOCK : (c + 1) * BLOCK, j * 2 * head_size : (j + 1) * 2 * head_size],
                NT,
                preferred_element_type=jnp.float32,
            )
            proj_ref[c % 2, j] = proj.astype(jnp.bfloat16)

    def collect(c):
        position = c * BLOCK + lax.broadcasted_iota(jnp.int32, (1, BLOCK), 1)
        live = jnp.where(position < begin, 1.0, 0.0).astype(jnp.bfloat16)
        for j in range(pairs):
            mapped = feature(proj_ref[c % 2, j]) * live
            some = [mapped[:, k * 128 : (k + 1) * 128] for k in range(BLOCK // 128)]
            while len(some) > 1:
                some = [x + y for x, y in zip(some[::2], some[1::2])]
            norm_ref[j] += some[0].astype(jnp.float32)
            state_ref[j] += jnp.dot(
                mapped,
                values_at[c * BLOCK : (c + 1) * BLOCK, j * 2 * head_size : (j + 1) * 2 * head_size],
                preferred_element_type=jnp.float32,
            )

    project(0)
    for c in range(chunks):
        if c + 1 < chunks:
            project(c + 1)
        collect(c)

    tile = []
    for g in range(heads):
        half = g % 2
        part = state_ref[g // 2, half * feats : (half + 1) * feats, half * head_size : (half + 1) * head_size]
        out_ref[g * feats : (g + 1) * feats, :] = part.astype(jnp.bfloat16)
        sums = norm_ref[g // 2, half * feats : (half + 1) * feats, :]
        tile.append(jnp.sum(sums.T, axis=0, keepdims=True))
    slot = first + lax.broadcasted_iota(jnp.int32, (1, head_size), 1)
    tile.append(jnp.zeros((MASK_ROW - heads, head_size), jnp.float32))
    tile.append(jnp.where((slot >= begin) & (slot < begin + WINDOW), 1.0, 0.0))
    tile.append(jnp.zeros((15 - MASK_ROW, head_size), jnp.float32))
    out_ref[heads * feats : heads * feats + 16, :] = jnp.concatenate(tile, axis=0).astype(jnp.bfloat16)
    for slab in slabs:
        slab.wait()


def prefill(keys, values, weight, lengths):
    heads, head_size, feats = weight.shape
    span, width = keys.shape[1:]
    vmem = pl.BlockSpec(memory_space=pltpu.VMEM)
    return pl.pallas_call(
        prefill_kernel,
        in_specs=[pl.BlockSpec(memory_space=pltpu.SMEM), vmem, vmem, vmem],
        out_specs=vmem,
        out_shape=jax.ShapeDtypeStruct((heads * feats + 16 + 2 * heads * SLAB, head_size), jnp.bfloat16),
        scratch_shapes=[
            pltpu.VMEM((heads // 2, 2 * feats, 2 * head_size), jnp.bfloat16),
            pltpu.VMEM((2, heads // 2, 2 * feats, BLOCK), jnp.bfloat16),
            pltpu.VMEM((heads // 2, 2 * feats, 2 * head_size), jnp.float32),
            pltpu.VMEM((heads // 2, 2 * feats, 128), jnp.float32),
            pltpu.SemaphoreType.DMA((2, heads)),
        ],
        compiler_params=pltpu.CompilerParams(vmem_limit_bytes=16 * 1024 * 1024),
        cost_estimate=pl.CostEstimate(
            flops=4 * span * width * feats, bytes_accessed=4 * span * width, transcendentals=span * width
        ),
        name="prefill",
    )(
        lengths,
        pltpu.with_memory_space_constraint(keys, pltpu.MemorySpace.VMEM),
        pltpu.with_memory_space_constraint(values, pltpu.MemorySpace.VMEM),
        pltpu.with_memory_space_constraint(weight, pltpu.MemorySpace.VMEM),
    )


def share(query, phi, scale, ref, g, heads):
    head_size = query.shape[1]
    feats = phi.shape[1]
    tile_at = heads * feats
    tile = ref[tile_at : tile_at + 16, :].astype(jnp.float32)
    linear = jnp.dot(phi, ref[g * feats : (g + 1) * feats, :], preferred_element_type=jnp.float32)
    at = tile_at + 16 + g * SLAB
    keys = ref[at : at + SLAB, :]
    at += heads * SLAB
    values = ref[at : at + SLAB, :]
    keys_wide = keys.astype(jnp.float32)
    key_scale = lax.rsqrt(jnp.mean((keys_wide * keys_wide).T, axis=0, keepdims=True) + EPS)
    score = lax.dot_general(query, keys, NT, preferred_element_type=jnp.float32) * scale * key_scale
    weights = jnp.exp(score) * tile[MASK_ROW : MASK_ROW + 1, :SLAB]
    back = 1.0 / (feats * feats)
    num = linear * back + jnp.dot(weights.astype(jnp.bfloat16), values, preferred_element_type=jnp.float32)
    den = jnp.sum(weights, axis=-1, keepdims=True)
    return num, den + jnp.sum(phi.astype(jnp.float32) * tile[g : g + 1], axis=-1, keepdims=True) * back


def begin_kernel(rows_ref, weight_ref, near_ref, query_ref, phi_ref, num_ref, den_ref, scale_ref):
    heads, head_size, feats = weight_ref.shape
    group = (rows_ref.shape[1] - 2 * heads * head_size) // (heads * head_size)
    keys_at = heads * group * head_size
    values_at = keys_at + heads * head_size
    ready = []
    for g in range(heads):
        query = jnp.concatenate(
            [
                rows_ref[:, (g * group + h) * head_size : (g * group + h + 1) * head_size]
                for h in range(group)
            ],
            axis=0,
        )
        wide = query.astype(jnp.float32)
        phi = feature(jnp.dot(query, weight_ref[g], preferred_element_type=jnp.float32)).astype(jnp.bfloat16)
        scale = (TAU / head_size) * lax.rsqrt(jnp.mean(wide * wide, axis=-1, keepdims=True) + EPS)
        own_key = rows_ref[:, keys_at + g * head_size : keys_at + (g + 1) * head_size].astype(jnp.float32)
        own_value = rows_ref[:, values_at + g * head_size : values_at + (g + 1) * head_size].astype(jnp.float32)
        own_key = own_key * lax.rsqrt(jnp.mean(own_key * own_key, axis=-1, keepdims=True) + EPS)
        own_score = jnp.sum(wide * jnp.concatenate([own_key] * group, axis=0), axis=-1, keepdims=True) * scale
        own_weight = jnp.exp(own_score)
        num, den = share(query, phi, scale, near_ref, g, heads)
        num += own_weight.astype(jnp.bfloat16).astype(jnp.float32) * jnp.concatenate([own_value] * group, axis=0)
        ready.append((query, phi, num, den + own_weight, scale))
    for g, (query, phi, num, den, scale) in enumerate(ready):
        query_ref[g] = query
        phi_ref[g] = phi
        num_ref[g] = num
        den_ref[g] = jnp.broadcast_to(den, num.shape)
        scale_ref[g] = jnp.broadcast_to(scale, num.shape)


def end_kernel(query_ref, phi_ref, num_ref, den_ref, scale_ref, far_ref, *out_refs):
    heads, asked, head_size = query_ref.shape
    each, width = out_refs[0].shape
    group = width // (heads * head_size)
    count = asked // group
    ready = []
    for g in range(heads):
        num, den = share(query_ref[g], phi_ref[g], scale_ref[g][:, :1], far_ref, g, heads)
        ready.append(((num_ref[g] + num) / (den_ref[g] + den)).astype(jnp.bfloat16))
    for g, result in enumerate(ready):
        for h in range(group):
            at = (g * group + h) * head_size
            for k, out_ref in enumerate(out_refs):
                start = h * count + k * each
                out_ref[:, at : at + head_size] = result[start : start + each]


def begin(rows, weight, near):
    heads, head_size, feats = weight.shape
    count = rows.shape[0]
    group = (rows.shape[1] - 2 * heads * head_size) // (heads * head_size)
    shape = (heads, group * count, head_size)
    vmem = pl.BlockSpec(memory_space=pltpu.VMEM)
    return pl.pallas_call(
        begin_kernel,
        in_specs=[vmem] * 3,
        out_specs=[vmem] * 5,
        out_shape=[jax.ShapeDtypeStruct(shape, jnp.bfloat16)] * 2 + [jax.ShapeDtypeStruct(shape, jnp.float32)] * 3,
        compiler_params=pltpu.CompilerParams(vmem_limit_bytes=32 * 1024 * 1024),
        cost_estimate=pl.CostEstimate(
            flops=6 * count * rows.shape[1] * feats, bytes_accessed=4 * rows.size, transcendentals=2 * rows.size
        ),
        name="begin",
    )(rows, weight, near)


def end(started, far, count, width, parts):
    vmem = pl.BlockSpec(memory_space=pltpu.VMEM)
    return pl.pallas_call(
        end_kernel,
        in_specs=[vmem] * 6,
        out_specs=[vmem] * parts,
        out_shape=[jax.ShapeDtypeStruct((count, width), jnp.bfloat16)] * parts,
        compiler_params=pltpu.CompilerParams(vmem_limit_bytes=32 * 1024 * 1024),
        cost_estimate=pl.CostEstimate(
            flops=4 * started[0].size * 128, bytes_accessed=4 * started[0].size, transcendentals=started[0].size
        ),
        name="end",
    )(*started, far)


def body(
    sects, prompt_keys, prompt_values, lengths, feature_weight, queries, new_keys, new_values, row_prompt
):
    sub = lax.axis_index("sub")
    sect = lax.axis_index("sect")
    steps = list(range(1, sects))
    steps[:2] = steps[:2][::-1]
    mine = pack(queries, new_keys, new_values)
    ask = shifted if sects == 4 else partner
    asked = {k: lax.ppermute(mine, "sect", [(ask(i, k, sects), i) for i in range(sects)]) for k in steps}
    if sects == 4:
        odd = (sect & 1) == 1
        asked[1], asked[3] = jnp.where(odd, asked[3], asked[1]), jnp.where(odd, asked[1], asked[3])
    blocks = [mine] + [asked[k] for k in steps]
    near = prefill(prompt_keys, prompt_values, feature_weight, lengths)
    far = lax.ppermute(near, "sub", [(0, 1), (1, 0)])
    started = begin(jnp.concatenate(blocks, axis=0), feature_weight, near)
    results = end(started, far, *queries.shape, sects)
    results = dict(zip([0] + steps, results))

    count = queries.shape[0]
    first_row = (sect * lax.axis_size("sub") + sub) * count
    prompts = lax.dynamic_slice_in_dim(row_prompt, first_row, count, 0)
    out = results[0]
    for k in range(1, sects):
        result = lax.ppermute(results[k], "sect", [(i, partner(i, k, sects)) for i in range(sects)])
        source = partner(sect, k if paired(sects) else sects - k, sects)
        out = jnp.where((prompts == source)[:, None], result, out)
    return out


def solution(mesh):
    placed = (
        P(("parts", "sect"), "sub", "tp"),
        P(("parts", "sect"), "sub", "tp"),
        P(("parts", "sect")),
        P("tp", None, None),
        P(("parts", "sect", "sub"), "tp"),
        P(("parts", "sect", "sub"), "tp"),
        P(("parts", "sect", "sub"), "tp"),
        P("parts"),
    )
    return jax.shard_map(
        functools.partial(body, mesh.shape["sect"]),
        mesh=mesh,
        in_specs=placed,
        out_specs=P(("parts", "sect", "sub"), "tp"),
        check_vma=False,
    )
```

```python
import functools

import jax
import jax.numpy as jnp
from jax import lax
from jax.experimental import pallas as pl
from jax.experimental.pallas import tpu as pltpu
from jax.sharding import PartitionSpec as P

WINDOW = 64
TAU = 10.0
EPS = 1e-06
BLOCK = 256
NT = (((1,), (1,)), ((), ()))


def paired(sects):
    return sects & (sects - 1) == 0


def shifted(sect, k, sects):
    return (sect + k) % sects


def partner(sect, k, sects):
    return sect ^ k if paired(sects) else shifted(sect, k, sects)


def feature(proj):
    return jnp.maximum(proj, 0.0) + jnp.exp(jnp.minimum(proj, 0.0))


def pack_kernel(queries_ref, keys_ref, values_ref, out_ref, sems):
    copies, at = [], 0
    for i, ref in enumerate((queries_ref, keys_ref, values_ref)):
        size = ref.shape[1]
        copies.append(pltpu.make_async_copy(ref, out_ref.at[:, at : at + size], sems.at[i]))
        copies[-1].start()
        at += size
    for copy in copies:
        copy.wait()


def pack(queries, new_keys, new_values):
    width = queries.shape[1] + 2 * new_keys.shape[1]
    arrays = [pltpu.with_memory_space_constraint(x, pltpu.MemorySpace.HBM) for x in (queries, new_keys, new_values)]
    return pl.pallas_call(
        pack_kernel,
        in_specs=[pl.BlockSpec(memory_space=pltpu.MemorySpace.HBM)] * 3,
        out_specs=pl.BlockSpec(memory_space=pltpu.VMEM),
        out_shape=jax.ShapeDtypeStruct((queries.shape[0], width), jnp.bfloat16),
        scratch_shapes=[pltpu.SemaphoreType.DMA((3,))],
        compiler_params=pltpu.CompilerParams(vmem_limit_bytes=8 * 1024 * 1024),
        cost_estimate=pl.CostEstimate(flops=10**10, bytes_accessed=2**25, transcendentals=0),
        name="pack",
    )(*arrays)


SLAB = WINDOW + 16
MASK_ROW = 8


def prefill_kernel(
    lengths_ref, keys_ref, values_ref, weight_ref, out_ref,
    wide_ref, proj_ref, state_ref, norm_ref,
    slab_sem,
):
    heads, head_size, feats = weight_ref.shape
    pairs = heads // 2
    span = keys_ref.shape[1]
    keys_at, values_at = keys_ref.at[0], values_ref.at[0]
    chunks = span // BLOCK
    state_ref[...] = jnp.zeros_like(state_ref)
    norm_ref[...] = jnp.zeros_like(norm_ref)
    wide_ref[...] = jnp.zeros_like(wide_ref)
    for g in range(heads):
        half = g % 2
        turned = weight_ref[g].astype(jnp.float32).T.astype(jnp.bfloat16)
        wide_ref[g // 2, half * feats : (half + 1) * feats, half * head_size : (half + 1) * head_size] = turned

    begin = lengths_ref[0] - WINDOW - lax.axis_index("sub") * span
    first = jnp.clip(begin, 0, span - SLAB)
    first = pl.multiple_of(first - lax.rem(first, 16), 16)
    slabs = []
    for i, source in enumerate((keys_ref, values_ref)):
        for g in range(heads):
            at = heads * feats + 16 + (i * heads + g) * SLAB
            slabs.append(
                pltpu.make_async_copy(
                    source.at[0, pl.ds(first, SLAB), g * head_size : (g + 1) * head_size],
                    out_ref.at[at : at + SLAB, :],
                    slab_sem.at[i, g],
                )
            )
            slabs[-1].start()

    def project(c):
        for j in range(pairs):
            proj = lax.dot_general(
                wide_ref[j],
                keys_at[c * BLOCK : (c + 1) * BLOCK, j * 2 * head_size : (j + 1) * 2 * head_size],
                NT,
                preferred_element_type=jnp.float32,
            )
            proj_ref[c % 2, j] = proj.astype(jnp.bfloat16)

    def collect(c):
        position = c * BLOCK + lax.broadcasted_iota(jnp.int32, (1, BLOCK), 1)
        live = jnp.where(position < begin, 1.0, 0.0).astype(jnp.bfloat16)
        for j in range(pairs):
            mapped = feature(proj_ref[c % 2, j]) * live
            some = [mapped[:, k * 128 : (k + 1) * 128] for k in range(BLOCK // 128)]
            while len(some) > 1:
                some = [x + y for x, y in zip(some[::2], some[1::2])]
            norm_ref[j] += some[0].astype(jnp.float32)
            state_ref[j] += jnp.dot(
                mapped,
                values_at[c * BLOCK : (c + 1) * BLOCK, j * 2 * head_size : (j + 1) * 2 * head_size],
                preferred_element_type=jnp.float32,
            )

    project(0)
    for c in range(chunks):
        if c + 1 < chunks:
            project(c + 1)
        collect(c)

    tile = []
    for g in range(heads):
        half = g % 2
        part = state_ref[g // 2, half * feats : (half + 1) * feats, half * head_size : (half + 1) * head_size]
        out_ref[g * feats : (g + 1) * feats, :] = part.astype(jnp.bfloat16)
        sums = norm_ref[g // 2, half * feats : (half + 1) * feats, :]
        tile.append(jnp.sum(sums.T, axis=0, keepdims=True))
    slot = first + lax.broadcasted_iota(jnp.int32, (1, head_size), 1)
    tile.append(jnp.zeros((MASK_ROW - heads, head_size), jnp.float32))
    tile.append(jnp.where((slot >= begin) & (slot < begin + WINDOW), 1.0, 0.0))
    tile.append(jnp.zeros((15 - MASK_ROW, head_size), jnp.float32))
    out_ref[heads * feats : heads * feats + 16, :] = jnp.concatenate(tile, axis=0).astype(jnp.bfloat16)
    for slab in slabs:
        slab.wait()


def prefill(keys, values, weight, lengths):
    heads, head_size, feats = weight.shape
    span, width = keys.shape[1:]
    vmem = pl.BlockSpec(memory_space=pltpu.VMEM)
    return pl.pallas_call(
        prefill_kernel,
        in_specs=[pl.BlockSpec(memory_space=pltpu.SMEM), vmem, vmem, vmem],
        out_specs=vmem,
        out_shape=jax.ShapeDtypeStruct((heads * feats + 16 + 2 * heads * SLAB, head_size), jnp.bfloat16),
        scratch_shapes=[
            pltpu.VMEM((heads // 2, 2 * feats, 2 * head_size), jnp.bfloat16),
            pltpu.VMEM((2, heads // 2, 2 * feats, BLOCK), jnp.bfloat16),
            pltpu.VMEM((heads // 2, 2 * feats, 2 * head_size), jnp.float32),
            pltpu.VMEM((heads // 2, 2 * feats, 128), jnp.float32),
            pltpu.SemaphoreType.DMA((2, heads)),
        ],
        compiler_params=pltpu.CompilerParams(vmem_limit_bytes=16 * 1024 * 1024),
        cost_estimate=pl.CostEstimate(
            flops=4 * span * width * feats, bytes_accessed=4 * span * width, transcendentals=span * width
        ),
        name="prefill",
    )(
        lengths,
        pltpu.with_memory_space_constraint(keys, pltpu.MemorySpace.VMEM),
        pltpu.with_memory_space_constraint(values, pltpu.MemorySpace.VMEM),
        pltpu.with_memory_space_constraint(weight, pltpu.MemorySpace.VMEM),
    )


def halves(wide):
    high = wide.astype(jnp.bfloat16)
    return high, (wide - high.astype(jnp.float32)).astype(jnp.bfloat16)


def share(query, phi, scale, ref, g, heads):
    head_size = query.shape[1]
    feats = phi.shape[1]
    tile_at = heads * feats
    tile = ref[tile_at : tile_at + 16, :].astype(jnp.float32)
    linear = jnp.dot(phi, ref[g * feats : (g + 1) * feats, :], preferred_element_type=jnp.float32)
    norms = jnp.broadcast_to(tile[g : g + 1], (head_size, feats)).astype(jnp.bfloat16)
    linear_den = lax.dot_general(phi, norms, NT, preferred_element_type=jnp.float32)
    at = tile_at + 16 + g * SLAB
    keys = ref[at : at + SLAB, :]
    at += heads * SLAB
    values = ref[at : at + SLAB, :]
    keys_wide = keys.astype(jnp.float32)
    ones = jnp.ones((16, head_size), jnp.bfloat16)
    squares = [
        lax.dot_general(ones, part, NT, preferred_element_type=jnp.float32) for part in halves(keys_wide * keys_wide)
    ]
    key_scale = lax.rsqrt((squares[0] + squares[1])[:1] * (1.0 / head_size) + EPS)
    score = lax.dot_general(query, keys, NT, preferred_element_type=jnp.float32) * scale[:, :SLAB] * key_scale
    weights = (jnp.exp(score) * tile[MASK_ROW : MASK_ROW + 1, :SLAB]).astype(jnp.bfloat16)
    back = 1.0 / (feats * feats)
    num = linear * back + jnp.dot(weights, values, preferred_element_type=jnp.float32)
    ones = jnp.ones((SLAB, head_size), jnp.bfloat16)
    return num, linear_den * back + jnp.dot(weights, ones, preferred_element_type=jnp.float32)


def begin_kernel(rows_ref, weight_ref, near_ref, query_ref, phi_ref, num_ref, den_ref, scale_ref):
    heads, head_size, feats = weight_ref.shape
    group = (rows_ref.shape[1] - 2 * heads * head_size) // (heads * head_size)
    keys_at = heads * group * head_size
    values_at = keys_at + heads * head_size
    ready = []
    for g in range(heads):
        query = jnp.concatenate(
            [
                rows_ref[:, (g * group + h) * head_size : (g * group + h + 1) * head_size]
                for h in range(group)
            ],
            axis=0,
        )
        wide = query.astype(jnp.float32)
        phi = feature(jnp.dot(query, weight_ref[g], preferred_element_type=jnp.float32)).astype(jnp.bfloat16)
        scale = (TAU / head_size) * lax.rsqrt(jnp.mean(wide * wide, axis=-1, keepdims=True) + EPS)
        own_key = rows_ref[:, keys_at + g * head_size : keys_at + (g + 1) * head_size].astype(jnp.float32)
        own_value = rows_ref[:, values_at + g * head_size : values_at + (g + 1) * head_size].astype(jnp.float32)
        own_key = own_key * lax.rsqrt(jnp.mean(own_key * own_key, axis=-1, keepdims=True) + EPS)
        own_score = jnp.sum(wide * jnp.concatenate([own_key] * group, axis=0), axis=-1, keepdims=True) * scale
        own_weight = jnp.exp(own_score)
        scale = jnp.broadcast_to(scale, query.shape)
        num, den = share(query, phi, scale, near_ref, g, heads)
        num += own_weight.astype(jnp.bfloat16).astype(jnp.float32) * jnp.concatenate([own_value] * group, axis=0)
        ready.append((query, phi, num, den + own_weight, scale))
    for g, (query, phi, num, den, scale) in enumerate(ready):
        query_ref[g] = query
        phi_ref[g] = phi
        num_ref[g] = num
        den_ref[g] = den
        scale_ref[g] = scale


def end_kernel(query_ref, phi_ref, num_ref, den_ref, scale_ref, far_ref, *out_refs):
    heads, asked, head_size = query_ref.shape
    each, width = out_refs[0].shape
    group = width // (heads * head_size)
    count = asked // group
    ready = []
    for g in range(heads):
        num, den = share(query_ref[g], phi_ref[g], scale_ref[g], far_ref, g, heads)
        ready.append(((num_ref[g] + num) / (den_ref[g] + den)).astype(jnp.bfloat16))
    for g, result in enumerate(ready):
        for h in range(group):
            at = (g * group + h) * head_size
            for k, out_ref in enumerate(out_refs):
                start = h * count + k * each
                out_ref[:, at : at + head_size] = result[start : start + each]


def begin(rows, weight, near):
    heads, head_size, feats = weight.shape
    count = rows.shape[0]
    group = (rows.shape[1] - 2 * heads * head_size) // (heads * head_size)
    shape = (heads, group * count, head_size)
    vmem = pl.BlockSpec(memory_space=pltpu.VMEM)
    return pl.pallas_call(
        begin_kernel,
        in_specs=[vmem] * 3,
        out_specs=[vmem] * 5,
        out_shape=[jax.ShapeDtypeStruct(shape, jnp.bfloat16)] * 2 + [jax.ShapeDtypeStruct(shape, jnp.float32)] * 3,
        compiler_params=pltpu.CompilerParams(vmem_limit_bytes=32 * 1024 * 1024),
        cost_estimate=pl.CostEstimate(
            flops=6 * count * rows.shape[1] * feats, bytes_accessed=4 * rows.size, transcendentals=2 * rows.size
        ),
        name="begin",
    )(rows, weight, near)


def end(started, far, count, width, parts):
    vmem = pl.BlockSpec(memory_space=pltpu.VMEM)
    return pl.pallas_call(
        end_kernel,
        in_specs=[vmem] * 6,
        out_specs=[vmem] * parts,
        out_shape=[jax.ShapeDtypeStruct((count, width), jnp.bfloat16)] * parts,
        compiler_params=pltpu.CompilerParams(vmem_limit_bytes=32 * 1024 * 1024),
        cost_estimate=pl.CostEstimate(
            flops=4 * started[0].size * 128, bytes_accessed=4 * started[0].size, transcendentals=started[0].size
        ),
        name="end",
    )(*started, far)


def body(
    sects, prompt_keys, prompt_values, lengths, feature_weight, queries, new_keys, new_values, row_prompt
):
    sub = lax.axis_index("sub")
    sect = lax.axis_index("sect")
    steps = list(range(1, sects))
    steps[:2] = steps[:2][::-1]
    mine = pack(queries, new_keys, new_values)
    ask = shifted if sects == 4 else partner
    asked = {k: lax.ppermute(mine, "sect", [(ask(i, k, sects), i) for i in range(sects)]) for k in steps}
    if sects == 4:
        odd = (sect & 1) == 1
        asked[1], asked[3] = jnp.where(odd, asked[3], asked[1]), jnp.where(odd, asked[1], asked[3])
    blocks = [mine] + [asked[k] for k in steps]
    near = prefill(prompt_keys, prompt_values, feature_weight, lengths)
    far = lax.ppermute(near, "sub", [(0, 1), (1, 0)])
    started = begin(jnp.concatenate(blocks, axis=0), feature_weight, near)
    results = end(started, far, *queries.shape, sects)
    results = dict(zip([0] + steps, results))

    count = queries.shape[0]
    first_row = (sect * lax.axis_size("sub") + sub) * count
    prompts = lax.dynamic_slice_in_dim(row_prompt, first_row, count, 0)
    out = results[0]
    for k in range(1, sects):
        result = lax.ppermute(results[k], "sect", [(i, partner(i, k, sects)) for i in range(sects)])
        source = partner(sect, k if paired(sects) else sects - k, sects)
        out = jnp.where((prompts == source)[:, None], result, out)
    return out


def solution(mesh):
    placed = (
        P(("parts", "sect"), "sub", "tp"),
        P(("parts", "sect"), "sub", "tp"),
        P(("parts", "sect")),
        P("tp", None, None),
        P(("parts", "sect", "sub"), "tp"),
        P(("parts", "sect", "sub"), "tp"),
        P(("parts", "sect", "sub"), "tp"),
        P("parts"),
    )
    return jax.shard_map(
        functools.partial(body, mesh.shape["sect"]),
        mesh=mesh,
        in_specs=placed,
        out_specs=P(("parts", "sect", "sub"), "tp"),
        check_vma=False,
    )
```

```python
import functools

import jax
import jax.numpy as jnp
from jax import lax
from jax.experimental import pallas as pl
from jax.experimental.pallas import tpu as pltpu
from jax.sharding import PartitionSpec as P

WINDOW = 64
TAU = 10.0
EPS = 1e-06
BLOCK = 256
NT = (((1,), (1,)), ((), ()))


def paired(sects):
    return sects & (sects - 1) == 0


def shifted(sect, k, sects):
    return (sect + k) % sects


def partner(sect, k, sects):
    return sect ^ k if paired(sects) else shifted(sect, k, sects)


def feature(proj):
    return jnp.maximum(proj, 0.0) + jnp.exp(jnp.minimum(proj, 0.0))


def pack_kernel(queries_ref, keys_ref, values_ref, out_ref, sems):
    copies, at = [], 0
    for i, ref in enumerate((queries_ref, keys_ref, values_ref)):
        size = ref.shape[1]
        copies.append(pltpu.make_async_copy(ref, out_ref.at[:, at : at + size], sems.at[i]))
        copies[-1].start()
        at += size
    for copy in copies:
        copy.wait()


def pack(queries, new_keys, new_values):
    width = queries.shape[1] + 2 * new_keys.shape[1]
    arrays = [pltpu.with_memory_space_constraint(x, pltpu.MemorySpace.HBM) for x in (queries, new_keys, new_values)]
    return pl.pallas_call(
        pack_kernel,
        in_specs=[pl.BlockSpec(memory_space=pltpu.MemorySpace.HBM)] * 3,
        out_specs=pl.BlockSpec(memory_space=pltpu.VMEM),
        out_shape=jax.ShapeDtypeStruct((queries.shape[0], width), jnp.bfloat16),
        scratch_shapes=[pltpu.SemaphoreType.DMA((3,))],
        compiler_params=pltpu.CompilerParams(vmem_limit_bytes=8 * 1024 * 1024),
        cost_estimate=pl.CostEstimate(flops=10**10, bytes_accessed=2**25, transcendentals=0),
        name="pack",
    )(*arrays)


SLAB = WINDOW + 16
MASK_ROW = 8


def prefill_kernel(
    lengths_ref, keys_ref, values_ref, weight_ref, out_ref,
    wide_ref, proj_ref, state_ref, norm_ref,
    slab_sem,
):
    heads, head_size, feats = weight_ref.shape
    pairs = heads // 2
    span = keys_ref.shape[1]
    keys_at, values_at = keys_ref.at[0], values_ref.at[0]
    chunks = span // BLOCK
    state_ref[...] = jnp.zeros_like(state_ref)
    norm_ref[...] = jnp.zeros_like(norm_ref)
    wide_ref[...] = jnp.zeros_like(wide_ref)
    for g in range(heads):
        half = g % 2
        turned = weight_ref[g].astype(jnp.float32).T.astype(jnp.bfloat16)
        wide_ref[g // 2, half * feats : (half + 1) * feats, half * head_size : (half + 1) * head_size] = turned

    begin = lengths_ref[0] - WINDOW - lax.axis_index("sub") * span
    first = jnp.clip(begin, 0, span - SLAB)
    first = pl.multiple_of(first - lax.rem(first, 16), 16)
    part = feats + SLAB
    slabs = []
    for i, source in enumerate((keys_ref, values_ref)):
        for g in range(heads):
            at = g * part + feats if i else heads * part + 16 + g * SLAB
            slabs.append(
                pltpu.make_async_copy(
                    source.at[0, pl.ds(first, SLAB), g * head_size : (g + 1) * head_size],
                    out_ref.at[at : at + SLAB, :],
                    slab_sem.at[i, g],
                )
            )
            slabs[-1].start()

    def project(c):
        for j in range(pairs):
            proj = lax.dot_general(
                wide_ref[j],
                keys_at[c * BLOCK : (c + 1) * BLOCK, j * 2 * head_size : (j + 1) * 2 * head_size],
                NT,
                preferred_element_type=jnp.float32,
            )
            proj_ref[c % 2, j] = proj.astype(jnp.bfloat16)

    def collect(c):
        position = c * BLOCK + lax.broadcasted_iota(jnp.int32, (1, BLOCK), 1)
        live = jnp.where(position < begin, 1.0, 0.0).astype(jnp.bfloat16)
        for j in range(pairs):
            mapped = feature(proj_ref[c % 2, j]) * live
            some = [mapped[:, k * 128 : (k + 1) * 128] for k in range(BLOCK // 128)]
            while len(some) > 1:
                some = [x + y for x, y in zip(some[::2], some[1::2])]
            norm_ref[j] += some[0].astype(jnp.float32)
            state_ref[j] += jnp.dot(
                mapped,
                values_at[c * BLOCK : (c + 1) * BLOCK, j * 2 * head_size : (j + 1) * 2 * head_size],
                preferred_element_type=jnp.float32,
            )

    project(0)
    for c in range(chunks):
        if c + 1 < chunks:
            project(c + 1)
        collect(c)

    back = 1.0 / (feats * feats)
    tile = []
    for g in range(heads):
        half = g % 2
        state = state_ref[g // 2, half * feats : (half + 1) * feats, half * head_size : (half + 1) * head_size]
        out_ref[g * part : g * part + feats, :] = (state * back).astype(jnp.bfloat16)
        sums = norm_ref[g // 2, half * feats : (half + 1) * feats, :]
        tile.append(jnp.sum(sums.T, axis=0, keepdims=True) * back)
    slot = first + lax.broadcasted_iota(jnp.int32, (1, head_size), 1)
    tile.append(jnp.zeros((MASK_ROW - heads, head_size), jnp.float32))
    tile.append(jnp.where((slot >= begin) & (slot < begin + WINDOW), 1.0, 0.0))
    tile.append(jnp.zeros((15 - MASK_ROW, head_size), jnp.float32))
    out_ref[heads * part : heads * part + 16, :] = jnp.concatenate(tile, axis=0).astype(jnp.bfloat16)
    for slab in slabs:
        slab.wait()


def prefill(keys, values, weight, lengths):
    heads, head_size, feats = weight.shape
    span, width = keys.shape[1:]
    vmem = pl.BlockSpec(memory_space=pltpu.VMEM)
    return pl.pallas_call(
        prefill_kernel,
        in_specs=[pl.BlockSpec(memory_space=pltpu.SMEM), vmem, vmem, vmem],
        out_specs=vmem,
        out_shape=jax.ShapeDtypeStruct((heads * feats + 16 + 2 * heads * SLAB, head_size), jnp.bfloat16),
        scratch_shapes=[
            pltpu.VMEM((heads // 2, 2 * feats, 2 * head_size), jnp.bfloat16),
            pltpu.VMEM((2, heads // 2, 2 * feats, BLOCK), jnp.bfloat16),
            pltpu.VMEM((heads // 2, 2 * feats, 2 * head_size), jnp.float32),
            pltpu.VMEM((heads // 2, 2 * feats, 128), jnp.float32),
            pltpu.SemaphoreType.DMA((2, heads)),
        ],
        compiler_params=pltpu.CompilerParams(vmem_limit_bytes=16 * 1024 * 1024),
        cost_estimate=pl.CostEstimate(
            flops=4 * span * width * feats, bytes_accessed=4 * span * width, transcendentals=span * width
        ),
        name="prefill",
    )(
        lengths,
        pltpu.with_memory_space_constraint(keys, pltpu.MemorySpace.VMEM),
        pltpu.with_memory_space_constraint(values, pltpu.MemorySpace.VMEM),
        pltpu.with_memory_space_constraint(weight, pltpu.MemorySpace.VMEM),
    )


def share(query, phi, scale, ref, g, heads):
    head_size = query.shape[1]
    feats = phi.shape[1]
    part = feats + SLAB
    tile_at = heads * part
    tile = ref[tile_at : tile_at + 16, :].astype(jnp.float32)
    at = tile_at + 16 + g * SLAB
    keys = ref[at : at + SLAB, :]
    keys_wide = keys.astype(jnp.float32)
    key_scale = lax.rsqrt(jnp.mean((keys_wide * keys_wide).T, axis=0, keepdims=True) + EPS)
    score = lax.dot_general(query, keys, NT, preferred_element_type=jnp.float32) * scale[:, :SLAB] * key_scale
    weights = jnp.exp(score) * tile[MASK_ROW : MASK_ROW + 1, :SLAB]
    both = jnp.concatenate([phi, weights.astype(jnp.bfloat16)], axis=1)
    num = jnp.dot(both, ref[g * part : (g + 1) * part, :], preferred_element_type=jnp.float32)
    rest = jnp.zeros((query.shape[0], feats - SLAB), jnp.float32)
    den = phi.astype(jnp.float32) * tile[g : g + 1] + jnp.concatenate([weights, rest], axis=1)
    return num, jnp.sum(den, axis=-1, keepdims=True)


def begin_kernel(rows_ref, weight_ref, near_ref, query_ref, phi_ref, num_ref, den_ref, scale_ref):
    heads, head_size, feats = weight_ref.shape
    group = (rows_ref.shape[1] - 2 * heads * head_size) // (heads * head_size)
    keys_at = heads * group * head_size
    values_at = keys_at + heads * head_size
    ready = []
    for g in range(heads):
        query = jnp.concatenate(
            [
                rows_ref[:, (g * group + h) * head_size : (g * group + h + 1) * head_size]
                for h in range(group)
            ],
            axis=0,
        )
        wide = query.astype(jnp.float32)
        phi = feature(jnp.dot(query, weight_ref[g], preferred_element_type=jnp.float32)).astype(jnp.bfloat16)
        scale = (TAU / head_size) * lax.rsqrt(jnp.mean(wide * wide, axis=-1, keepdims=True) + EPS)
        own_key = rows_ref[:, keys_at + g * head_size : keys_at + (g + 1) * head_size].astype(jnp.float32)
        own_value = rows_ref[:, values_at + g * head_size : values_at + (g + 1) * head_size].astype(jnp.float32)
        own_key = own_key * lax.rsqrt(jnp.mean(own_key * own_key, axis=-1, keepdims=True) + EPS)
        own_score = jnp.sum(wide * jnp.concatenate([own_key] * group, axis=0), axis=-1, keepdims=True) * scale
        own_weight = jnp.exp(own_score)
        scale = jnp.broadcast_to(scale, query.shape)
        num, den = share(query, phi, scale, near_ref, g, heads)
        num += own_weight.astype(jnp.bfloat16).astype(jnp.float32) * jnp.concatenate([own_value] * group, axis=0)
        ready.append((query, phi, num, den + own_weight, scale))
    for g, (query, phi, num, den, scale) in enumerate(ready):
        query_ref[g] = query
        phi_ref[g] = phi
        num_ref[g] = num
        den_ref[g] = jnp.broadcast_to(den, num.shape)
        scale_ref[g] = scale


def end_kernel(query_ref, phi_ref, num_ref, den_ref, scale_ref, far_ref, *out_refs):
    heads, asked, head_size = query_ref.shape
    each, width = out_refs[0].shape
    group = width // (heads * head_size)
    count = asked // group
    ready = []
    for g in range(heads):
        num, den = share(query_ref[g], phi_ref[g], scale_ref[g], far_ref, g, heads)
        ready.append(((num_ref[g] + num) / (den_ref[g] + den)).astype(jnp.bfloat16))
    for g, result in enumerate(ready):
        for h in range(group):
            at = (g * group + h) * head_size
            for k, out_ref in enumerate(out_refs):
                start = h * count + k * each
                out_ref[:, at : at + head_size] = result[start : start + each]


def begin(rows, weight, near):
    heads, head_size, feats = weight.shape
    count = rows.shape[0]
    group = (rows.shape[1] - 2 * heads * head_size) // (heads * head_size)
    shape = (heads, group * count, head_size)
    vmem = pl.BlockSpec(memory_space=pltpu.VMEM)
    return pl.pallas_call(
        begin_kernel,
        in_specs=[vmem] * 3,
        out_specs=[vmem] * 5,
        out_shape=[jax.ShapeDtypeStruct(shape, jnp.bfloat16)] * 2 + [jax.ShapeDtypeStruct(shape, jnp.float32)] * 3,
        compiler_params=pltpu.CompilerParams(vmem_limit_bytes=32 * 1024 * 1024),
        cost_estimate=pl.CostEstimate(
            flops=6 * count * rows.shape[1] * feats, bytes_accessed=4 * rows.size, transcendentals=2 * rows.size
        ),
        name="begin",
    )(rows, weight, near)


def end(started, far, count, width, parts):
    vmem = pl.BlockSpec(memory_space=pltpu.VMEM)
    return pl.pallas_call(
        end_kernel,
        in_specs=[vmem] * 6,
        out_specs=[vmem] * parts,
        out_shape=[jax.ShapeDtypeStruct((count, width), jnp.bfloat16)] * parts,
        compiler_params=pltpu.CompilerParams(vmem_limit_bytes=32 * 1024 * 1024),
        cost_estimate=pl.CostEstimate(
            flops=4 * started[0].size * 128, bytes_accessed=4 * started[0].size, transcendentals=started[0].size
        ),
        name="end",
    )(*started, far)


def body(
    sects, prompt_keys, prompt_values, lengths, feature_weight, queries, new_keys, new_values, row_prompt
):
    sub = lax.axis_index("sub")
    sect = lax.axis_index("sect")
    steps = list(range(1, sects))
    steps[:2] = steps[:2][::-1]
    mine = pack(queries, new_keys, new_values)
    ask = shifted if sects == 4 else partner
    asked = {k: lax.ppermute(mine, "sect", [(ask(i, k, sects), i) for i in range(sects)]) for k in steps}
    if sects == 4:
        odd = (sect & 1) == 1
        asked[1], asked[3] = jnp.where(odd, asked[3], asked[1]), jnp.where(odd, asked[1], asked[3])
    blocks = [mine] + [asked[k] for k in steps]
    near = prefill(prompt_keys, prompt_values, feature_weight, lengths)
    far = lax.ppermute(near, "sub", [(0, 1), (1, 0)])
    started = begin(jnp.concatenate(blocks, axis=0), feature_weight, near)
    results = end(started, far, *queries.shape, sects)
    results = dict(zip([0] + steps, results))

    count = queries.shape[0]
    first_row = (sect * lax.axis_size("sub") + sub) * count
    prompts = lax.dynamic_slice_in_dim(row_prompt, first_row, count, 0)
    out = results[0]
    for k in range(1, sects):
        result = lax.ppermute(results[k], "sect", [(i, partner(i, k, sects)) for i in range(sects)])
        source = partner(sect, k if paired(sects) else sects - k, sects)
        out = jnp.where((prompts == source)[:, None], result, out)
    return out


def solution(mesh):
    placed = (
        P(("parts", "sect"), "sub", "tp"),
        P(("parts", "sect"), "sub", "tp"),
        P(("parts", "sect")),
        P("tp", None, None),
        P(("parts", "sect", "sub"), "tp"),
        P(("parts", "sect", "sub"), "tp"),
        P(("parts", "sect", "sub"), "tp"),
        P("parts"),
    )
    return jax.shard_map(
        functools.partial(body, mesh.shape["sect"]),
        mesh=mesh,
        in_specs=placed,
        out_specs=P(("parts", "sect", "sub"), "tp"),
        check_vma=False,
    )
```

```python
import functools

import jax
import jax.numpy as jnp
from jax import lax
from jax.experimental import pallas as pl
from jax.experimental.pallas import tpu as pltpu
from jax.sharding import PartitionSpec as P

WINDOW = 64
TAU = 10.0
EPS = 1e-06
BLOCK = 256
NT = (((1,), (1,)), ((), ()))


def paired(sects):
    return sects & (sects - 1) == 0


def shifted(sect, k, sects):
    return (sect + k) % sects


def partner(sect, k, sects):
    return sect ^ k if paired(sects) else shifted(sect, k, sects)


def feature(proj):
    return jnp.maximum(proj, 0.0) + jnp.exp(jnp.minimum(proj, 0.0))


def pack_kernel(queries_ref, keys_ref, values_ref, out_ref, sems):
    copies, at = [], 0
    for i, ref in enumerate((queries_ref, keys_ref, values_ref)):
        size = ref.shape[1]
        copies.append(pltpu.make_async_copy(ref, out_ref.at[:, at : at + size], sems.at[i]))
        copies[-1].start()
        at += size
    for copy in copies:
        copy.wait()


def pack(queries, new_keys, new_values):
    width = queries.shape[1] + 2 * new_keys.shape[1]
    arrays = [pltpu.with_memory_space_constraint(x, pltpu.MemorySpace.HBM) for x in (queries, new_keys, new_values)]
    return pl.pallas_call(
        pack_kernel,
        in_specs=[pl.BlockSpec(memory_space=pltpu.MemorySpace.HBM)] * 3,
        out_specs=pl.BlockSpec(memory_space=pltpu.VMEM),
        out_shape=jax.ShapeDtypeStruct((queries.shape[0], width), jnp.bfloat16),
        scratch_shapes=[pltpu.SemaphoreType.DMA((3,))],
        compiler_params=pltpu.CompilerParams(vmem_limit_bytes=8 * 1024 * 1024),
        cost_estimate=pl.CostEstimate(flops=10**10, bytes_accessed=2**25, transcendentals=0),
        name="pack",
    )(*arrays)


SLAB = WINDOW + 16
MASK_ROW = 8


def prefill_kernel(
    lengths_ref, keys_ref, values_ref, weight_ref, out_ref,
    wide_ref, proj_ref, state_ref, norm_ref,
    slab_sem,
):
    heads, head_size, feats = weight_ref.shape
    pairs = heads // 2
    span = keys_ref.shape[1]
    keys_at, values_at = keys_ref.at[0], values_ref.at[0]
    chunks = span // BLOCK
    state_ref[...] = jnp.zeros_like(state_ref)
    norm_ref[...] = jnp.zeros_like(norm_ref)
    wide_ref[...] = jnp.zeros_like(wide_ref)
    for g in range(heads):
        half = g % 2
        wide_ref[g // 2, half * head_size : (half + 1) * head_size, half * feats : (half + 1) * feats] = weight_ref[g]

    begin = lengths_ref[0] - WINDOW - lax.axis_index("sub") * span
    first = jnp.clip(begin, 0, span - SLAB)
    first = pl.multiple_of(first - lax.rem(first, 16), 16)
    part = feats + SLAB
    slabs = []
    for i, source in enumerate((keys_ref, values_ref)):
        for g in range(heads):
            at = g * part + feats if i else heads * part + 16 + g * SLAB
            slabs.append(
                pltpu.make_async_copy(
                    source.at[0, pl.ds(first, SLAB), g * head_size : (g + 1) * head_size],
                    out_ref.at[at : at + SLAB, :],
                    slab_sem.at[i, g],
                )
            )
            slabs[-1].start()

    def project(c):
        for j in range(pairs):
            keys = keys_at[c * BLOCK : (c + 1) * BLOCK, j * 2 * head_size : (j + 1) * 2 * head_size]
            proj = jnp.dot(keys, wide_ref[j], preferred_element_type=jnp.float32)
            proj_ref[c % 2, j] = proj.astype(jnp.bfloat16).T

    def collect(c):
        position = c * BLOCK + lax.broadcasted_iota(jnp.int32, (1, BLOCK), 1)
        live = jnp.where(position < begin, 1.0, 0.0).astype(jnp.bfloat16)
        for j in range(pairs):
            mapped = feature(proj_ref[c % 2, j]) * live
            some = [mapped[:, k * 128 : (k + 1) * 128] for k in range(BLOCK // 128)]
            while len(some) > 1:
                some = [x + y for x, y in zip(some[::2], some[1::2])]
            norm_ref[j] += some[0].astype(jnp.float32)
            state_ref[j] += jnp.dot(
                mapped,
                values_at[c * BLOCK : (c + 1) * BLOCK, j * 2 * head_size : (j + 1) * 2 * head_size],
                preferred_element_type=jnp.float32,
            )

    project(0)
    for c in range(chunks):
        if c + 1 < chunks:
            project(c + 1)
        collect(c)

    back = 1.0 / (feats * feats)
    tile = []
    for g in range(heads):
        half = g % 2
        state = state_ref[g // 2, half * feats : (half + 1) * feats, half * head_size : (half + 1) * head_size]
        out_ref[g * part : g * part + feats, :] = (state * back).astype(jnp.bfloat16)
        sums = norm_ref[g // 2, half * feats : (half + 1) * feats, :]
        tile.append(jnp.sum(sums.T, axis=0, keepdims=True) * back)
    slot = first + lax.broadcasted_iota(jnp.int32, (1, head_size), 1)
    tile.append(jnp.zeros((MASK_ROW - heads, head_size), jnp.float32))
    tile.append(jnp.where((slot >= begin) & (slot < begin + WINDOW), 1.0, 0.0))
    tile.append(jnp.zeros((15 - MASK_ROW, head_size), jnp.float32))
    out_ref[heads * part : heads * part + 16, :] = jnp.concatenate(tile, axis=0).astype(jnp.bfloat16)
    for slab in slabs:
        slab.wait()


def prefill(keys, values, weight, lengths):
    heads, head_size, feats = weight.shape
    span, width = keys.shape[1:]
    vmem = pl.BlockSpec(memory_space=pltpu.VMEM)
    return pl.pallas_call(
        prefill_kernel,
        in_specs=[pl.BlockSpec(memory_space=pltpu.SMEM), vmem, vmem, vmem],
        out_specs=vmem,
        out_shape=jax.ShapeDtypeStruct((heads * feats + 16 + 2 * heads * SLAB, head_size), jnp.bfloat16),
        scratch_shapes=[
            pltpu.VMEM((heads // 2, 2 * feats, 2 * head_size), jnp.bfloat16),
            pltpu.VMEM((2, heads // 2, 2 * feats, BLOCK), jnp.bfloat16),
            pltpu.VMEM((heads // 2, 2 * feats, 2 * head_size), jnp.float32),
            pltpu.VMEM((heads // 2, 2 * feats, 128), jnp.float32),
            pltpu.SemaphoreType.DMA((2, heads)),
        ],
        compiler_params=pltpu.CompilerParams(vmem_limit_bytes=16 * 1024 * 1024),
        cost_estimate=pl.CostEstimate(
            flops=4 * span * width * feats, bytes_accessed=4 * span * width, transcendentals=span * width
        ),
        name="prefill",
    )(
        lengths,
        pltpu.with_memory_space_constraint(keys, pltpu.MemorySpace.VMEM),
        pltpu.with_memory_space_constraint(values, pltpu.MemorySpace.VMEM),
        pltpu.with_memory_space_constraint(weight, pltpu.MemorySpace.VMEM),
    )


def share(query, phi, scale, ref, g, heads):
    head_size = query.shape[1]
    feats = phi.shape[1]
    part = feats + SLAB
    tile_at = heads * part
    tile = ref[tile_at : tile_at + 16, :].astype(jnp.float32)
    at = tile_at + 16 + g * SLAB
    keys = ref[at : at + SLAB, :]
    keys_wide = keys.astype(jnp.float32)
    key_scale = lax.rsqrt(jnp.mean((keys_wide * keys_wide).T, axis=0, keepdims=True) + EPS)
    score = lax.dot_general(query, keys, NT, preferred_element_type=jnp.float32) * scale[:, :SLAB] * key_scale
    weights = jnp.exp(score) * tile[MASK_ROW : MASK_ROW + 1, :SLAB]
    both = jnp.concatenate([phi, weights.astype(jnp.bfloat16)], axis=1)
    num = jnp.dot(both, ref[g * part : (g + 1) * part, :], preferred_element_type=jnp.float32)
    rest = jnp.zeros((query.shape[0], feats - SLAB), jnp.float32)
    den = phi.astype(jnp.float32) * tile[g : g + 1] + jnp.concatenate([weights, rest], axis=1)
    return num, jnp.sum(den, axis=-1, keepdims=True)


def begin_kernel(rows_ref, weight_ref, near_ref, query_ref, phi_ref, num_ref, den_ref, scale_ref):
    heads, head_size, feats = weight_ref.shape
    group = (rows_ref.shape[1] - 2 * heads * head_size) // (heads * head_size)
    keys_at = heads * group * head_size
    values_at = keys_at + heads * head_size
    ready = []
    for g in range(heads):
        query = jnp.concatenate(
            [
                rows_ref[:, (g * group + h) * head_size : (g * group + h + 1) * head_size]
                for h in range(group)
            ],
            axis=0,
        )
        wide = query.astype(jnp.float32)
        phi = feature(jnp.dot(query, weight_ref[g], preferred_element_type=jnp.float32)).astype(jnp.bfloat16)
        scale = (TAU / head_size) * lax.rsqrt(jnp.mean(wide * wide, axis=-1, keepdims=True) + EPS)
        own_key = rows_ref[:, keys_at + g * head_size : keys_at + (g + 1) * head_size].astype(jnp.float32)
        own_value = rows_ref[:, values_at + g * head_size : values_at + (g + 1) * head_size].astype(jnp.float32)
        own_key = own_key * lax.rsqrt(jnp.mean(own_key * own_key, axis=-1, keepdims=True) + EPS)
        own_score = jnp.sum(wide * jnp.concatenate([own_key] * group, axis=0), axis=-1, keepdims=True) * scale
        own_weight = jnp.exp(own_score)
        scale = jnp.broadcast_to(scale, query.shape)
        num, den = share(query, phi, scale, near_ref, g, heads)
        num += own_weight.astype(jnp.bfloat16).astype(jnp.float32) * jnp.concatenate([own_value] * group, axis=0)
        ready.append((query, phi, num, den + own_weight, scale))
    for g, (query, phi, num, den, scale) in enumerate(ready):
        query_ref[g] = query
        phi_ref[g] = phi
        num_ref[g] = num
        den_ref[g] = jnp.broadcast_to(den, num.shape)
        scale_ref[g] = scale


def end_kernel(query_ref, phi_ref, num_ref, den_ref, scale_ref, far_ref, *out_refs):
    heads, asked, head_size = query_ref.shape
    each, width = out_refs[0].shape
    group = width // (heads * head_size)
    count = asked // group
    ready = []
    for g in range(heads):
        num, den = share(query_ref[g], phi_ref[g], scale_ref[g], far_ref, g, heads)
        ready.append(((num_ref[g] + num) / (den_ref[g] + den)).astype(jnp.bfloat16))
    for g, result in enumerate(ready):
        for h in range(group):
            at = (g * group + h) * head_size
            for k, out_ref in enumerate(out_refs):
                start = h * count + k * each
                out_ref[:, at : at + head_size] = result[start : start + each]


def begin(rows, weight, near):
    heads, head_size, feats = weight.shape
    count = rows.shape[0]
    group = (rows.shape[1] - 2 * heads * head_size) // (heads * head_size)
    shape = (heads, group * count, head_size)
    vmem = pl.BlockSpec(memory_space=pltpu.VMEM)
    return pl.pallas_call(
        begin_kernel,
        in_specs=[vmem] * 3,
        out_specs=[vmem] * 5,
        out_shape=[jax.ShapeDtypeStruct(shape, jnp.bfloat16)] * 2 + [jax.ShapeDtypeStruct(shape, jnp.float32)] * 3,
        compiler_params=pltpu.CompilerParams(vmem_limit_bytes=32 * 1024 * 1024),
        cost_estimate=pl.CostEstimate(
            flops=6 * count * rows.shape[1] * feats, bytes_accessed=4 * rows.size, transcendentals=2 * rows.size
        ),
        name="begin",
    )(rows, weight, near)


def end(started, far, count, width, parts):
    vmem = pl.BlockSpec(memory_space=pltpu.VMEM)
    return pl.pallas_call(
        end_kernel,
        in_specs=[vmem] * 6,
        out_specs=[vmem] * parts,
        out_shape=[jax.ShapeDtypeStruct((count, width), jnp.bfloat16)] * parts,
        compiler_params=pltpu.CompilerParams(vmem_limit_bytes=32 * 1024 * 1024),
        cost_estimate=pl.CostEstimate(
            flops=4 * started[0].size * 128, bytes_accessed=4 * started[0].size, transcendentals=started[0].size
        ),
        name="end",
    )(*started, far)


def body(
    sects, prompt_keys, prompt_values, lengths, feature_weight, queries, new_keys, new_values, row_prompt
):
    sub = lax.axis_index("sub")
    sect = lax.axis_index("sect")
    steps = list(range(1, sects))
    steps[:2] = steps[:2][::-1]
    mine = pack(queries, new_keys, new_values)
    ask = shifted if sects == 4 else partner
    asked = {k: lax.ppermute(mine, "sect", [(ask(i, k, sects), i) for i in range(sects)]) for k in steps}
    if sects == 4:
        odd = (sect & 1) == 1
        asked[1], asked[3] = jnp.where(odd, asked[3], asked[1]), jnp.where(odd, asked[1], asked[3])
    blocks = [mine] + [asked[k] for k in steps]
    near = prefill(prompt_keys, prompt_values, feature_weight, lengths)
    far = lax.ppermute(near, "sub", [(0, 1), (1, 0)])
    started = begin(jnp.concatenate(blocks, axis=0), feature_weight, near)
    results = end(started, far, *queries.shape, sects)
    results = dict(zip([0] + steps, results))

    count = queries.shape[0]
    first_row = (sect * lax.axis_size("sub") + sub) * count
    prompts = lax.dynamic_slice_in_dim(row_prompt, first_row, count, 0)
    out = results[0]
    for k in range(1, sects):
        result = lax.ppermute(results[k], "sect", [(i, partner(i, k, sects)) for i in range(sects)])
        source = partner(sect, k if paired(sects) else sects - k, sects)
        out = jnp.where((prompts == source)[:, None], result, out)
    return out


def solution(mesh):
    placed = (
        P(("parts", "sect"), "sub", "tp"),
        P(("parts", "sect"), "sub", "tp"),
        P(("parts", "sect")),
        P("tp", None, None),
        P(("parts", "sect", "sub"), "tp"),
        P(("parts", "sect", "sub"), "tp"),
        P(("parts", "sect", "sub"), "tp"),
        P("parts"),
    )
    return jax.shard_map(
        functools.partial(body, mesh.shape["sect"]),
        mesh=mesh,
        in_specs=placed,
        out_specs=P(("parts", "sect", "sub"), "tp"),
        check_vma=False,
    )
```

```python
import functools

import jax
import jax.numpy as jnp
from jax import lax
from jax.experimental import pallas as pl
from jax.experimental.pallas import tpu as pltpu
from jax.sharding import PartitionSpec as P

WINDOW = 64
TAU = 10.0
EPS = 1e-06
BLOCK = 256
NT = (((1,), (1,)), ((), ()))


def paired(sects):
    return sects & (sects - 1) == 0


def shifted(sect, k, sects):
    return (sect + k) % sects


def partner(sect, k, sects):
    return sect ^ k if paired(sects) else shifted(sect, k, sects)


def feature(proj):
    return jnp.maximum(proj, 0.0) + jnp.exp(jnp.minimum(proj, 0.0))


def pack_kernel(queries_ref, keys_ref, values_ref, out_ref, sems):
    copies, at = [], 0
    for i, ref in enumerate((queries_ref, keys_ref, values_ref)):
        size = ref.shape[1]
        copies.append(pltpu.make_async_copy(ref, out_ref.at[:, at : at + size], sems.at[i]))
        copies[-1].start()
        at += size
    for copy in copies:
        copy.wait()


def pack(queries, new_keys, new_values):
    width = queries.shape[1] + 2 * new_keys.shape[1]
    arrays = [pltpu.with_memory_space_constraint(x, pltpu.MemorySpace.HBM) for x in (queries, new_keys, new_values)]
    return pl.pallas_call(
        pack_kernel,
        in_specs=[pl.BlockSpec(memory_space=pltpu.MemorySpace.HBM)] * 3,
        out_specs=pl.BlockSpec(memory_space=pltpu.VMEM),
        out_shape=jax.ShapeDtypeStruct((queries.shape[0], width), jnp.bfloat16),
        scratch_shapes=[pltpu.SemaphoreType.DMA((3,))],
        compiler_params=pltpu.CompilerParams(vmem_limit_bytes=8 * 1024 * 1024),
        cost_estimate=pl.CostEstimate(flops=10**10, bytes_accessed=2**25, transcendentals=0),
        name="pack",
    )(*arrays)


SLAB = WINDOW + 16
MASK_ROW = 8


def prefill_kernel(
    lengths_ref, keys_ref, values_ref, weight_ref, out_ref,
    wide_ref, proj_ref, state_ref, norm_ref,
    slab_sem,
):
    heads, head_size, feats = weight_ref.shape
    pairs = heads // 2
    span = keys_ref.shape[1]
    keys_at, values_at = keys_ref.at[0], values_ref.at[0]
    chunks = span // BLOCK
    state_ref[...] = jnp.zeros_like(state_ref)
    norm_ref[...] = jnp.zeros_like(norm_ref)
    wide_ref[...] = jnp.zeros_like(wide_ref)
    for g in range(heads):
        half = g % 2
        turned = weight_ref[g].astype(jnp.float32).T.astype(jnp.bfloat16)
        wide_ref[g // 2, half * feats : (half + 1) * feats, half * head_size : (half + 1) * head_size] = turned

    begin = lengths_ref[0] - WINDOW - lax.axis_index("sub") * span
    first = jnp.clip(begin, 0, span - SLAB)
    first = pl.multiple_of(first - lax.rem(first, 16), 16)
    part = feats + SLAB
    slabs = []
    for i, source in enumerate((keys_ref, values_ref)):
        for g in range(heads):
            at = g * part + feats if i else heads * part + 16 + g * SLAB
            slabs.append(
                pltpu.make_async_copy(
                    source.at[0, pl.ds(first, SLAB), g * head_size : (g + 1) * head_size],
                    out_ref.at[at : at + SLAB, :],
                    slab_sem.at[i, g],
                )
            )
            slabs[-1].start()

    def project(c):
        for j in range(pairs):
            proj = lax.dot_general(
                wide_ref[j],
                keys_at[c * BLOCK : (c + 1) * BLOCK, j * 2 * head_size : (j + 1) * 2 * head_size],
                NT,
                preferred_element_type=jnp.float32,
            )
            proj_ref[c % 4, j] = proj.astype(jnp.bfloat16)

    def collect(first_chunk):
        for j in range(pairs):
            sums, parts = [], []
            for c in (first_chunk, first_chunk + 1):
                position = c * BLOCK + lax.broadcasted_iota(jnp.int32, (1, BLOCK), 1)
                live = jnp.where(position < begin, 1.0, 0.0).astype(jnp.bfloat16)
                mapped = feature(proj_ref[c % 4, j]) * live
                some = [mapped[:, k * 128 : (k + 1) * 128] for k in range(BLOCK // 128)]
                while len(some) > 1:
                    some = [x + y for x, y in zip(some[::2], some[1::2])]
                sums.append(some[0].astype(jnp.float32))
                parts.append(
                    jnp.dot(
                        mapped,
                        values_at[c * BLOCK : (c + 1) * BLOCK, j * 2 * head_size : (j + 1) * 2 * head_size],
                        preferred_element_type=jnp.float32,
                    )
                )
            norm_ref[j] += sums[0] + sums[1]
            state_ref[j] += parts[0] + parts[1]

    for c in range(0, chunks + 2, 2):
        if c < chunks:
            project(c)
            project(c + 1)
        if c > 0:
            collect(c - 2)

    back = 1.0 / (feats * feats)
    tile = []
    for g in range(heads):
        half = g % 2
        state = state_ref[g // 2, half * feats : (half + 1) * feats, half * head_size : (half + 1) * head_size]
        out_ref[g * part : g * part + feats, :] = (state * back).astype(jnp.bfloat16)
        sums = norm_ref[g // 2, half * feats : (half + 1) * feats, :]
        tile.append(jnp.sum(sums.T, axis=0, keepdims=True) * back)
    slot = first + lax.broadcasted_iota(jnp.int32, (1, head_size), 1)
    tile.append(jnp.zeros((MASK_ROW - heads, head_size), jnp.float32))
    tile.append(jnp.where((slot >= begin) & (slot < begin + WINDOW), 1.0, 0.0))
    tile.append(jnp.zeros((15 - MASK_ROW, head_size), jnp.float32))
    out_ref[heads * part : heads * part + 16, :] = jnp.concatenate(tile, axis=0).astype(jnp.bfloat16)
    for slab in slabs:
        slab.wait()


def prefill(keys, values, weight, lengths):
    heads, head_size, feats = weight.shape
    span, width = keys.shape[1:]
    vmem = pl.BlockSpec(memory_space=pltpu.VMEM)
    return pl.pallas_call(
        prefill_kernel,
        in_specs=[pl.BlockSpec(memory_space=pltpu.SMEM), vmem, vmem, vmem],
        out_specs=vmem,
        out_shape=jax.ShapeDtypeStruct((heads * feats + 16 + 2 * heads * SLAB, head_size), jnp.bfloat16),
        scratch_shapes=[
            pltpu.VMEM((heads // 2, 2 * feats, 2 * head_size), jnp.bfloat16),
            pltpu.VMEM((4, heads // 2, 2 * feats, BLOCK), jnp.bfloat16),
            pltpu.VMEM((heads // 2, 2 * feats, 2 * head_size), jnp.float32),
            pltpu.VMEM((heads // 2, 2 * feats, 128), jnp.float32),
            pltpu.SemaphoreType.DMA((2, heads)),
        ],
        compiler_params=pltpu.CompilerParams(vmem_limit_bytes=16 * 1024 * 1024),
        cost_estimate=pl.CostEstimate(
            flops=4 * span * width * feats, bytes_accessed=4 * span * width, transcendentals=span * width
        ),
        name="prefill",
    )(
        lengths,
        pltpu.with_memory_space_constraint(keys, pltpu.MemorySpace.VMEM),
        pltpu.with_memory_space_constraint(values, pltpu.MemorySpace.VMEM),
        pltpu.with_memory_space_constraint(weight, pltpu.MemorySpace.VMEM),
    )


def share(query, phi, scale, ref, g, heads):
    head_size = query.shape[1]
    feats = phi.shape[1]
    part = feats + SLAB
    tile_at = heads * part
    tile = ref[tile_at : tile_at + 16, :].astype(jnp.float32)
    at = tile_at + 16 + g * SLAB
    keys = ref[at : at + SLAB, :]
    keys_wide = keys.astype(jnp.float32)
    key_scale = lax.rsqrt(jnp.mean((keys_wide * keys_wide).T, axis=0, keepdims=True) + EPS)
    score = lax.dot_general(query, keys, NT, preferred_element_type=jnp.float32) * scale[:, :SLAB] * key_scale
    weights = jnp.exp(score) * tile[MASK_ROW : MASK_ROW + 1, :SLAB]
    both = jnp.concatenate([phi, weights.astype(jnp.bfloat16)], axis=1)
    num = jnp.dot(both, ref[g * part : (g + 1) * part, :], preferred_element_type=jnp.float32)
    rest = jnp.zeros((query.shape[0], feats - SLAB), jnp.float32)
    den = phi.astype(jnp.float32) * tile[g : g + 1] + jnp.concatenate([weights, rest], axis=1)
    return num, jnp.sum(den, axis=-1, keepdims=True)


def begin_kernel(rows_ref, weight_ref, near_ref, query_ref, phi_ref, num_ref, den_ref, scale_ref):
    heads, head_size, feats = weight_ref.shape
    group = (rows_ref.shape[1] - 2 * heads * head_size) // (heads * head_size)
    keys_at = heads * group * head_size
    values_at = keys_at + heads * head_size
    ready = []
    for g in range(heads):
        query = jnp.concatenate(
            [
                rows_ref[:, (g * group + h) * head_size : (g * group + h + 1) * head_size]
                for h in range(group)
            ],
            axis=0,
        )
        wide = query.astype(jnp.float32)
        phi = feature(jnp.dot(query, weight_ref[g], preferred_element_type=jnp.float32)).astype(jnp.bfloat16)
        scale = (TAU / head_size) * lax.rsqrt(jnp.mean(wide * wide, axis=-1, keepdims=True) + EPS)
        own_key = rows_ref[:, keys_at + g * head_size : keys_at + (g + 1) * head_size].astype(jnp.float32)
        own_value = rows_ref[:, values_at + g * head_size : values_at + (g + 1) * head_size].astype(jnp.float32)
        own_key = own_key * lax.rsqrt(jnp.mean(own_key * own_key, axis=-1, keepdims=True) + EPS)
        own_score = jnp.sum(wide * jnp.concatenate([own_key] * group, axis=0), axis=-1, keepdims=True) * scale
        own_weight = jnp.exp(own_score)
        scale = jnp.broadcast_to(scale, query.shape)
        num, den = share(query, phi, scale, near_ref, g, heads)
        num += own_weight.astype(jnp.bfloat16).astype(jnp.float32) * jnp.concatenate([own_value] * group, axis=0)
        ready.append((query, phi, num, den + own_weight, scale))
    for g, (query, phi, num, den, scale) in enumerate(ready):
        query_ref[g] = query
        phi_ref[g] = phi
        num_ref[g] = num
        den_ref[g] = jnp.broadcast_to(den, num.shape)
        scale_ref[g] = scale


def end_kernel(query_ref, phi_ref, num_ref, den_ref, scale_ref, far_ref, *out_refs):
    heads, asked, head_size = query_ref.shape
    each, width = out_refs[0].shape
    group = width // (heads * head_size)
    count = asked // group
    ready = []
    for g in range(heads):
        num, den = share(query_ref[g], phi_ref[g], scale_ref[g], far_ref, g, heads)
        ready.append(((num_ref[g] + num) / (den_ref[g] + den)).astype(jnp.bfloat16))
    for g, result in enumerate(ready):
        for h in range(group):
            at = (g * group + h) * head_size
            for k, out_ref in enumerate(out_refs):
                start = h * count + k * each
                out_ref[:, at : at + head_size] = result[start : start + each]


def begin(rows, weight, near):
    heads, head_size, feats = weight.shape
    count = rows.shape[0]
    group = (rows.shape[1] - 2 * heads * head_size) // (heads * head_size)
    shape = (heads, group * count, head_size)
    vmem = pl.BlockSpec(memory_space=pltpu.VMEM)
    return pl.pallas_call(
        begin_kernel,
        in_specs=[vmem] * 3,
        out_specs=[vmem] * 5,
        out_shape=[jax.ShapeDtypeStruct(shape, jnp.bfloat16)] * 2 + [jax.ShapeDtypeStruct(shape, jnp.float32)] * 3,
        compiler_params=pltpu.CompilerParams(vmem_limit_bytes=32 * 1024 * 1024),
        cost_estimate=pl.CostEstimate(
            flops=6 * count * rows.shape[1] * feats, bytes_accessed=4 * rows.size, transcendentals=2 * rows.size
        ),
        name="begin",
    )(rows, weight, near)


def end(started, far, count, width, parts):
    vmem = pl.BlockSpec(memory_space=pltpu.VMEM)
    return pl.pallas_call(
        end_kernel,
        in_specs=[vmem] * 6,
        out_specs=[vmem] * parts,
        out_shape=[jax.ShapeDtypeStruct((count, width), jnp.bfloat16)] * parts,
        compiler_params=pltpu.CompilerParams(vmem_limit_bytes=32 * 1024 * 1024),
        cost_estimate=pl.CostEstimate(
            flops=4 * started[0].size * 128, bytes_accessed=4 * started[0].size, transcendentals=started[0].size
        ),
        name="end",
    )(*started, far)


def body(
    sects, prompt_keys, prompt_values, lengths, feature_weight, queries, new_keys, new_values, row_prompt
):
    sub = lax.axis_index("sub")
    sect = lax.axis_index("sect")
    steps = list(range(1, sects))
    steps[:2] = steps[:2][::-1]
    mine = pack(queries, new_keys, new_values)
    ask = shifted if sects == 4 else partner
    asked = {k: lax.ppermute(mine, "sect", [(ask(i, k, sects), i) for i in range(sects)]) for k in steps}
    if sects == 4:
        odd = (sect & 1) == 1
        asked[1], asked[3] = jnp.where(odd, asked[3], asked[1]), jnp.where(odd, asked[1], asked[3])
    blocks = [mine] + [asked[k] for k in steps]
    near = prefill(prompt_keys, prompt_values, feature_weight, lengths)
    far = lax.ppermute(near, "sub", [(0, 1), (1, 0)])
    started = begin(jnp.concatenate(blocks, axis=0), feature_weight, near)
    results = end(started, far, *queries.shape, sects)
    results = dict(zip([0] + steps, results))

    count = queries.shape[0]
    first_row = (sect * lax.axis_size("sub") + sub) * count
    prompts = lax.dynamic_slice_in_dim(row_prompt, first_row, count, 0)
    out = results[0]
    for k in range(1, sects):
        result = lax.ppermute(results[k], "sect", [(i, partner(i, k, sects)) for i in range(sects)])
        source = partner(sect, k if paired(sects) else sects - k, sects)
        out = jnp.where((prompts == source)[:, None], result, out)
    return out


def solution(mesh):
    placed = (
        P(("parts", "sect"), "sub", "tp"),
        P(("parts", "sect"), "sub", "tp"),
        P(("parts", "sect")),
        P("tp", None, None),
        P(("parts", "sect", "sub"), "tp"),
        P(("parts", "sect", "sub"), "tp"),
        P(("parts", "sect", "sub"), "tp"),
        P("parts"),
    )
    return jax.shard_map(
        functools.partial(body, mesh.shape["sect"]),
        mesh=mesh,
        in_specs=placed,
        out_specs=P(("parts", "sect", "sub"), "tp"),
        check_vma=False,
    )
```

```python
import functools

import jax
import jax.numpy as jnp
from jax import lax
from jax.experimental import pallas as pl
from jax.experimental.pallas import tpu as pltpu
from jax.sharding import PartitionSpec as P

WINDOW = 64
TAU = 10.0
EPS = 1e-06
BLOCK = 256
NT = (((1,), (1,)), ((), ()))


def paired(sects):
    return sects & (sects - 1) == 0


def shifted(sect, k, sects):
    return (sect + k) % sects


def partner(sect, k, sects):
    return sect ^ k if paired(sects) else shifted(sect, k, sects)


def feature(proj):
    return jnp.maximum(proj, 0.0) + jnp.exp(jnp.minimum(proj, 0.0))


def pack_kernel(queries_ref, keys_ref, values_ref, out_ref, sems):
    copies, at = [], 0
    for i, ref in enumerate((queries_ref, keys_ref, values_ref)):
        size = ref.shape[1]
        copies.append(pltpu.make_async_copy(ref, out_ref.at[:, at : at + size], sems.at[i]))
        copies[-1].start()
        at += size
    for copy in copies:
        copy.wait()


def pack(queries, new_keys, new_values):
    width = queries.shape[1] + 2 * new_keys.shape[1]
    arrays = [pltpu.with_memory_space_constraint(x, pltpu.MemorySpace.HBM) for x in (queries, new_keys, new_values)]
    return pl.pallas_call(
        pack_kernel,
        in_specs=[pl.BlockSpec(memory_space=pltpu.MemorySpace.HBM)] * 3,
        out_specs=pl.BlockSpec(memory_space=pltpu.VMEM),
        out_shape=jax.ShapeDtypeStruct((queries.shape[0], width), jnp.bfloat16),
        scratch_shapes=[pltpu.SemaphoreType.DMA((3,))],
        compiler_params=pltpu.CompilerParams(vmem_limit_bytes=8 * 1024 * 1024),
        cost_estimate=pl.CostEstimate(flops=10**10, bytes_accessed=2**25, transcendentals=0),
        name="pack",
    )(*arrays)


SLAB = WINDOW + 16
MASK_ROW = 8


def prefill_kernel(
    lengths_ref, keys_ref, values_ref, weight_ref, out_ref,
    wide_ref, proj_ref, state_ref, norm_ref,
    slab_sem,
):
    heads, head_size, feats = weight_ref.shape
    pairs = heads // 2
    span = keys_ref.shape[1]
    keys_at, values_at = keys_ref.at[0], values_ref.at[0]
    chunks = span // BLOCK
    state_ref[...] = jnp.zeros_like(state_ref)
    norm_ref[...] = jnp.zeros_like(norm_ref)
    wide_ref[...] = jnp.zeros_like(wide_ref)
    for g in range(heads):
        half = g % 2
        turned = weight_ref[g].astype(jnp.float32).T.astype(jnp.bfloat16)
        wide_ref[g // 2, half * feats : (half + 1) * feats, half * head_size : (half + 1) * head_size] = turned

    begin = lengths_ref[0] - WINDOW - lax.axis_index("sub") * span
    first = jnp.clip(begin, 0, span - SLAB)
    first = pl.multiple_of(first - lax.rem(first, 16), 16)
    part = feats + SLAB
    slabs = []
    for i, source in enumerate((keys_ref, values_ref)):
        for g in range(heads):
            at = g * part + feats if i else heads * part + 16 + g * SLAB
            slabs.append(
                pltpu.make_async_copy(
                    source.at[0, pl.ds(first, SLAB), g * head_size : (g + 1) * head_size],
                    out_ref.at[at : at + SLAB, :],
                    slab_sem.at[i, g],
                )
            )
            slabs[-1].start()

    def project(unit):
        c, j = divmod(unit, pairs)
        proj = lax.dot_general(
            wide_ref[j],
            keys_at[c * BLOCK : (c + 1) * BLOCK, j * 2 * head_size : (j + 1) * 2 * head_size],
            NT,
            preferred_element_type=jnp.float32,
        )
        proj_ref[unit % 2] = proj.astype(jnp.bfloat16)

    def collect(unit):
        c, j = divmod(unit, pairs)
        position = c * BLOCK + lax.broadcasted_iota(jnp.int32, (1, BLOCK), 1)
        live = jnp.where(position < begin, 1.0, 0.0).astype(jnp.bfloat16)
        mapped = feature(proj_ref[unit % 2]) * live
        some = [mapped[:, k * 128 : (k + 1) * 128] for k in range(BLOCK // 128)]
        while len(some) > 1:
            some = [x + y for x, y in zip(some[::2], some[1::2])]
        norm_ref[j] += some[0].astype(jnp.float32)
        state_ref[j] += jnp.dot(
            mapped,
            values_at[c * BLOCK : (c + 1) * BLOCK, j * 2 * head_size : (j + 1) * 2 * head_size],
            preferred_element_type=jnp.float32,
        )

    project(0)
    for unit in range(chunks * pairs):
        if unit + 1 < chunks * pairs:
            project(unit + 1)
        collect(unit)

    back = 1.0 / (feats * feats)
    tile = []
    for g in range(heads):
        half = g % 2
        state = state_ref[g // 2, half * feats : (half + 1) * feats, half * head_size : (half + 1) * head_size]
        out_ref[g * part : g * part + feats, :] = (state * back).astype(jnp.bfloat16)
        sums = norm_ref[g // 2, half * feats : (half + 1) * feats, :]
        tile.append(jnp.sum(sums.T, axis=0, keepdims=True) * back)
    slot = first + lax.broadcasted_iota(jnp.int32, (1, head_size), 1)
    tile.append(jnp.zeros((MASK_ROW - heads, head_size), jnp.float32))
    tile.append(jnp.where((slot >= begin) & (slot < begin + WINDOW), 1.0, 0.0))
    tile.append(jnp.zeros((15 - MASK_ROW, head_size), jnp.float32))
    out_ref[heads * part : heads * part + 16, :] = jnp.concatenate(tile, axis=0).astype(jnp.bfloat16)
    for slab in slabs:
        slab.wait()


def prefill(keys, values, weight, lengths):
    heads, head_size, feats = weight.shape
    span, width = keys.shape[1:]
    vmem = pl.BlockSpec(memory_space=pltpu.VMEM)
    return pl.pallas_call(
        prefill_kernel,
        in_specs=[pl.BlockSpec(memory_space=pltpu.SMEM), vmem, vmem, vmem],
        out_specs=vmem,
        out_shape=jax.ShapeDtypeStruct((heads * feats + 16 + 2 * heads * SLAB, head_size), jnp.bfloat16),
        scratch_shapes=[
            pltpu.VMEM((heads // 2, 2 * feats, 2 * head_size), jnp.bfloat16),
            pltpu.VMEM((2, 2 * feats, BLOCK), jnp.bfloat16),
            pltpu.VMEM((heads // 2, 2 * feats, 2 * head_size), jnp.float32),
            pltpu.VMEM((heads // 2, 2 * feats, 128), jnp.float32),
            pltpu.SemaphoreType.DMA((2, heads)),
        ],
        compiler_params=pltpu.CompilerParams(vmem_limit_bytes=16 * 1024 * 1024),
        cost_estimate=pl.CostEstimate(
            flops=4 * span * width * feats, bytes_accessed=4 * span * width, transcendentals=span * width
        ),
        name="prefill",
    )(
        lengths,
        pltpu.with_memory_space_constraint(keys, pltpu.MemorySpace.VMEM),
        pltpu.with_memory_space_constraint(values, pltpu.MemorySpace.VMEM),
        pltpu.with_memory_space_constraint(weight, pltpu.MemorySpace.VMEM),
    )


def share(query, phi, scale, ref, g, heads):
    head_size = query.shape[1]
    feats = phi.shape[1]
    part = feats + SLAB
    tile_at = heads * part
    tile = ref[tile_at : tile_at + 16, :].astype(jnp.float32)
    at = tile_at + 16 + g * SLAB
    keys = ref[at : at + SLAB, :]
    keys_wide = keys.astype(jnp.float32)
    key_scale = lax.rsqrt(jnp.mean((keys_wide * keys_wide).T, axis=0, keepdims=True) + EPS)
    score = lax.dot_general(query, keys, NT, preferred_element_type=jnp.float32) * scale[:, :SLAB] * key_scale
    weights = jnp.exp(score) * tile[MASK_ROW : MASK_ROW + 1, :SLAB]
    both = jnp.concatenate([phi, weights.astype(jnp.bfloat16)], axis=1)
    num = jnp.dot(both, ref[g * part : (g + 1) * part, :], preferred_element_type=jnp.float32)
    rest = jnp.zeros((query.shape[0], feats - SLAB), jnp.float32)
    den = phi.astype(jnp.float32) * tile[g : g + 1] + jnp.concatenate([weights, rest], axis=1)
    return num, jnp.sum(den, axis=-1, keepdims=True)


def begin_kernel(rows_ref, weight_ref, near_ref, query_ref, phi_ref, num_ref, den_ref, scale_ref):
    heads, head_size, feats = weight_ref.shape
    group = (rows_ref.shape[1] - 2 * heads * head_size) // (heads * head_size)
    keys_at = heads * group * head_size
    values_at = keys_at + heads * head_size
    ready = []
    for g in range(heads):
        query = jnp.concatenate(
            [
                rows_ref[:, (g * group + h) * head_size : (g * group + h + 1) * head_size]
                for h in range(group)
            ],
            axis=0,
        )
        wide = query.astype(jnp.float32)
        phi = feature(jnp.dot(query, weight_ref[g], preferred_element_type=jnp.float32)).astype(jnp.bfloat16)
        scale = (TAU / head_size) * lax.rsqrt(jnp.mean(wide * wide, axis=-1, keepdims=True) + EPS)
        own_key = rows_ref[:, keys_at + g * head_size : keys_at + (g + 1) * head_size].astype(jnp.float32)
        own_value = rows_ref[:, values_at + g * head_size : values_at + (g + 1) * head_size].astype(jnp.float32)
        own_key = own_key * lax.rsqrt(jnp.mean(own_key * own_key, axis=-1, keepdims=True) + EPS)
        own_score = jnp.sum(wide * jnp.concatenate([own_key] * group, axis=0), axis=-1, keepdims=True) * scale
        own_weight = jnp.exp(own_score)
        scale = jnp.broadcast_to(scale, query.shape)
        num, den = share(query, phi, scale, near_ref, g, heads)
        num += own_weight.astype(jnp.bfloat16).astype(jnp.float32) * jnp.concatenate([own_value] * group, axis=0)
        ready.append((query, phi, num, den + own_weight, scale))
    for g, (query, phi, num, den, scale) in enumerate(ready):
        query_ref[g] = query
        phi_ref[g] = phi
        num_ref[g] = num
        den_ref[g] = jnp.broadcast_to(den, num.shape)
        scale_ref[g] = scale


def end_kernel(query_ref, phi_ref, num_ref, den_ref, scale_ref, far_ref, *out_refs):
    heads, asked, head_size = query_ref.shape
    each, width = out_refs[0].shape
    group = width // (heads * head_size)
    count = asked // group
    ready = []
    for g in range(heads):
        num, den = share(query_ref[g], phi_ref[g], scale_ref[g], far_ref, g, heads)
        ready.append(((num_ref[g] + num) / (den_ref[g] + den)).astype(jnp.bfloat16))
    for g, result in enumerate(ready):
        for h in range(group):
            at = (g * group + h) * head_size
            for k, out_ref in enumerate(out_refs):
                start = h * count + k * each
                out_ref[:, at : at + head_size] = result[start : start + each]


def begin(rows, weight, near):
    heads, head_size, feats = weight.shape
    count = rows.shape[0]
    group = (rows.shape[1] - 2 * heads * head_size) // (heads * head_size)
    shape = (heads, group * count, head_size)
    vmem = pl.BlockSpec(memory_space=pltpu.VMEM)
    return pl.pallas_call(
        begin_kernel,
        in_specs=[vmem] * 3,
        out_specs=[vmem] * 5,
        out_shape=[jax.ShapeDtypeStruct(shape, jnp.bfloat16)] * 2 + [jax.ShapeDtypeStruct(shape, jnp.float32)] * 3,
        compiler_params=pltpu.CompilerParams(vmem_limit_bytes=32 * 1024 * 1024),
        cost_estimate=pl.CostEstimate(
            flops=6 * count * rows.shape[1] * feats, bytes_accessed=4 * rows.size, transcendentals=2 * rows.size
        ),
        name="begin",
    )(rows, weight, near)


def end(started, far, count, width, parts):
    vmem = pl.BlockSpec(memory_space=pltpu.VMEM)
    return pl.pallas_call(
        end_kernel,
        in_specs=[vmem] * 6,
        out_specs=[vmem] * parts,
        out_shape=[jax.ShapeDtypeStruct((count, width), jnp.bfloat16)] * parts,
        compiler_params=pltpu.CompilerParams(vmem_limit_bytes=32 * 1024 * 1024),
        cost_estimate=pl.CostEstimate(
            flops=4 * started[0].size * 128, bytes_accessed=4 * started[0].size, transcendentals=started[0].size
        ),
        name="end",
    )(*started, far)


def body(
    sects, prompt_keys, prompt_values, lengths, feature_weight, queries, new_keys, new_values, row_prompt
):
    sub = lax.axis_index("sub")
    sect = lax.axis_index("sect")
    steps = list(range(1, sects))
    steps[:2] = steps[:2][::-1]
    mine = pack(queries, new_keys, new_values)
    ask = shifted if sects == 4 else partner
    asked = {k: lax.ppermute(mine, "sect", [(ask(i, k, sects), i) for i in range(sects)]) for k in steps}
    if sects == 4:
        odd = (sect & 1) == 1
        asked[1], asked[3] = jnp.where(odd, asked[3], asked[1]), jnp.where(odd, asked[1], asked[3])
    blocks = [mine] + [asked[k] for k in steps]
    near = prefill(prompt_keys, prompt_values, feature_weight, lengths)
    far = lax.ppermute(near, "sub", [(0, 1), (1, 0)])
    started = begin(jnp.concatenate(blocks, axis=0), feature_weight, near)
    results = end(started, far, *queries.shape, sects)
    results = dict(zip([0] + steps, results))

    count = queries.shape[0]
    first_row = (sect * lax.axis_size("sub") + sub) * count
    prompts = lax.dynamic_slice_in_dim(row_prompt, first_row, count, 0)
    out = results[0]
    for k in range(1, sects):
        result = lax.ppermute(results[k], "sect", [(i, partner(i, k, sects)) for i in range(sects)])
        source = partner(sect, k if paired(sects) else sects - k, sects)
        out = jnp.where((prompts == source)[:, None], result, out)
    return out


def solution(mesh):
    placed = (
        P(("parts", "sect"), "sub", "tp"),
        P(("parts", "sect"), "sub", "tp"),
        P(("parts", "sect")),
        P("tp", None, None),
        P(("parts", "sect", "sub"), "tp"),
        P(("parts", "sect", "sub"), "tp"),
        P(("parts", "sect", "sub"), "tp"),
        P("parts"),
    )
    return jax.shard_map(
        functools.partial(body, mesh.shape["sect"]),
        mesh=mesh,
        in_specs=placed,
        out_specs=P(("parts", "sect", "sub"), "tp"),
        check_vma=False,
    )
```

```python
import functools

import jax
import jax.numpy as jnp
from jax import lax
from jax.experimental import pallas as pl
from jax.experimental.pallas import tpu as pltpu
from jax.sharding import PartitionSpec as P

WINDOW = 64
TAU = 10.0
EPS = 1e-06
BLOCK = 256
NT = (((1,), (1,)), ((), ()))


def paired(sects):
    return sects & (sects - 1) == 0


def shifted(sect, k, sects):
    return (sect + k) % sects


def partner(sect, k, sects):
    return sect ^ k if paired(sects) else shifted(sect, k, sects)


def feature(proj):
    return jnp.maximum(proj, 0.0) + jnp.exp(jnp.minimum(proj, 0.0))


def pack_kernel(queries_ref, keys_ref, values_ref, out_ref, sems):
    copies, at = [], 0
    for i, ref in enumerate((queries_ref, keys_ref, values_ref)):
        size = ref.shape[1]
        copies.append(pltpu.make_async_copy(ref, out_ref.at[:, at : at + size], sems.at[i]))
        copies[-1].start()
        at += size
    for copy in copies:
        copy.wait()


def pack(queries, new_keys, new_values):
    width = queries.shape[1] + 2 * new_keys.shape[1]
    arrays = [pltpu.with_memory_space_constraint(x, pltpu.MemorySpace.HBM) for x in (queries, new_keys, new_values)]
    return pl.pallas_call(
        pack_kernel,
        in_specs=[pl.BlockSpec(memory_space=pltpu.MemorySpace.HBM)] * 3,
        out_specs=pl.BlockSpec(memory_space=pltpu.VMEM),
        out_shape=jax.ShapeDtypeStruct((queries.shape[0], width), jnp.bfloat16),
        scratch_shapes=[pltpu.SemaphoreType.DMA((3,))],
        compiler_params=pltpu.CompilerParams(vmem_limit_bytes=8 * 1024 * 1024),
        cost_estimate=pl.CostEstimate(flops=10**10, bytes_accessed=2**25, transcendentals=0),
        name="pack",
    )(*arrays)


SLAB = WINDOW + 16
MASK_ROW = 8


def prefill_kernel(
    lengths_ref, keys_ref, values_ref, weight_ref, out_ref,
    turned_ref, proj_ref, state_ref, norm_ref,
    slab_sem,
):
    heads, head_size, feats = weight_ref.shape
    span = keys_ref.shape[1]
    keys_at, values_at = keys_ref.at[0], values_ref.at[0]
    chunks = span // BLOCK
    state_ref[...] = jnp.zeros_like(state_ref)
    norm_ref[...] = jnp.zeros_like(norm_ref)
    for g in range(heads):
        turned_ref[g] = weight_ref[g].astype(jnp.float32).T.astype(jnp.bfloat16)

    begin = lengths_ref[0] - WINDOW - lax.axis_index("sub") * span
    first = jnp.clip(begin, 0, span - SLAB)
    first = pl.multiple_of(first - lax.rem(first, 16), 16)
    part = feats + SLAB
    slabs = []
    for i, source in enumerate((keys_ref, values_ref)):
        for g in range(heads):
            at = g * part + feats if i else heads * part + 16 + g * SLAB
            slabs.append(
                pltpu.make_async_copy(
                    source.at[0, pl.ds(first, SLAB), g * head_size : (g + 1) * head_size],
                    out_ref.at[at : at + SLAB, :],
                    slab_sem.at[i, g],
                )
            )
            slabs[-1].start()

    def project(unit):
        c, g = divmod(unit, heads)
        keys = keys_at[c * BLOCK : (c + 1) * BLOCK, g * head_size : (g + 1) * head_size]
        proj = lax.dot_general(turned_ref[g], keys, NT, preferred_element_type=jnp.float32)
        proj_ref[unit % 2] = proj.astype(jnp.bfloat16)

    def collect(unit):
        c, g = divmod(unit, heads)
        position = c * BLOCK + lax.broadcasted_iota(jnp.int32, (1, BLOCK), 1)
        live = jnp.where(position < begin, 1.0, 0.0).astype(jnp.bfloat16)
        mapped = feature(proj_ref[unit % 2]) * live
        some = [mapped[:, k * 128 : (k + 1) * 128] for k in range(BLOCK // 128)]
        while len(some) > 1:
            some = [x + y for x, y in zip(some[::2], some[1::2])]
        norm_ref[g] += some[0].astype(jnp.float32)
        values = values_at[c * BLOCK : (c + 1) * BLOCK, g * head_size : (g + 1) * head_size]
        state_ref[g] += jnp.dot(mapped, values, preferred_element_type=jnp.float32)

    project(0)
    for unit in range(chunks * heads):
        if unit + 1 < chunks * heads:
            project(unit + 1)
        collect(unit)

    back = 1.0 / (feats * feats)
    tile = []
    for g in range(heads):
        out_ref[g * part : g * part + feats, :] = (state_ref[g] * back).astype(jnp.bfloat16)
        sums = norm_ref[g]
        tile.append(jnp.sum(sums.T, axis=0, keepdims=True) * back)
    slot = first + lax.broadcasted_iota(jnp.int32, (1, head_size), 1)
    tile.append(jnp.zeros((MASK_ROW - heads, head_size), jnp.float32))
    tile.append(jnp.where((slot >= begin) & (slot < begin + WINDOW), 1.0, 0.0))
    tile.append(jnp.zeros((15 - MASK_ROW, head_size), jnp.float32))
    out_ref[heads * part : heads * part + 16, :] = jnp.concatenate(tile, axis=0).astype(jnp.bfloat16)
    for slab in slabs:
        slab.wait()


def prefill(keys, values, weight, lengths):
    heads, head_size, feats = weight.shape
    span, width = keys.shape[1:]
    vmem = pl.BlockSpec(memory_space=pltpu.VMEM)
    return pl.pallas_call(
        prefill_kernel,
        in_specs=[pl.BlockSpec(memory_space=pltpu.SMEM), vmem, vmem, vmem],
        out_specs=vmem,
        out_shape=jax.ShapeDtypeStruct((heads * feats + 16 + 2 * heads * SLAB, head_size), jnp.bfloat16),
        scratch_shapes=[
            pltpu.VMEM((heads, feats, head_size), jnp.bfloat16),
            pltpu.VMEM((2, feats, BLOCK), jnp.bfloat16),
            pltpu.VMEM((heads, feats, head_size), jnp.float32),
            pltpu.VMEM((heads, feats, 128), jnp.float32),
            pltpu.SemaphoreType.DMA((2, heads)),
        ],
        compiler_params=pltpu.CompilerParams(vmem_limit_bytes=16 * 1024 * 1024),
        cost_estimate=pl.CostEstimate(
            flops=4 * span * width * feats, bytes_accessed=4 * span * width, transcendentals=span * width
        ),
        name="prefill",
    )(
        lengths,
        pltpu.with_memory_space_constraint(keys, pltpu.MemorySpace.VMEM),
        pltpu.with_memory_space_constraint(values, pltpu.MemorySpace.VMEM),
        pltpu.with_memory_space_constraint(weight, pltpu.MemorySpace.VMEM),
    )


def share(query, phi, scale, ref, g, heads):
    head_size = query.shape[1]
    feats = phi.shape[1]
    part = feats + SLAB
    tile_at = heads * part
    tile = ref[tile_at : tile_at + 16, :].astype(jnp.float32)
    at = tile_at + 16 + g * SLAB
    keys = ref[at : at + SLAB, :]
    keys_wide = keys.astype(jnp.float32)
    key_scale = lax.rsqrt(jnp.mean((keys_wide * keys_wide).T, axis=0, keepdims=True) + EPS)
    score = lax.dot_general(query, keys, NT, preferred_element_type=jnp.float32) * scale[:, :SLAB] * key_scale
    weights = jnp.exp(score) * tile[MASK_ROW : MASK_ROW + 1, :SLAB]
    both = jnp.concatenate([phi, weights.astype(jnp.bfloat16)], axis=1)
    num = jnp.dot(both, ref[g * part : (g + 1) * part, :], preferred_element_type=jnp.float32)
    rest = jnp.zeros((query.shape[0], feats - SLAB), jnp.float32)
    den = phi.astype(jnp.float32) * tile[g : g + 1] + jnp.concatenate([weights, rest], axis=1)
    return num, jnp.sum(den, axis=-1, keepdims=True)


def begin_kernel(rows_ref, weight_ref, near_ref, query_ref, phi_ref, num_ref, den_ref, scale_ref):
    heads, head_size, feats = weight_ref.shape
    group = (rows_ref.shape[1] - 2 * heads * head_size) // (heads * head_size)
    keys_at = heads * group * head_size
    values_at = keys_at + heads * head_size
    ready = []
    for g in range(heads):
        query = jnp.concatenate(
            [
                rows_ref[:, (g * group + h) * head_size : (g * group + h + 1) * head_size]
                for h in range(group)
            ],
            axis=0,
        )
        wide = query.astype(jnp.float32)
        phi = feature(jnp.dot(query, weight_ref[g], preferred_element_type=jnp.float32)).astype(jnp.bfloat16)
        scale = (TAU / head_size) * lax.rsqrt(jnp.mean(wide * wide, axis=-1, keepdims=True) + EPS)
        own_key = rows_ref[:, keys_at + g * head_size : keys_at + (g + 1) * head_size].astype(jnp.float32)
        own_value = rows_ref[:, values_at + g * head_size : values_at + (g + 1) * head_size].astype(jnp.float32)
        own_key = own_key * lax.rsqrt(jnp.mean(own_key * own_key, axis=-1, keepdims=True) + EPS)
        own_score = jnp.sum(wide * jnp.concatenate([own_key] * group, axis=0), axis=-1, keepdims=True) * scale
        own_weight = jnp.exp(own_score)
        scale = jnp.broadcast_to(scale, query.shape)
        num, den = share(query, phi, scale, near_ref, g, heads)
        num += own_weight.astype(jnp.bfloat16).astype(jnp.float32) * jnp.concatenate([own_value] * group, axis=0)
        ready.append((query, phi, num, den + own_weight, scale))
    for g, (query, phi, num, den, scale) in enumerate(ready):
        query_ref[g] = query
        phi_ref[g] = phi
        num_ref[g] = num
        den_ref[g] = jnp.broadcast_to(den, num.shape)
        scale_ref[g] = scale


def end_kernel(query_ref, phi_ref, num_ref, den_ref, scale_ref, far_ref, *out_refs):
    heads, asked, head_size = query_ref.shape
    each, width = out_refs[0].shape
    group = width // (heads * head_size)
    count = asked // group
    ready = []
    for g in range(heads):
        num, den = share(query_ref[g], phi_ref[g], scale_ref[g], far_ref, g, heads)
        ready.append(((num_ref[g] + num) / (den_ref[g] + den)).astype(jnp.bfloat16))
    for g, result in enumerate(ready):
        for h in range(group):
            at = (g * group + h) * head_size
            for k, out_ref in enumerate(out_refs):
                start = h * count + k * each
                out_ref[:, at : at + head_size] = result[start : start + each]


def begin(rows, weight, near):
    heads, head_size, feats = weight.shape
    count = rows.shape[0]
    group = (rows.shape[1] - 2 * heads * head_size) // (heads * head_size)
    shape = (heads, group * count, head_size)
    vmem = pl.BlockSpec(memory_space=pltpu.VMEM)
    return pl.pallas_call(
        begin_kernel,
        in_specs=[vmem] * 3,
        out_specs=[vmem] * 5,
        out_shape=[jax.ShapeDtypeStruct(shape, jnp.bfloat16)] * 2 + [jax.ShapeDtypeStruct(shape, jnp.float32)] * 3,
        compiler_params=pltpu.CompilerParams(vmem_limit_bytes=32 * 1024 * 1024),
        cost_estimate=pl.CostEstimate(
            flops=6 * count * rows.shape[1] * feats, bytes_accessed=4 * rows.size, transcendentals=2 * rows.size
        ),
        name="begin",
    )(rows, weight, near)


def end(started, far, count, width, parts):
    vmem = pl.BlockSpec(memory_space=pltpu.VMEM)
    return pl.pallas_call(
        end_kernel,
        in_specs=[vmem] * 6,
        out_specs=[vmem] * parts,
        out_shape=[jax.ShapeDtypeStruct((count, width), jnp.bfloat16)] * parts,
        compiler_params=pltpu.CompilerParams(vmem_limit_bytes=32 * 1024 * 1024),
        cost_estimate=pl.CostEstimate(
            flops=4 * started[0].size * 128, bytes_accessed=4 * started[0].size, transcendentals=started[0].size
        ),
        name="end",
    )(*started, far)


def body(
    sects, prompt_keys, prompt_values, lengths, feature_weight, queries, new_keys, new_values, row_prompt
):
    sub = lax.axis_index("sub")
    sect = lax.axis_index("sect")
    steps = list(range(1, sects))
    steps[:2] = steps[:2][::-1]
    mine = pack(queries, new_keys, new_values)
    ask = shifted if sects == 4 else partner
    asked = {k: lax.ppermute(mine, "sect", [(ask(i, k, sects), i) for i in range(sects)]) for k in steps}
    if sects == 4:
        odd = (sect & 1) == 1
        asked[1], asked[3] = jnp.where(odd, asked[3], asked[1]), jnp.where(odd, asked[1], asked[3])
    blocks = [mine] + [asked[k] for k in steps]
    near = prefill(prompt_keys, prompt_values, feature_weight, lengths)
    far = lax.ppermute(near, "sub", [(0, 1), (1, 0)])
    started = begin(jnp.concatenate(blocks, axis=0), feature_weight, near)
    results = end(started, far, *queries.shape, sects)
    results = dict(zip([0] + steps, results))

    count = queries.shape[0]
    first_row = (sect * lax.axis_size("sub") + sub) * count
    prompts = lax.dynamic_slice_in_dim(row_prompt, first_row, count, 0)
    out = results[0]
    for k in range(1, sects):
        result = lax.ppermute(results[k], "sect", [(i, partner(i, k, sects)) for i in range(sects)])
        source = partner(sect, k if paired(sects) else sects - k, sects)
        out = jnp.where((prompts == source)[:, None], result, out)
    return out


def solution(mesh):
    placed = (
        P(("parts", "sect"), "sub", "tp"),
        P(("parts", "sect"), "sub", "tp"),
        P(("parts", "sect")),
        P("tp", None, None),
        P(("parts", "sect", "sub"), "tp"),
        P(("parts", "sect", "sub"), "tp"),
        P(("parts", "sect", "sub"), "tp"),
        P("parts"),
    )
    return jax.shard_map(
        functools.partial(body, mesh.shape["sect"]),
        mesh=mesh,
        in_specs=placed,
        out_specs=P(("parts", "sect", "sub"), "tp"),
        check_vma=False,
    )
```

```python
import functools

import jax
import jax.numpy as jnp
from jax import lax
from jax.experimental import pallas as pl
from jax.experimental.pallas import tpu as pltpu
from jax.sharding import PartitionSpec as P

WINDOW = 64
TAU = 10.0
EPS = 1e-06
BLOCK = 512
NT = (((1,), (1,)), ((), ()))


def paired(sects):
    return sects & (sects - 1) == 0


def shifted(sect, k, sects):
    return (sect + k) % sects


def partner(sect, k, sects):
    return sect ^ k if paired(sects) else shifted(sect, k, sects)


def feature(proj):
    return jnp.maximum(proj, 0.0) + jnp.exp(jnp.minimum(proj, 0.0))


def pack_kernel(queries_ref, keys_ref, values_ref, out_ref, sems):
    copies, at = [], 0
    for i, ref in enumerate((queries_ref, keys_ref, values_ref)):
        size = ref.shape[1]
        copies.append(pltpu.make_async_copy(ref, out_ref.at[:, at : at + size], sems.at[i]))
        copies[-1].start()
        at += size
    for copy in copies:
        copy.wait()


def pack(queries, new_keys, new_values):
    width = queries.shape[1] + 2 * new_keys.shape[1]
    arrays = [pltpu.with_memory_space_constraint(x, pltpu.MemorySpace.HBM) for x in (queries, new_keys, new_values)]
    return pl.pallas_call(
        pack_kernel,
        in_specs=[pl.BlockSpec(memory_space=pltpu.MemorySpace.HBM)] * 3,
        out_specs=pl.BlockSpec(memory_space=pltpu.VMEM),
        out_shape=jax.ShapeDtypeStruct((queries.shape[0], width), jnp.bfloat16),
        scratch_shapes=[pltpu.SemaphoreType.DMA((3,))],
        compiler_params=pltpu.CompilerParams(vmem_limit_bytes=8 * 1024 * 1024),
        cost_estimate=pl.CostEstimate(flops=10**10, bytes_accessed=2**25, transcendentals=0),
        name="pack",
    )(*arrays)


SLAB = WINDOW + 16
MASK_ROW = 8


def prefill_kernel(
    lengths_ref, keys_ref, values_ref, weight_ref, out_ref,
    turned_ref, proj_ref, state_ref, norm_ref,
    slab_sem,
):
    heads, head_size, feats = weight_ref.shape
    span = keys_ref.shape[1]
    keys_at, values_at = keys_ref.at[0], values_ref.at[0]
    chunks = span // BLOCK
    state_ref[...] = jnp.zeros_like(state_ref)
    norm_ref[...] = jnp.zeros_like(norm_ref)
    for g in range(heads):
        turned_ref[g] = weight_ref[g].astype(jnp.float32).T.astype(jnp.bfloat16)

    begin = lengths_ref[0] - WINDOW - lax.axis_index("sub") * span
    first = jnp.clip(begin, 0, span - SLAB)
    first = pl.multiple_of(first - lax.rem(first, 16), 16)
    part = feats + SLAB
    slabs = []
    for i, source in enumerate((keys_ref, values_ref)):
        for g in range(heads):
            at = g * part + feats if i else heads * part + 16 + g * SLAB
            slabs.append(
                pltpu.make_async_copy(
                    source.at[0, pl.ds(first, SLAB), g * head_size : (g + 1) * head_size],
                    out_ref.at[at : at + SLAB, :],
                    slab_sem.at[i, g],
                )
            )
            slabs[-1].start()

    def project(unit):
        c, g = divmod(unit, heads)
        keys = keys_at[c * BLOCK : (c + 1) * BLOCK, g * head_size : (g + 1) * head_size]
        proj = lax.dot_general(turned_ref[g], keys, NT, preferred_element_type=jnp.float32)
        proj_ref[unit % 2] = proj.astype(jnp.bfloat16)

    def collect(unit):
        c, g = divmod(unit, heads)
        position = c * BLOCK + lax.broadcasted_iota(jnp.int32, (1, BLOCK), 1)
        live = jnp.where(position < begin, 1.0, 0.0).astype(jnp.bfloat16)
        mapped = feature(proj_ref[unit % 2]) * live
        some = [mapped[:, k * 128 : (k + 1) * 128] for k in range(BLOCK // 128)]
        while len(some) > 1:
            some = [x + y for x, y in zip(some[::2], some[1::2])]
        norm_ref[g] += some[0].astype(jnp.float32)
        values = values_at[c * BLOCK : (c + 1) * BLOCK, g * head_size : (g + 1) * head_size]
        state_ref[g] += jnp.dot(mapped, values, preferred_element_type=jnp.float32)

    project(0)
    for unit in range(chunks * heads):
        if unit + 1 < chunks * heads:
            project(unit + 1)
        collect(unit)

    back = 1.0 / (feats * feats)
    tile = []
    for g in range(heads):
        out_ref[g * part : g * part + feats, :] = (state_ref[g] * back).astype(jnp.bfloat16)
        sums = norm_ref[g]
        tile.append(jnp.sum(sums.T, axis=0, keepdims=True) * back)
    slot = first + lax.broadcasted_iota(jnp.int32, (1, head_size), 1)
    tile.append(jnp.zeros((MASK_ROW - heads, head_size), jnp.float32))
    tile.append(jnp.where((slot >= begin) & (slot < begin + WINDOW), 1.0, 0.0))
    tile.append(jnp.zeros((15 - MASK_ROW, head_size), jnp.float32))
    out_ref[heads * part : heads * part + 16, :] = jnp.concatenate(tile, axis=0).astype(jnp.bfloat16)
    for slab in slabs:
        slab.wait()


def prefill(keys, values, weight, lengths):
    heads, head_size, feats = weight.shape
    span, width = keys.shape[1:]
    vmem = pl.BlockSpec(memory_space=pltpu.VMEM)
    return pl.pallas_call(
        prefill_kernel,
        in_specs=[pl.BlockSpec(memory_space=pltpu.SMEM), vmem, vmem, vmem],
        out_specs=vmem,
        out_shape=jax.ShapeDtypeStruct((heads * feats + 16 + 2 * heads * SLAB, head_size), jnp.bfloat16),
        scratch_shapes=[
            pltpu.VMEM((heads, feats, head_size), jnp.bfloat16),
            pltpu.VMEM((2, feats, BLOCK), jnp.bfloat16),
            pltpu.VMEM((heads, feats, head_size), jnp.float32),
            pltpu.VMEM((heads, feats, 128), jnp.float32),
            pltpu.SemaphoreType.DMA((2, heads)),
        ],
        compiler_params=pltpu.CompilerParams(vmem_limit_bytes=16 * 1024 * 1024),
        cost_estimate=pl.CostEstimate(
            flops=4 * span * width * feats, bytes_accessed=4 * span * width, transcendentals=span * width
        ),
        name="prefill",
    )(
        lengths,
        pltpu.with_memory_space_constraint(keys, pltpu.MemorySpace.VMEM),
        pltpu.with_memory_space_constraint(values, pltpu.MemorySpace.VMEM),
        pltpu.with_memory_space_constraint(weight, pltpu.MemorySpace.VMEM),
    )


def share(query, phi, scale, ref, g, heads):
    head_size = query.shape[1]
    feats = phi.shape[1]
    part = feats + SLAB
    tile_at = heads * part
    tile = ref[tile_at : tile_at + 16, :].astype(jnp.float32)
    at = tile_at + 16 + g * SLAB
    keys = ref[at : at + SLAB, :]
    keys_wide = keys.astype(jnp.float32)
    key_scale = lax.rsqrt(jnp.mean((keys_wide * keys_wide).T, axis=0, keepdims=True) + EPS)
    score = lax.dot_general(query, keys, NT, preferred_element_type=jnp.float32) * scale[:, :SLAB] * key_scale
    weights = jnp.exp(score) * tile[MASK_ROW : MASK_ROW + 1, :SLAB]
    both = jnp.concatenate([phi, weights.astype(jnp.bfloat16)], axis=1)
    num = jnp.dot(both, ref[g * part : (g + 1) * part, :], preferred_element_type=jnp.float32)
    rest = jnp.zeros((query.shape[0], feats - SLAB), jnp.float32)
    den = phi.astype(jnp.float32) * tile[g : g + 1] + jnp.concatenate([weights, rest], axis=1)
    return num, jnp.sum(den, axis=-1, keepdims=True)


def begin_kernel(rows_ref, weight_ref, near_ref, query_ref, phi_ref, num_ref, den_ref, scale_ref):
    heads, head_size, feats = weight_ref.shape
    group = (rows_ref.shape[1] - 2 * heads * head_size) // (heads * head_size)
    keys_at = heads * group * head_size
    values_at = keys_at + heads * head_size
    ready = []
    for g in range(heads):
        query = jnp.concatenate(
            [
                rows_ref[:, (g * group + h) * head_size : (g * group + h + 1) * head_size]
                for h in range(group)
            ],
            axis=0,
        )
        wide = query.astype(jnp.float32)
        phi = feature(jnp.dot(query, weight_ref[g], preferred_element_type=jnp.float32)).astype(jnp.bfloat16)
        scale = (TAU / head_size) * lax.rsqrt(jnp.mean(wide * wide, axis=-1, keepdims=True) + EPS)
        own_key = rows_ref[:, keys_at + g * head_size : keys_at + (g + 1) * head_size].astype(jnp.float32)
        own_value = rows_ref[:, values_at + g * head_size : values_at + (g + 1) * head_size].astype(jnp.float32)
        own_key = own_key * lax.rsqrt(jnp.mean(own_key * own_key, axis=-1, keepdims=True) + EPS)
        own_score = jnp.sum(wide * jnp.concatenate([own_key] * group, axis=0), axis=-1, keepdims=True) * scale
        own_weight = jnp.exp(own_score)
        scale = jnp.broadcast_to(scale, query.shape)
        num, den = share(query, phi, scale, near_ref, g, heads)
        num += own_weight.astype(jnp.bfloat16).astype(jnp.float32) * jnp.concatenate([own_value] * group, axis=0)
        ready.append((query, phi, num, den + own_weight, scale))
    for g, (query, phi, num, den, scale) in enumerate(ready):
        query_ref[g] = query
        phi_ref[g] = phi
        num_ref[g] = num
        den_ref[g] = jnp.broadcast_to(den, num.shape)
        scale_ref[g] = scale


def end_kernel(query_ref, phi_ref, num_ref, den_ref, scale_ref, far_ref, *out_refs):
    heads, asked, head_size = query_ref.shape
    each, width = out_refs[0].shape
    group = width // (heads * head_size)
    count = asked // group
    ready = []
    for g in range(heads):
        num, den = share(query_ref[g], phi_ref[g], scale_ref[g], far_ref, g, heads)
        ready.append(((num_ref[g] + num) / (den_ref[g] + den)).astype(jnp.bfloat16))
    for g, result in enumerate(ready):
        for h in range(group):
            at = (g * group + h) * head_size
            for k, out_ref in enumerate(out_refs):
                start = h * count + k * each
                out_ref[:, at : at + head_size] = result[start : start + each]


def begin(rows, weight, near):
    heads, head_size, feats = weight.shape
    count = rows.shape[0]
    group = (rows.shape[1] - 2 * heads * head_size) // (heads * head_size)
    shape = (heads, group * count, head_size)
    vmem = pl.BlockSpec(memory_space=pltpu.VMEM)
    return pl.pallas_call(
        begin_kernel,
        in_specs=[vmem] * 3,
        out_specs=[vmem] * 5,
        out_shape=[jax.ShapeDtypeStruct(shape, jnp.bfloat16)] * 2 + [jax.ShapeDtypeStruct(shape, jnp.float32)] * 3,
        compiler_params=pltpu.CompilerParams(vmem_limit_bytes=32 * 1024 * 1024),
        cost_estimate=pl.CostEstimate(
            flops=6 * count * rows.shape[1] * feats, bytes_accessed=4 * rows.size, transcendentals=2 * rows.size
        ),
        name="begin",
    )(rows, weight, near)


def end(started, far, count, width, parts):
    vmem = pl.BlockSpec(memory_space=pltpu.VMEM)
    return pl.pallas_call(
        end_kernel,
        in_specs=[vmem] * 6,
        out_specs=[vmem] * parts,
        out_shape=[jax.ShapeDtypeStruct((count, width), jnp.bfloat16)] * parts,
        compiler_params=pltpu.CompilerParams(vmem_limit_bytes=32 * 1024 * 1024),
        cost_estimate=pl.CostEstimate(
            flops=4 * started[0].size * 128, bytes_accessed=4 * started[0].size, transcendentals=started[0].size
        ),
        name="end",
    )(*started, far)


def body(
    sects, prompt_keys, prompt_values, lengths, feature_weight, queries, new_keys, new_values, row_prompt
):
    sub = lax.axis_index("sub")
    sect = lax.axis_index("sect")
    steps = list(range(1, sects))
    steps[:2] = steps[:2][::-1]
    mine = pack(queries, new_keys, new_values)
    ask = shifted if sects == 4 else partner
    asked = {k: lax.ppermute(mine, "sect", [(ask(i, k, sects), i) for i in range(sects)]) for k in steps}
    if sects == 4:
        odd = (sect & 1) == 1
        asked[1], asked[3] = jnp.where(odd, asked[3], asked[1]), jnp.where(odd, asked[1], asked[3])
    blocks = [mine] + [asked[k] for k in steps]
    near = prefill(prompt_keys, prompt_values, feature_weight, lengths)
    far = lax.ppermute(near, "sub", [(0, 1), (1, 0)])
    started = begin(jnp.concatenate(blocks, axis=0), feature_weight, near)
    results = end(started, far, *queries.shape, sects)
    results = dict(zip([0] + steps, results))

    count = queries.shape[0]
    first_row = (sect * lax.axis_size("sub") + sub) * count
    prompts = lax.dynamic_slice_in_dim(row_prompt, first_row, count, 0)
    out = results[0]
    for k in range(1, sects):
        result = lax.ppermute(results[k], "sect", [(i, partner(i, k, sects)) for i in range(sects)])
        source = partner(sect, k if paired(sects) else sects - k, sects)
        out = jnp.where((prompts == source)[:, None], result, out)
    return out


def solution(mesh):
    placed = (
        P(("parts", "sect"), "sub", "tp"),
        P(("parts", "sect"), "sub", "tp"),
        P(("parts", "sect")),
        P("tp", None, None),
        P(("parts", "sect", "sub"), "tp"),
        P(("parts", "sect", "sub"), "tp"),
        P(("parts", "sect", "sub"), "tp"),
        P("parts"),
    )
    return jax.shard_map(
        functools.partial(body, mesh.shape["sect"]),
        mesh=mesh,
        in_specs=placed,
        out_specs=P(("parts", "sect", "sub"), "tp"),
        check_vma=False,
    )
```
